32 devices in a mesh: groups: 2 (over y), cand: 4 (over z), eig: 2 (over x), rep: 2 (over core).
Axes of the slice: x: 2, y: 2, z: 4, core: 2. Of those that a mesh axis runs over, the one named last changes fastest.
Arguments:
- acts: bfloat16 [4096, 5120], P(('groups', 'cand'), ('eig', 'rep')), parts along dimension 0, may hold values from -6 to 6
- grads: bfloat16 [4096, 27648], P(('groups', 'cand'), ('eig', 'rep')), parts along dimension 0, may hold values from -6 to 6
- basis_in: bfloat16 [10240, 512], P(('groups', 'eig', 'rep'), 'cand'), parts along dimension 0, may hold values from -0.078125 to 0.078125
- basis_out: bfloat16 [55296, 512], P(('groups', 'eig', 'rep'), 'cand'), parts along dimension 0, may hold values from -0.0390625 to 0.0390625
- eigval: float32 [1024, 512], P(('groups', 'cand', 'eig', 'rep')), parts along dimension 0, may hold values from 0.5 to 5
- test_grads: bfloat16 [128, 512, 512], P('groups', ('cand', 'eig', 'rep')), parts along dimension 0, may hold values from -0.005859375 to 0.005859375
- pair_tiles: int32 [16], P('groups'), parts along dimension 0, may hold values from 1 to 4, 16 in all
- last_rows: int32 [16], P('groups'), parts along dimension 0, may hold values from 1 to 128
Outputs:
- scores: float32 [16, 64], P(('groups', 'cand'), ('eig', 'rep')), parts along dimension 0
The draws below stay inside these ranges and needn't reach their ends.
There are 2 independent parts, one for each index of `groups`. The reference program is written for one: setup_inputs(seed, part) draws one part's arguments, and reference() takes and returns one part's arrays. A program takes and returns all parts, laid end to end along the dimension named above; each array names one. Nothing has to cross between parts.
Inputs may be any that keep to these rules, and one draw needn't show every extreme that they name: `pair_tiles`: 8 pairs laid end to end over the 16 tiles in order; the counts sum to 16 and some pair has 4 tiles. `last_rows`: rows of a pair's last tile past this count are padding.
All inputs are finite; a program needn't handle non-finite values.
Results may differ from the reference program's by a relative error of at most 0.006.
Values may be sent and summed in bfloat16 or wider, within the bound.
No kernel may reach another device: no remote copies, remote signals or barrier semaphores. Data moves between devices by JAX's collectives and lax.ppermute only.
A program may use at most 64 MiB of HBM per device.

```python
import math
import jax
import jax.numpy as jnp
import numpy as np
from jax import lax

D = 5120
F = 27648
EA = 512
ES = 512
TILE = 128
PAIR_MAX = 4
NTEST = 64
NTILES = 16
TOKENS = 2048
NPAIRS = 8


def plant(entries, stream_key, least, largest):
    index_at = [jax.random.randint(jax.random.fold_in(stream_key, axis), (), 0, length) for axis, length in enumerate(entries.shape)]
    longest = entries.shape.index(max(entries.shape))
    beside = index_at[:longest] + [(index_at[longest] + 1) % entries.shape[longest]] + index_at[longest + 1:]
    return entries.at[tuple(index_at)].set(least).at[tuple(beside)].set(largest)


def block_scale(rng, extent, pieces, low, largest):
    gain, own = 1.0, jax.random.fold_in(rng, 6)
    for axis_at, blocks in pieces:
        draws = jnp.exp(jax.random.uniform(jax.random.fold_in(own, axis_at), (blocks,), jnp.float32, low / len(pieces), largest / len(pieces)))
        gain = gain * jnp.repeat(draws, extent[axis_at] // blocks).reshape([-1 if axis == axis_at else 1 for axis in range(len(extent))])
    return gain


def split_up(amount, total, most, lean):
    portions = [(1 << 20) // math.isqrt(grade ** lean) + 1 for grade in range(2, amount + 1)]
    rest, holding = total - most - (amount - 1), [1] * (amount - 1)
    while rest > 0:
        candidates = [i for i in range(amount - 1) if holding[i] < most]
        mass, budget = sum([portions[i] for i in candidates]), rest
        for i in candidates:
            extra = min(most - holding[i], max(1, budget * portions[i] // mass), rest)
            holding[i] = holding[i] + extra
            rest = rest - extra
    return np.array([most] + holding)


def ragged(stream_key, number_of, total, most, skew):
    if number_of == 2:
        one = jax.random.randint(stream_key, (), max(1, total - most), min(most, total - 1) + 1)
        return jnp.stack([one, total - one])
    sizes = jnp.asarray(split_up(number_of, total, most, skew), jnp.int32)
    pairs = (number_of - 1) // 2
    giver, receiver = sizes[1:1 + 2 * pairs:2], sizes[2:2 + 2 * pairs:2]
    room = jnp.minimum(giver - 1, most - receiver)
    shifted = jax.random.randint(jax.random.fold_in(stream_key, 1), (pairs,), 0, 1 << 20) % (room + 1)
    sizes = sizes.at[1:1 + 2 * pairs:2].set(giver - shifted).at[2:2 + 2 * pairs:2].set(receiver + shifted)
    return sizes[jax.random.permutation(jax.random.fold_in(stream_key, 2), number_of)]


def gaussian(stream_key, dims, spread, most, cuts=(), kind=jnp.bfloat16):
    entries = spread * jax.random.normal(stream_key, dims, jnp.float32)
    if cuts:
        entries = entries * block_scale(stream_key, dims, cuts, -0.22, 0.18)
    return jnp.clip(entries, -most, most).astype(kind)


def setup_inputs(seed: int = 0, part: int = 0) -> dict:
    key_list = jax.random.split(jax.random.key(seed), 9)
    part_splits = jax.random.split(jax.random.fold_in(key_list[8], part), 9)
    acts = gaussian(part_splits[0], (TOKENS, D), 1.0, 6.0, ((0, 4), (1, 4)))
    grads = gaussian(part_splits[1], (TOKENS, F), 1.0, 6.0, ((0, 4), (1, 4)))
    basis_in = gaussian(part_splits[2], (D, EA), D ** -0.5, 0.078125, ((0, 4), (1, 4)))
    basis_out = gaussian(part_splits[3], (F, ES), F ** -0.5, 0.0390625, ((0, 4), (1, 4)))
    eigval = jnp.clip(jnp.exp(math.log(5.0) - 2.3025851 * jax.random.uniform(part_splits[4], (ES, EA), jnp.float32) ** block_scale(part_splits[4], (ES, EA), ((0, 16),), -0.2, 0.2)), 0.5, 5.0)
    test_grads = gaussian(part_splits[5], (NTEST, ES, EA), (0.2 * ES ** -1), 0.005859375, ((1, 16),))
    pair_tiles = ragged(part_splits[6], NPAIRS, NTILES, PAIR_MAX, 1).astype(jnp.int32)
    last_rows = plant(jax.random.randint(part_splits[7], (NPAIRS,), 1, TILE + 1), jax.random.fold_in(part_splits[7], 1), 1, TILE).astype(jnp.int32)
    return {"acts": acts, "grads": grads, "basis_in": basis_in, "basis_out": basis_out, "eigval": eigval, "test_grads": test_grads, "pair_tiles": pair_tiles, "last_rows": last_rows}


damping = 0.01


def tile_layout(pair_tiles, last_rows, first_tile, count):
    tiles = first_tile + jnp.arange(count, dtype=jnp.int32)
    ends = jnp.cumsum(pair_tiles).astype(jnp.int32)
    owner = jnp.sum((ends[None, :] <= tiles[:, None]).astype(jnp.int32), axis=1).astype(jnp.int32)
    onehot = owner[:, None] == jnp.arange(pair_tiles.shape[0], dtype=jnp.int32)[None, :]
    last_of = jnp.sum(jnp.where(onehot, last_rows[None, :], 0), axis=1)
    end_of = jnp.sum(jnp.where(onehot, ends[None, :], 0), axis=1)
    limit = jnp.where(tiles == end_of - 1, last_of, TILE)
    rowmask = jnp.arange(TILE, dtype=jnp.int32)[None, :] < limit[:, None]
    return rowmask, onehot


def reference(acts, grads, basis_in, basis_out, eigval, test_grads, pair_tiles, last_rows):
    rot_in = jnp.dot(acts, basis_in, preferred_element_type=jnp.float32).astype(jnp.bfloat16)
    rot_out = jnp.dot(grads, basis_out, preferred_element_type=jnp.float32).astype(jnp.bfloat16)
    count = rot_in.shape[0] // TILE
    rowmask, onehot = tile_layout(pair_tiles, last_rows, 0, count)
    masked = rot_out.reshape(count, TILE, ES) * rowmask[:, :, None].astype(jnp.bfloat16)
    prods = jnp.einsum("tre,tra->tea", masked.astype(jnp.float32),
                       rot_in.reshape(count, TILE, EA).astype(jnp.float32)).astype(jnp.bfloat16)
    precond = (test_grads.astype(jnp.float32) / (eigval + damping)).astype(jnp.bfloat16)
    tile_scores = jnp.einsum("tea,jea->tj", prods.astype(jnp.float32), precond.astype(jnp.float32))
    return jnp.dot(onehot.astype(jnp.float32).T, tile_scores, precision=lax.Precision.HIGHEST)
```

```python
import jax
import jax.numpy as jnp
from jax import lax
from jax.sharding import PartitionSpec as P

TILE = 128
CHUNKS = 3
FEAT = ("eig", "rep")

damping = 0.01


def tile_layout(pair_tiles, last_rows, first_tile, count, tile_rows):
    tiles = first_tile + jnp.arange(count, dtype=jnp.int32)
    ends = jnp.cumsum(pair_tiles)
    owner = jnp.sum((ends[None, :] <= tiles[:, None]).astype(jnp.int32), axis=1)
    onehot = owner[:, None] == jnp.arange(pair_tiles.shape[0], dtype=jnp.int32)[None, :]
    last_of = jnp.sum(jnp.where(onehot, last_rows[None, :], 0), axis=1)
    end_of = jnp.sum(jnp.where(onehot, ends[None, :], 0), axis=1)
    limit = jnp.where(tiles == end_of - 1, last_of, tile_rows)
    rowmask = jnp.arange(tile_rows, dtype=jnp.int32)[None, :] < limit[:, None]
    return (rowmask, onehot)


def hop(x, by):
    n = lax.axis_size("cand")
    return lax.ppermute(x, "cand", [(i, i + by) for i in range(n) if 0 <= i + by < n])


def swap(x, step):
    n = lax.axis_size(FEAT)
    return lax.ppermute(x, FEAT, [(i, i ^ step) for i in range(n)])


def scatter_sum(part, axis):
    n = lax.axis_size(FEAT)
    me = lax.axis_index(FEAT)
    width = part.shape[axis] // n
    total = lax.dynamic_slice_in_dim(part, me * width, width, axis)
    sent = part.astype(jnp.bfloat16)
    for step in range(1, n):
        block = lax.dynamic_slice_in_dim(sent, (me ^ step) * width, width, axis)
        total = total + swap(block, step).astype(jnp.float32)
    return total


def gather_rows(x):
    n = lax.axis_size(FEAT)
    me = lax.axis_index(FEAT)
    rows = x.shape[0]
    whole = jnp.zeros((rows * n,) + x.shape[1:], x.dtype)
    whole = lax.dynamic_update_slice_in_dim(whole, x, me * rows, 0)
    for step in range(1, n):
        whole = lax.dynamic_update_slice_in_dim(whole, swap(x, step), (me ^ step) * rows, 0)
    return whole


def spread(x):
    n = lax.axis_size("cand")
    found = {}
    up, down = x, x
    for k in range(1, n):
        up, down = hop(up, 1), hop(down, -1)
        found[k], found[-k] = up, down
    return found


def dot_t(basis, rows):
    return lax.dot_general(basis, rows, (((0,), (1,)), ((), ())), preferred_element_type=jnp.float32)


def line_plan(acts, grads, basis_in, basis_out, eigval, test_grads, pair_tiles, last_rows):
    ncand = lax.axis_size("cand")
    nfeat = lax.axis_size(FEAT)
    plane = lax.axis_index("cand")
    tok_rows = acts.shape[0]
    cols = basis_in.shape[1]
    width_in = cols * ncand
    tiles_here = tok_rows // TILE
    slim = basis_out.shape[1] // nfeat

    ins = {0: basis_in, **spread(basis_in)}
    depth = basis_out.shape[0] // CHUNKS
    pieces = [basis_out[i * depth : (i + 1) * depth] for i in range(CHUNKS)]
    outs = [{0: piece, **spread(piece)} for piece in pieces]

    part_in = jnp.zeros((tok_rows, width_in), jnp.float32)
    for k in range(ncand):
        part = jnp.dot(acts, ins[k], preferred_element_type=jnp.float32)
        if k:
            part = part + jnp.dot(acts, ins[k - ncand], preferred_element_type=jnp.float32)
        part_in = lax.dynamic_update_slice_in_dim(
            part_in, part, lax.rem(plane - k + ncand, ncand) * cols, 1
        )
    rot_in = gather_rows(scatter_sum(part_in, 0).astype(jnp.bfloat16))
    rot_in = rot_in.reshape(tiles_here, TILE, width_in)

    rowmask, ignored = tile_layout(pair_tiles, last_rows, plane * tiles_here, tiles_here, TILE)
    keep = rowmask.reshape(1, tok_rows).astype(jnp.bfloat16)
    precond = (test_grads.astype(jnp.float32) / (eigval + damping)).astype(jnp.bfloat16)

    def partial_out(at):
        total = None
        for i in range(CHUNKS):
            term = dot_t(outs[i][at], grads[:, i * depth : (i + 1) * depth])
            total = term if total is None else total + term
        return total

    def tile_prods(part):
        rot_out = scatter_sum(part, 0).astype(jnp.bfloat16) * keep
        return jnp.einsum(
            "etr,tra->tea",
            rot_out.reshape(slim, tiles_here, TILE),
            rot_in,
            preferred_element_type=jnp.float32,
        ).astype(jnp.bfloat16)

    def pair_scores(prods, source):
        scores = jnp.einsum("tea,jea->tj", prods, precond, preferred_element_type=jnp.float32)
        ignored_mask, onehot = tile_layout(
            pair_tiles, last_rows, source * tiles_here, tiles_here, TILE
        )
        return jnp.sum(jnp.where(onehot[:, :, None], scores[:, None, :], 0.0), axis=0)

    total = pair_scores(tile_prods(partial_out(0)), plane)
    for k in range(1, ncand):
        if 2 * k < ncand:
            total = total + pair_scores(hop(tile_prods(partial_out(k)), -k), plane + k)
            total = total + pair_scores(hop(tile_prods(partial_out(-k)), k), plane - k)
        else:
            prods = tile_prods(partial_out(k) + partial_out(-k))
            pairs = [(i, i - k) for i in range(k, ncand)] + [(i, i + k) for i in range(ncand - k)]
            back = lax.ppermute(prods, "cand", pairs)
            source = jnp.where(plane + k < ncand, plane + k, plane - k)
            total = total + pair_scores(back, source)

    mine = scatter_sum_small(total, FEAT, 1)
    return scatter_sum_small(mine, "cand", 0)


def scatter_sum_small(part, axis_name, axis):
    n = lax.axis_size(axis_name)
    me = lax.axis_index(axis_name)
    width = part.shape[axis] // n
    total = lax.dynamic_slice_in_dim(part, me * width, width, axis)
    for step in range(1, n):
        block = lax.dynamic_slice_in_dim(part, lax.rem(me + step, n) * width, width, axis)
        total = total + lax.ppermute(block, axis_name, [(i, (i + step) % n) for i in range(n)])
    return total


def gather_plan(acts, grads, basis_in, basis_out, eigval, test_grads, pair_tiles, last_rows):
    ncand = lax.axis_size("cand")
    nfeat = lax.axis_size(FEAT)
    tok_rows = acts.shape[0]
    width_in = basis_in.shape[1] * ncand
    width_out = basis_out.shape[1] * ncand
    slim = width_out // (ncand * nfeat)
    part_in = jnp.dot(
        acts,
        lax.all_gather(basis_in, "cand", axis=1, tiled=True),
        preferred_element_type=jnp.float32,
    )
    part_out = jnp.dot(
        grads,
        lax.all_gather(basis_out, "cand", axis=1, tiled=True),
        preferred_element_type=jnp.float32,
    )
    part_out = part_out.reshape(tok_rows, ncand, nfeat, slim).transpose(0, 2, 1, 3)
    part_out = part_out.reshape(tok_rows, nfeat * ncand * slim)
    summed_in, summed_out = lax.psum((part_in, part_out), FEAT)
    own = lax.dynamic_slice_in_dim(
        summed_out, lax.axis_index(FEAT) * (ncand * slim), ncand * slim, 1
    )
    rot_in = summed_in.astype(jnp.bfloat16)
    rot_out = own.astype(jnp.bfloat16)
    tiles_here = tok_rows // TILE
    rowmask, ignored = tile_layout(
        pair_tiles, last_rows, lax.axis_index("cand") * tiles_here, tiles_here, TILE
    )
    masked = rot_out.reshape(tiles_here, TILE, ncand * slim) * rowmask[:, :, None].astype(
        jnp.bfloat16
    )
    prods = jnp.einsum(
        "tre,tra->tea",
        masked,
        rot_in.reshape(tiles_here, TILE, width_in),
        preferred_element_type=jnp.float32,
    ).astype(jnp.bfloat16)
    prods = prods.reshape(tiles_here, ncand, slim, width_in)
    received = lax.all_to_all(prods, "cand", split_axis=1, concat_axis=0, tiled=True)
    all_tiles = received.shape[0]
    received = received.reshape(all_tiles, slim, width_in)
    precond = (test_grads.astype(jnp.float32) / (eigval + damping)).astype(jnp.bfloat16)
    tile_part = jnp.einsum("tea,jea->tj", received, precond, preferred_element_type=jnp.float32)
    ignored_mask, onehot = tile_layout(pair_tiles, last_rows, 0, all_tiles, TILE)
    pair_part = jnp.dot(onehot.astype(jnp.float32).T, tile_part, precision=lax.Precision.HIGHEST)
    npairs = pair_part.shape[0]
    ntest = pair_part.shape[1]
    total = lax.psum(pair_part, ("cand", "eig", "rep"))
    rows = lax.dynamic_slice_in_dim(
        total, lax.axis_index("cand") * (npairs // ncand), npairs // ncand, 0
    )
    return lax.dynamic_slice_in_dim(
        rows, lax.axis_index(FEAT) * (ntest // nfeat), ntest // nfeat, 1
    )


def solution(mesh):
    in_specs = (
        P(("groups", "cand"), ("eig", "rep")),
        P(("groups", "cand"), ("eig", "rep")),
        P(("groups", "eig", "rep"), "cand"),
        P(("groups", "eig", "rep"), "cand"),
        P(("groups", "cand", "eig", "rep"), None),
        P("groups", ("cand", "eig", "rep"), None),
        P("groups"),
        P("groups"),
    )
    out_specs = P(("groups", "cand"), ("eig", "rep"))
    per_device = line_plan if mesh.shape["cand"] <= 4 else gather_plan
    return jax.shard_map(
        per_device, mesh=mesh, in_specs=in_specs, out_specs=out_specs, check_vma=False
    )
```

```python
import jax
import jax.numpy as jnp
from jax import lax
from jax.sharding import PartitionSpec as P

TILE = 128
FEAT = ("eig", "rep")
SIDE = ((0, 1), (1, 0), (2, 3), (3, 2))
MIDDLE = ((0, 0), (1, 2), (2, 1), (3, 3))
FAR = ((0, 3), (3, 0), (1, 1), (2, 2))
TWO = ((0, 2), (2, 0), (1, 3), (3, 1))

damping = 0.01


def tile_layout(pair_tiles, last_rows, first_tile, count, tile_rows):
    tiles = first_tile + jnp.arange(count, dtype=jnp.int32)
    ends = jnp.cumsum(pair_tiles)
    owner = jnp.sum((ends[None, :] <= tiles[:, None]).astype(jnp.int32), axis=1)
    onehot = owner[:, None] == jnp.arange(pair_tiles.shape[0], dtype=jnp.int32)[None, :]
    last_of = jnp.sum(jnp.where(onehot, last_rows[None, :], 0), axis=1)
    end_of = jnp.sum(jnp.where(onehot, ends[None, :], 0), axis=1)
    limit = jnp.where(tiles == end_of - 1, last_of, tile_rows)
    rowmask = jnp.arange(tile_rows, dtype=jnp.int32)[None, :] < limit[:, None]
    return (rowmask, onehot)


def after(x, *earlier):
    return lax.optimization_barrier((x, *earlier))[0]


def swap(x, axis_name):
    return lax.ppermute(x, axis_name, [(0, 1), (1, 0)])


def halves(x, axis_name):
    first = lax.axis_index(axis_name) == 0
    low, high = x[0], x[1]
    return jnp.where(first, low, high), jnp.where(first, high, low)


def scatter_sum(part):
    keep, give = halves(part.transpose(2, 1, 0, 3, 4), "rep")
    keep = keep + swap(give, "rep")
    keep, give = halves(keep, "eig")
    return keep + swap(give, "eig")


def gather_rows(x):
    other = swap(x, "eig")
    first = lax.axis_index("eig") == 0
    both = jnp.stack([jnp.where(first, x, other), jnp.where(first, other, x)])
    other = swap(both, "rep")
    first = lax.axis_index("rep") == 0
    whole = jnp.stack([jnp.where(first, both, other), jnp.where(first, other, both)], axis=1)
    return whole.reshape((-1,) + x.shape[1:])


def dot_t(basis, rows):
    return lax.dot_general(basis, rows, (((0,), (1,)), ((), ())), preferred_element_type=jnp.float32)


def dot_tt(basis, columns):
    return lax.dot_general(
        basis, columns, (((0,), (0,)), ((), ())), preferred_element_type=jnp.float32
    )


def line_plan(acts, grads, basis_in, basis_out, eigval, test_grads, pair_tiles, last_rows):
    plane = lax.axis_index("cand")
    end = (plane == 0) | (plane == 3)
    eig, rep = lax.axis_size("eig"), lax.axis_size("rep")
    tok_rows = acts.shape[0]
    cols = basis_in.shape[1]
    width_in = 4 * cols
    tiles_here = tok_rows // TILE
    slim = cols // (eig * rep)
    depth = basis_out.shape[0] // 3
    rows_in = basis_in.shape[0]

    def pick(at_end, at_middle):
        return jnp.where(end, at_end, at_middle)

    def side(at_end, at_middle):
        return lax.ppermute(pick(at_end, at_middle), "cand", SIDE)

    def middle(x):
        return lax.ppermute(x, "cand", MIDDLE)

    own = [basis_out[i * depth : (i + 1) * depth] for i in range(3)]
    grad = [grads[:, i * depth : (i + 1) * depth] for i in range(3)]
    quarter = tok_rows // 4
    turned = [grad[0][i * quarter : (i + 1) * quarter].T for i in range(4)]

    s0 = lax.ppermute(basis_in, "cand", SIDE)
    m0 = middle(basis_in)
    s1 = lax.ppermute(own[1], "cand", SIDE)
    m1 = middle(after(s0, m0))
    s2 = side(after(own[0], s0), own[2])
    m2 = middle(after(own[1], m0))
    s3 = side(after(basis_out[3 * depth - 2 * rows_in :], s1), jnp.concatenate([m0, m1]))
    m3 = middle(after(own[2], m1))
    s4 = side(after(turned[0], s2), m2)
    m4 = middle(after(own[0], m2))
    s5 = side(after(turned[1], s3), m3)
    m5 = middle(after(s1, m3))
    s6 = side(after(turned[2], s4), m5)
    m6 = middle(after(s3[2 * rows_in - depth :], m4))
    s7 = side(after(turned[3], s5), m6)
    m7 = middle(after(s2, m5))

    in_b, in_c = pick(s3[:rows_in], m0), pick(s3[rows_in:], m1)
    at_b = jnp.where(end, plane ^ 2, plane ^ 3)
    at_c = jnp.where(end, plane ^ 3, plane ^ 2)
    part_in = jnp.zeros((tok_rows, width_in), jnp.float32)
    for shard, at in ((basis_in, plane), (s0, plane ^ 1), (in_b, at_b), (in_c, at_c)):
        part = jnp.dot(acts, shard, preferred_element_type=jnp.float32)
        part_in = lax.dynamic_update_slice_in_dim(part_in, part, at * cols, 1)
    part_in = part_in.reshape(1, eig, rep, tok_rows // (eig * rep), width_in)
    rot_in = gather_rows(scatter_sum(part_in)[0].astype(jnp.bfloat16))
    rot_in = rot_in.reshape(tiles_here, TILE, width_in)

    only_middle = jnp.where(end, 0.0, 1.0)

    def blocks(*parts):
        return jnp.stack([part.reshape(eig, rep, slim, part.shape[1]) for part in parts])

    part_own = dot_t(basis_out, grads)
    part_a = dot_t(s1, grad[1]) + dot_t(pick(s2, s3[2 * rows_in - depth :]), grad[2])
    part_a = part_a + only_middle * dot_t(s2, grad[0])
    sum_own, sum_a = scatter_sum(blocks(part_own, part_a))

    part_b = dot_t(pick(s4, m2), grad[1]) + dot_t(pick(s5, m3), grad[2])
    part_b = part_b + only_middle * dot_t(m4, grad[0])
    sum_b = scatter_sum(blocks(part_b))[0]

    part_c = dot_t(pick(s6, m5), grad[1]) + dot_t(pick(s7, m6), grad[2])
    part_c = part_c + only_middle * dot_t(m7, grad[0])
    theirs = [
        jnp.concatenate([dot_tt(shard, tokens) for tokens in (s4, s5, s6, s7)], axis=1)
        for shard in (own[0], m4, m7)
    ]
    sums = scatter_sum(blocks(part_c, *theirs))
    sum_c = sums[0]
    back = lax.ppermute(sums[1:], "cand", SIDE)
    back = jnp.where(end, back, 0.0)

    rowmask, ignored = tile_layout(pair_tiles, last_rows, plane * tiles_here, tiles_here, TILE)
    keep = rowmask.reshape(1, tok_rows).astype(jnp.bfloat16)
    precond = (test_grads.astype(jnp.float32) / (eigval + damping)).astype(jnp.bfloat16)

    def tile_prods(rot_out):
        return jnp.einsum(
            "etr,tra->tea",
            (rot_out.astype(jnp.bfloat16) * keep).reshape(slim, tiles_here, TILE),
            rot_in,
            preferred_element_type=jnp.float32,
        ).astype(jnp.bfloat16)

    def pair_scores(prods, source):
        scores = jnp.einsum("tea,jea->tj", prods, precond, preferred_element_type=jnp.float32)
        ignored_mask, onehot = tile_layout(
            pair_tiles, last_rows, source * tiles_here, tiles_here, TILE
        )
        return jnp.sum(jnp.where(onehot[:, :, None], scores[:, None, :], 0.0), axis=0)

    prods_a = tile_prods(sum_a + back[0])
    prods_b = tile_prods(sum_b + back[1])
    prods_c = tile_prods(sum_c + back[2])
    total = pair_scores(tile_prods(sum_own), plane)
    total = total + pair_scores(lax.ppermute(prods_a, "cand", SIDE), plane ^ 1)
    total = total + pair_scores(lax.ppermute(pick(prods_b, prods_c), "cand", TWO), plane ^ 2)
    three = [(0, 3), (3, 0), (1, 2), (2, 1)]
    total = total + pair_scores(lax.ppermute(pick(prods_c, prods_b), "cand", three), plane ^ 3)

    return final_sum(total)


def final_sum(total):
    npairs, ntest = total.shape
    mine = total.reshape(npairs, 2, 2, ntest // 4).transpose(2, 1, 0, 3)
    keep, give = halves(mine, "rep")
    keep = keep + swap(give, "rep")
    keep, give = halves(keep, "eig")
    keep = keep + swap(give, "eig")
    plane = lax.axis_index("cand")
    rows = npairs // 4
    result = lax.dynamic_slice_in_dim(keep, plane * rows, rows, 0)
    for step in range(1, 4):
        block = lax.dynamic_slice_in_dim(keep, (plane ^ step) * rows, rows, 0)
        result = result + lax.ppermute(block, "cand", [(i, i ^ step) for i in range(4)])
    return result


def gather_plan(acts, grads, basis_in, basis_out, eigval, test_grads, pair_tiles, last_rows):
    ncand = lax.axis_size("cand")
    nfeat = lax.axis_size(FEAT)
    tok_rows = acts.shape[0]
    width_in = basis_in.shape[1] * ncand
    width_out = basis_out.shape[1] * ncand
    slim = width_out // (ncand * nfeat)
    part_in = jnp.dot(
        acts,
        lax.all_gather(basis_in, "cand", axis=1, tiled=True),
        preferred_element_type=jnp.float32,
    )
    part_out = jnp.dot(
        grads,
        lax.all_gather(basis_out, "cand", axis=1, tiled=True),
        preferred_element_type=jnp.float32,
    )
    part_out = part_out.reshape(tok_rows, ncand, nfeat, slim).transpose(0, 2, 1, 3)
    part_out = part_out.reshape(tok_rows, nfeat * ncand * slim)
    summed_in, summed_out = lax.psum((part_in, part_out), FEAT)
    own = lax.dynamic_slice_in_dim(
        summed_out, lax.axis_index(FEAT) * (ncand * slim), ncand * slim, 1
    )
    rot_in = summed_in.astype(jnp.bfloat16)
    rot_out = own.astype(jnp.bfloat16)
    tiles_here = tok_rows // TILE
    rowmask, ignored = tile_layout(
        pair_tiles, last_rows, lax.axis_index("cand") * tiles_here, tiles_here, TILE
    )
    masked = rot_out.reshape(tiles_here, TILE, ncand * slim) * rowmask[:, :, None].astype(
        jnp.bfloat16
    )
    prods = jnp.einsum(
        "tre,tra->tea",
        masked,
        rot_in.reshape(tiles_here, TILE, width_in),
        preferred_element_type=jnp.float32,
    ).astype(jnp.bfloat16)
    prods = prods.reshape(tiles_here, ncand, slim, width_in)
    received = lax.all_to_all(prods, "cand", split_axis=1, concat_axis=0, tiled=True)
    all_tiles = received.shape[0]
    received = received.reshape(all_tiles, slim, width_in)
    precond = (test_grads.astype(jnp.float32) / (eigval + damping)).astype(jnp.bfloat16)
    tile_part = jnp.einsum("tea,jea->tj", received, precond, preferred_element_type=jnp.float32)
    ignored_mask, onehot = tile_layout(pair_tiles, last_rows, 0, all_tiles, TILE)
    pair_part = jnp.dot(onehot.astype(jnp.float32).T, tile_part, precision=lax.Precision.HIGHEST)
    npairs = pair_part.shape[0]
    ntest = pair_part.shape[1]
    total = lax.psum(pair_part, ("cand", "eig", "rep"))
    rows = lax.dynamic_slice_in_dim(
        total, lax.axis_index("cand") * (npairs // ncand), npairs // ncand, 0
    )
    return lax.dynamic_slice_in_dim(
        rows, lax.axis_index(FEAT) * (ntest // nfeat), ntest // nfeat, 1
    )


def solution(mesh):
    in_specs = (
        P(("groups", "cand"), ("eig", "rep")),
        P(("groups", "cand"), ("eig", "rep")),
        P(("groups", "eig", "rep"), "cand"),
        P(("groups", "eig", "rep"), "cand"),
        P(("groups", "cand", "eig", "rep"), None),
        P("groups", ("cand", "eig", "rep"), None),
        P("groups"),
        P("groups"),
    )
    out_specs = P(("groups", "cand"), ("eig", "rep"))
    sizes = (mesh.shape["cand"], mesh.shape["eig"], mesh.shape["rep"])
    per_device = line_plan if sizes == (4, 2, 2) else gather_plan
    return jax.shard_map(
        per_device, mesh=mesh, in_specs=in_specs, out_specs=out_specs, check_vma=False
    )
```

```python
import jax
import jax.numpy as jnp
from jax import lax
from jax.experimental import pallas as pl
from jax.experimental.pallas import tpu as pltpu
from jax.sharding import PartitionSpec as P

TILE = 128
FEAT = ("eig", "rep")
ALL = ("cand", "eig", "rep")
STEPS = 3
SIDE = ((0, 1), (1, 0), (2, 3), (3, 2))
TWO = ((0, 2), (2, 0), (1, 3), (3, 1))
THREE = ((0, 3), (3, 0), (1, 2), (2, 1))

damping = 0.01


def tile_layout(pair_tiles, last_rows, first_tile, count, tile_rows):
    tiles = first_tile + jnp.arange(count, dtype=jnp.int32)
    ends = jnp.cumsum(pair_tiles)
    owner = jnp.sum((ends[None, :] <= tiles[:, None]).astype(jnp.int32), axis=1)
    onehot = owner[:, None] == jnp.arange(pair_tiles.shape[0], dtype=jnp.int32)[None, :]
    last_of = jnp.sum(jnp.where(onehot, last_rows[None, :], 0), axis=1)
    end_of = jnp.sum(jnp.where(onehot, ends[None, :], 0), axis=1)
    limit = jnp.where(tiles == end_of - 1, last_of, tile_rows)
    rowmask = jnp.arange(tile_rows, dtype=jnp.int32)[None, :] < limit[:, None]
    return (rowmask, onehot)


def after(x, *earlier):
    return lax.optimization_barrier((x, *earlier))[0]


def swap(x, axis_name):
    return lax.ppermute(x, axis_name, [(0, 1), (1, 0)])


def halves(x, axis_name):
    first = lax.axis_index(axis_name) == 0
    low, high = jnp.split(x, 2)
    return jnp.where(first, low, high), jnp.where(first, high, low)


def scatter_sum(keep, give):
    keep, give = halves(keep + swap(give, "rep"), "eig")
    return keep + swap(give, "eig")


def gather_rows(x):
    other = swap(x, "eig")
    first = lax.axis_index("eig") == 0
    both = jnp.stack([jnp.where(first, x, other), jnp.where(first, other, x)])
    other = swap(both, "rep")
    first = lax.axis_index("rep") == 0
    whole = jnp.stack([jnp.where(first, both, other), jnp.where(first, other, both)], axis=1)
    return whole.reshape((-1,) + x.shape[1:])


def split_rows(full_ref, keep_ref, give_ref, rep, columns=None):
    rows = full_ref.shape[0] // 4
    columns = slice(None) if columns is None else columns
    for e in range(2):
        here = pl.ds(e * rows, rows)
        mine = pl.ds(pl.multiple_of((2 * e + rep) * rows, rows), rows)
        theirs = pl.ds(pl.multiple_of((2 * e + 1 - rep) * rows, rows), rows)
        keep_ref[here, columns] = full_ref[mine, :]
        give_ref[here, columns] = full_ref[theirs, :]


def feature_dots(flags, grads, segments, start=None, split=True):
    tok = grads.shape[0]
    cols = segments[0][0][0][0].shape[1]
    depth = grads.shape[1] // (3 * STEPS)
    firsts = [sum(s[3] for s in segments[:at]) for at in range(len(segments))]
    total = sum(s[3] for s in segments)

    def grads_at(i, flags_ref):
        at = 0
        for first, (choices, at_end, at_middle, steps, only) in zip(firsts, segments):
            base = at_end + flags_ref[0] * 0 if at_end == at_middle else (
                flags_ref[0] * at_end + (1 - flags_ref[0]) * at_middle
            )
            at = jnp.where(i >= first, base + i - first, at)
        return (0, at)

    def rows_at(first, steps, row, wanted):
        def index(i, flags_ref):
            step = jnp.clip(i - first, 0, steps - 1)
            if wanted is not None:
                step = step * (flags_ref[0] if wanted else 1 - flags_ref[0])
            return (row + step, 0)

        return index

    operands, specs = [grads], [pl.BlockSpec((tok, depth), grads_at)]
    for first, (choices, at_end, at_middle, steps, only) in zip(firsts, segments):
        for which, (array, row) in enumerate(choices):
            wanted = None if len(choices) == 1 else which == 0
            operands.append(array)
            specs.append(pl.BlockSpec((depth, cols), rows_at(first, steps, row, wanted)))
    if start is not None:
        operands.append(start)
        specs.append(pl.BlockSpec((tok, cols), lambda i, flags_ref: (0, 0)))

    def kernel(flags_ref, grads_ref, *refs):
        i = pl.program_id(0)
        end = flags_ref[0] == 1
        inputs, rest = list(refs[: len(operands) - 1]), refs[len(operands) - 1 :]
        if split:
            keep_ref, give_ref, total_ref, turned_ref = rest
        else:
            (total_ref,) = rest

        @pl.when(i == 0)
        def begin():
            total_ref[...] = jnp.zeros_like(total_ref) if start is None else inputs[-1][...]

        at = 0
        for first, (choices, at_end, at_middle, steps, only) in zip(firsts, segments):
            here = inputs[at : at + len(choices)]
            at += len(choices)
            active = (i >= first) & (i < first + steps)
            if only:
                active = active & (flags_ref[0] == 0)

            @pl.when(active)
            def add(here=here):
                shard = here[0][...]
                if len(here) == 2:
                    shard = jnp.where(end, shard, here[1][...])
                total_ref[...] += jnp.dot(
                    grads_ref[...], shard, preferred_element_type=jnp.float32
                )

        if split:

            @pl.when(i == total - 1)
            def finish():
                turned_ref[...] = total_ref[...].T
                split_rows(turned_ref, keep_ref, give_ref, flags_ref[1])

    whole = lambda i, flags_ref: (0, 0)
    if split:
        out_shape = [jax.ShapeDtypeStruct((cols // 2, tok), jnp.float32)] * 2
        out_specs = [pl.BlockSpec((cols // 2, tok), whole)] * 2
        scratch = [pltpu.VMEM((tok, cols), jnp.float32), pltpu.VMEM((cols, tok), jnp.float32)]
    else:
        out_shape = jax.ShapeDtypeStruct((tok, cols), jnp.float32)
        out_specs = pl.BlockSpec((tok, cols), whole)
        scratch = []
    return pl.pallas_call(
        kernel,
        out_shape=out_shape,
        grid_spec=pltpu.PrefetchScalarGridSpec(
            num_scalar_prefetch=1,
            grid=(total,),
            in_specs=specs,
            out_specs=out_specs,
            scratch_shapes=scratch,
        ),
        compiler_params=pltpu.CompilerParams(vmem_limit_bytes=16 << 20),
        cost_estimate=pl.CostEstimate(
            flops=2 * tok * cols * depth * total,
            bytes_accessed=2 * total * depth * (tok + cols),
            transcendentals=0,
        ),
    )(flags, *operands)


def partner_dots(flags, pieces, shards, tail=None):
    blocks = pieces[0][2]
    cols = shards[0][0].shape[1]
    depth = blocks // STEPS
    count = len(pieces)
    width = len(shards) * count * TILE
    tok = 0 if tail is None else tail[0].shape[0]

    def at(row):
        return lambda i, flags_ref: (row + i, 0)

    operands, specs = [], []
    for array, row, _ in pieces:
        operands.append(array)
        specs.append(pl.BlockSpec((depth, cols), at(row)))
    for array, row in shards:
        operands.append(array)
        specs.append(pl.BlockSpec((depth, cols), at(row)))
    whole = lambda i, flags_ref: (0, 0)
    if tail is not None:
        operands += list(tail)
        specs.append(pl.BlockSpec((tok, depth), lambda i, flags_ref: (0, 2 * STEPS + i)))
        specs.append(pl.BlockSpec((depth, cols), lambda i, flags_ref: (i * flags_ref[0], 0)))
        specs.append(pl.BlockSpec((depth, cols), lambda i, flags_ref: (i * (1 - flags_ref[0]), 0)))
        specs.append(pl.BlockSpec((tok, cols), whole))

    def kernel(flags_ref, *refs):
        i = pl.program_id(0)
        piece_refs, shard_refs = refs[:count], refs[count : count + len(shards)]
        refs = refs[count + len(shards) :]
        if tail is not None:
            grads_ref, end_ref, middle_ref, start_ref = refs[:4]
            refs = refs[4:]
            keep_ref, give_ref, sums_ref, turned_ref, total_ref, wide_ref = refs
        else:
            keep_ref, give_ref, sums_ref, turned_ref = refs

        @pl.when(i == 0)
        def begin():
            sums_ref[...] = jnp.zeros_like(sums_ref)
            if tail is not None:
                total_ref[...] = start_ref[...]

        for t, piece_ref in enumerate(piece_refs):
            tokens = jnp.concatenate(
                [piece_ref[q * TILE : (q + 1) * TILE, :] for q in range(depth // TILE)], axis=1
            )
            for j, shard_ref in enumerate(shard_refs):
                sums_ref[j * count + t] += jnp.dot(
                    tokens, shard_ref[...], preferred_element_type=jnp.float32
                )
        if tail is not None:
            shard = jnp.where(flags_ref[0] == 1, end_ref[...], middle_ref[...])
            total_ref[...] += jnp.dot(grads_ref[...], shard, preferred_element_type=jnp.float32)

        @pl.when(i == STEPS - 1)
        def finish():
            if tail is not None:
                wide_ref[...] = total_ref[...].T
                split_rows(wide_ref, keep_ref, give_ref, flags_ref[1], pl.ds(0, tok))
            for at_block in range(len(shards) * count):
                turned_ref[...] = sums_ref[at_block].T
                columns = pl.ds(tok + at_block * TILE, TILE)
                split_rows(turned_ref, keep_ref, give_ref, flags_ref[1], columns)

    scratch = [
        pltpu.VMEM((len(shards) * count, TILE, cols), jnp.float32),
        pltpu.VMEM((cols, TILE), jnp.float32),
    ]
    if tail is not None:
        scratch += [pltpu.VMEM((tok, cols), jnp.float32), pltpu.VMEM((cols, tok), jnp.float32)]
    return pl.pallas_call(
        kernel,
        out_shape=[jax.ShapeDtypeStruct((cols // 2, tok + width), jnp.float32)] * 2,
        grid_spec=pltpu.PrefetchScalarGridSpec(
            num_scalar_prefetch=1,
            grid=(STEPS,),
            in_specs=specs,
            out_specs=[pl.BlockSpec((cols // 2, tok + width), whole)] * 2,
            scratch_shapes=scratch,
        ),
        compiler_params=pltpu.CompilerParams(vmem_limit_bytes=16 << 20),
        cost_estimate=pl.CostEstimate(
            flops=2 * blocks * cols * (width + tok),
            bytes_accessed=2 * blocks * (cols * (count + len(shards)) + tok),
            transcendentals=0,
        ),
    )(flags, *operands)


def input_dots(flags, acts, shards):
    tok, depth = acts.shape
    cols = shards[0][0][0].shape[1]
    operands, specs = [acts], [pl.BlockSpec((tok, depth), lambda i, flags_ref: (0, 0))]
    for choices in shards:
        for array, row in choices:
            operands.append(array)
            specs.append(pl.BlockSpec((depth, cols), lambda i, flags_ref, row=row: (row, 0)))

    def kernel(flags_ref, acts_ref, *refs):
        i = pl.program_id(0)
        inputs = list(refs[: len(operands) - 1])
        keep_ref, give_ref, part_ref = refs[len(operands) - 1 :]
        at = 0
        for slot, choices in enumerate(shards):
            here = inputs[at : at + len(choices)]
            at += len(choices)

            @pl.when(i == slot)
            def add(here=here):
                shard = here[0][...]
                if len(here) == 2:
                    shard = jnp.where(flags_ref[0] == 1, shard, here[1][...])
                part_ref[...] = jnp.dot(acts_ref[...], shard, preferred_element_type=jnp.float32)

        split_rows(part_ref, keep_ref, give_ref, flags_ref[1])

    place = pl.BlockSpec((tok // 2, cols), lambda i, flags_ref: (0, flags_ref[2 + i]))
    return pl.pallas_call(
        kernel,
        out_shape=[jax.ShapeDtypeStruct((tok // 2, cols * len(shards)), jnp.float32)] * 2,
        grid_spec=pltpu.PrefetchScalarGridSpec(
            num_scalar_prefetch=1,
            grid=(len(shards),),
            in_specs=specs,
            out_specs=[place, place],
            scratch_shapes=[pltpu.VMEM((tok, cols), jnp.float32)],
        ),
        compiler_params=pltpu.CompilerParams(vmem_limit_bytes=16 << 20),
        cost_estimate=pl.CostEstimate(
            flops=2 * tok * depth * cols * len(shards),
            bytes_accessed=2 * depth * (tok + 7 * cols) + 4 * tok * cols * len(shards),
            transcendentals=0,
        ),
    )(flags, *operands)


def line_plan(acts, grads, basis_in, basis_out, eigval, test_grads, pair_tiles, last_rows):
    plane = lax.axis_index("cand")
    end = (plane == 0) | (plane == 3)
    tok_rows = acts.shape[0]
    cols = basis_in.shape[1]
    tiles_here = tok_rows // TILE
    slim = cols // 4
    depth = basis_out.shape[0] // 3
    rows_in = basis_in.shape[0]

    def pick(at_end, at_middle):
        return jnp.where(end, at_end, at_middle)

    def side(at_end, at_middle):
        return lax.ppermute(pick(at_end, at_middle), "cand", SIDE)

    among = []
    for at in range(16):
        mid = 4 <= at < 12
        among.append((at, (12 - at + 2 * (at % 4)) if mid else at ^ 1))

    def middle(x):
        return lax.ppermute(x, ALL, among)

    at_b = jnp.where(end, plane ^ 2, plane ^ 3)
    at_c = jnp.where(end, plane ^ 3, plane ^ 2)
    rep = lax.axis_index("rep")
    flags = jnp.stack([end.astype(jnp.int32), rep, plane, plane ^ 1, at_b, at_c])

    rows = lax.dynamic_slice_in_dim(basis_out, jnp.where(end, 0, depth), 2 * depth, 0)
    s0 = lax.ppermute(basis_in, "cand", SIDE)
    m0 = middle(basis_in)
    s12 = lax.ppermute(rows, "cand", SIDE)
    late_rows = basis_out[depth:]
    m23 = middle(late_rows)
    started = after(flags, rows, late_rows)
    m1 = middle(after(s0, m0))
    stacked = grads[:, :depth].reshape(tiles_here, TILE, depth // TILE, TILE)
    stacked = after(stacked, s0).transpose(0, 2, 1, 3).reshape(tiles_here * depth, TILE)
    third = jnp.concatenate([basis_out[2 * depth :], basis_out[: 2 * rows_in - depth]])
    s3 = side(third, jnp.concatenate([m0, m1]))
    m5 = middle(s12[depth:])
    s45 = side(stacked[: 2 * depth], after(m23, s12))
    m6 = middle(s3[:depth])
    m47 = middle(after(jnp.concatenate([basis_out[:depth], s12[:depth]]), m5))
    s6 = side(after(stacked[2 * depth : 3 * depth], s3), m5)
    s7 = side(after(stacked[3 * depth :], s45), m6)

    early = after(flags, s3)
    keep, give = input_dots(
        early, acts, [[(basis_in, 0)], [(s0, 0)], [(s3, 0), (m0, 0)], [(s3, 1), (m1, 0)]]
    )
    rot_in = gather_rows(scatter_sum(keep, give).astype(jnp.bfloat16))
    rot_in = rot_in.reshape(tiles_here, TILE, 4 * cols)

    sum_own = scatter_sum(
        *feature_dots(started, grads, [([(basis_out, 0)], 0, 0, 3 * STEPS, False)])
    )
    sum_a = scatter_sum(
        *feature_dots(
            flags,
            grads,
            [
                ([(s12, 0)], STEPS, 0, 2 * STEPS, False),
                ([(s3, 0)], 2 * STEPS, 2 * STEPS, STEPS, True),
            ],
        )
    )
    part_b = feature_dots(
        flags, grads, [([(s45, 0), (m23, 0)], STEPS, STEPS, 2 * STEPS, False),
                       ([(m47, 0)], 0, 0, STEPS, True)]
    )
    sum_b = scatter_sum(*part_b)
    part_c = feature_dots(
        flags, grads, [([(s6, 0), (m5, 0)], STEPS, STEPS, STEPS, False),
                       ([(m47, STEPS)], 0, 0, STEPS, True)], split=False
    )
    shards = [(basis_out, 0), (m47, 0), (m47, STEPS)]
    first = partner_dots(flags, [(s45, 0, depth), (s45, STEPS, depth), (s6, 0, depth)], shards)
    sum_first = scatter_sum(*first)
    last = partner_dots(flags, [(s7, 0, depth)], shards, (grads, s7, m6, part_c))
    sum_last = scatter_sum(*last)
    sum_c, sum_last = sum_last[:, :tok_rows], sum_last[:, tok_rows:]
    back = [
        jnp.where(end, lax.ppermute(x, "cand", SIDE), 0.0).reshape(slim, 3, -1)
        for x in (sum_first, sum_last)
    ]
    back = jnp.concatenate(back, axis=2)

    rowmask, ignored = tile_layout(pair_tiles, last_rows, plane * tiles_here, tiles_here, TILE)
    keep = rowmask.reshape(1, tok_rows).astype(jnp.bfloat16)
    precond = (test_grads.astype(jnp.float32) / (eigval + damping)).astype(jnp.bfloat16)

    def tile_prods(rot_out):
        return jnp.einsum(
            "etr,tra->tea",
            (rot_out.astype(jnp.bfloat16) * keep).reshape(slim, tiles_here, TILE),
            rot_in,
            preferred_element_type=jnp.float32,
        ).astype(jnp.bfloat16)

    def pair_scores(prods, source):
        scores = jnp.einsum("tea,jea->tj", prods, precond, preferred_element_type=jnp.float32)
        ignored_mask, onehot = tile_layout(
            pair_tiles, last_rows, source * tiles_here, tiles_here, TILE
        )
        return jnp.sum(jnp.where(onehot[:, :, None], scores[:, None, :], 0.0), axis=0)

    prods_a = tile_prods(sum_a + back[:, 0])
    prods_b = tile_prods(sum_b + back[:, 1])
    prods_c = tile_prods(sum_c + back[:, 2])
    total = pair_scores(tile_prods(sum_own), plane)
    total = total + pair_scores(lax.ppermute(prods_a, "cand", SIDE), plane ^ 1)
    total = total + pair_scores(lax.ppermute(pick(prods_b, prods_c), "cand", TWO), plane ^ 2)
    total = total + pair_scores(lax.ppermute(pick(prods_c, prods_b), "cand", THREE), plane ^ 3)
    return final_sum(total)


def final_sum(total):
    npairs, ntest = total.shape
    mine = total.reshape(npairs, 2, 2, ntest // 4).transpose(2, 1, 0, 3)
    keep, give = halves(mine, "rep")
    keep, give = halves((keep + swap(give, "rep"))[0], "eig")
    keep = (keep + swap(give, "eig"))[0]
    plane = lax.axis_index("cand")
    rows = npairs // 4
    result = lax.dynamic_slice_in_dim(keep, plane * rows, rows, 0)
    for step in range(1, 4):
        block = lax.dynamic_slice_in_dim(keep, (plane ^ step) * rows, rows, 0)
        result = result + lax.ppermute(block, "cand", [(i, i ^ step) for i in range(4)])
    return result


def gather_plan(acts, grads, basis_in, basis_out, eigval, test_grads, pair_tiles, last_rows):
    ncand = lax.axis_size("cand")
    nfeat = lax.axis_size(FEAT)
    tok_rows = acts.shape[0]
    width_in = basis_in.shape[1] * ncand
    width_out = basis_out.shape[1] * ncand
    slim = width_out // (ncand * nfeat)
    part_in = jnp.dot(
        acts,
        lax.all_gather(basis_in, "cand", axis=1, tiled=True),
        preferred_element_type=jnp.float32,
    )
    part_out = jnp.dot(
        grads,
        lax.all_gather(basis_out, "cand", axis=1, tiled=True),
        preferred_element_type=jnp.float32,
    )
    part_out = part_out.reshape(tok_rows, ncand, nfeat, slim).transpose(0, 2, 1, 3)
    part_out = part_out.reshape(tok_rows, nfeat * ncand * slim)
    summed_in, summed_out = lax.psum((part_in, part_out), FEAT)
    own = lax.dynamic_slice_in_dim(
        summed_out, lax.axis_index(FEAT) * (ncand * slim), ncand * slim, 1
    )
    rot_in = summed_in.astype(jnp.bfloat16)
    rot_out = own.astype(jnp.bfloat16)
    tiles_here = tok_rows // TILE
    rowmask, ignored = tile_layout(
        pair_tiles, last_rows, lax.axis_index("cand") * tiles_here, tiles_here, TILE
    )
    masked = rot_out.reshape(tiles_here, TILE, ncand * slim) * rowmask[:, :, None].astype(
        jnp.bfloat16
    )
    prods = jnp.einsum(
        "tre,tra->tea",
        masked,
        rot_in.reshape(tiles_here, TILE, width_in),
        preferred_element_type=jnp.float32,
    ).astype(jnp.bfloat16)
    prods = prods.reshape(tiles_here, ncand, slim, width_in)
    received = lax.all_to_all(prods, "cand", split_axis=1, concat_axis=0, tiled=True)
    all_tiles = received.shape[0]
    received = received.reshape(all_tiles, slim, width_in)
    precond = (test_grads.astype(jnp.float32) / (eigval + damping)).astype(jnp.bfloat16)
    tile_part = jnp.einsum("tea,jea->tj", received, precond, preferred_element_type=jnp.float32)
    ignored_mask, onehot = tile_layout(pair_tiles, last_rows, 0, all_tiles, TILE)
    pair_part = jnp.dot(onehot.astype(jnp.float32).T, tile_part, precision=lax.Precision.HIGHEST)
    npairs = pair_part.shape[0]
    ntest = pair_part.shape[1]
    total = lax.psum(pair_part, ("cand", "eig", "rep"))
    rows = lax.dynamic_slice_in_dim(
        total, lax.axis_index("cand") * (npairs // ncand), npairs // ncand, 0
    )
    return lax.dynamic_slice_in_dim(
        rows, lax.axis_index(FEAT) * (ntest // nfeat), ntest // nfeat, 1
    )


def solution(mesh):
    in_specs = (
        P(("groups", "cand"), ("eig", "rep")),
        P(("groups", "cand"), ("eig", "rep")),
        P(("groups", "eig", "rep"), "cand"),
        P(("groups", "eig", "rep"), "cand"),
        P(("groups", "cand", "eig", "rep"), None),
        P("groups", ("cand", "eig", "rep"), None),
        P("groups"),
        P("groups"),
    )
    out_specs = P(("groups", "cand"), ("eig", "rep"))
    sizes = (mesh.shape["cand"], mesh.shape["eig"], mesh.shape["rep"])
    per_device = line_plan if sizes == (4, 2, 2) else gather_plan
    return jax.shard_map(
        per_device, mesh=mesh, in_specs=in_specs, out_specs=out_specs, check_vma=False
    )
```

```python
import jax
import jax.numpy as jnp
from jax import lax
from jax.experimental import pallas as pl
from jax.experimental.pallas import tpu as pltpu
from jax.sharding import PartitionSpec as P

TILE = 128
FEAT = ("eig", "rep")
ALL = ("cand", "eig", "rep")
STEPS = 3
SHORT = pl.CostEstimate(flops=1, bytes_accessed=1, transcendentals=0)
SIDE = ((0, 1), (1, 0), (2, 3), (3, 2))
TWO = ((0, 2), (2, 0), (1, 3), (3, 1))
THREE = ((0, 3), (3, 0), (1, 2), (2, 1))

damping = 0.01


def tile_layout(pair_tiles, last_rows, first_tile, count, tile_rows):
    tiles = first_tile + jnp.arange(count, dtype=jnp.int32)
    ends = jnp.cumsum(pair_tiles)
    owner = jnp.sum((ends[None, :] <= tiles[:, None]).astype(jnp.int32), axis=1)
    onehot = owner[:, None] == jnp.arange(pair_tiles.shape[0], dtype=jnp.int32)[None, :]
    last_of = jnp.sum(jnp.where(onehot, last_rows[None, :], 0), axis=1)
    end_of = jnp.sum(jnp.where(onehot, ends[None, :], 0), axis=1)
    limit = jnp.where(tiles == end_of - 1, last_of, tile_rows)
    rowmask = jnp.arange(tile_rows, dtype=jnp.int32)[None, :] < limit[:, None]
    return (rowmask, onehot)


def after(x, *earlier):
    return lax.optimization_barrier((x, *earlier))[0]


def swap(x, axis_name):
    return lax.ppermute(x, axis_name, [(0, 1), (1, 0)])


def halves(x, axis_name):
    first = lax.axis_index(axis_name) == 0
    low, high = jnp.split(x, 2)
    return jnp.where(first, low, high), jnp.where(first, high, low)


def scatter_sum(keep, give):
    keep, give = halves(keep + swap(give, "rep"), "eig")
    return keep + swap(give, "eig")


def gather_rows(x):
    other = swap(x, "eig")
    first = lax.axis_index("eig") == 0
    both = jnp.stack([jnp.where(first, x, other), jnp.where(first, other, x)])
    other = swap(both, "rep")
    first = lax.axis_index("rep") == 0
    whole = jnp.stack([jnp.where(first, both, other), jnp.where(first, other, both)], axis=1)
    return whole.reshape((-1,) + x.shape[1:])


def split_rows(full_ref, keep_ref, give_ref, rep, columns=None):
    rows = full_ref.shape[0] // 4
    columns = slice(None) if columns is None else columns
    for e in range(2):
        here = pl.ds(e * rows, rows)
        mine = pl.ds(pl.multiple_of((2 * e + rep) * rows, rows), rows)
        theirs = pl.ds(pl.multiple_of((2 * e + 1 - rep) * rows, rows), rows)
        keep_ref[here, columns] = full_ref[mine, :]
        give_ref[here, columns] = full_ref[theirs, :]


def feature_dots(flags, grads, segments, start=None, split=True):
    tok = grads.shape[0]
    cols = segments[0][0][0][0].shape[1]
    depth = grads.shape[1] // (3 * STEPS)
    firsts = [sum(s[3] for s in segments[:at]) for at in range(len(segments))]
    total = sum(s[3] for s in segments)

    def grads_at(i, flags_ref):
        at = 0
        for first, (choices, at_end, at_middle, steps, only) in zip(firsts, segments):
            base = at_end + flags_ref[0] * 0 if at_end == at_middle else (
                flags_ref[0] * at_end + (1 - flags_ref[0]) * at_middle
            )
            at = jnp.where(i >= first, base + i - first, at)
        return (0, at)

    def rows_at(first, steps, row, wanted):
        def index(i, flags_ref):
            step = jnp.clip(i - first, 0, steps - 1)
            if wanted is not None:
                step = step * (flags_ref[0] if wanted else 1 - flags_ref[0])
            return (row + step, 0)

        return index

    operands, specs = [grads], [pl.BlockSpec((tok, depth), grads_at)]
    for first, (choices, at_end, at_middle, steps, only) in zip(firsts, segments):
        for which, (array, row) in enumerate(choices):
            wanted = None if len(choices) == 1 else which == 0
            operands.append(array)
            specs.append(pl.BlockSpec((depth, cols), rows_at(first, steps, row, wanted)))
    if start is not None:
        operands.append(start)
        specs.append(pl.BlockSpec((tok, cols), lambda i, flags_ref: (0, 0)))

    def kernel(flags_ref, grads_ref, *refs):
        i = pl.program_id(0)
        end = flags_ref[0] == 1
        inputs, rest = list(refs[: len(operands) - 1]), refs[len(operands) - 1 :]
        if split:
            keep_ref, give_ref, total_ref, turned_ref = rest
        else:
            (total_ref,) = rest

        @pl.when(i == 0)
        def begin():
            total_ref[...] = jnp.zeros_like(total_ref) if start is None else inputs[-1][...]

        at = 0
        for first, (choices, at_end, at_middle, steps, only) in zip(firsts, segments):
            here = inputs[at : at + len(choices)]
            at += len(choices)
            active = (i >= first) & (i < first + steps)
            if only:
                active = active & (flags_ref[0] == 0)

            @pl.when(active)
            def add(here=here):
                shard = here[0][...]
                if len(here) == 2:
                    shard = jnp.where(end, shard, here[1][...])
                total_ref[...] += jnp.dot(
                    grads_ref[...], shard, preferred_element_type=jnp.float32
                )

        if split:

            @pl.when(i == total - 1)
            def finish():
                turned_ref[...] = total_ref[...].T
                split_rows(turned_ref, keep_ref, give_ref, flags_ref[1])

    whole = lambda i, flags_ref: (0, 0)
    if split:
        out_shape = [jax.ShapeDtypeStruct((cols // 2, tok), jnp.float32)] * 2
        out_specs = [pl.BlockSpec((cols // 2, tok), whole)] * 2
        scratch = [pltpu.VMEM((tok, cols), jnp.float32), pltpu.VMEM((cols, tok), jnp.float32)]
    else:
        out_shape = jax.ShapeDtypeStruct((tok, cols), jnp.float32)
        out_specs = pl.BlockSpec((tok, cols), whole)
        scratch = []
    return pl.pallas_call(
        kernel,
        out_shape=out_shape,
        grid_spec=pltpu.PrefetchScalarGridSpec(
            num_scalar_prefetch=1,
            grid=(total,),
            in_specs=specs,
            out_specs=out_specs,
            scratch_shapes=scratch,
        ),
        compiler_params=pltpu.CompilerParams(vmem_limit_bytes=16 << 20),
        cost_estimate=SHORT,
    )(flags, *operands)


def partner_dots(flags, pieces, shards, wanted, depth, tail=None):
    cols = shards[0][0].shape[1]
    step = depth // STEPS
    count = len(pieces)
    width = len(wanted) * TILE
    tok = 0 if tail is None else tail[0].shape[0]

    def at(row):
        return lambda i, flags_ref: (row + i, 0)

    operands, specs = [], []
    for array, row in list(pieces) + list(shards):
        operands.append(array)
        specs.append(pl.BlockSpec((step, cols), at(row)))
    whole = lambda i, flags_ref: (0, 0)
    if tail is not None:
        grads, at_end, at_middle, first, start = tail
        operands += [grads, grads, at_end, at_middle, first[0], start]
        specs.append(pl.BlockSpec((tok, step), lambda i, flags_ref: (0, 2 * STEPS + i)))
        specs.append(pl.BlockSpec((tok, step), lambda i, flags_ref: (0, i * (1 - flags_ref[0]))))
        specs.append(pl.BlockSpec((step, cols), lambda i, flags_ref: (i * flags_ref[0], 0)))
        specs.append(pl.BlockSpec((step, cols), lambda i, flags_ref: (i * (1 - flags_ref[0]), 0)))
        specs.append(pl.BlockSpec((step, cols), at(first[1])))
        specs.append(pl.BlockSpec((tok, cols), whole))

    def kernel(flags_ref, *refs):
        i = pl.program_id(0)
        piece_refs, shard_refs = refs[:count], refs[count : count + len(shards)]
        refs = refs[count + len(shards) :]
        if tail is not None:
            grads_ref, first_grads_ref, end_ref, middle_ref, first_ref, start_ref = refs[:6]
            keep_ref, give_ref, sums_ref, turned_ref, total_ref, wide_ref = refs[6:]
        else:
            keep_ref, give_ref, sums_ref, turned_ref = refs

        @pl.when(i == 0)
        def begin():
            sums_ref[...] = jnp.zeros_like(sums_ref)
            if tail is not None:
                total_ref[...] = start_ref[...]

        @pl.when(flags_ref[0] == 0)
        def at_a_middle_plane():
            for t, piece_ref in enumerate(piece_refs):
                tokens = jnp.concatenate(
                    [piece_ref[q * TILE : (q + 1) * TILE, :] for q in range(step // TILE)], axis=1
                )
                for block, (shard, piece) in enumerate(wanted):
                    if piece == t:
                        sums_ref[block] += jnp.dot(
                            tokens, shard_refs[shard][...], preferred_element_type=jnp.float32
                        )
            if tail is not None:
                total_ref[...] += jnp.dot(
                    first_grads_ref[...], first_ref[...], preferred_element_type=jnp.float32
                )

        if tail is not None:
            shard = jnp.where(flags_ref[0] == 1, end_ref[...], middle_ref[...])
            total_ref[...] += jnp.dot(grads_ref[...], shard, preferred_element_type=jnp.float32)

        @pl.when(i == STEPS - 1)
        def finish():
            if tail is not None:
                wide_ref[...] = total_ref[...].T
                split_rows(wide_ref, keep_ref, give_ref, flags_ref[1], pl.ds(0, tok))
            for block in range(len(wanted)):
                turned_ref[...] = sums_ref[block].T
                columns = pl.ds(tok + block * TILE, TILE)
                split_rows(turned_ref, keep_ref, give_ref, flags_ref[1], columns)

    scratch = [
        pltpu.VMEM((len(wanted), TILE, cols), jnp.float32),
        pltpu.VMEM((cols, TILE), jnp.float32),
    ]
    if tail is not None:
        scratch += [pltpu.VMEM((tok, cols), jnp.float32), pltpu.VMEM((cols, tok), jnp.float32)]
    return pl.pallas_call(
        kernel,
        out_shape=[jax.ShapeDtypeStruct((cols // 2, tok + width), jnp.float32)] * 2,
        grid_spec=pltpu.PrefetchScalarGridSpec(
            num_scalar_prefetch=1,
            grid=(STEPS,),
            in_specs=specs,
            out_specs=[pl.BlockSpec((cols // 2, tok + width), whole)] * 2,
            scratch_shapes=scratch,
        ),
        compiler_params=pltpu.CompilerParams(vmem_limit_bytes=24 << 20),
        cost_estimate=SHORT,
    )(flags, *operands)


def stack_blocks(flags, grads, depth):
    tiles = grads.shape[0] // TILE

    def kernel(flags_ref, grads_ref, out_ref):
        for q in range(depth // TILE):
            out_ref[q * TILE : (q + 1) * TILE, :] = grads_ref[:, q * TILE : (q + 1) * TILE]

    return pl.pallas_call(
        kernel,
        out_shape=jax.ShapeDtypeStruct((tiles * depth, TILE), grads.dtype),
        grid_spec=pltpu.PrefetchScalarGridSpec(
            num_scalar_prefetch=1,
            grid=(tiles,),
            in_specs=[pl.BlockSpec((TILE, depth), lambda t, flags_ref: (t, 0))],
            out_specs=pl.BlockSpec((depth, TILE), lambda t, flags_ref: (t, 0)),
        ),
        compiler_params=pltpu.CompilerParams(vmem_limit_bytes=16 << 20),
        cost_estimate=SHORT,
    )(flags, grads)


def input_dots(flags, acts, shards):
    tok, depth = acts.shape
    cols = shards[0][0][0].shape[1]
    operands, specs = [acts], [pl.BlockSpec((tok, depth), lambda i, flags_ref: (0, 0))]
    for choices in shards:
        for array, row in choices:
            operands.append(array)
            specs.append(pl.BlockSpec((depth, cols), lambda i, flags_ref, row=row: (row, 0)))

    def kernel(flags_ref, acts_ref, *refs):
        i = pl.program_id(0)
        inputs = list(refs[: len(operands) - 1])
        keep_ref, give_ref, part_ref = refs[len(operands) - 1 :]
        at = 0
        for slot, choices in enumerate(shards):
            here = inputs[at : at + len(choices)]
            at += len(choices)

            @pl.when(i == slot)
            def add(here=here):
                shard = here[0][...]
                if len(here) == 2:
                    shard = jnp.where(flags_ref[0] == 1, shard, here[1][...])
                part_ref[...] = jnp.dot(acts_ref[...], shard, preferred_element_type=jnp.float32)

        split_rows(part_ref, keep_ref, give_ref, flags_ref[1])

    place = pl.BlockSpec((tok // 2, cols), lambda i, flags_ref: (0, flags_ref[2 + i]))
    return pl.pallas_call(
        kernel,
        out_shape=[jax.ShapeDtypeStruct((tok // 2, cols * len(shards)), jnp.float32)] * 2,
        grid_spec=pltpu.PrefetchScalarGridSpec(
            num_scalar_prefetch=1,
            grid=(len(shards),),
            in_specs=specs,
            out_specs=[place, place],
            scratch_shapes=[pltpu.VMEM((tok, cols), jnp.float32)],
        ),
        compiler_params=pltpu.CompilerParams(vmem_limit_bytes=16 << 20),
        cost_estimate=SHORT,
    )(flags, *operands)


def line_plan(acts, grads, basis_in, basis_out, eigval, test_grads, pair_tiles, last_rows):
    plane = lax.axis_index("cand")
    end = (plane == 0) | (plane == 3)
    tok_rows = acts.shape[0]
    cols = basis_in.shape[1]
    tiles_here = tok_rows // TILE
    slim = cols // 4
    depth = basis_out.shape[0] // 3
    rows_in = basis_in.shape[0]

    def pick(at_end, at_middle):
        return jnp.where(end, at_end, at_middle)

    def side(at_end, at_middle):
        return lax.ppermute(pick(at_end, at_middle), "cand", SIDE)

    among = []
    for at in range(16):
        mid = 4 <= at < 12
        among.append((at, (12 - at + 2 * (at % 4)) if mid else at ^ 1))

    def middle(x):
        return lax.ppermute(x, ALL, among)

    at_b = jnp.where(end, plane ^ 2, plane ^ 3)
    at_c = jnp.where(end, plane ^ 3, plane ^ 2)
    rep = lax.axis_index("rep")
    flags = jnp.stack([end.astype(jnp.int32), rep, plane, plane ^ 1, at_b, at_c])

    rows = lax.dynamic_slice_in_dim(basis_out, jnp.where(end, 0, depth), 2 * depth, 0)
    s0 = lax.ppermute(basis_in, "cand", SIDE)
    m0 = middle(basis_in)
    s12 = lax.ppermute(rows, "cand", SIDE)
    late_rows = basis_out[depth:]
    m23 = middle(late_rows)
    started = after(flags, rows, late_rows)
    stacked = stack_blocks(started, grads, depth)
    part_own = feature_dots(started, grads, [([(basis_out, 0)], 0, 0, 3 * STEPS, False)])
    precond = (test_grads.astype(jnp.float32) / (eigval + damping)).astype(jnp.bfloat16)
    m1 = middle(after(s0, m0, precond, stacked, *part_own))
    third = jnp.concatenate([basis_out[2 * depth :], basis_out[: 2 * rows_in - depth]])
    s3 = side(third, jnp.concatenate([m0, m1]))
    m5 = middle(s12[depth:])
    s45 = side(stacked[: 2 * depth], after(m23, s12))
    to_m6 = s3[:depth]
    m6 = middle(to_m6)
    m4 = middle(after(basis_out[:depth], m5))
    s6 = side(after(stacked[2 * depth : 3 * depth], s3), m5)
    m7 = middle(after(s12[:depth], m6))
    s7 = side(after(stacked[3 * depth :], s45), m6)

    part_in = input_dots(
        after(flags, to_m6),
        acts,
        [[(basis_in, 0)], [(s0, 0)], [(s3, 0), (m0, 0)], [(s3, 1), (m1, 0)]],
    )
    part_a = feature_dots(
        after(flags, *part_in),
        grads,
        [
            ([(s12, 0)], STEPS, 0, 2 * STEPS, False),
            ([(s3, 0)], 2 * STEPS, 2 * STEPS, STEPS, True),
        ],
    )
    rot_in = gather_rows(scatter_sum(*after(part_in, s45)).astype(jnp.bfloat16))
    rot_in = rot_in.reshape(tiles_here, TILE, 4 * cols)
    sums = [jnp.concatenate(parts, axis=1) for parts in zip(part_own, part_a)]
    sums = scatter_sum(*after(sums, s45))
    sum_own, sum_a = sums[:, :tok_rows], sums[:, tok_rows:]
    part_b = feature_dots(
        after(flags, rot_in, sums),
        grads,
        [
            ([(s45, 0), (m23, 0)], STEPS, STEPS, 2 * STEPS, False),
            ([(m4, 0)], 0, 0, STEPS, True),
        ],
    )
    part_c = feature_dots(
        after(flags, *part_b),
        grads,
        [([(s6, 0), (m5, 0)], STEPS, STEPS, STEPS, False)],
        split=False,
    )
    shards = [(basis_out, 0), (m4, 0), (m7, 0)]
    pieces = [(s45, 0), (s45, STEPS), (s6, 0), (s7, 0)]
    early = [(shard, piece) for shard in range(2) for piece in range(3)]
    part_early = partner_dots(after(flags, part_c), pieces[:3], shards[:2], early, depth)
    late = [(2, 0), (2, 1), (2, 2), (0, 3), (1, 3), (2, 3)]
    part_late = partner_dots(
        after(flags, *part_early), pieces, shards, late, depth, (grads, s7, m6, (m7, 0), part_c)
    )
    sums = scatter_sum(*[jnp.concatenate(parts, axis=1) for parts in zip(part_b, part_early)])
    sum_b = sums[:, :tok_rows]
    sum_late = scatter_sum(*part_late)
    sum_c = sum_late[:, :tok_rows]
    back_early = jnp.where(end, lax.ppermute(sums[:, tok_rows:], "cand", SIDE), 0.0)
    back_late = jnp.where(end, lax.ppermute(sum_late[:, tok_rows:], "cand", SIDE), 0.0)
    few = 3 * TILE
    back_a = jnp.concatenate([back_early[:, :few], back_late[:, few : few + TILE]], axis=1)
    back_b = jnp.concatenate([back_early[:, few:], back_late[:, few + TILE : few + 2 * TILE]], axis=1)
    back_c = jnp.concatenate([back_late[:, :few], back_late[:, few + 2 * TILE :]], axis=1)

    rowmask, ignored = tile_layout(pair_tiles, last_rows, plane * tiles_here, tiles_here, TILE)
    keep = rowmask.reshape(1, tok_rows).astype(jnp.bfloat16)

    def tile_prods(rot_out):
        return jnp.einsum(
            "etr,tra->tea",
            (rot_out.astype(jnp.bfloat16) * keep).reshape(slim, tiles_here, TILE),
            rot_in,
            preferred_element_type=jnp.float32,
        ).astype(jnp.bfloat16)

    def pair_scores(prods, source):
        scores = jnp.einsum("tea,jea->tj", prods, precond, preferred_element_type=jnp.float32)
        ignored_mask, onehot = tile_layout(
            pair_tiles, last_rows, source * tiles_here, tiles_here, TILE
        )
        return jnp.sum(jnp.where(onehot[:, :, None], scores[:, None, :], 0.0), axis=0)

    prods_a = tile_prods(sum_a + back_a)
    prods_b = tile_prods(sum_b + back_b)
    prods_c = tile_prods(sum_c + back_c)
    total = pair_scores(tile_prods(sum_own), plane)
    total = total + pair_scores(lax.ppermute(prods_a, "cand", SIDE), plane ^ 1)
    total = total + pair_scores(lax.ppermute(pick(prods_b, prods_c), "cand", TWO), plane ^ 2)
    total = total + pair_scores(lax.ppermute(pick(prods_c, prods_b), "cand", THREE), plane ^ 3)
    return final_sum(total)


def final_sum(total):
    npairs, ntest = total.shape
    blocks = total.reshape(4, npairs // 4, 4, ntest // 4).transpose(0, 2, 1, 3)
    blocks = blocks.reshape(16, npairs // 4, ntest // 4)
    return jnp.sum(lax.all_to_all(blocks, ALL, 0, 0, tiled=True), axis=0)


def gather_plan(acts, grads, basis_in, basis_out, eigval, test_grads, pair_tiles, last_rows):
    ncand = lax.axis_size("cand")
    nfeat = lax.axis_size(FEAT)
    tok_rows = acts.shape[0]
    width_in = basis_in.shape[1] * ncand
    width_out = basis_out.shape[1] * ncand
    slim = width_out // (ncand * nfeat)
    part_in = jnp.dot(
        acts,
        lax.all_gather(basis_in, "cand", axis=1, tiled=True),
        preferred_element_type=jnp.float32,
    )
    part_out = jnp.dot(
        grads,
        lax.all_gather(basis_out, "cand", axis=1, tiled=True),
        preferred_element_type=jnp.float32,
    )
    part_out = part_out.reshape(tok_rows, ncand, nfeat, slim).transpose(0, 2, 1, 3)
    part_out = part_out.reshape(tok_rows, nfeat * ncand * slim)
    summed_in, summed_out = lax.psum((part_in, part_out), FEAT)
    own = lax.dynamic_slice_in_dim(
        summed_out, lax.axis_index(FEAT) * (ncand * slim), ncand * slim, 1
    )
    rot_in = summed_in.astype(jnp.bfloat16)
    rot_out = own.astype(jnp.bfloat16)
    tiles_here = tok_rows // TILE
    rowmask, ignored = tile_layout(
        pair_tiles, last_rows, lax.axis_index("cand") * tiles_here, tiles_here, TILE
    )
    masked = rot_out.reshape(tiles_here, TILE, ncand * slim) * rowmask[:, :, None].astype(
        jnp.bfloat16
    )
    prods = jnp.einsum(
        "tre,tra->tea",
        masked,
        rot_in.reshape(tiles_here, TILE, width_in),
        preferred_element_type=jnp.float32,
    ).astype(jnp.bfloat16)
    prods = prods.reshape(tiles_here, ncand, slim, width_in)
    received = lax.all_to_all(prods, "cand", split_axis=1, concat_axis=0, tiled=True)
    all_tiles = received.shape[0]
    received = received.reshape(all_tiles, slim, width_in)
    precond = (test_grads.astype(jnp.float32) / (eigval + damping)).astype(jnp.bfloat16)
    tile_part = jnp.einsum("tea,jea->tj", received, precond, preferred_element_type=jnp.float32)
    ignored_mask, onehot = tile_layout(pair_tiles, last_rows, 0, all_tiles, TILE)
    pair_part = jnp.dot(onehot.astype(jnp.float32).T, tile_part, precision=lax.Precision.HIGHEST)
    npairs = pair_part.shape[0]
    ntest = pair_part.shape[1]
    total = lax.psum(pair_part, ("cand", "eig", "rep"))
    rows = lax.dynamic_slice_in_dim(
        total, lax.axis_index("cand") * (npairs // ncand), npairs // ncand, 0
    )
    return lax.dynamic_slice_in_dim(
        rows, lax.axis_index(FEAT) * (ntest // nfeat), ntest // nfeat, 1
    )


def solution(mesh):
    in_specs = (
        P(("groups", "cand"), ("eig", "rep")),
        P(("groups", "cand"), ("eig", "rep")),
        P(("groups", "eig", "rep"), "cand"),
        P(("groups", "eig", "rep"), "cand"),
        P(("groups", "cand", "eig", "rep"), None),
        P("groups", ("cand", "eig", "rep"), None),
        P("groups"),
        P("groups"),
    )
    out_specs = P(("groups", "cand"), ("eig", "rep"))
    sizes = (mesh.shape["cand"], mesh.shape["eig"], mesh.shape["rep"])
    per_device = line_plan if sizes == (4, 2, 2) else gather_plan
    return jax.shard_map(
        per_device, mesh=mesh, in_specs=in_specs, out_specs=out_specs, check_vma=False
    )
```

```python
import jax
import jax.numpy as jnp
from jax import lax
from jax.experimental import pallas as pl
from jax.experimental.pallas import tpu as pltpu
from jax.sharding import PartitionSpec as P

TILE = 128
FEAT = ("eig", "rep")
ALL = ("cand", "eig", "rep")
STEPS = 3
SHORT = pl.CostEstimate(flops=1, bytes_accessed=1, transcendentals=0)
SIDE = ((0, 1), (1, 0), (2, 3), (3, 2))
TWO = ((0, 2), (2, 0), (1, 3), (3, 1))
THREE = ((0, 3), (3, 0), (1, 2), (2, 1))

damping = 0.01


def tile_layout(pair_tiles, last_rows, first_tile, count, tile_rows):
    tiles = first_tile + jnp.arange(count, dtype=jnp.int32)
    ends = jnp.cumsum(pair_tiles)
    owner = jnp.sum((ends[None, :] <= tiles[:, None]).astype(jnp.int32), axis=1)
    onehot = owner[:, None] == jnp.arange(pair_tiles.shape[0], dtype=jnp.int32)[None, :]
    last_of = jnp.sum(jnp.where(onehot, last_rows[None, :], 0), axis=1)
    end_of = jnp.sum(jnp.where(onehot, ends[None, :], 0), axis=1)
    limit = jnp.where(tiles == end_of - 1, last_of, tile_rows)
    rowmask = jnp.arange(tile_rows, dtype=jnp.int32)[None, :] < limit[:, None]
    return (rowmask, onehot)


def after(x, *earlier):
    return lax.optimization_barrier((x, *earlier))[0]


def swap(x, axis_name):
    return lax.ppermute(x, axis_name, [(0, 1), (1, 0)])


def halves(x, axis_name):
    first = lax.axis_index(axis_name) == 0
    low, high = jnp.split(x, 2)
    return jnp.where(first, low, high), jnp.where(first, high, low)


def scatter_sum(keep, give):
    keep, give = halves(keep + swap(give, "rep"), "eig")
    return keep + swap(give, "eig")


def gather_rows(x):
    other = swap(x, "eig")
    first = lax.axis_index("eig") == 0
    both = jnp.stack([jnp.where(first, x, other), jnp.where(first, other, x)])
    other = swap(both, "rep")
    first = lax.axis_index("rep") == 0
    whole = jnp.stack([jnp.where(first, both, other), jnp.where(first, other, both)], axis=1)
    return whole.reshape((-1,) + x.shape[1:])


def split_rows(full_ref, keep_ref, give_ref, rep, columns=None):
    rows = full_ref.shape[0] // 4
    columns = slice(None) if columns is None else columns
    for e in range(2):
        here = pl.ds(e * rows, rows)
        mine = pl.ds(pl.multiple_of((2 * e + rep) * rows, rows), rows)
        theirs = pl.ds(pl.multiple_of((2 * e + 1 - rep) * rows, rows), rows)
        keep_ref[here, columns] = full_ref[mine, :]
        give_ref[here, columns] = full_ref[theirs, :]


def add_dot(total_ref, rows_ref, shard):
    half = total_ref.shape[0] // 2
    for here in (pl.ds(0, half), pl.ds(half, half)):
        total_ref[here, :] += jnp.dot(
            rows_ref[here, :], shard, preferred_element_type=jnp.float32
        )


def feature_dots(flags, grads, segments, start=None, split=True):
    tok = grads.shape[0]
    cols = segments[0][0][0][0].shape[1]
    depth = grads.shape[1] // (3 * STEPS)
    firsts = [sum(s[3] for s in segments[:at]) for at in range(len(segments))]
    total = sum(s[3] for s in segments)

    def grads_at(i, flags_ref):
        at = 0
        for first, (choices, at_end, at_middle, steps, only) in zip(firsts, segments):
            base = at_end + flags_ref[0] * 0 if at_end == at_middle else (
                flags_ref[0] * at_end + (1 - flags_ref[0]) * at_middle
            )
            at = jnp.where(i >= first, base + i - first, at)
        return (0, at)

    def rows_at(first, steps, row, wanted):
        def index(i, flags_ref):
            step = jnp.clip(i - first, 0, steps - 1)
            if wanted is not None:
                step = step * (flags_ref[0] if wanted else 1 - flags_ref[0])
            return (row + step, 0)

        return index

    operands, specs = [grads], [pl.BlockSpec((tok, depth), grads_at)]
    for first, (choices, at_end, at_middle, steps, only) in zip(firsts, segments):
        for which, (array, row) in enumerate(choices):
            wanted = None if len(choices) == 1 else which == 0
            operands.append(array)
            specs.append(pl.BlockSpec((depth, cols), rows_at(first, steps, row, wanted)))
    if start is not None:
        operands.append(start)
        specs.append(pl.BlockSpec((tok, cols), lambda i, flags_ref: (0, 0)))

    def kernel(flags_ref, grads_ref, *refs):
        i = pl.program_id(0)
        end = flags_ref[0] == 1
        inputs, rest = list(refs[: len(operands) - 1]), refs[len(operands) - 1 :]
        if split:
            keep_ref, give_ref, total_ref, turned_ref = rest
        else:
            (total_ref,) = rest

        @pl.when(i == 0)
        def begin():
            total_ref[...] = jnp.zeros_like(total_ref) if start is None else inputs[-1][...]

        at = 0
        for first, (choices, at_end, at_middle, steps, only) in zip(firsts, segments):
            here = inputs[at : at + len(choices)]
            at += len(choices)
            active = (i >= first) & (i < first + steps)
            if only:
                active = active & (flags_ref[0] == 0)

            @pl.when(active)
            def add(here=here):
                shard = here[0][...]
                if len(here) == 2:
                    shard = jnp.where(end, shard, here[1][...])
                add_dot(total_ref, grads_ref, shard)

        if split:

            @pl.when(i == total - 1)
            def finish():
                turned_ref[...] = total_ref[...].T
                split_rows(turned_ref, keep_ref, give_ref, flags_ref[1])

    whole = lambda i, flags_ref: (0, 0)
    if split:
        out_shape = [jax.ShapeDtypeStruct((cols // 2, tok), jnp.float32)] * 2
        out_specs = [pl.BlockSpec((cols // 2, tok), whole)] * 2
        scratch = [pltpu.VMEM((tok, cols), jnp.float32), pltpu.VMEM((cols, tok), jnp.float32)]
    else:
        out_shape = jax.ShapeDtypeStruct((tok, cols), jnp.float32)
        out_specs = pl.BlockSpec((tok, cols), whole)
        scratch = []
    return pl.pallas_call(
        kernel,
        out_shape=out_shape,
        grid_spec=pltpu.PrefetchScalarGridSpec(
            num_scalar_prefetch=1,
            grid=(total,),
            in_specs=specs,
            out_specs=out_specs,
            scratch_shapes=scratch,
        ),
        compiler_params=pltpu.CompilerParams(vmem_limit_bytes=16 << 20),
        cost_estimate=SHORT,
    )(flags, *operands)


def partner_dots(flags, pieces, shards, wanted, depth, tail=(), grads=None):
    cols = shards[0][0].shape[1]
    step = depth // STEPS
    count = len(pieces)
    width = len(wanted) * TILE
    tok = grads.shape[0] if tail else 0

    def at(row, wanted_at=None):
        def index(i, flags_ref):
            if wanted_at is not None:
                i = i * (flags_ref[0] if wanted_at else 1 - flags_ref[0])
            return (row + i, 0)

        return index

    operands, specs = [], []
    for array, row in list(pieces) + list(shards):
        operands.append(array)
        specs.append(pl.BlockSpec((step, cols), at(row)))
    whole = lambda i, flags_ref: (0, 0)
    for choices, column, only in tail:
        operands.append(grads)
        specs.append(
            pl.BlockSpec((tok, step), lambda i, flags_ref, column=column: (0, column + i))
        )
        for which, (array, row) in enumerate(choices):
            operands.append(array)
            specs.append(
                pl.BlockSpec((step, cols), at(row, None if len(choices) == 1 else which == 0))
            )

    def kernel(flags_ref, *refs):
        i = pl.program_id(0)
        piece_refs, shard_refs = refs[:count], refs[count : count + len(shards)]
        tail_refs = refs[count + len(shards) : len(operands)]
        refs = refs[len(operands) :]
        if tail:
            keep_ref, give_ref, sums_ref, turned_ref, total_ref, wide_ref = refs
        else:
            keep_ref, give_ref, sums_ref, turned_ref = refs

        @pl.when(i == 0)
        def begin():
            sums_ref[...] = jnp.zeros_like(sums_ref)
            if tail:
                total_ref[...] = jnp.zeros_like(total_ref)

        at = 0
        for choices, column, only in tail:
            grads_ref, here = tail_refs[at], tail_refs[at + 1 : at + 1 + len(choices)]
            at += 1 + len(choices)

            @pl.when((flags_ref[0] == 0) | (not only))
            def add(grads_ref=grads_ref, here=here):
                shard = here[0][...]
                if len(here) == 2:
                    shard = jnp.where(flags_ref[0] == 1, shard, here[1][...])
                add_dot(total_ref, grads_ref, shard)

        @pl.when(flags_ref[0] == 0)
        def at_a_middle_plane():
            for t, piece_ref in enumerate(piece_refs):
                tokens = jnp.concatenate(
                    [piece_ref[q * TILE : (q + 1) * TILE, :] for q in range(step // TILE)], axis=1
                )
                for block, (shard, piece) in enumerate(wanted):
                    if piece == t:
                        sums_ref[block] += jnp.dot(
                            tokens, shard_refs[shard][...], preferred_element_type=jnp.float32
                        )

        @pl.when(i == STEPS - 1)
        def finish():
            if tail:
                wide_ref[...] = total_ref[...].T
                split_rows(wide_ref, keep_ref, give_ref, flags_ref[1], pl.ds(0, tok))
            for block in range(len(wanted)):
                turned_ref[...] = sums_ref[block].T
                columns = pl.ds(tok + block * TILE, TILE)
                split_rows(turned_ref, keep_ref, give_ref, flags_ref[1], columns)

    scratch = [
        pltpu.VMEM((len(wanted), TILE, cols), jnp.float32),
        pltpu.VMEM((cols, TILE), jnp.float32),
    ]
    if tail:
        scratch += [pltpu.VMEM((tok, cols), jnp.float32), pltpu.VMEM((cols, tok), jnp.float32)]
    return pl.pallas_call(
        kernel,
        out_shape=[jax.ShapeDtypeStruct((cols // 2, tok + width), jnp.float32)] * 2,
        grid_spec=pltpu.PrefetchScalarGridSpec(
            num_scalar_prefetch=1,
            grid=(STEPS,),
            in_specs=specs,
            out_specs=[pl.BlockSpec((cols // 2, tok + width), whole)] * 2,
            scratch_shapes=scratch,
        ),
        compiler_params=pltpu.CompilerParams(vmem_limit_bytes=24 << 20),
        cost_estimate=SHORT,
    )(flags, *operands)


def stack_blocks(flags, grads, depth):
    tiles = grads.shape[0] // TILE
    half = tiles // 2

    def kernel(flags_ref, grads_ref, first_ref, second_ref):
        for at, out_ref in enumerate((first_ref, second_ref)):

            @pl.when(pl.program_id(0) // half == at)
            def copy(out_ref=out_ref):
                for q in range(depth // TILE):
                    here = slice(q * TILE, (q + 1) * TILE)
                    out_ref[here, :] = grads_ref[:, here]

    return pl.pallas_call(
        kernel,
        out_shape=[jax.ShapeDtypeStruct((half * depth, TILE), grads.dtype)] * 2,
        grid_spec=pltpu.PrefetchScalarGridSpec(
            num_scalar_prefetch=1,
            grid=(tiles,),
            in_specs=[pl.BlockSpec((TILE, depth), lambda t, flags_ref: (t, 0))],
            out_specs=[
                pl.BlockSpec((depth, TILE), lambda t, flags_ref: (jnp.minimum(t, half - 1), 0)),
                pl.BlockSpec((depth, TILE), lambda t, flags_ref: (jnp.maximum(t - half, 0), 0)),
            ],
        ),
        compiler_params=pltpu.CompilerParams(vmem_limit_bytes=16 << 20),
        cost_estimate=SHORT,
    )(flags, grads)


def input_dots(flags, acts, shards):
    tok, depth = acts.shape
    cols = shards[0][0][0].shape[1]
    operands, specs = [acts], [pl.BlockSpec((tok, depth), lambda i, flags_ref: (0, 0))]
    for choices in shards:
        for array, row in choices:
            operands.append(array)
            specs.append(pl.BlockSpec((depth, cols), lambda i, flags_ref, row=row: (row, 0)))

    def kernel(flags_ref, acts_ref, *refs):
        i = pl.program_id(0)
        inputs = list(refs[: len(operands) - 1])
        keep_ref, give_ref, part_ref = refs[len(operands) - 1 :]
        at = 0
        for slot, choices in enumerate(shards):
            here = inputs[at : at + len(choices)]
            at += len(choices)

            @pl.when(i == slot)
            def add(here=here):
                shard = here[0][...]
                if len(here) == 2:
                    shard = jnp.where(flags_ref[0] == 1, shard, here[1][...])
                part_ref[...] = jnp.dot(acts_ref[...], shard, preferred_element_type=jnp.float32)

        split_rows(part_ref, keep_ref, give_ref, flags_ref[1])

    place = pl.BlockSpec((tok // 2, cols), lambda i, flags_ref: (0, flags_ref[2 + i]))
    return pl.pallas_call(
        kernel,
        out_shape=[jax.ShapeDtypeStruct((tok // 2, cols * len(shards)), jnp.float32)] * 2,
        grid_spec=pltpu.PrefetchScalarGridSpec(
            num_scalar_prefetch=1,
            grid=(len(shards),),
            in_specs=specs,
            out_specs=[place, place],
            scratch_shapes=[pltpu.VMEM((tok, cols), jnp.float32)],
        ),
        compiler_params=pltpu.CompilerParams(vmem_limit_bytes=16 << 20),
        cost_estimate=SHORT,
    )(flags, *operands)


def line_plan(acts, grads, basis_in, basis_out, eigval, test_grads, pair_tiles, last_rows):
    plane = lax.axis_index("cand")
    end = (plane == 0) | (plane == 3)
    tok_rows = acts.shape[0]
    cols = basis_in.shape[1]
    tiles_here = tok_rows // TILE
    slim = cols // 4
    depth = basis_out.shape[0] // 3
    rows_in = basis_in.shape[0]

    def pick(at_end, at_middle):
        return jnp.where(end, at_end, at_middle)

    def side(at_end, at_middle):
        return lax.ppermute(pick(at_end, at_middle), "cand", SIDE)

    among = []
    for at in range(16):
        mid = 4 <= at < 12
        among.append((at, (12 - at + 2 * (at % 4)) if mid else at ^ 1))

    def middle(x):
        return lax.ppermute(x, ALL, among)

    at_b = jnp.where(end, plane ^ 2, plane ^ 3)
    at_c = jnp.where(end, plane ^ 3, plane ^ 2)
    rep = lax.axis_index("rep")
    flags = jnp.stack([end.astype(jnp.int32), rep, plane, plane ^ 1, at_b, at_c])

    rows = lax.dynamic_slice_in_dim(basis_out, jnp.where(end, 0, depth), 2 * depth, 0)
    s0 = lax.ppermute(basis_in, "cand", SIDE)
    m0 = middle(basis_in)
    s12 = lax.ppermute(rows, "cand", SIDE)
    second = basis_out[depth : 2 * depth]
    m2 = middle(second)
    started = after(flags, rows, second)
    stacked, more_stacked = stack_blocks(started, grads, depth)
    part_own = feature_dots(started, grads, [([(basis_out, 0)], 0, 0, 3 * STEPS, False)])
    precond = (test_grads.astype(jnp.float32) / (eigval + damping)).astype(jnp.bfloat16)
    m1 = middle(after(s0, m0, precond, stacked, more_stacked, *part_own))
    third = jnp.concatenate([basis_out[2 * depth :], basis_out[: 2 * rows_in - depth]])
    s3 = side(third, jnp.concatenate([m0, m1]))
    m3 = middle(after(basis_out[2 * depth :], m1, m2))
    m5 = middle(s12[depth:])
    to_s45 = pick(stacked, jnp.concatenate([m2, m3]))
    s45 = lax.ppermute(after(to_s45, s3), "cand", SIDE)
    m6 = middle(s3[:depth])
    m4 = middle(after(basis_out[:depth], m5))
    to_s67 = pick(more_stacked, jnp.concatenate([m5, m6]))
    s67 = lax.ppermute(to_s67, "cand", SIDE)
    m7 = middle(after(s12[:depth], m6))

    part_in = input_dots(
        after(flags, s3, m5),
        acts,
        [[(basis_in, 0)], [(s0, 0)], [(s3, 0), (m0, 0)], [(s3, 1), (m1, 0)]],
    )
    part_a = feature_dots(
        after(flags, *part_in),
        grads,
        [
            ([(s12, 0)], STEPS, 0, 2 * STEPS, False),
            ([(s3, 0)], 2 * STEPS, 2 * STEPS, STEPS, True),
        ],
    )
    rot_in = gather_rows(scatter_sum(*after(part_in, s45, to_s67)).astype(jnp.bfloat16))
    rot_in = rot_in.reshape(tiles_here, TILE, 4 * cols)
    part_b = feature_dots(
        after(flags, *part_a, s45, to_s67),
        grads,
        [
            ([(s45, 0), (m2, 0)], STEPS, STEPS, STEPS, False),
            ([(s45, STEPS), (m3, 0)], 2 * STEPS, 2 * STEPS, STEPS, False),
            ([(m4, 0)], 0, 0, STEPS, True),
        ],
    )
    shards = [(basis_out, 0), (m4, 0), (m7, 0)]
    pieces = [(s45, 0), (s45, STEPS), (s67, 0), (s67, STEPS)]
    early = [(shard, piece) for shard in range(2) for piece in range(2)]
    part_early = partner_dots(after(flags, *part_b), pieces[:2], shards[:2], early, depth)
    late = [(2, 0), (2, 1)] + [(shard, piece) for shard in range(3) for piece in (2, 3)]
    parts = [part_own, part_a, part_b, part_early]
    sums = scatter_sum(*[jnp.concatenate(part, axis=1) for part in zip(*parts)])
    part_late = partner_dots(
        after(flags, sums),
        pieces,
        shards,
        late,
        depth,
        [
            ([(s67, 0), (m5, 0)], STEPS, False),
            ([(s67, STEPS), (m6, 0)], 2 * STEPS, False),
            ([(m7, 0)], 0, True),
        ],
        grads,
    )
    sum_own, sum_a, sum_b = [sums[:, i * tok_rows : (i + 1) * tok_rows] for i in range(3)]
    back_early = jnp.where(end, lax.ppermute(sums[:, 3 * tok_rows :], "cand", SIDE), 0.0)
    sum_late = scatter_sum(*part_late)
    sum_c = sum_late[:, :tok_rows]
    back_late = jnp.where(end, lax.ppermute(sum_late[:, tok_rows:], "cand", SIDE), 0.0)
    two = 2 * TILE
    back_a = jnp.concatenate([back_early[:, :two], back_late[:, two : 2 * two]], axis=1)
    back_b = jnp.concatenate([back_early[:, two:], back_late[:, 2 * two : 3 * two]], axis=1)
    back_c = jnp.concatenate([back_late[:, :two], back_late[:, 3 * two :]], axis=1)

    rowmask, ignored = tile_layout(pair_tiles, last_rows, plane * tiles_here, tiles_here, TILE)
    keep = rowmask.reshape(1, tok_rows).astype(jnp.bfloat16)

    def tile_prods(rot_out):
        return jnp.einsum(
            "etr,tra->tea",
            (rot_out.astype(jnp.bfloat16) * keep).reshape(slim, tiles_here, TILE),
            rot_in,
            preferred_element_type=jnp.float32,
        ).astype(jnp.bfloat16)

    def pair_scores(prods, source):
        scores = jnp.einsum("tea,jea->tj", prods, precond, preferred_element_type=jnp.float32)
        ignored_mask, onehot = tile_layout(
            pair_tiles, last_rows, source * tiles_here, tiles_here, TILE
        )
        return jnp.sum(jnp.where(onehot[:, :, None], scores[:, None, :], 0.0), axis=0)

    prods_a = tile_prods(sum_a + back_a)
    prods_b = tile_prods(sum_b + back_b)
    prods_c = tile_prods(sum_c + back_c)
    total = pair_scores(tile_prods(sum_own), plane)
    total = total + pair_scores(lax.ppermute(prods_a, "cand", SIDE), plane ^ 1)
    total = total + pair_scores(lax.ppermute(pick(prods_b, prods_c), "cand", TWO), plane ^ 2)
    total = total + pair_scores(lax.ppermute(pick(prods_c, prods_b), "cand", THREE), plane ^ 3)
    return final_sum(total)


def final_sum(total):
    npairs, ntest = total.shape
    blocks = total.reshape(4, npairs // 4, 4, ntest // 4).transpose(0, 2, 1, 3)
    blocks = blocks.reshape(16, npairs // 4, ntest // 4)
    return jnp.sum(lax.all_to_all(blocks, ALL, 0, 0, tiled=True), axis=0)


def gather_plan(acts, grads, basis_in, basis_out, eigval, test_grads, pair_tiles, last_rows):
    ncand = lax.axis_size("cand")
    nfeat = lax.axis_size(FEAT)
    tok_rows = acts.shape[0]
    width_in = basis_in.shape[1] * ncand
    width_out = basis_out.shape[1] * ncand
    slim = width_out // (ncand * nfeat)
    part_in = jnp.dot(
        acts,
        lax.all_gather(basis_in, "cand", axis=1, tiled=True),
        preferred_element_type=jnp.float32,
    )
    part_out = jnp.dot(
        grads,
        lax.all_gather(basis_out, "cand", axis=1, tiled=True),
        preferred_element_type=jnp.float32,
    )
    part_out = part_out.reshape(tok_rows, ncand, nfeat, slim).transpose(0, 2, 1, 3)
    part_out = part_out.reshape(tok_rows, nfeat * ncand * slim)
    summed_in, summed_out = lax.psum((part_in, part_out), FEAT)
    own = lax.dynamic_slice_in_dim(
        summed_out, lax.axis_index(FEAT) * (ncand * slim), ncand * slim, 1
    )
    rot_in = summed_in.astype(jnp.bfloat16)
    rot_out = own.astype(jnp.bfloat16)
    tiles_here = tok_rows // TILE
    rowmask, ignored = tile_layout(
        pair_tiles, last_rows, lax.axis_index("cand") * tiles_here, tiles_here, TILE
    )
    masked = rot_out.reshape(tiles_here, TILE, ncand * slim) * rowmask[:, :, None].astype(
        jnp.bfloat16
    )
    prods = jnp.einsum(
        "tre,tra->tea",
        masked,
        rot_in.reshape(tiles_here, TILE, width_in),
        preferred_element_type=jnp.float32,
    ).astype(jnp.bfloat16)
    prods = prods.reshape(tiles_here, ncand, slim, width_in)
    received = lax.all_to_all(prods, "cand", split_axis=1, concat_axis=0, tiled=True)
    all_tiles = received.shape[0]
    received = received.reshape(all_tiles, slim, width_in)
    precond = (test_grads.astype(jnp.float32) / (eigval + damping)).astype(jnp.bfloat16)
    tile_part = jnp.einsum("tea,jea->tj", received, precond, preferred_element_type=jnp.float32)
    ignored_mask, onehot = tile_layout(pair_tiles, last_rows, 0, all_tiles, TILE)
    pair_part = jnp.dot(onehot.astype(jnp.float32).T, tile_part, precision=lax.Precision.HIGHEST)
    npairs = pair_part.shape[0]
    ntest = pair_part.shape[1]
    total = lax.psum(pair_part, ("cand", "eig", "rep"))
    rows = lax.dynamic_slice_in_dim(
        total, lax.axis_index("cand") * (npairs // ncand), npairs // ncand, 0
    )
    return lax.dynamic_slice_in_dim(
        rows, lax.axis_index(FEAT) * (ntest // nfeat), ntest // nfeat, 1
    )


def solution(mesh):
    in_specs = (
        P(("groups", "cand"), ("eig", "rep")),
        P(("groups", "cand"), ("eig", "rep")),
        P(("groups", "eig", "rep"), "cand"),
        P(("groups", "eig", "rep"), "cand"),
        P(("groups", "cand", "eig", "rep"), None),
        P("groups", ("cand", "eig", "rep"), None),
        P("groups"),
        P("groups"),
    )
    out_specs = P(("groups", "cand"), ("eig", "rep"))
    sizes = (mesh.shape["cand"], mesh.shape["eig"], mesh.shape["rep"])
    per_device = line_plan if sizes == (4, 2, 2) else gather_plan
    return jax.shard_map(
        per_device, mesh=mesh, in_specs=in_specs, out_specs=out_specs, check_vma=False
    )
```

```python
import jax
import jax.numpy as jnp
from jax import lax
from jax.experimental import pallas as pl
from jax.experimental.pallas import tpu as pltpu
from jax.sharding import PartitionSpec as P

TILE = 128
FEAT = ("eig", "rep")
ALL = ("cand", "eig", "rep")
STEPS = 3
PARAMS = pltpu.CompilerParams(vmem_limit_bytes=56 << 20)
SHORT = pl.CostEstimate(flops=1, bytes_accessed=1, transcendentals=0)
SIDE = ((0, 1), (1, 0), (2, 3), (3, 2))
TWO = ((0, 2), (2, 0), (1, 3), (3, 1))
THREE = ((0, 3), (3, 0), (1, 2), (2, 1))

damping = 0.01


def tile_layout(pair_tiles, last_rows, first_tile, count, tile_rows):
    tiles = first_tile + jnp.arange(count, dtype=jnp.int32)
    ends = jnp.cumsum(pair_tiles)
    owner = jnp.sum((ends[None, :] <= tiles[:, None]).astype(jnp.int32), axis=1)
    onehot = owner[:, None] == jnp.arange(pair_tiles.shape[0], dtype=jnp.int32)[None, :]
    last_of = jnp.sum(jnp.where(onehot, last_rows[None, :], 0), axis=1)
    end_of = jnp.sum(jnp.where(onehot, ends[None, :], 0), axis=1)
    limit = jnp.where(tiles == end_of - 1, last_of, tile_rows)
    rowmask = jnp.arange(tile_rows, dtype=jnp.int32)[None, :] < limit[:, None]
    return (rowmask, onehot)


def after(x, *earlier):
    return lax.optimization_barrier((x, *earlier))[0]


def swap(x, axis_name):
    return lax.ppermute(x, axis_name, [(0, 1), (1, 0)])


def halves(x, axis_name):
    first = lax.axis_index(axis_name) == 0
    low, high = jnp.split(x, 2)
    return jnp.where(first, low, high), jnp.where(first, high, low)


def core_sum(keep, give):
    return keep + swap(give, "rep")


def chip_sum(part):
    keep, give = halves(part, "eig")
    return keep + swap(give, "eig")


def gather_rows(x):
    other = swap(x, "eig")
    first = lax.axis_index("eig") == 0
    both = jnp.stack([jnp.where(first, x, other), jnp.where(first, other, x)])
    other = swap(both, "rep")
    first = lax.axis_index("rep") == 0
    whole = jnp.stack([jnp.where(first, both, other), jnp.where(first, other, both)], axis=1)
    return whole.reshape((-1,) + x.shape[1:])


def split_rows(full_ref, keep_ref, give_ref, rep, columns=None):
    rows = full_ref.shape[0] // 4
    columns = slice(None) if columns is None else columns
    for e in range(2):
        here = pl.ds(e * rows, rows)
        mine = pl.ds(pl.multiple_of((2 * e + rep) * rows, rows), rows)
        theirs = pl.ds(pl.multiple_of((2 * e + 1 - rep) * rows, rows), rows)
        keep_ref[here, columns] = full_ref[mine, :]
        give_ref[here, columns] = full_ref[theirs, :]


def add_dot(total_ref, rows_ref, shard):
    half = total_ref.shape[0] // 2
    for here in (pl.ds(0, half), pl.ds(half, half)):
        total_ref[here, :] += jnp.dot(
            rows_ref[here, :], shard, preferred_element_type=jnp.float32
        )


def feature_dots(flags, grads, segments, start=None, split=True):
    tok = grads.shape[0]
    cols = segments[0][0][0][0].shape[1]
    depth = grads.shape[1] // (3 * STEPS)
    firsts = [sum(s[3] for s in segments[:at]) for at in range(len(segments))]
    total = sum(s[3] for s in segments)

    def grads_at(i, flags_ref):
        at = 0
        for first, (choices, at_end, at_middle, steps, only) in zip(firsts, segments):
            base = at_end + flags_ref[0] * 0 if at_end == at_middle else (
                flags_ref[0] * at_end + (1 - flags_ref[0]) * at_middle
            )
            at = jnp.where(i >= first, base + i - first, at)
        return (0, at)

    def rows_at(first, steps, row, wanted):
        def index(i, flags_ref):
            step = jnp.clip(i - first, 0, steps - 1)
            if wanted is not None:
                step = step * (flags_ref[0] if wanted else 1 - flags_ref[0])
            return (row + step, 0)

        return index

    operands, specs = [grads], [pl.BlockSpec((tok, depth), grads_at)]
    for first, (choices, at_end, at_middle, steps, only) in zip(firsts, segments):
        for which, (array, row) in enumerate(choices):
            wanted = None if len(choices) == 1 else which == 0
            operands.append(array)
            specs.append(pl.BlockSpec((depth, cols), rows_at(first, steps, row, wanted)))
    if start is not None:
        operands.append(start)
        specs.append(pl.BlockSpec((tok, cols), lambda i, flags_ref: (0, 0)))

    def kernel(flags_ref, grads_ref, *refs):
        i = pl.program_id(0)
        end = flags_ref[0] == 1
        inputs, rest = list(refs[: len(operands) - 1]), refs[len(operands) - 1 :]
        if split:
            keep_ref, give_ref, total_ref, turned_ref = rest
        else:
            (total_ref,) = rest

        @pl.when(i == 0)
        def begin():
            total_ref[...] = jnp.zeros_like(total_ref) if start is None else inputs[-1][...]

        at = 0
        for first, (choices, at_end, at_middle, steps, only) in zip(firsts, segments):
            here = inputs[at : at + len(choices)]
            at += len(choices)
            active = (i >= first) & (i < first + steps)
            if only:
                active = active & (flags_ref[0] == 0)

            @pl.when(active)
            def add(here=here):
                shard = here[0][...]
                if len(here) == 2:
                    shard = jnp.where(end, shard, here[1][...])
                add_dot(total_ref, grads_ref, shard)

        if split:

            @pl.when(i == total - 1)
            def finish():
                turned_ref[...] = total_ref[...].T
                split_rows(turned_ref, keep_ref, give_ref, flags_ref[1])

    whole = lambda i, flags_ref: (0, 0)
    if split:
        out_shape = [jax.ShapeDtypeStruct((cols // 2, tok), jnp.float32)] * 2
        out_specs = [pl.BlockSpec((cols // 2, tok), whole)] * 2
        scratch = [pltpu.VMEM((tok, cols), jnp.float32), pltpu.VMEM((cols, tok), jnp.float32)]
    else:
        out_shape = jax.ShapeDtypeStruct((tok, cols), jnp.float32)
        out_specs = pl.BlockSpec((tok, cols), whole)
        scratch = []
    return pl.pallas_call(
        kernel,
        out_shape=out_shape,
        grid_spec=pltpu.PrefetchScalarGridSpec(
            num_scalar_prefetch=1,
            grid=(total,),
            in_specs=specs,
            out_specs=out_specs,
            scratch_shapes=scratch,
        ),
        compiler_params=PARAMS,
        cost_estimate=SHORT,
    )(flags, *operands)


def partner_dots(flags, pieces, shards, wanted, depth, grads=None, tail=(), start=None):
    cols = shards[0][0].shape[1]
    step = depth // STEPS
    count = len(pieces)
    tok = grads.shape[0] if tail else 0
    ahead = tok if start is not None else 0
    width = ahead + len(wanted) * TILE

    def at(row, wanted_at=None):
        def index(i, flags_ref):
            if wanted_at is not None:
                i = i * (flags_ref[0] if wanted_at else 1 - flags_ref[0])
            return (row + i, 0)

        return index

    operands, specs = [], []
    for array, row in list(pieces) + list(shards):
        operands.append(array)
        specs.append(pl.BlockSpec((step, cols), at(row)))
    whole = lambda i, flags_ref: (0, 0)
    for choices, column, only in tail:
        operands.append(grads)
        specs.append(
            pl.BlockSpec((tok, step), lambda i, flags_ref, column=column: (0, column + i))
        )
        for which, (array, row) in enumerate(choices):
            operands.append(array)
            specs.append(
                pl.BlockSpec((step, cols), at(row, None if len(choices) == 1 else which == 0))
            )
    if start is not None:
        operands.append(start)
        specs.append(pl.BlockSpec((tok, cols), whole))

    def kernel(flags_ref, *refs):
        i = pl.program_id(0)
        piece_refs, shard_refs = refs[:count], refs[count : count + len(shards)]
        tail_refs = refs[count + len(shards) : len(operands)]
        keep_ref, give_ref, *rest = refs[len(operands) :]
        if tail and start is None:
            total_ref, sums_ref, turned_ref = rest
        elif tail:
            sums_ref, turned_ref, total_ref, wide_ref = rest
        else:
            sums_ref, turned_ref = rest

        @pl.when(i == 0)
        def begin():
            sums_ref[...] = jnp.zeros_like(sums_ref)
            if tail:
                total_ref[...] = jnp.zeros_like(total_ref) if start is None else tail_refs[-1][...]

        at = 0
        for choices, column, only in tail:
            grads_ref, here = tail_refs[at], tail_refs[at + 1 : at + 1 + len(choices)]
            at += 1 + len(choices)

            @pl.when((flags_ref[0] == 0) | (not only))
            def add(grads_ref=grads_ref, here=here):
                shard = here[0][...]
                if len(here) == 2:
                    shard = jnp.where(flags_ref[0] == 1, shard, here[1][...])
                add_dot(total_ref, grads_ref, shard)

        @pl.when(flags_ref[0] == 0)
        def at_a_middle_plane():
            for t, piece_ref in enumerate(piece_refs):
                tokens = jnp.concatenate(
                    [piece_ref[q * TILE : (q + 1) * TILE, :] for q in range(step // TILE)], axis=1
                )
                for block, (shard, piece) in enumerate(wanted):
                    if piece == t:
                        sums_ref[block] += jnp.dot(
                            tokens, shard_refs[shard][...], preferred_element_type=jnp.float32
                        )

        @pl.when(i == STEPS - 1)
        def finish():
            if ahead:
                wide_ref[...] = total_ref[...].T
                split_rows(wide_ref, keep_ref, give_ref, flags_ref[1], pl.ds(0, tok))
            for block in range(len(wanted)):
                turned_ref[...] = sums_ref[block].T
                columns = pl.ds(ahead + block * TILE, TILE)
                split_rows(turned_ref, keep_ref, give_ref, flags_ref[1], columns)

    out_shape = [jax.ShapeDtypeStruct((cols // 2, width), jnp.float32)] * 2
    out_specs = [pl.BlockSpec((cols // 2, width), whole)] * 2
    scratch = [
        pltpu.VMEM((len(wanted), TILE, cols), jnp.float32),
        pltpu.VMEM((cols, TILE), jnp.float32),
    ]
    if tail and start is None:
        out_shape.append(jax.ShapeDtypeStruct((tok, cols), jnp.float32))
        out_specs.append(pl.BlockSpec((tok, cols), whole))
    elif tail:
        scratch += [pltpu.VMEM((tok, cols), jnp.float32), pltpu.VMEM((cols, tok), jnp.float32)]
    return pl.pallas_call(
        kernel,
        out_shape=out_shape,
        grid_spec=pltpu.PrefetchScalarGridSpec(
            num_scalar_prefetch=1,
            grid=(STEPS,),
            in_specs=specs,
            out_specs=out_specs,
            scratch_shapes=scratch,
        ),
        compiler_params=PARAMS,
        cost_estimate=SHORT,
    )(flags, *operands)


def stack_blocks(flags, grads, depth):
    tiles = grads.shape[0] // TILE
    firsts = [0] + list(range(tiles // 2, tiles))
    counts = [tiles // 2] + [1] * (tiles // 2)

    def kernel(flags_ref, grads_ref, *out_refs):
        t = pl.program_id(0)
        for first, count, out_ref in zip(firsts, counts, out_refs):

            @pl.when((t >= first) & (t < first + count))
            def copy(out_ref=out_ref):
                for q in range(depth // TILE):
                    here = slice(q * TILE, (q + 1) * TILE)
                    out_ref[here, :] = grads_ref[:, here]

    def place(first, count):
        return lambda t, flags_ref: (jnp.clip(t - first, 0, count - 1), 0)

    return pl.pallas_call(
        kernel,
        out_shape=[jax.ShapeDtypeStruct((count * depth, TILE), grads.dtype) for count in counts],
        grid_spec=pltpu.PrefetchScalarGridSpec(
            num_scalar_prefetch=1,
            grid=(tiles,),
            in_specs=[pl.BlockSpec((TILE, depth), lambda t, flags_ref: (t, 0))],
            out_specs=[
                pl.BlockSpec((depth, TILE), place(first, count))
                for first, count in zip(firsts, counts)
            ],
        ),
        compiler_params=PARAMS,
        cost_estimate=SHORT,
    )(flags, grads)


def input_dots(flags, acts, shards):
    tok, depth = acts.shape
    cols = shards[0][0][0].shape[1]
    operands, specs = [acts], [pl.BlockSpec((tok, depth), lambda i, flags_ref: (0, 0))]
    for choices in shards:
        for array, row in choices:
            operands.append(array)
            specs.append(pl.BlockSpec((depth, cols), lambda i, flags_ref, row=row: (row, 0)))

    def kernel(flags_ref, acts_ref, *refs):
        i = pl.program_id(0)
        inputs = list(refs[: len(operands) - 1])
        keep_ref, give_ref, part_ref = refs[len(operands) - 1 :]
        at = 0
        for slot, choices in enumerate(shards):
            here = inputs[at : at + len(choices)]
            at += len(choices)

            @pl.when(i == slot)
            def add(here=here):
                shard = here[0][...]
                if len(here) == 2:
                    shard = jnp.where(flags_ref[0] == 1, shard, here[1][...])
                part_ref[...] = jnp.dot(acts_ref[...], shard, preferred_element_type=jnp.float32)

        split_rows(part_ref, keep_ref, give_ref, flags_ref[1])

    place = pl.BlockSpec((tok // 2, cols), lambda i, flags_ref: (0, flags_ref[2 + i]))
    return pl.pallas_call(
        kernel,
        out_shape=[jax.ShapeDtypeStruct((tok // 2, cols * len(shards)), jnp.float32)] * 2,
        grid_spec=pltpu.PrefetchScalarGridSpec(
            num_scalar_prefetch=1,
            grid=(len(shards),),
            in_specs=specs,
            out_specs=[place, place],
            scratch_shapes=[pltpu.VMEM((tok, cols), jnp.float32)],
        ),
        compiler_params=PARAMS,
        cost_estimate=SHORT,
    )(flags, *operands)


def line_plan(acts, grads, basis_in, basis_out, eigval, test_grads, pair_tiles, last_rows):
    plane = lax.axis_index("cand")
    end = (plane == 0) | (plane == 3)
    tok_rows = acts.shape[0]
    cols = basis_in.shape[1]
    tiles_here = tok_rows // TILE
    slim = cols // 4
    depth = basis_out.shape[0] // 3
    rows_in = basis_in.shape[0]

    def pick(at_end, at_middle):
        return jnp.where(end, at_end, at_middle)

    def side(at_end, at_middle):
        return lax.ppermute(pick(at_end, at_middle), "cand", SIDE)

    among = []
    for at in range(16):
        mid = 4 <= at < 12
        among.append((at, (12 - at + 2 * (at % 4)) if mid else at ^ 1))

    def middle(x):
        return lax.ppermute(x, ALL, among)

    at_b = jnp.where(end, plane ^ 2, plane ^ 3)
    at_c = jnp.where(end, plane ^ 3, plane ^ 2)
    rep = lax.axis_index("rep")
    flags = jnp.stack([end.astype(jnp.int32), rep, plane, plane ^ 1, at_b, at_c])

    rows = lax.dynamic_slice_in_dim(basis_out, jnp.where(end, 0, depth), 2 * depth, 0)
    s0 = lax.ppermute(basis_in, "cand", SIDE)
    m0 = middle(basis_in)
    s12 = lax.ppermute(rows, "cand", SIDE)
    second = basis_out[depth : 2 * depth]
    m2 = middle(second)
    started = after(flags, rows, second)
    stacked, *more_stacked = stack_blocks(started, grads, depth)
    part_own = feature_dots(started, grads, [([(basis_out, 0)], 0, 0, 3 * STEPS, False)])
    precond = (test_grads.astype(jnp.float32) / (eigval + damping)).astype(jnp.bfloat16)
    m1 = middle(after(s0, m0, precond, stacked, *more_stacked, *part_own))
    third = jnp.concatenate([basis_out[2 * depth :], basis_out[: 2 * rows_in - depth]])
    s3 = side(third, jnp.concatenate([m0, m1]))
    m3 = middle(after(basis_out[2 * depth :], m1, m2))
    m5 = middle(s12[depth:])
    to_s45 = pick(stacked, jnp.concatenate([m2, m3]))
    s45 = lax.ppermute(after(to_s45, s3), "cand", SIDE)
    m6 = middle(s3[:depth])
    m4 = middle(after(basis_out[:depth], m5))
    s6 = side(more_stacked[0], m5)
    s7 = side(after(more_stacked[1], s45), m6)
    m7 = middle(after(s12[:depth], m6))

    part_in = input_dots(
        after(flags, s3, m5),
        acts,
        [[(basis_in, 0)], [(s0, 0)], [(s3, 0), (m0, 0)], [(s3, 1), (m1, 0)]],
    )
    part_a = feature_dots(
        after(flags, *part_in),
        grads,
        [
            ([(s12, 0)], STEPS, 0, 2 * STEPS, False),
            ([(s3, 0)], 2 * STEPS, 2 * STEPS, STEPS, True),
        ],
    )
    part_b = feature_dots(
        after(flags, *part_a, s45),
        grads,
        [
            ([(s45, 0), (m2, 0)], STEPS, STEPS, STEPS, False),
            ([(s45, STEPS), (m3, 0)], 2 * STEPS, 2 * STEPS, STEPS, False),
            ([(m4, 0)], 0, 0, STEPS, True),
        ],
    )
    shards = [(basis_out, 0), (m4, 0), (m7, 0)]
    pieces = [(s45, 0), (s45, STEPS), (s6, 0), (s7, 0)]
    blocks = [(shard, piece) for piece in (0, 1) for shard in (0, 1)]
    part_first = partner_dots(after(flags, *part_b), pieces[:2], shards[:2], blocks, depth)
    *part_second, part_c = partner_dots(
        after(flags, *part_first),
        pieces[:3],
        shards,
        [(2, 0), (2, 1), (0, 2), (1, 2), (2, 2)],
        depth,
        grads,
        [([(s6, 0), (m5, 0)], STEPS, False), ([(m7, 0)], 0, True)],
    )
    rot_in = chip_sum(core_sum(*after(part_in, s6, m7)))
    rot_in = gather_rows(rot_in.astype(jnp.bfloat16))
    rot_in = rot_in.reshape(tiles_here, TILE, 4 * cols)
    parts = [part_own, part_a, part_b, part_first]
    parts = [jnp.concatenate(part, axis=1) for part in zip(*parts)]
    core_sums = core_sum(*after(parts, s6, m7))
    sums = chip_sum(jnp.concatenate([core_sums, core_sum(*part_second)], axis=1))
    sum_own, sum_a, sum_b = [sums[:, i * tok_rows : (i + 1) * tok_rows] for i in range(3)]
    part_last = partner_dots(
        after(flags, part_c, core_sums),
        pieces[3:],
        shards,
        [(0, 0), (1, 0), (2, 0)],
        depth,
        grads,
        [([(s7, 0), (m6, 0)], 2 * STEPS, False)],
        part_c,
    )
    sum_last = chip_sum(core_sum(*part_last))
    sum_c = sum_last[:, :tok_rows]
    back = jnp.where(end, lax.ppermute(sums[:, 3 * tok_rows :], "cand", SIDE), 0.0)
    last = jnp.where(end, lax.ppermute(sum_last[:, tok_rows:], "cand", SIDE), 0.0)
    back = [back[:, i * TILE : (i + 1) * TILE] for i in range(9)]
    last = [last[:, i * TILE : (i + 1) * TILE] for i in range(3)]
    back_a = jnp.concatenate([back[0], back[2], back[6], last[0]], axis=1)
    back_b = jnp.concatenate([back[1], back[3], back[7], last[1]], axis=1)
    back_c = jnp.concatenate([back[4], back[5], back[8], last[2]], axis=1)

    rowmask, ignored = tile_layout(pair_tiles, last_rows, plane * tiles_here, tiles_here, TILE)
    keep = rowmask.reshape(1, tok_rows).astype(jnp.bfloat16)

    def tile_prods(rot_out):
        return jnp.einsum(
            "etr,tra->tea",
            (rot_out.astype(jnp.bfloat16) * keep).reshape(slim, tiles_here, TILE),
            rot_in,
            preferred_element_type=jnp.float32,
        ).astype(jnp.bfloat16)

    def pair_scores(prods, source):
        scores = jnp.einsum("tea,jea->tj", prods, precond, preferred_element_type=jnp.float32)
        ignored_mask, onehot = tile_layout(
            pair_tiles, last_rows, source * tiles_here, tiles_here, TILE
        )
        return jnp.sum(jnp.where(onehot[:, :, None], scores[:, None, :], 0.0), axis=0)

    prods_a = tile_prods(sum_a + back_a)
    prods_b = tile_prods(sum_b + back_b)
    prods_c = tile_prods(sum_c + back_c)
    total = pair_scores(tile_prods(sum_own), plane)
    total = total + pair_scores(lax.ppermute(prods_a, "cand", SIDE), plane ^ 1)
    total = total + pair_scores(lax.ppermute(pick(prods_b, prods_c), "cand", TWO), plane ^ 2)
    total = total + pair_scores(lax.ppermute(pick(prods_c, prods_b), "cand", THREE), plane ^ 3)
    return final_sum(total)


def final_sum(total):
    npairs, ntest = total.shape
    blocks = total.reshape(4, npairs // 4, 4, ntest // 4).transpose(0, 2, 1, 3)
    blocks = blocks.reshape(16, npairs // 4, ntest // 4)
    return jnp.sum(lax.all_to_all(blocks, ALL, 0, 0, tiled=True), axis=0)


def gather_plan(acts, grads, basis_in, basis_out, eigval, test_grads, pair_tiles, last_rows):
    ncand = lax.axis_size("cand")
    nfeat = lax.axis_size(FEAT)
    tok_rows = acts.shape[0]
    width_in = basis_in.shape[1] * ncand
    width_out = basis_out.shape[1] * ncand
    slim = width_out // (ncand * nfeat)
    part_in = jnp.dot(
        acts,
        lax.all_gather(basis_in, "cand", axis=1, tiled=True),
        preferred_element_type=jnp.float32,
    )
    part_out = jnp.dot(
        grads,
        lax.all_gather(basis_out, "cand", axis=1, tiled=True),
        preferred_element_type=jnp.float32,
    )
    part_out = part_out.reshape(tok_rows, ncand, nfeat, slim).transpose(0, 2, 1, 3)
    part_out = part_out.reshape(tok_rows, nfeat * ncand * slim)
    summed_in, summed_out = lax.psum((part_in, part_out), FEAT)
    own = lax.dynamic_slice_in_dim(
        summed_out, lax.axis_index(FEAT) * (ncand * slim), ncand * slim, 1
    )
    rot_in = summed_in.astype(jnp.bfloat16)
    rot_out = own.astype(jnp.bfloat16)
    tiles_here = tok_rows // TILE
    rowmask, ignored = tile_layout(
        pair_tiles, last_rows, lax.axis_index("cand") * tiles_here, tiles_here, TILE
    )
    masked = rot_out.reshape(tiles_here, TILE, ncand * slim) * rowmask[:, :, None].astype(
        jnp.bfloat16
    )
    prods = jnp.einsum(
        "tre,tra->tea",
        masked,
        rot_in.reshape(tiles_here, TILE, width_in),
        preferred_element_type=jnp.float32,
    ).astype(jnp.bfloat16)
    prods = prods.reshape(tiles_here, ncand, slim, width_in)
    received = lax.all_to_all(prods, "cand", split_axis=1, concat_axis=0, tiled=True)
    all_tiles = received.shape[0]
    received = received.reshape(all_tiles, slim, width_in)
    precond = (test_grads.astype(jnp.float32) / (eigval + damping)).astype(jnp.bfloat16)
    tile_part = jnp.einsum("tea,jea->tj", received, precond, preferred_element_type=jnp.float32)
    ignored_mask, onehot = tile_layout(pair_tiles, last_rows, 0, all_tiles, TILE)
    pair_part = jnp.dot(onehot.astype(jnp.float32).T, tile_part, precision=lax.Precision.HIGHEST)
    npairs = pair_part.shape[0]
    ntest = pair_part.shape[1]
    total = lax.psum(pair_part, ("cand", "eig", "rep"))
    rows = lax.dynamic_slice_in_dim(
        total, lax.axis_index("cand") * (npairs // ncand), npairs // ncand, 0
    )
    return lax.dynamic_slice_in_dim(
        rows, lax.axis_index(FEAT) * (ntest // nfeat), ntest // nfeat, 1
    )


def solution(mesh):
    in_specs = (
        P(("groups", "cand"), ("eig", "rep")),
        P(("groups", "cand"), ("eig", "rep")),
        P(("groups", "eig", "rep"), "cand"),
        P(("groups", "eig", "rep"), "cand"),
        P(("groups", "cand", "eig", "rep"), None),
        P("groups", ("cand", "eig", "rep"), None),
        P("groups"),
        P("groups"),
    )
    out_specs = P(("groups", "cand"), ("eig", "rep"))
    sizes = (mesh.shape["cand"], mesh.shape["eig"], mesh.shape["rep"])
    per_device = line_plan if sizes == (4, 2, 2) else gather_plan
    return jax.shard_map(
        per_device, mesh=mesh, in_specs=in_specs, out_specs=out_specs, check_vma=False
    )
```

```python
import jax
import jax.numpy as jnp
from jax import lax
from jax.experimental import pallas as pl
from jax.experimental.pallas import tpu as pltpu
from jax.sharding import PartitionSpec as P

TILE = 128
FEAT = ("eig", "rep")
ALL = ("cand", "eig", "rep")
STEPS = 3
PARAMS = pltpu.CompilerParams(vmem_limit_bytes=20 << 20)
SHORT = pl.CostEstimate(flops=1, bytes_accessed=1, transcendentals=0)
SIDE = ((0, 1), (1, 0), (2, 3), (3, 2))
TWO = ((0, 2), (2, 0), (1, 3), (3, 1))

damping = 0.01


def tile_layout(pair_tiles, last_rows, first_tile, count, tile_rows):
    tiles = first_tile + jnp.arange(count, dtype=jnp.int32)
    ends = jnp.cumsum(pair_tiles)
    owner = jnp.sum((ends[None, :] <= tiles[:, None]).astype(jnp.int32), axis=1)
    onehot = owner[:, None] == jnp.arange(pair_tiles.shape[0], dtype=jnp.int32)[None, :]
    last_of = jnp.sum(jnp.where(onehot, last_rows[None, :], 0), axis=1)
    end_of = jnp.sum(jnp.where(onehot, ends[None, :], 0), axis=1)
    limit = jnp.where(tiles == end_of - 1, last_of, tile_rows)
    rowmask = jnp.arange(tile_rows, dtype=jnp.int32)[None, :] < limit[:, None]
    return (rowmask, onehot)


def after(x, *earlier):
    return lax.optimization_barrier((x, *earlier))[0]


def swap(x, axis_name):
    return lax.ppermute(x, axis_name, [(0, 1), (1, 0)])


def halves(x, axis_name):
    first = lax.axis_index(axis_name) == 0
    low, high = jnp.split(x, 2)
    return jnp.where(first, low, high), jnp.where(first, high, low)


def core_sum(keep, give):
    return keep + swap(give, "rep")


def chip_sum(part):
    keep, give = halves(part, "eig")
    return keep + swap(give, "eig")


def gather_rows(x):
    other = swap(x, "eig")
    first = lax.axis_index("eig") == 0
    both = jnp.stack([jnp.where(first, x, other), jnp.where(first, other, x)])
    other = swap(both, "rep")
    first = lax.axis_index("rep") == 0
    whole = jnp.stack([jnp.where(first, both, other), jnp.where(first, other, both)], axis=1)
    return whole.reshape((-1,) + x.shape[1:])


def split_rows(full_ref, keep_ref, give_ref, rep, columns=None):
    rows = full_ref.shape[0] // 4
    columns = slice(None) if columns is None else columns
    for e in range(2):
        here = pl.ds(e * rows, rows)
        mine = pl.ds(pl.multiple_of((2 * e + rep) * rows, rows), rows)
        theirs = pl.ds(pl.multiple_of((2 * e + 1 - rep) * rows, rows), rows)
        keep_ref[here, columns] = full_ref[mine, :]
        give_ref[here, columns] = full_ref[theirs, :]


def add_dot(total_ref, rows_ref, shard):
    half = total_ref.shape[0] // 2
    for here in (pl.ds(0, half), pl.ds(half, half)):
        total_ref[here, :] += jnp.dot(
            rows_ref[here, :], shard, preferred_element_type=jnp.float32
        )


def feature_dots(flags, grads, segments, start=None, split=True):
    tok = grads.shape[0]
    cols = segments[0][0][0][0].shape[1]
    depth = grads.shape[1] // (3 * STEPS)
    firsts = [sum(s[3] for s in segments[:at]) for at in range(len(segments))]
    total = sum(s[3] for s in segments)

    def grads_at(i, flags_ref):
        at = 0
        for first, (choices, at_end, at_middle, steps, only) in zip(firsts, segments):
            base = at_end + flags_ref[0] * 0 if at_end == at_middle else (
                flags_ref[0] * at_end + (1 - flags_ref[0]) * at_middle
            )
            at = jnp.where(i >= first, base + i - first, at)
        return (0, at)

    def rows_at(first, steps, row, wanted):
        def index(i, flags_ref):
            step = jnp.clip(i - first, 0, steps - 1)
            if wanted is not None:
                step = step * (flags_ref[0] if wanted else 1 - flags_ref[0])
            return (row + step, 0)

        return index

    operands, specs = [grads], [pl.BlockSpec((tok, depth), grads_at)]
    for first, (choices, at_end, at_middle, steps, only) in zip(firsts, segments):
        for which, (array, row) in enumerate(choices):
            wanted = None if len(choices) == 1 else which == 0
            operands.append(array)
            specs.append(pl.BlockSpec((depth, cols), rows_at(first, steps, row, wanted)))
    if start is not None:
        operands.append(start)
        specs.append(pl.BlockSpec((tok, cols), lambda i, flags_ref: (0, 0)))

    def kernel(flags_ref, grads_ref, *refs):
        i = pl.program_id(0)
        end = flags_ref[0] == 1
        inputs, rest = list(refs[: len(operands) - 1]), refs[len(operands) - 1 :]
        if split:
            keep_ref, give_ref, total_ref, turned_ref = rest
        else:
            (total_ref,) = rest

        @pl.when(i == 0)
        def begin():
            total_ref[...] = jnp.zeros_like(total_ref) if start is None else inputs[-1][...]

        at = 0
        for first, (choices, at_end, at_middle, steps, only) in zip(firsts, segments):
            here = inputs[at : at + len(choices)]
            at += len(choices)
            active = (i >= first) & (i < first + steps)
            if only:
                active = active & (flags_ref[0] == 0)

            @pl.when(active)
            def add(here=here):
                shard = here[0][...]
                if len(here) == 2:
                    shard = jnp.where(end, shard, here[1][...])
                add_dot(total_ref, grads_ref, shard)

        if split:

            @pl.when(i == total - 1)
            def finish():
                turned_ref[...] = total_ref[...].T
                split_rows(turned_ref, keep_ref, give_ref, flags_ref[1])

    whole = lambda i, flags_ref: (0, 0)
    if split:
        out_shape = [jax.ShapeDtypeStruct((cols // 2, tok), jnp.float32)] * 2
        out_specs = [pl.BlockSpec((cols // 2, tok), whole)] * 2
        scratch = [pltpu.VMEM((tok, cols), jnp.float32), pltpu.VMEM((cols, tok), jnp.float32)]
    else:
        out_shape = jax.ShapeDtypeStruct((tok, cols), jnp.float32)
        out_specs = pl.BlockSpec((tok, cols), whole)
        scratch = []
    return pl.pallas_call(
        kernel,
        out_shape=out_shape,
        grid_spec=pltpu.PrefetchScalarGridSpec(
            num_scalar_prefetch=1,
            grid=(total,),
            in_specs=specs,
            out_specs=out_specs,
            scratch_shapes=scratch,
        ),
        compiler_params=PARAMS,
        cost_estimate=SHORT,
    )(flags, *operands)


def partner_dots(flags, pieces, shards, wanted, depth, grads=None, tail=(), start=None):
    cols = shards[0][0].shape[1]
    step = depth // STEPS
    count = len(pieces)
    tok = grads.shape[0] if tail else 0
    ahead = tok if start is not None else 0
    width = ahead + len(wanted) * TILE

    def at(row, wanted_at=None):
        def index(i, flags_ref):
            if wanted_at is not None:
                i = i * (flags_ref[0] if wanted_at else 1 - flags_ref[0])
            return (row + i, 0)

        return index

    operands, specs = [], []
    for array, row in list(pieces) + list(shards):
        operands.append(array)
        specs.append(pl.BlockSpec((step, cols), at(row)))
    whole = lambda i, flags_ref: (0, 0)
    for choices, column, only in tail:
        operands.append(grads)
        specs.append(
            pl.BlockSpec((tok, step), lambda i, flags_ref, column=column: (0, column + i))
        )
        for which, (array, row) in enumerate(choices):
            operands.append(array)
            specs.append(
                pl.BlockSpec((step, cols), at(row, None if len(choices) == 1 else which == 0))
            )
    if start is not None:
        operands.append(start)
        specs.append(pl.BlockSpec((tok, cols), whole))

    def kernel(flags_ref, *refs):
        i = pl.program_id(0)
        piece_refs, shard_refs = refs[:count], refs[count : count + len(shards)]
        tail_refs = refs[count + len(shards) : len(operands)]
        keep_ref, give_ref, *rest = refs[len(operands) :]
        if tail and start is None:
            total_ref, sums_ref, turned_ref = rest
        elif tail:
            sums_ref, turned_ref, total_ref, wide_ref = rest
        else:
            sums_ref, turned_ref = rest

        @pl.when(i == 0)
        def begin():
            sums_ref[...] = jnp.zeros_like(sums_ref)
            if tail:
                total_ref[...] = jnp.zeros_like(total_ref) if start is None else tail_refs[-1][...]

        at = 0
        for choices, column, only in tail:
            grads_ref, here = tail_refs[at], tail_refs[at + 1 : at + 1 + len(choices)]
            at += 1 + len(choices)

            @pl.when((flags_ref[0] == 0) | (not only))
            def add(grads_ref=grads_ref, here=here):
                shard = here[0][...]
                if len(here) == 2:
                    shard = jnp.where(flags_ref[0] == 1, shard, here[1][...])
                add_dot(total_ref, grads_ref, shard)

        @pl.when(flags_ref[0] == 0)
        def at_a_middle_plane():
            for t, piece_ref in enumerate(piece_refs):
                tokens = jnp.concatenate(
                    [piece_ref[q * TILE : (q + 1) * TILE, :] for q in range(step // TILE)], axis=1
                )
                for block, (shard, piece) in enumerate(wanted):
                    if piece == t:
                        sums_ref[block] += jnp.dot(
                            tokens, shard_refs[shard][...], preferred_element_type=jnp.float32
                        )

        @pl.when(i == STEPS - 1)
        def finish():
            if ahead:
                wide_ref[...] = total_ref[...].T
                split_rows(wide_ref, keep_ref, give_ref, flags_ref[1], pl.ds(0, tok))
            for block in range(len(wanted)):
                turned_ref[...] = sums_ref[block].T
                columns = pl.ds(ahead + block * TILE, TILE)
                split_rows(turned_ref, keep_ref, give_ref, flags_ref[1], columns)

    out_shape = [jax.ShapeDtypeStruct((cols // 2, width), jnp.float32)] * 2
    out_specs = [pl.BlockSpec((cols // 2, width), whole)] * 2
    scratch = [
        pltpu.VMEM((len(wanted), TILE, cols), jnp.float32),
        pltpu.VMEM((cols, TILE), jnp.float32),
    ]
    if tail and start is None:
        out_shape.append(jax.ShapeDtypeStruct((tok, cols), jnp.float32))
        out_specs.append(pl.BlockSpec((tok, cols), whole))
    elif tail:
        scratch += [pltpu.VMEM((tok, cols), jnp.float32), pltpu.VMEM((cols, tok), jnp.float32)]
    return pl.pallas_call(
        kernel,
        out_shape=out_shape,
        grid_spec=pltpu.PrefetchScalarGridSpec(
            num_scalar_prefetch=1,
            grid=(STEPS,),
            in_specs=specs,
            out_specs=out_specs,
            scratch_shapes=scratch,
        ),
        compiler_params=PARAMS,
        cost_estimate=SHORT,
    )(flags, *operands)


def stack_blocks(flags, grads, depth):
    tiles = grads.shape[0] // TILE
    firsts = [0] + list(range(tiles // 2, tiles))
    counts = [tiles // 2] + [1] * (tiles // 2)

    def kernel(flags_ref, grads_ref, *out_refs):
        t = pl.program_id(0)
        for first, count, out_ref in zip(firsts, counts, out_refs):

            @pl.when((t >= first) & (t < first + count))
            def copy(out_ref=out_ref):
                for q in range(depth // TILE):
                    here = slice(q * TILE, (q + 1) * TILE)
                    out_ref[here, :] = grads_ref[:, here]

    def place(first, count):
        return lambda t, flags_ref: (jnp.clip(t - first, 0, count - 1), 0)

    return pl.pallas_call(
        kernel,
        out_shape=[jax.ShapeDtypeStruct((count * depth, TILE), grads.dtype) for count in counts],
        grid_spec=pltpu.PrefetchScalarGridSpec(
            num_scalar_prefetch=1,
            grid=(tiles,),
            in_specs=[pl.BlockSpec((TILE, depth), lambda t, flags_ref: (t, 0))],
            out_specs=[
                pl.BlockSpec((depth, TILE), place(first, count))
                for first, count in zip(firsts, counts)
            ],
        ),
        compiler_params=PARAMS,
        cost_estimate=SHORT,
    )(flags, grads)


def input_dots(flags, acts, shards):
    tok, depth = acts.shape
    cols = shards[0][0][0].shape[1]
    operands, specs = [acts], [pl.BlockSpec((tok, depth), lambda i, flags_ref: (0, 0))]
    for choices in shards:
        for array, row in choices:
            operands.append(array)
            specs.append(pl.BlockSpec((depth, cols), lambda i, flags_ref, row=row: (row, 0)))

    def kernel(flags_ref, acts_ref, *refs):
        i = pl.program_id(0)
        inputs = list(refs[: len(operands) - 1])
        keep_ref, give_ref, part_ref = refs[len(operands) - 1 :]
        at = 0
        for slot, choices in enumerate(shards):
            here = inputs[at : at + len(choices)]
            at += len(choices)

            @pl.when(i == slot)
            def add(here=here):
                shard = here[0][...]
                if len(here) == 2:
                    shard = jnp.where(flags_ref[0] == 1, shard, here[1][...])
                part_ref[...] = jnp.dot(acts_ref[...], shard, preferred_element_type=jnp.float32)

        split_rows(part_ref, keep_ref, give_ref, flags_ref[1])

    place = pl.BlockSpec((tok // 2, cols), lambda i, flags_ref: (0, flags_ref[2 + i]))
    return pl.pallas_call(
        kernel,
        out_shape=[jax.ShapeDtypeStruct((tok // 2, cols * len(shards)), jnp.float32)] * 2,
        grid_spec=pltpu.PrefetchScalarGridSpec(
            num_scalar_prefetch=1,
            grid=(len(shards),),
            in_specs=specs,
            out_specs=[place, place],
            scratch_shapes=[pltpu.VMEM((tok, cols), jnp.float32)],
        ),
        compiler_params=PARAMS,
        cost_estimate=SHORT,
    )(flags, *operands)


def line_plan(acts, grads, basis_in, basis_out, eigval, test_grads, pair_tiles, last_rows):
    plane = lax.axis_index("cand")
    end = (plane == 0) | (plane == 3)
    tok_rows = acts.shape[0]
    cols = basis_in.shape[1]
    tiles_here = tok_rows // TILE
    slim = cols // 4
    depth = basis_out.shape[0] // 3
    rows_in = basis_in.shape[0]

    def pick(at_end, at_middle):
        return jnp.where(end, at_end, at_middle)

    def side(at_end, at_middle):
        return lax.ppermute(pick(at_end, at_middle), "cand", SIDE)

    among, far = [], []
    for at in range(16):
        between = 4 <= at < 12
        across = 12 - 4 * (at // 4) + at % 4
        among.append((at, across if between else at ^ 1))
        far.append((at, at ^ 1 if between else across))

    def middle(x):
        return lax.ppermute(x, ALL, among)

    at_b = jnp.where(end, plane ^ 2, plane ^ 3)
    at_c = jnp.where(end, plane ^ 3, plane ^ 2)
    rep = lax.axis_index("rep")
    flags = jnp.stack([end.astype(jnp.int32), rep, plane, plane ^ 1, at_b, at_c])

    rows = lax.dynamic_slice_in_dim(basis_out, jnp.where(end, 0, depth), 2 * depth, 0)
    s0 = lax.ppermute(basis_in, "cand", SIDE)
    m0 = middle(basis_in)
    s12 = lax.ppermute(rows, "cand", SIDE)
    second = basis_out[depth : 2 * depth]
    m2 = middle(second)
    started = after(flags, rows, second)
    stacked, *more_stacked = stack_blocks(started, grads, depth)
    part_own = feature_dots(started, grads, [([(basis_out, 0)], 0, 0, 3 * STEPS, False)])
    precond = (test_grads.astype(jnp.float32) / (eigval + damping)).astype(jnp.bfloat16)
    m1 = middle(after(s0, m0))
    third = jnp.concatenate([basis_out[2 * depth :], basis_out[: 2 * rows_in - depth]])
    s3 = side(third, jnp.concatenate([m0, m1]))
    m3 = middle(after(basis_out[2 * depth :], m1, m2, precond, stacked, *more_stacked, *part_own))
    m5 = middle(s12[depth:])
    to_s45 = pick(stacked, jnp.concatenate([m2, m3]))
    s45 = lax.ppermute(after(to_s45, s3), "cand", SIDE)
    m6 = middle(s3[:depth])
    m4 = middle(after(basis_out[:depth], m5))
    s6 = side(more_stacked[0], m5)
    s7 = side(after(more_stacked[1], s45), m6)
    m7 = middle(after(s12[:depth], m6))

    part_in = input_dots(
        after(flags, s3, m5),
        acts,
        [[(basis_in, 0)], [(s0, 0)], [(s3, 0), (m0, 0)], [(s3, 1), (m1, 0)]],
    )
    part_a = feature_dots(
        after(flags, *part_in),
        grads,
        [
            ([(s12, 0)], STEPS, 0, 2 * STEPS, False),
            ([(s3, 0)], 2 * STEPS, 2 * STEPS, STEPS, True),
        ],
    )
    part_b = feature_dots(
        after(flags, *part_a, s45),
        grads,
        [
            ([(s45, 0), (m2, 0)], STEPS, STEPS, STEPS, False),
            ([(s45, STEPS), (m3, 0)], 2 * STEPS, 2 * STEPS, STEPS, False),
            ([(m4, 0)], 0, 0, STEPS, True),
        ],
    )
    shards = [(basis_out, 0), (m4, 0), (m7, 0)]
    pieces = [(s45, 0), (s45, STEPS), (s6, 0), (s7, 0)]
    blocks = [(shard, piece) for piece in (0, 1) for shard in (0, 1)]
    part_first = partner_dots(after(flags, *part_b), pieces[:2], shards[:2], blocks, depth)
    *part_second, part_c = partner_dots(
        after(flags, *part_first),
        pieces[:3],
        shards,
        [(2, 0), (2, 1), (0, 2), (1, 2), (2, 2)],
        depth,
        grads,
        [([(s6, 0), (m5, 0)], STEPS, False), ([(m7, 0)], 0, True)],
    )
    rot_in = chip_sum(core_sum(*after(part_in, s6, m7)))
    rot_in = gather_rows(rot_in.astype(jnp.bfloat16))
    rot_in = rot_in.reshape(tiles_here, TILE, 4 * cols)
    parts = [part_own, part_a, part_b, part_first]
    parts = [jnp.concatenate(part, axis=1) for part in zip(*parts)]
    core_sums = core_sum(*after(parts, s6, m7))
    sums = chip_sum(jnp.concatenate([core_sums, core_sum(*part_second)], axis=1))
    sum_own, sum_a, sum_b = [sums[:, i * tok_rows : (i + 1) * tok_rows] for i in range(3)]
    part_last = partner_dots(
        after(flags, part_c, core_sums),
        pieces[3:],
        shards,
        [(0, 0), (1, 0), (2, 0)],
        depth,
        grads,
        [([(s7, 0), (m6, 0)], 2 * STEPS, False)],
        part_c,
    )
    sum_last = chip_sum(core_sum(*part_last))
    sum_c = sum_last[:, :tok_rows]

    rowmask, ignored = tile_layout(pair_tiles, last_rows, plane * tiles_here, tiles_here, TILE)
    keep = rowmask.reshape(1, tok_rows).astype(jnp.bfloat16)

    def tile_prods(rot_out):
        return jnp.einsum(
            "etr,tra->tea",
            (rot_out.astype(jnp.bfloat16) * keep).reshape(slim, tiles_here, TILE),
            rot_in,
            preferred_element_type=jnp.float32,
        ).astype(jnp.bfloat16)

    def pair_scores(prods, source):
        scores = jnp.einsum("tea,jea->tj", prods, precond, preferred_element_type=jnp.float32)
        ignored_mask, onehot = tile_layout(
            pair_tiles, last_rows, source * tiles_here, tiles_here, TILE
        )
        return jnp.sum(jnp.where(onehot[:, :, None], scores[:, None, :], 0.0), axis=0)

    def columns(x, *which):
        return jnp.concatenate([x[:, i * TILE : (i + 1) * TILE] for i in which], axis=1)

    total = pair_scores(tile_prods(sum_own), plane)
    prods_middle = tile_prods(sum_b)
    from_middle = middle(prods_middle)
    last = lax.ppermute(after(sum_last[:, tok_rows:], total, prods_middle), "cand", SIDE)
    back = lax.ppermute(sums[:, 3 * tok_rows :], "cand", SIDE)
    both = jnp.where(end, jnp.concatenate([back, last], axis=1), 0.0)
    prods_a = tile_prods(sum_a + columns(both, 0, 2, 6, 9))
    prods_b = tile_prods(sum_b + columns(both, 1, 3, 7, 10))
    prods_c = tile_prods(sum_c + columns(both, 4, 5, 8, 11))
    from_far = lax.ppermute(prods_c, ALL, far)
    from_two = lax.ppermute(pick(prods_b, prods_c), "cand", TWO)
    from_side = lax.ppermute(prods_a, "cand", SIDE)
    total = total + pair_scores(from_side, plane ^ 1)
    total = total + pair_scores(from_two, plane ^ 2)
    total = total + pair_scores(pick(from_far, from_middle), plane ^ 3)
    return final_sum(total)


def final_sum(total):
    npairs, ntest = total.shape
    blocks = total.reshape(4, npairs // 4, 4, ntest // 4).transpose(0, 2, 1, 3)
    blocks = blocks.reshape(16, npairs // 4, ntest // 4)
    return jnp.sum(lax.all_to_all(blocks, ALL, 0, 0, tiled=True), axis=0)


def gather_plan(acts, grads, basis_in, basis_out, eigval, test_grads, pair_tiles, last_rows):
    ncand = lax.axis_size("cand")
    nfeat = lax.axis_size(FEAT)
    tok_rows = acts.shape[0]
    width_in = basis_in.shape[1] * ncand
    width_out = basis_out.shape[1] * ncand
    slim = width_out // (ncand * nfeat)
    part_in = jnp.dot(
        acts,
        lax.all_gather(basis_in, "cand", axis=1, tiled=True),
        preferred_element_type=jnp.float32,
    )
    part_out = jnp.dot(
        grads,
        lax.all_gather(basis_out, "cand", axis=1, tiled=True),
        preferred_element_type=jnp.float32,
    )
    part_out = part_out.reshape(tok_rows, ncand, nfeat, slim).transpose(0, 2, 1, 3)
    part_out = part_out.reshape(tok_rows, nfeat * ncand * slim)
    summed_in, summed_out = lax.psum((part_in, part_out), FEAT)
    own = lax.dynamic_slice_in_dim(
        summed_out, lax.axis_index(FEAT) * (ncand * slim), ncand * slim, 1
    )
    rot_in = summed_in.astype(jnp.bfloat16)
    rot_out = own.astype(jnp.bfloat16)
    tiles_here = tok_rows // TILE
    rowmask, ignored = tile_layout(
        pair_tiles, last_rows, lax.axis_index("cand") * tiles_here, tiles_here, TILE
    )
    masked = rot_out.reshape(tiles_here, TILE, ncand * slim) * rowmask[:, :, None].astype(
        jnp.bfloat16
    )
    prods = jnp.einsum(
        "tre,tra->tea",
        masked,
        rot_in.reshape(tiles_here, TILE, width_in),
        preferred_element_type=jnp.float32,
    ).astype(jnp.bfloat16)
    prods = prods.reshape(tiles_here, ncand, slim, width_in)
    received = lax.all_to_all(prods, "cand", split_axis=1, concat_axis=0, tiled=True)
    all_tiles = received.shape[0]
    received = received.reshape(all_tiles, slim, width_in)
    precond = (test_grads.astype(jnp.float32) / (eigval + damping)).astype(jnp.bfloat16)
    tile_part = jnp.einsum("tea,jea->tj", received, precond, preferred_element_type=jnp.float32)
    ignored_mask, onehot = tile_layout(pair_tiles, last_rows, 0, all_tiles, TILE)
    pair_part = jnp.dot(onehot.astype(jnp.float32).T, tile_part, precision=lax.Precision.HIGHEST)
    npairs = pair_part.shape[0]
    ntest = pair_part.shape[1]
    total = lax.psum(pair_part, ("cand", "eig", "rep"))
    rows = lax.dynamic_slice_in_dim(
        total, lax.axis_index("cand") * (npairs // ncand), npairs // ncand, 0
    )
    return lax.dynamic_slice_in_dim(
        rows, lax.axis_index(FEAT) * (ntest // nfeat), ntest // nfeat, 1
    )


def solution(mesh):
    in_specs = (
        P(("groups", "cand"), ("eig", "rep")),
        P(("groups", "cand"), ("eig", "rep")),
        P(("groups", "eig", "rep"), "cand"),
        P(("groups", "eig", "rep"), "cand"),
        P(("groups", "cand", "eig", "rep"), None),
        P("groups", ("cand", "eig", "rep"), None),
        P("groups"),
        P("groups"),
    )
    out_specs = P(("groups", "cand"), ("eig", "rep"))
    sizes = (mesh.shape["cand"], mesh.shape["eig"], mesh.shape["rep"])
    per_device = line_plan if sizes == (4, 2, 2) else gather_plan
    return jax.shard_map(
        per_device, mesh=mesh, in_specs=in_specs, out_specs=out_specs, check_vma=False
    )
```

```python
import jax
import jax.numpy as jnp
from jax import lax
from jax.experimental import pallas as pl
from jax.experimental.pallas import tpu as pltpu
from jax.sharding import PartitionSpec as P

TILE = 128
FEAT = ("eig", "rep")
ALL = ("cand", "eig", "rep")
STEPS = 3
PARAMS = pltpu.CompilerParams(vmem_limit_bytes=20 << 20)
SHORT = pl.CostEstimate(flops=1, bytes_accessed=1, transcendentals=0)
SIDE = ((0, 1), (1, 0), (2, 3), (3, 2))
TWO = ((0, 2), (2, 0), (1, 3), (3, 1))

damping = 0.01


def tile_layout(pair_tiles, last_rows, first_tile, count, tile_rows):
    tiles = first_tile + jnp.arange(count, dtype=jnp.int32)
    ends = jnp.cumsum(pair_tiles)
    owner = jnp.sum((ends[None, :] <= tiles[:, None]).astype(jnp.int32), axis=1)
    onehot = owner[:, None] == jnp.arange(pair_tiles.shape[0], dtype=jnp.int32)[None, :]
    last_of = jnp.sum(jnp.where(onehot, last_rows[None, :], 0), axis=1)
    end_of = jnp.sum(jnp.where(onehot, ends[None, :], 0), axis=1)
    limit = jnp.where(tiles == end_of - 1, last_of, tile_rows)
    rowmask = jnp.arange(tile_rows, dtype=jnp.int32)[None, :] < limit[:, None]
    return (rowmask, onehot)


def after(x, *earlier):
    return lax.optimization_barrier((x, *earlier))[0]


def swap(x, axis_name):
    return lax.ppermute(x, axis_name, [(0, 1), (1, 0)])


def halves(x, axis_name):
    first = lax.axis_index(axis_name) == 0
    low, high = jnp.split(x, 2)
    return jnp.where(first, low, high), jnp.where(first, high, low)


def core_sum(keep, give):
    return keep + swap(give, "rep")


def chip_sum(part):
    keep, give = halves(part, "eig")
    return keep + swap(give, "eig")


def gather_rows(x):
    other = swap(x, "eig")
    first = lax.axis_index("eig") == 0
    both = jnp.stack([jnp.where(first, x, other), jnp.where(first, other, x)])
    other = swap(both, "rep")
    first = lax.axis_index("rep") == 0
    whole = jnp.stack([jnp.where(first, both, other), jnp.where(first, other, both)], axis=1)
    return whole.reshape((-1,) + x.shape[1:])


def split_rows(full_ref, keep_ref, give_ref, rep, columns=None):
    rows = full_ref.shape[0] // 4
    columns = slice(None) if columns is None else columns
    for e in range(2):
        here = pl.ds(e * rows, rows)
        mine = pl.ds(pl.multiple_of((2 * e + rep) * rows, rows), rows)
        theirs = pl.ds(pl.multiple_of((2 * e + 1 - rep) * rows, rows), rows)
        keep_ref[here, columns] = full_ref[mine, :]
        give_ref[here, columns] = full_ref[theirs, :]


def add_dot(total_ref, rows_ref, shard):
    half = total_ref.shape[0] // 2
    for here in (pl.ds(0, half), pl.ds(half, half)):
        total_ref[here, :] += jnp.dot(
            rows_ref[here, :], shard, preferred_element_type=jnp.float32
        )


def feature_dots(flags, grads, segments, start=None, split=True):
    tok = grads.shape[0]
    cols = segments[0][0][0][0].shape[1]
    depth = grads.shape[1] // (3 * STEPS)
    firsts = [sum(s[3] for s in segments[:at]) for at in range(len(segments))]
    total = sum(s[3] for s in segments)

    def grads_at(i, flags_ref):
        at = 0
        for first, (choices, at_end, at_middle, steps, only) in zip(firsts, segments):
            base = at_end + flags_ref[0] * 0 if at_end == at_middle else (
                flags_ref[0] * at_end + (1 - flags_ref[0]) * at_middle
            )
            at = jnp.where(i >= first, base + i - first, at)
        return (0, at)

    def rows_at(first, steps, row, wanted):
        def index(i, flags_ref):
            step = jnp.clip(i - first, 0, steps - 1)
            if wanted is not None:
                step = step * (flags_ref[0] if wanted else 1 - flags_ref[0])
            return (row + step, 0)

        return index

    operands, specs = [grads], [pl.BlockSpec((tok, depth), grads_at)]
    for first, (choices, at_end, at_middle, steps, only) in zip(firsts, segments):
        for which, (array, row) in enumerate(choices):
            wanted = None if len(choices) == 1 else which == 0
            operands.append(array)
            specs.append(pl.BlockSpec((depth, cols), rows_at(first, steps, row, wanted)))
    if start is not None:
        operands.append(start)
        specs.append(pl.BlockSpec((tok, cols), lambda i, flags_ref: (0, 0)))

    def kernel(flags_ref, grads_ref, *refs):
        i = pl.program_id(0)
        end = flags_ref[0] == 1
        inputs, rest = list(refs[: len(operands) - 1]), refs[len(operands) - 1 :]
        if split:
            keep_ref, give_ref, total_ref, turned_ref = rest
        else:
            (total_ref,) = rest

        @pl.when(i == 0)
        def begin():
            total_ref[...] = jnp.zeros_like(total_ref) if start is None else inputs[-1][...]

        at = 0
        for first, (choices, at_end, at_middle, steps, only) in zip(firsts, segments):
            here = inputs[at : at + len(choices)]
            at += len(choices)
            active = (i >= first) & (i < first + steps)
            if only:
                active = active & (flags_ref[0] == 0)

            @pl.when(active)
            def add(here=here):
                shard = here[0][...]
                if len(here) == 2:
                    shard = jnp.where(end, shard, here[1][...])
                add_dot(total_ref, grads_ref, shard)

        if split:

            @pl.when(i == total - 1)
            def finish():
                turned_ref[...] = total_ref[...].T
                split_rows(turned_ref, keep_ref, give_ref, flags_ref[1])

    whole = lambda i, flags_ref: (0, 0)
    if split:
        out_shape = [jax.ShapeDtypeStruct((cols // 2, tok), jnp.float32)] * 2
        out_specs = [pl.BlockSpec((cols // 2, tok), whole)] * 2
        scratch = [pltpu.VMEM((tok, cols), jnp.float32), pltpu.VMEM((cols, tok), jnp.float32)]
    else:
        out_shape = jax.ShapeDtypeStruct((tok, cols), jnp.float32)
        out_specs = pl.BlockSpec((tok, cols), whole)
        scratch = []
    return pl.pallas_call(
        kernel,
        out_shape=out_shape,
        grid_spec=pltpu.PrefetchScalarGridSpec(
            num_scalar_prefetch=1,
            grid=(total,),
            in_specs=specs,
            out_specs=out_specs,
            scratch_shapes=scratch,
        ),
        compiler_params=PARAMS,
        cost_estimate=SHORT,
    )(flags, *operands)


def partner_dots(flags, pieces, shards, wanted, depth, grads=None, tail=(), start=None):
    cols = shards[0][0].shape[1]
    step = depth // STEPS
    count = len(pieces)
    tok = grads.shape[0] if tail else 0
    ahead = tok if start is not None else 0
    width = ahead + len(wanted) * TILE

    def at(row, wanted_at=None):
        def index(i, flags_ref):
            if wanted_at is not None:
                i = i * (flags_ref[0] if wanted_at else 1 - flags_ref[0])
            return (row + i, 0)

        return index

    operands, specs = [], []
    for array, row in list(pieces) + list(shards):
        operands.append(array)
        specs.append(pl.BlockSpec((step, cols), at(row)))
    whole = lambda i, flags_ref: (0, 0)
    for choices, column, only in tail:
        operands.append(grads)
        specs.append(
            pl.BlockSpec((tok, step), lambda i, flags_ref, column=column: (0, column + i))
        )
        for which, (array, row) in enumerate(choices):
            operands.append(array)
            specs.append(
                pl.BlockSpec((step, cols), at(row, None if len(choices) == 1 else which == 0))
            )
    if start is not None:
        operands.append(start)
        specs.append(pl.BlockSpec((tok, cols), whole))
    elif tail:
        operands.append(grads)
        specs.append(pl.BlockSpec((tok, step), lambda i, flags_ref: (0, 2 * STEPS + i)))

    def kernel(flags_ref, *refs):
        i = pl.program_id(0)
        piece_refs, shard_refs = refs[:count], refs[count : count + len(shards)]
        tail_refs = refs[count + len(shards) : len(operands)]
        keep_ref, give_ref, *rest = refs[len(operands) :]
        if tail and start is None:
            total_ref, copied_ref, sums_ref, turned_ref = rest
            copied_ref[...] = tail_refs[-1][...]
        elif tail:
            sums_ref, turned_ref, total_ref, wide_ref = rest
        else:
            sums_ref, turned_ref = rest

        @pl.when(i == 0)
        def begin():
            sums_ref[...] = jnp.zeros_like(sums_ref)
            if tail:
                total_ref[...] = jnp.zeros_like(total_ref) if start is None else tail_refs[-1][...]

        at = 0
        for choices, column, only in tail:
            grads_ref, here = tail_refs[at], tail_refs[at + 1 : at + 1 + len(choices)]
            at += 1 + len(choices)

            @pl.when((flags_ref[0] == 0) | (not only))
            def add(grads_ref=grads_ref, here=here):
                shard = here[0][...]
                if len(here) == 2:
                    shard = jnp.where(flags_ref[0] == 1, shard, here[1][...])
                add_dot(total_ref, grads_ref, shard)

        @pl.when(flags_ref[0] == 0)
        def at_a_middle_plane():
            for t, piece_ref in enumerate(piece_refs):
                tokens = jnp.concatenate(
                    [piece_ref[q * TILE : (q + 1) * TILE, :] for q in range(step // TILE)], axis=1
                )
                for block, (shard, piece) in enumerate(wanted):
                    if piece == t:
                        sums_ref[block] += jnp.dot(
                            tokens, shard_refs[shard][...], preferred_element_type=jnp.float32
                        )

        @pl.when(i == STEPS - 1)
        def finish():
            if ahead:
                wide_ref[...] = total_ref[...].T
                split_rows(wide_ref, keep_ref, give_ref, flags_ref[1], pl.ds(0, tok))
            for block in range(len(wanted)):
                turned_ref[...] = sums_ref[block].T
                columns = pl.ds(ahead + block * TILE, TILE)
                split_rows(turned_ref, keep_ref, give_ref, flags_ref[1], columns)

    out_shape = [jax.ShapeDtypeStruct((cols // 2, width), jnp.float32)] * 2
    out_specs = [pl.BlockSpec((cols // 2, width), whole)] * 2
    scratch = [
        pltpu.VMEM((len(wanted), TILE, cols), jnp.float32),
        pltpu.VMEM((cols, TILE), jnp.float32),
    ]
    if tail and start is None:
        out_shape.append(jax.ShapeDtypeStruct((tok, cols), jnp.float32))
        out_specs.append(pl.BlockSpec((tok, cols), whole))
        out_shape.append(jax.ShapeDtypeStruct((tok, depth), grads.dtype))
        out_specs.append(pl.BlockSpec((tok, step), lambda i, flags_ref: (0, i)))
    elif tail:
        scratch += [pltpu.VMEM((tok, cols), jnp.float32), pltpu.VMEM((cols, tok), jnp.float32)]
    return pl.pallas_call(
        kernel,
        out_shape=out_shape,
        grid_spec=pltpu.PrefetchScalarGridSpec(
            num_scalar_prefetch=1,
            grid=(STEPS,),
            in_specs=specs,
            out_specs=out_specs,
            scratch_shapes=scratch,
        ),
        compiler_params=PARAMS,
        cost_estimate=SHORT,
    )(flags, *operands)


def stack_blocks(flags, grads, depth):
    tiles = grads.shape[0] // TILE
    firsts = [0] + list(range(tiles // 2, tiles))
    counts = [tiles // 2] + [1] * (tiles // 2)

    def kernel(flags_ref, grads_ref, *out_refs):
        t = pl.program_id(0)
        for first, count, out_ref in zip(firsts, counts, out_refs):

            @pl.when((t >= first) & (t < first + count))
            def copy(out_ref=out_ref):
                for q in range(depth // TILE):
                    here = slice(q * TILE, (q + 1) * TILE)
                    out_ref[here, :] = grads_ref[:, here]

    def place(first, count):
        return lambda t, flags_ref: (jnp.clip(t - first, 0, count - 1), 0)

    return pl.pallas_call(
        kernel,
        out_shape=[jax.ShapeDtypeStruct((count * depth, TILE), grads.dtype) for count in counts],
        grid_spec=pltpu.PrefetchScalarGridSpec(
            num_scalar_prefetch=1,
            grid=(tiles,),
            in_specs=[pl.BlockSpec((TILE, depth), lambda t, flags_ref: (t, 0))],
            out_specs=[
                pl.BlockSpec((depth, TILE), place(first, count))
                for first, count in zip(firsts, counts)
            ],
        ),
        compiler_params=PARAMS,
        cost_estimate=SHORT,
    )(flags, grads)


def input_dots(flags, acts, shards):
    tok, depth = acts.shape
    cols = shards[0][0][0].shape[1]
    operands, specs = [acts], [pl.BlockSpec((tok, depth), lambda i, flags_ref: (0, 0))]
    for choices in shards:
        for array, row in choices:
            operands.append(array)
            specs.append(pl.BlockSpec((depth, cols), lambda i, flags_ref, row=row: (row, 0)))

    def kernel(flags_ref, acts_ref, *refs):
        i = pl.program_id(0)
        inputs = list(refs[: len(operands) - 1])
        keep_ref, give_ref, part_ref = refs[len(operands) - 1 :]
        at = 0
        for slot, choices in enumerate(shards):
            here = inputs[at : at + len(choices)]
            at += len(choices)

            @pl.when(i == slot)
            def add(here=here):
                shard = here[0][...]
                if len(here) == 2:
                    shard = jnp.where(flags_ref[0] == 1, shard, here[1][...])
                part_ref[...] = jnp.dot(acts_ref[...], shard, preferred_element_type=jnp.float32)

        split_rows(part_ref, keep_ref, give_ref, flags_ref[1])

    place = pl.BlockSpec((tok // 2, cols), lambda i, flags_ref: (0, flags_ref[2 + i]))
    return pl.pallas_call(
        kernel,
        out_shape=[jax.ShapeDtypeStruct((tok // 2, cols * len(shards)), jnp.float32)] * 2,
        grid_spec=pltpu.PrefetchScalarGridSpec(
            num_scalar_prefetch=1,
            grid=(len(shards),),
            in_specs=specs,
            out_specs=[place, place],
            scratch_shapes=[pltpu.VMEM((tok, cols), jnp.float32)],
        ),
        compiler_params=PARAMS,
        cost_estimate=SHORT,
    )(flags, *operands)


def line_plan(acts, grads, basis_in, basis_out, eigval, test_grads, pair_tiles, last_rows):
    plane = lax.axis_index("cand")
    end = (plane == 0) | (plane == 3)
    tok_rows = acts.shape[0]
    cols = basis_in.shape[1]
    tiles_here = tok_rows // TILE
    slim = cols // 4
    depth = basis_out.shape[0] // 3
    rows_in = basis_in.shape[0]

    def pick(at_end, at_middle):
        return jnp.where(end, at_end, at_middle)

    def side(at_end, at_middle):
        return lax.ppermute(pick(at_end, at_middle), "cand", SIDE)

    among, far = [], []
    for at in range(16):
        between = 4 <= at < 12
        across = 12 - 4 * (at // 4) + at % 4
        among.append((at, across if between else at ^ 1))
        far.append((at, at ^ 1 if between else across))

    def middle(x):
        return lax.ppermute(x, ALL, among)

    at_b = jnp.where(end, plane ^ 2, plane ^ 3)
    at_c = jnp.where(end, plane ^ 3, plane ^ 2)
    rep = lax.axis_index("rep")
    flags = jnp.stack([end.astype(jnp.int32), rep, plane, plane ^ 1, at_b, at_c])

    rows = lax.dynamic_slice_in_dim(basis_out, jnp.where(end, 0, depth), 2 * depth, 0)
    s0 = lax.ppermute(basis_in, "cand", SIDE)
    m0 = middle(basis_in)
    s12 = lax.ppermute(rows, "cand", SIDE)
    second = basis_out[depth : 2 * depth]
    m2 = middle(second)
    started = after(flags, rows, second)
    stacked, *more_stacked = stack_blocks(started, grads, depth)
    part_own = feature_dots(
        after(started, s0, m0), grads, [([(basis_out, 0)], 0, 0, 3 * STEPS, False)]
    )
    precond = (test_grads.astype(jnp.float32) / (eigval + damping)).astype(jnp.bfloat16)
    m1 = middle(after(s0, m0))
    third = jnp.concatenate([basis_out[2 * depth :], basis_out[: 2 * rows_in - depth]])
    s3 = side(third, jnp.concatenate([m0, m1]))
    m3 = middle(after(basis_out[2 * depth :], precond, stacked, *more_stacked, *part_own))
    m5 = middle(s12[depth:])
    to_s45 = pick(stacked, jnp.concatenate([m2, m3]))
    s45 = lax.ppermute(after(to_s45, s3), "cand", SIDE)
    m6 = middle(s3[:depth])
    m4 = middle(after(basis_out[:depth], m5))
    s6 = side(more_stacked[0], m5)
    to_s7 = pick(after(more_stacked[1], s45), m6)
    s7 = lax.ppermute(to_s7, "cand", SIDE)
    m7 = middle(after(s12[:depth], m6))

    part_in = input_dots(
        after(flags, s3, m5),
        acts,
        [[(basis_in, 0)], [(s0, 0)], [(s3, 0), (m0, 0)], [(s3, 1), (m1, 0)]],
    )
    part_a = feature_dots(
        after(flags, *part_in),
        grads,
        [
            ([(s12, 0)], STEPS, 0, 2 * STEPS, False),
            ([(s3, 0)], 2 * STEPS, 2 * STEPS, STEPS, True),
        ],
    )
    part_b = feature_dots(
        after(flags, *part_a, s45),
        grads,
        [
            ([(s45, 0), (m2, 0)], STEPS, STEPS, STEPS, False),
            ([(s45, STEPS), (m3, 0)], 2 * STEPS, 2 * STEPS, STEPS, False),
            ([(m4, 0)], 0, 0, STEPS, True),
        ],
    )
    shards = [(basis_out, 0), (m4, 0), (m7, 0)]
    pieces = [(s45, 0), (s45, STEPS), (s6, 0), (s7, 0)]
    blocks = [(shard, piece) for piece in (0, 1) for shard in (0, 1)]
    part_first = partner_dots(after(flags, to_s7, *part_b), pieces[:2], shards[:2], blocks, depth)
    parts = [part_own, part_a, part_b, part_first]
    parts = [jnp.concatenate(part, axis=1) for part in zip(*parts)]
    core_sums = core_sum(*after(parts, s6, m7))
    *part_second, part_c, last_grads = partner_dots(
        after(flags, core_sums),
        pieces[:3],
        shards,
        [(2, 0), (2, 1), (0, 2), (1, 2), (2, 2)],
        depth,
        grads,
        [([(s6, 0), (m5, 0)], STEPS, False), ([(m7, 0)], 0, True)],
    )
    rot_in = chip_sum(core_sum(*after(part_in, s6, m7)))
    rot_in = gather_rows(rot_in.astype(jnp.bfloat16))
    rot_in = rot_in.reshape(tiles_here, TILE, 4 * cols)
    sums = chip_sum(jnp.concatenate([core_sums, core_sum(*part_second)], axis=1))
    sum_own, sum_a, sum_b = [sums[:, i * tok_rows : (i + 1) * tok_rows] for i in range(3)]
    part_last = partner_dots(
        after(flags, part_c),
        pieces[3:],
        shards,
        [(0, 0), (1, 0), (2, 0)],
        depth,
        last_grads,
        [([(s7, 0), (m6, 0)], 0, False)],
        part_c,
    )
    sum_last = chip_sum(core_sum(*part_last))
    sum_c = sum_last[:, :tok_rows]

    rowmask, ignored = tile_layout(pair_tiles, last_rows, plane * tiles_here, tiles_here, TILE)
    keep = rowmask.reshape(1, tok_rows).astype(jnp.bfloat16)

    def tile_prods(rot_out):
        return jnp.einsum(
            "etr,tra->tea",
            (rot_out.astype(jnp.bfloat16) * keep).reshape(slim, tiles_here, TILE),
            rot_in,
            preferred_element_type=jnp.float32,
        ).astype(jnp.bfloat16)

    def pair_scores(*received):
        prods = jnp.concatenate([x for x, source in received])
        scores = jnp.einsum("tea,jea->tj", prods, precond, preferred_element_type=jnp.float32)
        onehot = jnp.concatenate([
            tile_layout(pair_tiles, last_rows, source * tiles_here, tiles_here, TILE)[1]
            for x, source in received
        ])
        return jnp.sum(jnp.where(onehot[:, :, None], scores[:, None, :], 0.0), axis=0)

    def columns(x, *which):
        return jnp.concatenate([x[:, i * TILE : (i + 1) * TILE] for i in which], axis=1)

    prods_own = tile_prods(sum_own)
    prods_middle = tile_prods(sum_b)
    from_middle = middle(prods_middle)
    last = lax.ppermute(after(sum_last[:, tok_rows:], prods_own, prods_middle), "cand", SIDE)
    back = lax.ppermute(sums[:, 3 * tok_rows :], "cand", SIDE)
    both = jnp.where(end, jnp.concatenate([back, last], axis=1), 0.0)
    prods_a = tile_prods(sum_a + columns(both, 0, 2, 6, 9))
    prods_b = tile_prods(sum_b + columns(both, 1, 3, 7, 10))
    prods_c = tile_prods(sum_c + columns(both, 4, 5, 8, 11))
    from_far = lax.ppermute(prods_c, ALL, far)
    from_two = lax.ppermute(pick(prods_b, prods_c), "cand", TWO)
    from_side = lax.ppermute(prods_a, "cand", SIDE)
    total = pair_scores((prods_own, plane), (from_side, plane ^ 1))
    total = total + pair_scores((from_two, plane ^ 2), (pick(from_far, from_middle), plane ^ 3))
    return final_sum(total)


def final_sum(total):
    npairs, ntest = total.shape
    blocks = total.reshape(4, npairs // 4, 4, ntest // 4).transpose(0, 2, 1, 3)
    blocks = blocks.reshape(16, npairs // 4, ntest // 4)
    return jnp.sum(lax.all_to_all(blocks, ALL, 0, 0, tiled=True), axis=0)


def gather_plan(acts, grads, basis_in, basis_out, eigval, test_grads, pair_tiles, last_rows):
    ncand = lax.axis_size("cand")
    nfeat = lax.axis_size(FEAT)
    tok_rows = acts.shape[0]
    width_in = basis_in.shape[1] * ncand
    width_out = basis_out.shape[1] * ncand
    slim = width_out // (ncand * nfeat)
    part_in = jnp.dot(
        acts,
        lax.all_gather(basis_in, "cand", axis=1, tiled=True),
        preferred_element_type=jnp.float32,
    )
    part_out = jnp.dot(
        grads,
        lax.all_gather(basis_out, "cand", axis=1, tiled=True),
        preferred_element_type=jnp.float32,
    )
    part_out = part_out.reshape(tok_rows, ncand, nfeat, slim).transpose(0, 2, 1, 3)
    part_out = part_out.reshape(tok_rows, nfeat * ncand * slim)
    summed_in, summed_out = lax.psum((part_in, part_out), FEAT)
    own = lax.dynamic_slice_in_dim(
        summed_out, lax.axis_index(FEAT) * (ncand * slim), ncand * slim, 1
    )
    rot_in = summed_in.astype(jnp.bfloat16)
    rot_out = own.astype(jnp.bfloat16)
    tiles_here = tok_rows // TILE
    rowmask, ignored = tile_layout(
        pair_tiles, last_rows, lax.axis_index("cand") * tiles_here, tiles_here, TILE
    )
    masked = rot_out.reshape(tiles_here, TILE, ncand * slim) * rowmask[:, :, None].astype(
        jnp.bfloat16
    )
    prods = jnp.einsum(
        "tre,tra->tea",
        masked,
        rot_in.reshape(tiles_here, TILE, width_in),
        preferred_element_type=jnp.float32,
    ).astype(jnp.bfloat16)
    prods = prods.reshape(tiles_here, ncand, slim, width_in)
    received = lax.all_to_all(prods, "cand", split_axis=1, concat_axis=0, tiled=True)
    all_tiles = received.shape[0]
    received = received.reshape(all_tiles, slim, width_in)
    precond = (test_grads.astype(jnp.float32) / (eigval + damping)).astype(jnp.bfloat16)
    tile_part = jnp.einsum("tea,jea->tj", received, precond, preferred_element_type=jnp.float32)
    ignored_mask, onehot = tile_layout(pair_tiles, last_rows, 0, all_tiles, TILE)
    pair_part = jnp.dot(onehot.astype(jnp.float32).T, tile_part, precision=lax.Precision.HIGHEST)
    npairs = pair_part.shape[0]
    ntest = pair_part.shape[1]
    total = lax.psum(pair_part, ("cand", "eig", "rep"))
    rows = lax.dynamic_slice_in_dim(
        total, lax.axis_index("cand") * (npairs // ncand), npairs // ncand, 0
    )
    return lax.dynamic_slice_in_dim(
        rows, lax.axis_index(FEAT) * (ntest // nfeat), ntest // nfeat, 1
    )


def solution(mesh):
    in_specs = (
        P(("groups", "cand"), ("eig", "rep")),
        P(("groups", "cand"), ("eig", "rep")),
        P(("groups", "eig", "rep"), "cand"),
        P(("groups", "eig", "rep"), "cand"),
        P(("groups", "cand", "eig", "rep"), None),
        P("groups", ("cand", "eig", "rep"), None),
        P("groups"),
        P("groups"),
    )
    out_specs = P(("groups", "cand"), ("eig", "rep"))
    sizes = (mesh.shape["cand"], mesh.shape["eig"], mesh.shape["rep"])
    per_device = line_plan if sizes == (4, 2, 2) else gather_plan
    return jax.shard_map(
        per_device, mesh=mesh, in_specs=in_specs, out_specs=out_specs, check_vma=False
    )
```

```python
import jax
import jax.numpy as jnp
from jax import lax
from jax.experimental import pallas as pl
from jax.experimental.pallas import tpu as pltpu
from jax.sharding import PartitionSpec as P

TILE = 128
FEAT = ("eig", "rep")
ALL = ("cand", "eig", "rep")
STEPS = 3
PARAMS = pltpu.CompilerParams(vmem_limit_bytes=20 << 20)
SHORT = pl.CostEstimate(flops=1, bytes_accessed=1, transcendentals=0)
SIDE = ((0, 1), (1, 0), (2, 3), (3, 2))
TWO = ((0, 2), (2, 0), (1, 3), (3, 1))

damping = 0.01


def tile_layout(pair_tiles, last_rows, first_tile, count, tile_rows):
    tiles = first_tile + jnp.arange(count, dtype=jnp.int32)
    ends = jnp.cumsum(pair_tiles)
    owner = jnp.sum((ends[None, :] <= tiles[:, None]).astype(jnp.int32), axis=1)
    onehot = owner[:, None] == jnp.arange(pair_tiles.shape[0], dtype=jnp.int32)[None, :]
    last_of = jnp.sum(jnp.where(onehot, last_rows[None, :], 0), axis=1)
    end_of = jnp.sum(jnp.where(onehot, ends[None, :], 0), axis=1)
    limit = jnp.where(tiles == end_of - 1, last_of, tile_rows)
    rowmask = jnp.arange(tile_rows, dtype=jnp.int32)[None, :] < limit[:, None]
    return (rowmask, onehot)


def after(x, *earlier):
    return lax.optimization_barrier((x, *earlier))[0]


def swap(x, axis_name):
    return lax.ppermute(x, axis_name, [(0, 1), (1, 0)])


def halves(x, axis_name):
    first = lax.axis_index(axis_name) == 0
    low, high = jnp.split(x, 2)
    return jnp.where(first, low, high), jnp.where(first, high, low)


def core_sum(keep, give):
    return keep + swap(give, "rep")


def chip_sum(part):
    keep, give = halves(part, "eig")
    return keep + swap(give, "eig")


def gather_rows(x):
    other = swap(x, "eig")
    first = lax.axis_index("eig") == 0
    both = jnp.stack([jnp.where(first, x, other), jnp.where(first, other, x)])
    other = swap(both, "rep")
    first = lax.axis_index("rep") == 0
    whole = jnp.stack([jnp.where(first, both, other), jnp.where(first, other, both)], axis=1)
    return whole.reshape((-1,) + x.shape[1:])


def split_rows(full_ref, keep_ref, give_ref, rep, columns=None):
    rows = full_ref.shape[0] // 4
    columns = slice(None) if columns is None else columns
    for e in range(2):
        here = pl.ds(e * rows, rows)
        mine = pl.ds(pl.multiple_of((2 * e + rep) * rows, rows), rows)
        theirs = pl.ds(pl.multiple_of((2 * e + 1 - rep) * rows, rows), rows)
        keep_ref[here, columns] = full_ref[mine, :]
        give_ref[here, columns] = full_ref[theirs, :]


def add_dot(total_ref, rows_ref, shard):
    half = total_ref.shape[0] // 2
    for here in (pl.ds(0, half), pl.ds(half, half)):
        total_ref[here, :] += jnp.dot(
            rows_ref[here, :], shard, preferred_element_type=jnp.float32
        )


def feature_dots(flags, grads, segments, start=None, split=True):
    tok = grads.shape[0]
    cols = segments[0][0][0][0].shape[1]
    depth = grads.shape[1] // (3 * STEPS)
    firsts = [sum(s[3] for s in segments[:at]) for at in range(len(segments))]
    total = sum(s[3] for s in segments)

    def grads_at(i, flags_ref):
        at = 0
        for first, (choices, at_end, at_middle, steps, only) in zip(firsts, segments):
            base = at_end + flags_ref[0] * 0 if at_end == at_middle else (
                flags_ref[0] * at_end + (1 - flags_ref[0]) * at_middle
            )
            at = jnp.where(i >= first, base + i - first, at)
        return (0, at)

    def rows_at(first, steps, row, wanted):
        def index(i, flags_ref):
            step = jnp.clip(i - first, 0, steps - 1)
            if wanted is not None:
                step = step * (flags_ref[0] if wanted else 1 - flags_ref[0])
            return (row + step, 0)

        return index

    operands, specs = [grads], [pl.BlockSpec((tok, depth), grads_at)]
    for first, (choices, at_end, at_middle, steps, only) in zip(firsts, segments):
        for which, (array, row) in enumerate(choices):
            wanted = None if len(choices) == 1 else which == 0
            operands.append(array)
            specs.append(pl.BlockSpec((depth, cols), rows_at(first, steps, row, wanted)))
    if start is not None:
        operands.append(start)
        specs.append(pl.BlockSpec((tok, cols), lambda i, flags_ref: (0, 0)))

    def kernel(flags_ref, grads_ref, *refs):
        i = pl.program_id(0)
        end = flags_ref[0] == 1
        inputs, rest = list(refs[: len(operands) - 1]), refs[len(operands) - 1 :]
        if split:
            keep_ref, give_ref, total_ref, turned_ref = rest
        else:
            (total_ref,) = rest

        @pl.when(i == 0)
        def begin():
            total_ref[...] = jnp.zeros_like(total_ref) if start is None else inputs[-1][...]

        at = 0
        for first, (choices, at_end, at_middle, steps, only) in zip(firsts, segments):
            here = inputs[at : at + len(choices)]
            at += len(choices)
            active = (i >= first) & (i < first + steps)
            if only:
                active = active & (flags_ref[0] == 0)

            @pl.when(active)
            def add(here=here):
                shard = here[0][...]
                if len(here) == 2:
                    shard = jnp.where(end, shard, here[1][...])
                add_dot(total_ref, grads_ref, shard)

        if split:

            @pl.when(i == total - 1)
            def finish():
                turned_ref[...] = total_ref[...].T
                split_rows(turned_ref, keep_ref, give_ref, flags_ref[1])

    whole = lambda i, flags_ref: (0, 0)
    if split:
        out_shape = [jax.ShapeDtypeStruct((cols // 2, tok), jnp.float32)] * 2
        out_specs = [pl.BlockSpec((cols // 2, tok), whole)] * 2
        scratch = [pltpu.VMEM((tok, cols), jnp.float32), pltpu.VMEM((cols, tok), jnp.float32)]
    else:
        out_shape = jax.ShapeDtypeStruct((tok, cols), jnp.float32)
        out_specs = pl.BlockSpec((tok, cols), whole)
        scratch = []
    return pl.pallas_call(
        kernel,
        out_shape=out_shape,
        grid_spec=pltpu.PrefetchScalarGridSpec(
            num_scalar_prefetch=1,
            grid=(total,),
            in_specs=specs,
            out_specs=out_specs,
            scratch_shapes=scratch,
        ),
        compiler_params=PARAMS,
        cost_estimate=SHORT,
    )(flags, *operands)


def both_dots(flags, grads, at_end, at_middle):
    tok = grads.shape[0]
    cols = at_end[0].shape[1]
    step = grads.shape[1] // (3 * STEPS)

    def third_at(first):
        def index(i, flags_ref):
            return (jnp.clip(i - first, 0, STEPS - 1) * (1 - flags_ref[0]), 0)

        return index

    operands = [grads, at_end[0]] + [array for pair in at_middle for array in pair]
    specs = [
        pl.BlockSpec((tok, step), lambda i, flags_ref: (0, STEPS + i)),
        pl.BlockSpec((step, cols), lambda i, flags_ref: (at_end[1] + i * flags_ref[0], 0)),
    ]
    for first in (0, STEPS):
        specs += [pl.BlockSpec((step, cols), third_at(first))] * 2

    def kernel(flags_ref, grads_ref, end_ref, b1_ref, c1_ref, b2_ref, c2_ref, total_ref):
        i = pl.program_id(0)

        @pl.when(i == 0)
        def begin():
            total_ref[...] = jnp.zeros_like(total_ref)

        @pl.when(flags_ref[0] == 1)
        def one():
            total_ref[:, :cols] += jnp.dot(
                grads_ref[...], end_ref[...], preferred_element_type=jnp.float32
            )

        for first, b_ref, c_ref in ((0, b1_ref, c1_ref), (STEPS, b2_ref, c2_ref)):

            @pl.when((flags_ref[0] == 0) & (i >= first) & (i < first + STEPS))
            def two(b_ref=b_ref, c_ref=c_ref):
                shards = jnp.concatenate([b_ref[...], c_ref[...]], axis=1)
                total_ref[...] += jnp.dot(
                    grads_ref[...], shards, preferred_element_type=jnp.float32
                )

    return pl.pallas_call(
        kernel,
        out_shape=jax.ShapeDtypeStruct((tok, 2 * cols), jnp.float32),
        grid_spec=pltpu.PrefetchScalarGridSpec(
            num_scalar_prefetch=1,
            grid=(2 * STEPS,),
            in_specs=specs,
            out_specs=pl.BlockSpec((tok, 2 * cols), lambda i, flags_ref: (0, 0)),
        ),
        compiler_params=PARAMS,
        cost_estimate=SHORT,
    )(flags, *operands)


def partner_dots(flags, pieces, shards, grads, column, shard, start):
    tok = grads.shape[0]
    cols = shards[0][0].shape[1]
    step = shard[2] // STEPS
    count = len(pieces)
    two = start.shape[1] == 2 * cols
    width = tok + len(shards) * count * TILE

    def at(row):
        return lambda i, flags_ref: (row + i, 0)

    whole = lambda i, flags_ref: (0, 0)
    operands, specs = [], []
    for array, row in list(pieces) + list(shards) + [shard[:2]]:
        operands.append(array)
        specs.append(pl.BlockSpec((step, cols), at(row)))
    operands += [grads, start]
    specs.append(
        pl.BlockSpec(
            (tok, step),
            lambda i, flags_ref: (0, column * (flags_ref[0] if two else 1) + i),
        )
    )
    specs.append(pl.BlockSpec(start.shape, whole))
    if two:
        operands.append(grads)
        specs.append(pl.BlockSpec((tok, step), lambda i, flags_ref: (0, 2 * STEPS + i)))

    def kernel(flags_ref, *refs):
        i = pl.program_id(0)
        piece_refs, shard_refs = refs[:count], refs[count : count + len(shards)]
        end_ref, grads_ref, start_ref = refs[count + len(shards) : count + len(shards) + 3]
        keep_ref, give_ref, *rest = refs[len(operands) :]
        if two:
            second_ref, copied_ref, total_ref, sums_ref, turned_ref, wide_ref = rest
            copied_ref[...] = refs[len(operands) - 1][...]
        else:
            total_ref, sums_ref, turned_ref, wide_ref = rest

        @pl.when(i == 0)
        def begin():
            total_ref[...] = start_ref[...]
            sums_ref[...] = jnp.zeros_like(sums_ref)

        @pl.when(flags_ref[0] == 1)
        def at_an_end_plane():
            total_ref[:, total_ref.shape[1] - cols :] += jnp.dot(
                grads_ref[...], end_ref[...], preferred_element_type=jnp.float32
            )

        @pl.when(flags_ref[0] == 0)
        def at_a_middle_plane():
            side_by_side = jnp.concatenate([ref[...] for ref in shard_refs], axis=1)
            tokens = jnp.concatenate(
                [
                    jnp.concatenate(
                        [ref[q * TILE : (q + 1) * TILE, :] for q in range(step // TILE)], axis=1
                    )
                    for ref in piece_refs
                ]
            )
            sums_ref[...] += jnp.dot(tokens, side_by_side, preferred_element_type=jnp.float32)
            if two:
                total_ref[...] += jnp.dot(
                    grads_ref[...], side_by_side[:, cols:], preferred_element_type=jnp.float32
                )

        @pl.when(i == STEPS - 1)
        def finish():
            wide_ref[...] = total_ref[:, :cols].T
            split_rows(wide_ref, keep_ref, give_ref, flags_ref[1], pl.ds(0, tok))
            for j in range(len(shards)):
                turned_ref[...] = sums_ref[:, j * cols : (j + 1) * cols].T
                columns = pl.ds(tok + j * count * TILE, count * TILE)
                split_rows(turned_ref, keep_ref, give_ref, flags_ref[1], columns)
            if two:
                second_ref[...] = total_ref[:, cols:]

    out_shape = [jax.ShapeDtypeStruct((cols // 2, width), jnp.float32)] * 2
    out_specs = [pl.BlockSpec((cols // 2, width), whole)] * 2
    if two:
        out_shape.append(jax.ShapeDtypeStruct((tok, cols), jnp.float32))
        out_specs.append(pl.BlockSpec((tok, cols), whole))
        out_shape.append(jax.ShapeDtypeStruct((tok, STEPS * step), grads.dtype))
        out_specs.append(pl.BlockSpec((tok, step), lambda i, flags_ref: (0, i)))
    return pl.pallas_call(
        kernel,
        out_shape=out_shape,
        grid_spec=pltpu.PrefetchScalarGridSpec(
            num_scalar_prefetch=1,
            grid=(STEPS,),
            in_specs=specs,
            out_specs=out_specs,
            scratch_shapes=[
                pltpu.VMEM(start.shape, jnp.float32),
                pltpu.VMEM((count * TILE, len(shards) * cols), jnp.float32),
                pltpu.VMEM((cols, count * TILE), jnp.float32),
                pltpu.VMEM((cols, tok), jnp.float32),
            ],
        ),
        compiler_params=PARAMS,
        cost_estimate=SHORT,
    )(flags, *operands)


def stack_blocks(flags, grads, depth):
    tiles = grads.shape[0] // TILE
    firsts = [0] + list(range(tiles // 2, tiles))
    counts = [tiles // 2] + [1] * (tiles // 2)

    def kernel(flags_ref, grads_ref, *out_refs):
        t = pl.program_id(0)
        for first, count, out_ref in zip(firsts, counts, out_refs):

            @pl.when((t >= first) & (t < first + count))
            def copy(out_ref=out_ref):
                for q in range(depth // TILE):
                    here = slice(q * TILE, (q + 1) * TILE)
                    out_ref[here, :] = grads_ref[:, here]

    def place(first, count):
        return lambda t, flags_ref: (jnp.clip(t - first, 0, count - 1), 0)

    return pl.pallas_call(
        kernel,
        out_shape=[jax.ShapeDtypeStruct((count * depth, TILE), grads.dtype) for count in counts],
        grid_spec=pltpu.PrefetchScalarGridSpec(
            num_scalar_prefetch=1,
            grid=(tiles,),
            in_specs=[pl.BlockSpec((TILE, depth), lambda t, flags_ref: (t, 0))],
            out_specs=[
                pl.BlockSpec((depth, TILE), place(first, count))
                for first, count in zip(firsts, counts)
            ],
        ),
        compiler_params=PARAMS,
        cost_estimate=SHORT,
    )(flags, grads)


def input_dots(flags, acts, shards):
    tok, depth = acts.shape
    cols = shards[0][0][0].shape[1]
    operands, specs = [acts], [pl.BlockSpec((tok, depth), lambda i, flags_ref: (0, 0))]
    for choices in shards:
        for array, row in choices:
            operands.append(array)
            specs.append(pl.BlockSpec((depth, cols), lambda i, flags_ref, row=row: (row, 0)))

    def kernel(flags_ref, acts_ref, *refs):
        i = pl.program_id(0)
        inputs = list(refs[: len(operands) - 1])
        keep_ref, give_ref, part_ref = refs[len(operands) - 1 :]
        at = 0
        for slot, choices in enumerate(shards):
            here = inputs[at : at + len(choices)]
            at += len(choices)

            @pl.when(i == slot)
            def add(here=here):
                shard = here[0][...]
                if len(here) == 2:
                    shard = jnp.where(flags_ref[0] == 1, shard, here[1][...])
                part_ref[...] = jnp.dot(acts_ref[...], shard, preferred_element_type=jnp.float32)

        split_rows(part_ref, keep_ref, give_ref, flags_ref[1])

    place = pl.BlockSpec((tok // 2, cols), lambda i, flags_ref: (0, flags_ref[2 + i]))
    return pl.pallas_call(
        kernel,
        out_shape=[jax.ShapeDtypeStruct((tok // 2, cols * len(shards)), jnp.float32)] * 2,
        grid_spec=pltpu.PrefetchScalarGridSpec(
            num_scalar_prefetch=1,
            grid=(len(shards),),
            in_specs=specs,
            out_specs=[place, place],
            scratch_shapes=[pltpu.VMEM((tok, cols), jnp.float32)],
        ),
        compiler_params=PARAMS,
        cost_estimate=SHORT,
    )(flags, *operands)


def line_plan(acts, grads, basis_in, basis_out, eigval, test_grads, pair_tiles, last_rows):
    plane = lax.axis_index("cand")
    end = (plane == 0) | (plane == 3)
    tok_rows = acts.shape[0]
    cols = basis_in.shape[1]
    tiles_here = tok_rows // TILE
    slim = cols // 4
    depth = basis_out.shape[0] // 3
    rows_in = basis_in.shape[0]

    def pick(at_end, at_middle):
        return jnp.where(end, at_end, at_middle)

    def side(at_end, at_middle):
        return lax.ppermute(pick(at_end, at_middle), "cand", SIDE)

    among, far = [], []
    for at in range(16):
        between = 4 <= at < 12
        across = 12 - 4 * (at // 4) + at % 4
        among.append((at, across if between else at ^ 1))
        far.append((at, at ^ 1 if between else across))

    def middle(x):
        return lax.ppermute(x, ALL, among)

    at_b = jnp.where(end, plane ^ 2, plane ^ 3)
    at_c = jnp.where(end, plane ^ 3, plane ^ 2)
    rep = lax.axis_index("rep")
    flags = jnp.stack([end.astype(jnp.int32), rep, plane, plane ^ 1, at_b, at_c])

    rows = lax.dynamic_slice_in_dim(basis_out, jnp.where(end, 0, depth), 2 * depth, 0)
    s0 = lax.ppermute(basis_in, "cand", SIDE)
    m0 = middle(basis_in)
    s12 = lax.ppermute(rows, "cand", SIDE)
    second = basis_out[depth : 2 * depth]
    m2 = middle(second)
    started = after(flags, rows, second)
    stacked, *more_stacked = stack_blocks(started, grads, depth)
    part_own = feature_dots(
        after(started, s0, m0), grads, [([(basis_out, 0)], 0, 0, 3 * STEPS, False)]
    )
    precond = (test_grads.astype(jnp.float32) / (eigval + damping)).astype(jnp.bfloat16)
    m1 = middle(after(s0, m0))
    third = jnp.concatenate([basis_out[2 * depth :], basis_out[: 2 * rows_in - depth]])
    s3 = side(third, jnp.concatenate([m0, m1]))
    m3 = middle(after(basis_out[2 * depth :], precond, stacked, *more_stacked, *part_own))
    m5 = middle(s12[depth:])
    to_s45 = pick(stacked, jnp.concatenate([m2, m3]))
    s45 = lax.ppermute(after(to_s45, s3), "cand", SIDE)
    m6 = middle(s3[:depth])
    m4 = middle(after(basis_out[:depth], m5))
    s6 = side(more_stacked[0], m5)
    to_s7 = pick(after(more_stacked[1], s45), m6)
    s7 = lax.ppermute(to_s7, "cand", SIDE)
    m7 = middle(after(s12[:depth], m6))

    part_in = input_dots(
        after(flags, s3, m5),
        acts,
        [[(basis_in, 0)], [(s0, 0)], [(s3, 0), (m0, 0)], [(s3, 1), (m1, 0)]],
    )
    part_a = feature_dots(
        after(flags, *part_in),
        grads,
        [
            ([(s12, 0)], STEPS, 0, 2 * STEPS, False),
            ([(s3, 0)], 2 * STEPS, 2 * STEPS, STEPS, True),
        ],
    )
    totals = both_dots(after(flags, to_s7, s45), grads, (s45, 0), ((m2, m5), (m3, m6)))
    core_in = core_sum(*after(part_in, s6, m4, m7, totals))
    rot_in = chip_sum(core_in)
    rot_in = gather_rows(rot_in.astype(jnp.bfloat16))
    rot_in = rot_in.reshape(tiles_here, TILE, 4 * cols)
    parts = [jnp.concatenate(part, axis=1) for part in zip(part_own, part_a)]
    core_a = core_sum(*after(parts, s6, m4, m7, totals))
    sums = chip_sum(core_a)
    sum_own, sum_a = sums[:, :tok_rows], sums[:, tok_rows:]

    shards = [(basis_out, 0), (m4, 0), (m7, 0)]
    *part_b, part_c, last_grads = partner_dots(
        after(flags, totals, core_in, core_a),
        [(s45, 0), (s45, STEPS), (s6, 0)],
        shards,
        grads,
        STEPS,
        (s6, 0, depth),
        totals,
    )
    core_b = core_sum(*part_b)
    sums = chip_sum(core_b)
    sum_b, sums = sums[:, :tok_rows], sums[:, tok_rows:]
    part_last = partner_dots(
        after(flags, part_c), [(s7, 0)], shards, last_grads, 0, (s7, 0, depth), part_c
    )
    sum_last = chip_sum(core_sum(*part_last))
    sum_c, sum_last = sum_last[:, :tok_rows], sum_last[:, tok_rows:]

    rowmask, ignored = tile_layout(pair_tiles, last_rows, plane * tiles_here, tiles_here, TILE)
    keep = rowmask.reshape(1, tok_rows).astype(jnp.bfloat16)

    def tile_prods(rot_out):
        return jnp.einsum(
            "etr,tra->tea",
            (rot_out.astype(jnp.bfloat16) * keep).reshape(slim, tiles_here, TILE),
            rot_in,
            preferred_element_type=jnp.float32,
        ).astype(jnp.bfloat16)

    def pair_scores(*received):
        prods = jnp.concatenate([x for x, source in received])
        scores = jnp.einsum("tea,jea->tj", prods, precond, preferred_element_type=jnp.float32)
        onehot = jnp.concatenate([
            tile_layout(pair_tiles, last_rows, source * tiles_here, tiles_here, TILE)[1]
            for x, source in received
        ])
        return jnp.sum(jnp.where(onehot[:, :, None], scores[:, None, :], 0.0), axis=0)

    prods_own = tile_prods(sum_own)
    prods_middle = tile_prods(sum_b)
    from_middle = middle(prods_middle)
    last = lax.ppermute(after(sum_last, prods_own, prods_middle), "cand", SIDE)
    back = lax.ppermute(sums, "cand", SIDE)
    back = jnp.where(end, back, 0.0).reshape(slim, 3, tok_rows - TILE)
    last = jnp.where(end, last, 0.0).reshape(slim, 3, TILE)

    def with_partner(whole, at):
        return whole + jnp.concatenate([back[:, at], last[:, at]], axis=1)

    prods_a = tile_prods(with_partner(sum_a, 0))
    prods_b = tile_prods(with_partner(sum_b, 1))
    prods_c = tile_prods(with_partner(sum_c, 2))
    from_far = lax.ppermute(prods_c, ALL, far)
    from_two = lax.ppermute(pick(prods_b, prods_c), "cand", TWO)
    from_side = lax.ppermute(prods_a, "cand", SIDE)
    total = pair_scores(
        (prods_own, plane),
        (from_side, plane ^ 1),
        (from_two, plane ^ 2),
        (pick(from_far, from_middle), plane ^ 3),
    )
    return final_sum(total)


def final_sum(total):
    npairs, ntest = total.shape
    blocks = total.reshape(4, npairs // 4, 4, ntest // 4).transpose(0, 2, 1, 3)
    blocks = blocks.reshape(16, npairs // 4, ntest // 4)
    return jnp.sum(lax.all_to_all(blocks, ALL, 0, 0, tiled=True), axis=0)


def gather_plan(acts, grads, basis_in, basis_out, eigval, test_grads, pair_tiles, last_rows):
    ncand = lax.axis_size("cand")
    nfeat = lax.axis_size(FEAT)
    tok_rows = acts.shape[0]
    width_in = basis_in.shape[1] * ncand
    width_out = basis_out.shape[1] * ncand
    slim = width_out // (ncand * nfeat)
    part_in = jnp.dot(
        acts,
        lax.all_gather(basis_in, "cand", axis=1, tiled=True),
        preferred_element_type=jnp.float32,
    )
    part_out = jnp.dot(
        grads,
        lax.all_gather(basis_out, "cand", axis=1, tiled=True),
        preferred_element_type=jnp.float32,
    )
    part_out = part_out.reshape(tok_rows, ncand, nfeat, slim).transpose(0, 2, 1, 3)
    part_out = part_out.reshape(tok_rows, nfeat * ncand * slim)
    summed_in, summed_out = lax.psum((part_in, part_out), FEAT)
    own = lax.dynamic_slice_in_dim(
        summed_out, lax.axis_index(FEAT) * (ncand * slim), ncand * slim, 1
    )
    rot_in = summed_in.astype(jnp.bfloat16)
    rot_out = own.astype(jnp.bfloat16)
    tiles_here = tok_rows // TILE
    rowmask, ignored = tile_layout(
        pair_tiles, last_rows, lax.axis_index("cand") * tiles_here, tiles_here, TILE
    )
    masked = rot_out.reshape(tiles_here, TILE, ncand * slim) * rowmask[:, :, None].astype(
        jnp.bfloat16
    )
    prods = jnp.einsum(
        "tre,tra->tea",
        masked,
        rot_in.reshape(tiles_here, TILE, width_in),
        preferred_element_type=jnp.float32,
    ).astype(jnp.bfloat16)
    prods = prods.reshape(tiles_here, ncand, slim, width_in)
    received = lax.all_to_all(prods, "cand", split_axis=1, concat_axis=0, tiled=True)
    all_tiles = received.shape[0]
    received = received.reshape(all_tiles, slim, width_in)
    precond = (test_grads.astype(jnp.float32) / (eigval + damping)).astype(jnp.bfloat16)
    tile_part = jnp.einsum("tea,jea->tj", received, precond, preferred_element_type=jnp.float32)
    ignored_mask, onehot = tile_layout(pair_tiles, last_rows, 0, all_tiles, TILE)
    pair_part = jnp.dot(onehot.astype(jnp.float32).T, tile_part, precision=lax.Precision.HIGHEST)
    npairs = pair_part.shape[0]
    ntest = pair_part.shape[1]
    total = lax.psum(pair_part, ("cand", "eig", "rep"))
    rows = lax.dynamic_slice_in_dim(
        total, lax.axis_index("cand") * (npairs // ncand), npairs // ncand, 0
    )
    return lax.dynamic_slice_in_dim(
        rows, lax.axis_index(FEAT) * (ntest // nfeat), ntest // nfeat, 1
    )


def solution(mesh):
    in_specs = (
        P(("groups", "cand"), ("eig", "rep")),
        P(("groups", "cand"), ("eig", "rep")),
        P(("groups", "eig", "rep"), "cand"),
        P(("groups", "eig", "rep"), "cand"),
        P(("groups", "cand", "eig", "rep"), None),
        P("groups", ("cand", "eig", "rep"), None),
        P("groups"),
        P("groups"),
    )
    out_specs = P(("groups", "cand"), ("eig", "rep"))
    sizes = (mesh.shape["cand"], mesh.shape["eig"], mesh.shape["rep"])
    per_device = line_plan if sizes == (4, 2, 2) else gather_plan
    return jax.shard_map(
        per_device, mesh=mesh, in_specs=in_specs, out_specs=out_specs, check_vma=False
    )
```

```python
import jax
import jax.numpy as jnp
from jax import lax
from jax.experimental import pallas as pl
from jax.experimental.pallas import tpu as pltpu
from jax.sharding import PartitionSpec as P

TILE = 128
FEAT = ("eig", "rep")
ALL = ("cand", "eig", "rep")
STEPS = 3
PARAMS = pltpu.CompilerParams(vmem_limit_bytes=20 << 20)
SHORT = pl.CostEstimate(flops=1, bytes_accessed=1, transcendentals=0)
SIDE = ((0, 1), (1, 0), (2, 3), (3, 2))
TWO = ((0, 2), (2, 0), (1, 3), (3, 1))

damping = 0.01


def tile_layout(pair_tiles, last_rows, first_tile, count, tile_rows):
    tiles = first_tile + jnp.arange(count, dtype=jnp.int32)
    ends = jnp.cumsum(pair_tiles)
    owner = jnp.sum((ends[None, :] <= tiles[:, None]).astype(jnp.int32), axis=1)
    onehot = owner[:, None] == jnp.arange(pair_tiles.shape[0], dtype=jnp.int32)[None, :]
    last_of = jnp.sum(jnp.where(onehot, last_rows[None, :], 0), axis=1)
    end_of = jnp.sum(jnp.where(onehot, ends[None, :], 0), axis=1)
    limit = jnp.where(tiles == end_of - 1, last_of, tile_rows)
    rowmask = jnp.arange(tile_rows, dtype=jnp.int32)[None, :] < limit[:, None]
    return (rowmask, onehot)


def after(x, *earlier):
    return lax.optimization_barrier((x, *earlier))[0]


def swap(x, axis_name):
    return lax.ppermute(x, axis_name, [(0, 1), (1, 0)])


def halves(x, axis_name):
    first = lax.axis_index(axis_name) == 0
    low, high = jnp.split(x, 2)
    return jnp.where(first, low, high), jnp.where(first, high, low)


def chip_parts(keep, received):
    keep, their_keep = halves(keep, "eig")
    received, their_received = halves(received, "eig")
    return keep + received, (their_keep + their_received).astype(jnp.bfloat16)


def chip_sum(keep, give):
    return keep + swap(give, "eig").astype(jnp.float32)


def gather_rows(x):
    other = swap(x, "eig")
    first = lax.axis_index("eig") == 0
    both = jnp.stack([jnp.where(first, x, other), jnp.where(first, other, x)])
    other = swap(both, "rep")
    first = lax.axis_index("rep") == 0
    whole = jnp.stack([jnp.where(first, both, other), jnp.where(first, other, both)], axis=1)
    return whole.reshape((-1,) + x.shape[1:])


def split_rows(full_ref, keep_ref, give_ref, rep, columns=None):
    rows = full_ref.shape[0] // 4
    columns = slice(None) if columns is None else columns
    for e in range(2):
        here = pl.ds(e * rows, rows)
        mine = pl.ds(pl.multiple_of((2 * e + rep) * rows, rows), rows)
        theirs = pl.ds(pl.multiple_of((2 * e + 1 - rep) * rows, rows), rows)
        keep_ref[here, columns] = full_ref[mine, :]
        give_ref[here, columns] = full_ref[theirs, :]


def add_dot(total_ref, rows_ref, shard):
    half = total_ref.shape[0] // 2
    for here in (pl.ds(0, half), pl.ds(half, half)):
        total_ref[here, :] += jnp.dot(
            rows_ref[here, :], shard, preferred_element_type=jnp.float32
        )


def feature_dots(flags, grads, segments, start=None, split=True):
    tok = grads.shape[0]
    cols = segments[0][0][0][0].shape[1]
    depth = grads.shape[1] // (3 * STEPS)
    firsts = [sum(s[3] for s in segments[:at]) for at in range(len(segments))]
    total = sum(s[3] for s in segments)

    def grads_at(i, flags_ref):
        at = 0
        for first, (choices, at_end, at_middle, steps, only) in zip(firsts, segments):
            base = at_end + flags_ref[0] * 0 if at_end == at_middle else (
                flags_ref[0] * at_end + (1 - flags_ref[0]) * at_middle
            )
            at = jnp.where(i >= first, base + i - first, at)
        return (0, at)

    def rows_at(first, steps, row, wanted):
        def index(i, flags_ref):
            step = jnp.clip(i - first, 0, steps - 1)
            if wanted is not None:
                step = step * (flags_ref[0] if wanted else 1 - flags_ref[0])
            return (row + step, 0)

        return index

    operands, specs = [grads], [pl.BlockSpec((tok, depth), grads_at)]
    for first, (choices, at_end, at_middle, steps, only) in zip(firsts, segments):
        for which, (array, row) in enumerate(choices):
            wanted = None if len(choices) == 1 else which == 0
            operands.append(array)
            specs.append(pl.BlockSpec((depth, cols), rows_at(first, steps, row, wanted)))
    if start is not None:
        operands.append(start)
        specs.append(pl.BlockSpec((tok, cols), lambda i, flags_ref: (0, 0)))

    def kernel(flags_ref, grads_ref, *refs):
        i = pl.program_id(0)
        end = flags_ref[0] == 1
        inputs, rest = list(refs[: len(operands) - 1]), refs[len(operands) - 1 :]
        if split:
            keep_ref, give_ref, total_ref, turned_ref = rest
        else:
            (total_ref,) = rest

        @pl.when(i == 0)
        def begin():
            total_ref[...] = jnp.zeros_like(total_ref) if start is None else inputs[-1][...]

        at = 0
        for first, (choices, at_end, at_middle, steps, only) in zip(firsts, segments):
            here = inputs[at : at + len(choices)]
            at += len(choices)
            active = (i >= first) & (i < first + steps)
            if only:
                active = active & (flags_ref[0] == 0)

            @pl.when(active)
            def add(here=here):
                shard = here[0][...]
                if len(here) == 2:
                    shard = jnp.where(end, shard, here[1][...])
                add_dot(total_ref, grads_ref, shard)

        if split:

            @pl.when(i == total - 1)
            def finish():
                turned_ref[...] = total_ref[...].T
                split_rows(turned_ref, keep_ref, give_ref, flags_ref[1])

    whole = lambda i, flags_ref: (0, 0)
    if split:
        out_shape = [jax.ShapeDtypeStruct((cols // 2, tok), jnp.float32)] * 2
        out_specs = [pl.BlockSpec((cols // 2, tok), whole)] * 2
        scratch = [pltpu.VMEM((tok, cols), jnp.float32), pltpu.VMEM((cols, tok), jnp.float32)]
    else:
        out_shape = jax.ShapeDtypeStruct((tok, cols), jnp.float32)
        out_specs = pl.BlockSpec((tok, cols), whole)
        scratch = []
    return pl.pallas_call(
        kernel,
        out_shape=out_shape,
        grid_spec=pltpu.PrefetchScalarGridSpec(
            num_scalar_prefetch=1,
            grid=(total,),
            in_specs=specs,
            out_specs=out_specs,
            scratch_shapes=scratch,
        ),
        compiler_params=PARAMS,
        cost_estimate=SHORT,
    )(flags, *operands)


def both_dots(flags, grads, at_end, at_middle):
    tok = grads.shape[0]
    cols = at_end[0].shape[1]
    step = grads.shape[1] // (3 * STEPS)

    def third_at(first):
        def index(i, flags_ref):
            return (jnp.clip(i - first, 0, STEPS - 1) * (1 - flags_ref[0]), 0)

        return index

    operands = [grads, at_end[0]] + [array for pair in at_middle for array in pair]
    specs = [
        pl.BlockSpec((tok, step), lambda i, flags_ref: (0, STEPS + i)),
        pl.BlockSpec((step, cols), lambda i, flags_ref: (at_end[1] + i * flags_ref[0], 0)),
    ]
    for first in (0, STEPS):
        specs += [pl.BlockSpec((step, cols), third_at(first))] * 2

    def kernel(flags_ref, grads_ref, end_ref, b1_ref, c1_ref, b2_ref, c2_ref, total_ref):
        i = pl.program_id(0)

        @pl.when(i == 0)
        def begin():
            total_ref[...] = jnp.zeros_like(total_ref)

        @pl.when(flags_ref[0] == 1)
        def one():
            total_ref[:, :cols] += jnp.dot(
                grads_ref[...], end_ref[...], preferred_element_type=jnp.float32
            )

        for first, b_ref, c_ref in ((0, b1_ref, c1_ref), (STEPS, b2_ref, c2_ref)):

            @pl.when((flags_ref[0] == 0) & (i >= first) & (i < first + STEPS))
            def two(b_ref=b_ref, c_ref=c_ref):
                shards = jnp.concatenate([b_ref[...], c_ref[...]], axis=1)
                total_ref[...] += jnp.dot(
                    grads_ref[...], shards, preferred_element_type=jnp.float32
                )

    return pl.pallas_call(
        kernel,
        out_shape=jax.ShapeDtypeStruct((tok, 2 * cols), jnp.float32),
        grid_spec=pltpu.PrefetchScalarGridSpec(
            num_scalar_prefetch=1,
            grid=(2 * STEPS,),
            in_specs=specs,
            out_specs=pl.BlockSpec((tok, 2 * cols), lambda i, flags_ref: (0, 0)),
        ),
        compiler_params=PARAMS,
        cost_estimate=SHORT,
    )(flags, *operands)


def partner_dots(flags, pieces, shards, grads, column, shard, start):
    tok = grads.shape[0]
    cols = shards[0][0].shape[1]
    step = shard[2] // STEPS
    count = len(pieces)
    two = start.shape[1] == 2 * cols
    width = tok + len(shards) * count * TILE

    def at(row):
        return lambda i, flags_ref: (row + i, 0)

    whole = lambda i, flags_ref: (0, 0)
    operands, specs = [], []
    for array, row in list(pieces) + list(shards) + [shard[:2]]:
        operands.append(array)
        specs.append(pl.BlockSpec((step, cols), at(row)))
    operands += [grads, start]
    specs.append(
        pl.BlockSpec(
            (tok, step),
            lambda i, flags_ref: (0, column * (flags_ref[0] if two else 1) + i),
        )
    )
    specs.append(pl.BlockSpec(start.shape, whole))
    if two:
        operands.append(grads)
        specs.append(pl.BlockSpec((tok, step), lambda i, flags_ref: (0, 2 * STEPS + i)))

    def kernel(flags_ref, *refs):
        i = pl.program_id(0)
        piece_refs, shard_refs = refs[:count], refs[count : count + len(shards)]
        end_ref, grads_ref, start_ref = refs[count + len(shards) : count + len(shards) + 3]
        keep_ref, give_ref, *rest = refs[len(operands) :]
        if two:
            second_ref, copied_ref, total_ref, sums_ref, turned_ref, wide_ref = rest
            copied_ref[...] = refs[len(operands) - 1][...]
        else:
            total_ref, sums_ref, turned_ref, wide_ref = rest

        @pl.when(i == 0)
        def begin():
            total_ref[...] = start_ref[...]
            sums_ref[...] = jnp.zeros_like(sums_ref)

        @pl.when(flags_ref[0] == 1)
        def at_an_end_plane():
            total_ref[:, total_ref.shape[1] - cols :] += jnp.dot(
                grads_ref[...], end_ref[...], preferred_element_type=jnp.float32
            )

        @pl.when(flags_ref[0] == 0)
        def at_a_middle_plane():
            side_by_side = jnp.concatenate([ref[...] for ref in shard_refs], axis=1)
            tokens = jnp.concatenate(
                [
                    jnp.concatenate(
                        [ref[q * TILE : (q + 1) * TILE, :] for q in range(step // TILE)], axis=1
                    )
                    for ref in piece_refs
                ]
            )
            sums_ref[...] += jnp.dot(tokens, side_by_side, preferred_element_type=jnp.float32)
            if two:
                total_ref[...] += jnp.dot(
                    grads_ref[...], side_by_side[:, cols:], preferred_element_type=jnp.float32
                )

        @pl.when(i == STEPS - 1)
        def finish():
            wide_ref[...] = total_ref[:, :cols].T
            split_rows(wide_ref, keep_ref, give_ref, flags_ref[1], pl.ds(0, tok))
            for j in range(len(shards)):
                turned_ref[...] = sums_ref[:, j * cols : (j + 1) * cols].T
                columns = pl.ds(tok + j * count * TILE, count * TILE)
                split_rows(turned_ref, keep_ref, give_ref, flags_ref[1], columns)
            if two:
                second_ref[...] = total_ref[:, cols:]

    out_shape = [jax.ShapeDtypeStruct((cols // 2, width), jnp.float32)] * 2
    out_specs = [pl.BlockSpec((cols // 2, width), whole)] * 2
    if two:
        out_shape.append(jax.ShapeDtypeStruct((tok, cols), jnp.float32))
        out_specs.append(pl.BlockSpec((tok, cols), whole))
        out_shape.append(jax.ShapeDtypeStruct((tok, STEPS * step), grads.dtype))
        out_specs.append(pl.BlockSpec((tok, step), lambda i, flags_ref: (0, i)))
    return pl.pallas_call(
        kernel,
        out_shape=out_shape,
        grid_spec=pltpu.PrefetchScalarGridSpec(
            num_scalar_prefetch=1,
            grid=(STEPS,),
            in_specs=specs,
            out_specs=out_specs,
            scratch_shapes=[
                pltpu.VMEM(start.shape, jnp.float32),
                pltpu.VMEM((count * TILE, len(shards) * cols), jnp.float32),
                pltpu.VMEM((cols, count * TILE), jnp.float32),
                pltpu.VMEM((cols, tok), jnp.float32),
            ],
        ),
        compiler_params=PARAMS,
        cost_estimate=SHORT,
    )(flags, *operands)


def stack_blocks(flags, grads, depth):
    tiles = grads.shape[0] // TILE
    firsts = [0] + list(range(tiles // 2, tiles))
    counts = [tiles // 2] + [1] * (tiles // 2)

    def kernel(flags_ref, grads_ref, *out_refs):
        t = pl.program_id(0)
        for first, count, out_ref in zip(firsts, counts, out_refs):

            @pl.when((t >= first) & (t < first + count))
            def copy(out_ref=out_ref):
                for q in range(depth // TILE):
                    here = slice(q * TILE, (q + 1) * TILE)
                    out_ref[here, :] = grads_ref[:, here]

    def place(first, count):
        return lambda t, flags_ref: (jnp.clip(t - first, 0, count - 1), 0)

    return pl.pallas_call(
        kernel,
        out_shape=[jax.ShapeDtypeStruct((count * depth, TILE), grads.dtype) for count in counts],
        grid_spec=pltpu.PrefetchScalarGridSpec(
            num_scalar_prefetch=1,
            grid=(tiles,),
            in_specs=[pl.BlockSpec((TILE, depth), lambda t, flags_ref: (t, 0))],
            out_specs=[
                pl.BlockSpec((depth, TILE), place(first, count))
                for first, count in zip(firsts, counts)
            ],
        ),
        compiler_params=PARAMS,
        cost_estimate=SHORT,
    )(flags, grads)


def input_dots(flags, acts, shards):
    tok, depth = acts.shape
    cols = shards[0][0][0].shape[1]
    operands, specs = [acts], [pl.BlockSpec((tok, depth), lambda i, flags_ref: (0, 0))]
    for choices in shards:
        for array, row in choices:
            operands.append(array)
            specs.append(pl.BlockSpec((depth, cols), lambda i, flags_ref, row=row: (row, 0)))

    def kernel(flags_ref, acts_ref, *refs):
        i = pl.program_id(0)
        inputs = list(refs[: len(operands) - 1])
        keep_ref, give_ref, part_ref = refs[len(operands) - 1 :]
        at = 0
        for slot, choices in enumerate(shards):
            here = inputs[at : at + len(choices)]
            at += len(choices)

            @pl.when(i == slot)
            def add(here=here):
                shard = here[0][...]
                if len(here) == 2:
                    shard = jnp.where(flags_ref[0] == 1, shard, here[1][...])
                part_ref[...] = jnp.dot(acts_ref[...], shard, preferred_element_type=jnp.float32)

        split_rows(part_ref, keep_ref, give_ref, flags_ref[1])

    place = pl.BlockSpec((tok // 2, cols), lambda i, flags_ref: (0, flags_ref[2 + i]))
    return pl.pallas_call(
        kernel,
        out_shape=[jax.ShapeDtypeStruct((tok // 2, cols * len(shards)), jnp.float32)] * 2,
        grid_spec=pltpu.PrefetchScalarGridSpec(
            num_scalar_prefetch=1,
            grid=(len(shards),),
            in_specs=specs,
            out_specs=[place, place],
            scratch_shapes=[pltpu.VMEM((tok, cols), jnp.float32)],
        ),
        compiler_params=PARAMS,
        cost_estimate=SHORT,
    )(flags, *operands)


def line_plan(acts, grads, basis_in, basis_out, eigval, test_grads, pair_tiles, last_rows):
    plane = lax.axis_index("cand")
    end = (plane == 0) | (plane == 3)
    tok_rows = acts.shape[0]
    cols = basis_in.shape[1]
    tiles_here = tok_rows // TILE
    slim = cols // 4
    depth = basis_out.shape[0] // 3
    rows_in = basis_in.shape[0]

    def pick(at_end, at_middle):
        return jnp.where(end, at_end, at_middle)

    def side(at_end, at_middle):
        return lax.ppermute(pick(at_end, at_middle), "cand", SIDE)

    among, far = [], []
    for at in range(16):
        between = 4 <= at < 12
        across = 12 - 4 * (at // 4) + at % 4
        among.append((at, across if between else at ^ 1))
        far.append((at, at ^ 1 if between else across))

    def middle(x):
        return lax.ppermute(x, ALL, among)

    at_b = jnp.where(end, plane ^ 2, plane ^ 3)
    at_c = jnp.where(end, plane ^ 3, plane ^ 2)
    rep = lax.axis_index("rep")
    flags = jnp.stack([end.astype(jnp.int32), rep, plane, plane ^ 1, at_b, at_c])

    rows = lax.dynamic_slice_in_dim(basis_out, jnp.where(end, 0, depth), 2 * depth, 0)
    s0 = lax.ppermute(basis_in, "cand", SIDE)
    m0 = middle(basis_in)
    s12 = lax.ppermute(rows, "cand", SIDE)
    second = basis_out[depth : 2 * depth]
    m2 = middle(second)
    started = after(flags, rows, second)
    stacked, *more_stacked = stack_blocks(started, grads, depth)
    part_own = feature_dots(
        after(started, s0, m0), grads, [([(basis_out, 0)], 0, 0, 3 * STEPS, False)]
    )
    precond = (test_grads.astype(jnp.float32) / (eigval + damping)).astype(jnp.bfloat16)
    m1 = middle(after(s0, m0))
    third = jnp.concatenate([basis_out[2 * depth :], basis_out[: 2 * rows_in - depth]])
    s3 = side(third, jnp.concatenate([m0, m1]))
    m3 = middle(after(basis_out[2 * depth :], precond, stacked, *more_stacked, *part_own))
    m5 = middle(s12[depth:])
    to_s45 = pick(stacked, jnp.concatenate([m2, m3]))
    s45 = lax.ppermute(after(to_s45, s3), "cand", SIDE)
    m6 = middle(s3[:depth])
    m4 = middle(after(basis_out[:depth], m5))
    s6 = side(more_stacked[0], m5)
    to_s7 = pick(after(more_stacked[1], s45), m6)
    s7 = lax.ppermute(to_s7, "cand", SIDE)
    m7 = middle(after(s12[:depth], m6))

    part_in = input_dots(
        after(flags, s3, m5),
        acts,
        [[(basis_in, 0)], [(s0, 0)], [(s3, 0), (m0, 0)], [(s3, 1), (m1, 0)]],
    )
    part_a = feature_dots(
        after(flags, *part_in),
        grads,
        [
            ([(s12, 0)], STEPS, 0, 2 * STEPS, False),
            ([(s3, 0)], 2 * STEPS, 2 * STEPS, STEPS, True),
        ],
    )
    totals = both_dots(after(flags, to_s7, s45, *part_a), grads, (s45, 0), ((m2, m5), (m3, m6)))
    parts = [jnp.concatenate(part, axis=1) for part in zip(part_own, part_a)]
    keep_a, give_a = after(parts, s6, m4, totals)
    core_a = swap(give_a, "rep")

    shards = [(basis_out, 0), (m4, 0), (m7, 0)]
    *part_b, part_c, last_grads = partner_dots(
        after(flags, totals, core_a),
        [(s45, 0), (s45, STEPS), (s6, 0)],
        shards,
        grads,
        STEPS,
        (s6, 0, depth),
        totals,
    )
    keep_in, give_in = after(part_in, part_c)
    core_in = swap(give_in, "rep")
    rot_in = gather_rows(chip_sum(*chip_parts(keep_in, core_in)).astype(jnp.bfloat16))
    rot_in = rot_in.reshape(tiles_here, TILE, 4 * cols)
    keep_b, give_b = part_b
    keep_b, give_b = chip_parts(
        jnp.concatenate([keep_a, keep_b], axis=1),
        jnp.concatenate([core_a, swap(give_b, "rep")], axis=1),
    )
    sums = chip_sum(keep_b, give_b)
    sum_own, sum_a, sum_b = [sums[:, i * tok_rows : (i + 1) * tok_rows] for i in range(3)]
    sums = sums[:, 3 * tok_rows :].astype(jnp.bfloat16)
    keep_last, give_last = partner_dots(
        after(flags, part_c),
        [(s7, 0)],
        shards,
        last_grads,
        0,
        (s7, 0, depth),
        part_c,
    )
    keep_last, give_last = after((keep_last, give_last), give_b)
    sum_last = chip_sum(*chip_parts(keep_last, swap(give_last, "rep")))
    sum_c, sum_last = sum_last[:, :tok_rows], sum_last[:, tok_rows:].astype(jnp.bfloat16)

    rowmask, ignored = tile_layout(pair_tiles, last_rows, plane * tiles_here, tiles_here, TILE)
    keep = rowmask.reshape(1, tok_rows).astype(jnp.bfloat16)

    def tile_prods(rot_out):
        return jnp.einsum(
            "etr,tra->tea",
            (rot_out.astype(jnp.bfloat16) * keep).reshape(slim, tiles_here, TILE),
            rot_in,
            preferred_element_type=jnp.float32,
        ).astype(jnp.bfloat16)

    def pair_scores(*received):
        prods = jnp.concatenate([x for x, source in received])
        scores = jnp.einsum("tea,jea->tj", prods, precond, preferred_element_type=jnp.float32)
        onehot = jnp.concatenate([
            tile_layout(pair_tiles, last_rows, source * tiles_here, tiles_here, TILE)[1]
            for x, source in received
        ])
        return jnp.sum(jnp.where(onehot[:, :, None], scores[:, None, :], 0.0), axis=0)

    prods_own = tile_prods(sum_own)
    prods_middle = tile_prods(sum_b)
    from_middle = middle(prods_middle)
    last = lax.ppermute(after(sum_last, prods_own, prods_middle), "cand", SIDE)
    back = lax.ppermute(sums, "cand", SIDE)
    back = jnp.where(end, back, jnp.zeros_like(back)).reshape(slim, 3, tok_rows - TILE)
    last = jnp.where(end, last, jnp.zeros_like(last)).reshape(slim, 3, TILE)

    def with_partner(whole, at):
        return whole + jnp.concatenate([back[:, at], last[:, at]], axis=1).astype(jnp.float32)

    prods_a = tile_prods(with_partner(sum_a, 0))
    prods_b = tile_prods(with_partner(sum_b, 1))
    prods_c = tile_prods(with_partner(sum_c, 2))
    from_far = lax.ppermute(prods_c, ALL, far)
    from_two = lax.ppermute(pick(prods_b, prods_c), "cand", TWO)
    from_side = lax.ppermute(prods_a, "cand", SIDE)
    total = pair_scores(
        (prods_own, plane),
        (from_side, plane ^ 1),
        (from_two, plane ^ 2),
        (pick(from_far, from_middle), plane ^ 3),
    )
    return final_sum(total)


def final_sum(total):
    npairs, ntest = total.shape
    blocks = total.reshape(4, npairs // 4, 4, ntest // 4).transpose(0, 2, 1, 3)
    blocks = blocks.reshape(16, npairs // 4, ntest // 4)
    return jnp.sum(lax.all_to_all(blocks, ALL, 0, 0, tiled=True), axis=0)


def gather_plan(acts, grads, basis_in, basis_out, eigval, test_grads, pair_tiles, last_rows):
    ncand = lax.axis_size("cand")
    nfeat = lax.axis_size(FEAT)
    tok_rows = acts.shape[0]
    width_in = basis_in.shape[1] * ncand
    width_out = basis_out.shape[1] * ncand
    slim = width_out // (ncand * nfeat)
    part_in = jnp.dot(
        acts,
        lax.all_gather(basis_in, "cand", axis=1, tiled=True),
        preferred_element_type=jnp.float32,
    )
    part_out = jnp.dot(
        grads,
        lax.all_gather(basis_out, "cand", axis=1, tiled=True),
        preferred_element_type=jnp.float32,
    )
    part_out = part_out.reshape(tok_rows, ncand, nfeat, slim).transpose(0, 2, 1, 3)
    part_out = part_out.reshape(tok_rows, nfeat * ncand * slim)
    summed_in, summed_out = lax.psum((part_in, part_out), FEAT)
    own = lax.dynamic_slice_in_dim(
        summed_out, lax.axis_index(FEAT) * (ncand * slim), ncand * slim, 1
    )
    rot_in = summed_in.astype(jnp.bfloat16)
    rot_out = own.astype(jnp.bfloat16)
    tiles_here = tok_rows // TILE
    rowmask, ignored = tile_layout(
        pair_tiles, last_rows, lax.axis_index("cand") * tiles_here, tiles_here, TILE
    )
    masked = rot_out.reshape(tiles_here, TILE, ncand * slim) * rowmask[:, :, None].astype(
        jnp.bfloat16
    )
    prods = jnp.einsum(
        "tre,tra->tea",
        masked,
        rot_in.reshape(tiles_here, TILE, width_in),
        preferred_element_type=jnp.float32,
    ).astype(jnp.bfloat16)
    prods = prods.reshape(tiles_here, ncand, slim, width_in)
    received = lax.all_to_all(prods, "cand", split_axis=1, concat_axis=0, tiled=True)
    all_tiles = received.shape[0]
    received = received.reshape(all_tiles, slim, width_in)
    precond = (test_grads.astype(jnp.float32) / (eigval + damping)).astype(jnp.bfloat16)
    tile_part = jnp.einsum("tea,jea->tj", received, precond, preferred_element_type=jnp.float32)
    ignored_mask, onehot = tile_layout(pair_tiles, last_rows, 0, all_tiles, TILE)
    pair_part = jnp.dot(onehot.astype(jnp.float32).T, tile_part, precision=lax.Precision.HIGHEST)
    npairs = pair_part.shape[0]
    ntest = pair_part.shape[1]
    total = lax.psum(pair_part, ("cand", "eig", "rep"))
    rows = lax.dynamic_slice_in_dim(
        total, lax.axis_index("cand") * (npairs // ncand), npairs // ncand, 0
    )
    return lax.dynamic_slice_in_dim(
        rows, lax.axis_index(FEAT) * (ntest // nfeat), ntest // nfeat, 1
    )


def solution(mesh):
    in_specs = (
        P(("groups", "cand"), ("eig", "rep")),
        P(("groups", "cand"), ("eig", "rep")),
        P(("groups", "eig", "rep"), "cand"),
        P(("groups", "eig", "rep"), "cand"),
        P(("groups", "cand", "eig", "rep"), None),
        P("groups", ("cand", "eig", "rep"), None),
        P("groups"),
        P("groups"),
    )
    out_specs = P(("groups", "cand"), ("eig", "rep"))
    sizes = (mesh.shape["cand"], mesh.shape["eig"], mesh.shape["rep"])
    per_device = line_plan if sizes == (4, 2, 2) else gather_plan
    return jax.shard_map(
        per_device, mesh=mesh, in_specs=in_specs, out_specs=out_specs, check_vma=False
    )
```

```python
import jax
import jax.numpy as jnp
from jax import lax
from jax.experimental import pallas as pl
from jax.experimental.pallas import tpu as pltpu
from jax.sharding import PartitionSpec as P

TILE = 128
FEAT = ("eig", "rep")
ALL = ("cand", "eig", "rep")
STEPS = 3
PARAMS = pltpu.CompilerParams(vmem_limit_bytes=20 << 20)
SHORT = pl.CostEstimate(flops=1, bytes_accessed=1, transcendentals=0)
SIDE = ((0, 1), (1, 0), (2, 3), (3, 2))
TWO = ((0, 2), (2, 0), (1, 3), (3, 1))

damping = 0.01


def tile_layout(pair_tiles, last_rows, first_tile, count, tile_rows):
    tiles = first_tile + jnp.arange(count, dtype=jnp.int32)
    ends = jnp.cumsum(pair_tiles)
    owner = jnp.sum((ends[None, :] <= tiles[:, None]).astype(jnp.int32), axis=1)
    onehot = owner[:, None] == jnp.arange(pair_tiles.shape[0], dtype=jnp.int32)[None, :]
    last_of = jnp.sum(jnp.where(onehot, last_rows[None, :], 0), axis=1)
    end_of = jnp.sum(jnp.where(onehot, ends[None, :], 0), axis=1)
    limit = jnp.where(tiles == end_of - 1, last_of, tile_rows)
    rowmask = jnp.arange(tile_rows, dtype=jnp.int32)[None, :] < limit[:, None]
    return (rowmask, onehot)


def after(x, *earlier):
    return lax.optimization_barrier((x, *earlier))[0]


def swap(x, axis_name):
    return lax.ppermute(x, axis_name, [(0, 1), (1, 0)])


def halves(x, axis_name):
    first = lax.axis_index(axis_name) == 0
    low, high = jnp.split(x, 2)
    return jnp.where(first, low, high), jnp.where(first, high, low)


def chip_parts(keep, received):
    keep, their_keep = halves(keep, "eig")
    received, their_received = halves(received, "eig")
    return keep + received, (their_keep + their_received).astype(jnp.bfloat16)


def chip_sum(keep, give):
    return keep + swap(give, "eig").astype(jnp.float32)


def gather_rows(x):
    other = swap(x, "eig")
    first = lax.axis_index("eig") == 0
    both = jnp.stack([jnp.where(first, x, other), jnp.where(first, other, x)])
    other = swap(both, "rep")
    first = lax.axis_index("rep") == 0
    whole = jnp.stack([jnp.where(first, both, other), jnp.where(first, other, both)], axis=1)
    return whole.reshape((-1,) + x.shape[1:])


def split_rows(full_ref, keep_ref, give_ref, rep, columns=None):
    rows = full_ref.shape[0] // 4
    columns = slice(None) if columns is None else columns
    for e in range(2):
        here = pl.ds(e * rows, rows)
        mine = pl.ds(pl.multiple_of((2 * e + rep) * rows, rows), rows)
        theirs = pl.ds(pl.multiple_of((2 * e + 1 - rep) * rows, rows), rows)
        keep_ref[here, columns] = full_ref[mine, :]
        give_ref[here, columns] = full_ref[theirs, :]


def add_dot(total_ref, rows_ref, shard):
    half = total_ref.shape[0] // 2
    for here in (pl.ds(0, half), pl.ds(half, half)):
        total_ref[here, :] += jnp.dot(
            rows_ref[here, :], shard, preferred_element_type=jnp.float32
        )


def feature_dots(flags, grads, segments, start=None, split=True):
    tok = grads.shape[0]
    cols = segments[0][0][0][0].shape[1]
    depth = grads.shape[1] // (3 * STEPS)
    firsts = [sum(s[3] for s in segments[:at]) for at in range(len(segments))]
    total = sum(s[3] for s in segments)

    def grads_at(i, flags_ref):
        at = 0
        for first, (choices, at_end, at_middle, steps, only) in zip(firsts, segments):
            base = at_end + flags_ref[0] * 0 if at_end == at_middle else (
                flags_ref[0] * at_end + (1 - flags_ref[0]) * at_middle
            )
            at = jnp.where(i >= first, base + i - first, at)
        return (0, at)

    def rows_at(first, steps, row, wanted):
        def index(i, flags_ref):
            step = jnp.clip(i - first, 0, steps - 1)
            if wanted is not None:
                step = step * (flags_ref[0] if wanted else 1 - flags_ref[0])
            return (row + step, 0)

        return index

    operands, specs = [grads], [pl.BlockSpec((tok, depth), grads_at)]
    for first, (choices, at_end, at_middle, steps, only) in zip(firsts, segments):
        for which, (array, row) in enumerate(choices):
            wanted = None if len(choices) == 1 else which == 0
            operands.append(array)
            specs.append(pl.BlockSpec((depth, cols), rows_at(first, steps, row, wanted)))
    if start is not None:
        operands.append(start)
        specs.append(pl.BlockSpec((tok, cols), lambda i, flags_ref: (0, 0)))

    def kernel(flags_ref, grads_ref, *refs):
        i = pl.program_id(0)
        end = flags_ref[0] == 1
        inputs, rest = list(refs[: len(operands) - 1]), refs[len(operands) - 1 :]
        if split:
            keep_ref, give_ref, total_ref, turned_ref = rest
        else:
            (total_ref,) = rest

        @pl.when(i == 0)
        def begin():
            total_ref[...] = jnp.zeros_like(total_ref) if start is None else inputs[-1][...]

        at = 0
        for first, (choices, at_end, at_middle, steps, only) in zip(firsts, segments):
            here = inputs[at : at + len(choices)]
            at += len(choices)
            active = (i >= first) & (i < first + steps)
            if only:
                active = active & (flags_ref[0] == 0)

            @pl.when(active)
            def add(here=here):
                shard = here[0][...]
                if len(here) == 2:
                    shard = jnp.where(end, shard, here[1][...])
                add_dot(total_ref, grads_ref, shard)

        if split:

            @pl.when(i == total - 1)
            def finish():
                turned_ref[...] = total_ref[...].T
                split_rows(turned_ref, keep_ref, give_ref, flags_ref[1])

    whole = lambda i, flags_ref: (0, 0)
    if split:
        out_shape = [jax.ShapeDtypeStruct((cols // 2, tok), jnp.float32)] * 2
        out_specs = [pl.BlockSpec((cols // 2, tok), whole)] * 2
        scratch = [pltpu.VMEM((tok, cols), jnp.float32), pltpu.VMEM((cols, tok), jnp.float32)]
    else:
        out_shape = jax.ShapeDtypeStruct((tok, cols), jnp.float32)
        out_specs = pl.BlockSpec((tok, cols), whole)
        scratch = []
    return pl.pallas_call(
        kernel,
        out_shape=out_shape,
        grid_spec=pltpu.PrefetchScalarGridSpec(
            num_scalar_prefetch=1,
            grid=(total,),
            in_specs=specs,
            out_specs=out_specs,
            scratch_shapes=scratch,
        ),
        compiler_params=PARAMS,
        cost_estimate=SHORT,
    )(flags, *operands)


def both_dots(flags, grads, at_end, at_middle):
    tok = grads.shape[0]
    cols = at_end[0].shape[1]
    step = grads.shape[1] // (3 * STEPS)

    def third_at(first):
        def index(i, flags_ref):
            return (jnp.clip(i - first, 0, STEPS - 1) * (1 - flags_ref[0]), 0)

        return index

    operands = [grads, at_end[0]] + [array for pair in at_middle for array in pair] + [grads]
    specs = [
        pl.BlockSpec((tok, step), lambda i, flags_ref: (0, STEPS + i)),
        pl.BlockSpec((step, cols), lambda i, flags_ref: (at_end[1] + i * flags_ref[0], 0)),
    ]
    for first in (0, STEPS):
        specs += [pl.BlockSpec((step, cols), third_at(first))] * 2
    specs.append(
        pl.BlockSpec(
            (tok, step),
            lambda i, flags_ref: (0, flags_ref[0] * STEPS + jnp.minimum(i, STEPS - 1)),
        )
    )

    def kernel(flags_ref, grads_ref, end_ref, b1_ref, c1_ref, b2_ref, c2_ref, next_ref, *out_refs):
        total_ref, handed_ref, last_ref = out_refs
        i = pl.program_id(0)

        @pl.when(i == 0)
        def begin():
            total_ref[...] = jnp.zeros_like(total_ref)

        @pl.when(i < STEPS)
        def hand_on_next():
            handed_ref[...] = next_ref[...]

        @pl.when(i >= STEPS)
        def hand_on_last():
            last_ref[...] = grads_ref[...]

        @pl.when(flags_ref[0] == 1)
        def one():
            total_ref[:, :cols] += jnp.dot(
                grads_ref[...], end_ref[...], preferred_element_type=jnp.float32
            )

        for first, b_ref, c_ref in ((0, b1_ref, c1_ref), (STEPS, b2_ref, c2_ref)):

            @pl.when((flags_ref[0] == 0) & (i >= first) & (i < first + STEPS))
            def two(b_ref=b_ref, c_ref=c_ref):
                shards = jnp.concatenate([b_ref[...], c_ref[...]], axis=1)
                total_ref[...] += jnp.dot(
                    grads_ref[...], shards, preferred_element_type=jnp.float32
                )

    third = jax.ShapeDtypeStruct((tok, STEPS * step), grads.dtype)
    return pl.pallas_call(
        kernel,
        out_shape=[jax.ShapeDtypeStruct((tok, 2 * cols), jnp.float32), third, third],
        grid_spec=pltpu.PrefetchScalarGridSpec(
            num_scalar_prefetch=1,
            grid=(2 * STEPS,),
            in_specs=specs,
            out_specs=[
                pl.BlockSpec((tok, 2 * cols), lambda i, flags_ref: (0, 0)),
                pl.BlockSpec((tok, step), lambda i, flags_ref: (0, jnp.minimum(i, STEPS - 1))),
                pl.BlockSpec((tok, step), lambda i, flags_ref: (0, jnp.maximum(i - STEPS, 0))),
            ],
        ),
        compiler_params=PARAMS,
        cost_estimate=SHORT,
    )(flags, *operands)


def partner_dots(flags, pieces, shards, grads, shard, start):
    tok = grads.shape[0]
    cols = shards[0][0].shape[1]
    step = shard[2] // STEPS
    count = len(pieces)
    two = start.shape[1] == 2 * cols
    width = tok + len(shards) * count * TILE

    def at(row):
        return lambda i, flags_ref: (row + i, 0)

    whole = lambda i, flags_ref: (0, 0)
    operands, specs = [], []
    for array, row in list(pieces) + list(shards) + [shard[:2]]:
        operands.append(array)
        specs.append(pl.BlockSpec((step, cols), at(row)))
    operands += [grads, start]
    specs.append(pl.BlockSpec((tok, step), lambda i, flags_ref: (0, i)))
    specs.append(pl.BlockSpec(start.shape, whole))

    def kernel(flags_ref, *refs):
        i = pl.program_id(0)
        piece_refs, shard_refs = refs[:count], refs[count : count + len(shards)]
        end_ref, grads_ref, start_ref = refs[count + len(shards) : count + len(shards) + 3]
        keep_ref, give_ref, *rest = refs[len(operands) :]
        if two:
            second_ref, total_ref, sums_ref, turned_ref, wide_ref = rest
        else:
            total_ref, sums_ref, turned_ref, wide_ref = rest

        @pl.when(i == 0)
        def begin():
            total_ref[...] = start_ref[...]
            sums_ref[...] = jnp.zeros_like(sums_ref)

        @pl.when(flags_ref[0] == 1)
        def at_an_end_plane():
            total_ref[:, total_ref.shape[1] - cols :] += jnp.dot(
                grads_ref[...], end_ref[...], preferred_element_type=jnp.float32
            )

        @pl.when(flags_ref[0] == 0)
        def at_a_middle_plane():
            side_by_side = jnp.concatenate([ref[...] for ref in shard_refs], axis=1)
            tokens = jnp.concatenate(
                [
                    jnp.concatenate(
                        [ref[q * TILE : (q + 1) * TILE, :] for q in range(step // TILE)], axis=1
                    )
                    for ref in piece_refs
                ]
            )
            sums_ref[...] += jnp.dot(tokens, side_by_side, preferred_element_type=jnp.float32)
            if two:
                total_ref[...] += jnp.dot(
                    grads_ref[...], side_by_side[:, cols:], preferred_element_type=jnp.float32
                )

        @pl.when(i == STEPS - 1)
        def finish():
            wide_ref[...] = total_ref[:, :cols].T
            split_rows(wide_ref, keep_ref, give_ref, flags_ref[1], pl.ds(0, tok))
            for j in range(len(shards)):
                turned_ref[...] = sums_ref[:, j * cols : (j + 1) * cols].T
                columns = pl.ds(tok + j * count * TILE, count * TILE)
                split_rows(turned_ref, keep_ref, give_ref, flags_ref[1], columns)
            if two:
                second_ref[...] = total_ref[:, cols:]

    out_shape = [jax.ShapeDtypeStruct((cols // 2, width), jnp.float32)] * 2
    out_specs = [pl.BlockSpec((cols // 2, width), whole)] * 2
    if two:
        out_shape.append(jax.ShapeDtypeStruct((tok, cols), jnp.float32))
        out_specs.append(pl.BlockSpec((tok, cols), whole))
    return pl.pallas_call(
        kernel,
        out_shape=out_shape,
        grid_spec=pltpu.PrefetchScalarGridSpec(
            num_scalar_prefetch=1,
            grid=(STEPS,),
            in_specs=specs,
            out_specs=out_specs,
            scratch_shapes=[
                pltpu.VMEM(start.shape, jnp.float32),
                pltpu.VMEM((count * TILE, len(shards) * cols), jnp.float32),
                pltpu.VMEM((cols, count * TILE), jnp.float32),
                pltpu.VMEM((cols, tok), jnp.float32),
            ],
        ),
        compiler_params=PARAMS,
        cost_estimate=SHORT,
    )(flags, *operands)


def stack_blocks(flags, grads, depth):
    tiles = grads.shape[0] // TILE
    firsts = [0] + list(range(tiles // 2, tiles))
    counts = [tiles // 2] + [1] * (tiles // 2)

    def kernel(flags_ref, grads_ref, *out_refs):
        t = pl.program_id(0)
        for first, count, out_ref in zip(firsts, counts, out_refs):

            @pl.when((t >= first) & (t < first + count))
            def copy(out_ref=out_ref):
                for q in range(depth // TILE):
                    here = slice(q * TILE, (q + 1) * TILE)
                    out_ref[here, :] = grads_ref[:, here]

    def place(first, count):
        return lambda t, flags_ref: (jnp.clip(t - first, 0, count - 1), 0)

    return pl.pallas_call(
        kernel,
        out_shape=[jax.ShapeDtypeStruct((count * depth, TILE), grads.dtype) for count in counts],
        grid_spec=pltpu.PrefetchScalarGridSpec(
            num_scalar_prefetch=1,
            grid=(tiles,),
            in_specs=[pl.BlockSpec((TILE, depth), lambda t, flags_ref: (t, 0))],
            out_specs=[
                pl.BlockSpec((depth, TILE), place(first, count))
                for first, count in zip(firsts, counts)
            ],
        ),
        compiler_params=PARAMS,
        cost_estimate=SHORT,
    )(flags, grads)


def input_dots(flags, acts, shards):
    tok, depth = acts.shape
    cols = shards[0][0][0].shape[1]
    operands, specs = [acts], [pl.BlockSpec((tok, depth), lambda i, flags_ref: (0, 0))]
    for choices in shards:
        for array, row in choices:
            operands.append(array)
            specs.append(pl.BlockSpec((depth, cols), lambda i, flags_ref, row=row: (row, 0)))

    def kernel(flags_ref, acts_ref, *refs):
        i = pl.program_id(0)
        inputs = list(refs[: len(operands) - 1])
        keep_ref, give_ref, part_ref = refs[len(operands) - 1 :]
        at = 0
        for slot, choices in enumerate(shards):
            here = inputs[at : at + len(choices)]
            at += len(choices)

            @pl.when(i == slot)
            def add(here=here):
                shard = here[0][...]
                if len(here) == 2:
                    shard = jnp.where(flags_ref[0] == 1, shard, here[1][...])
                part_ref[...] = jnp.dot(acts_ref[...], shard, preferred_element_type=jnp.float32)

        split_rows(part_ref, keep_ref, give_ref, flags_ref[1])

    place = pl.BlockSpec((tok // 2, cols), lambda i, flags_ref: (0, flags_ref[2 + i]))
    return pl.pallas_call(
        kernel,
        out_shape=[jax.ShapeDtypeStruct((tok // 2, cols * len(shards)), jnp.float32)] * 2,
        grid_spec=pltpu.PrefetchScalarGridSpec(
            num_scalar_prefetch=1,
            grid=(len(shards),),
            in_specs=specs,
            out_specs=[place, place],
            scratch_shapes=[pltpu.VMEM((tok, cols), jnp.float32)],
        ),
        compiler_params=PARAMS,
        cost_estimate=SHORT,
    )(flags, *operands)


def line_plan(acts, grads, basis_in, basis_out, eigval, test_grads, pair_tiles, last_rows):
    plane = lax.axis_index("cand")
    end = (plane == 0) | (plane == 3)
    tok_rows = acts.shape[0]
    cols = basis_in.shape[1]
    tiles_here = tok_rows // TILE
    slim = cols // 4
    depth = basis_out.shape[0] // 3
    rows_in = basis_in.shape[0]

    def pick(at_end, at_middle):
        return jnp.where(end, at_end, at_middle)

    def side(at_end, at_middle):
        return lax.ppermute(pick(at_end, at_middle), "cand", SIDE)

    among, far = [], []
    for at in range(16):
        between = 4 <= at < 12
        across = 12 - 4 * (at // 4) + at % 4
        among.append((at, across if between else at ^ 1))
        far.append((at, at ^ 1 if between else across))

    def middle(x):
        return lax.ppermute(x, ALL, among)

    at_b = jnp.where(end, plane ^ 2, plane ^ 3)
    at_c = jnp.where(end, plane ^ 3, plane ^ 2)
    rep = lax.axis_index("rep")
    flags = jnp.stack([end.astype(jnp.int32), rep, plane, plane ^ 1, at_b, at_c])

    rows = lax.dynamic_slice_in_dim(basis_out, jnp.where(end, 0, depth), 2 * depth, 0)
    s0 = lax.ppermute(basis_in, "cand", SIDE)
    m0 = middle(basis_in)
    s12 = lax.ppermute(rows, "cand", SIDE)
    second = basis_out[depth : 2 * depth]
    m2 = middle(second)
    started = after(flags, rows, second)
    stacked, *more_stacked = stack_blocks(started, grads, depth)
    part_own = feature_dots(
        after(started, s0, m0), grads, [([(basis_out, 0)], 0, 0, 3 * STEPS, False)]
    )
    precond = (test_grads.astype(jnp.float32) / (eigval + damping)).astype(jnp.bfloat16)
    m1 = middle(after(s0, m0))
    third = jnp.concatenate([basis_out[2 * depth :], basis_out[: 2 * rows_in - depth]])
    s3 = side(third, jnp.concatenate([m0, m1]))
    m3 = middle(after(basis_out[2 * depth :], precond, stacked, *more_stacked, *part_own))
    m5 = middle(s12[depth:])
    to_s45 = pick(stacked, jnp.concatenate([m2, m3]))
    s45 = lax.ppermute(after(to_s45, s3), "cand", SIDE)
    m6 = middle(s3[:depth])
    m4 = middle(after(basis_out[:depth], m5))
    s6 = side(more_stacked[0], m5)
    to_s7 = pick(after(more_stacked[1], s45), m6)
    s7 = lax.ppermute(to_s7, "cand", SIDE)
    m7 = middle(after(s12[:depth], m6))

    part_in = input_dots(
        after(flags, s3, m5),
        acts,
        [[(basis_in, 0)], [(s0, 0)], [(s3, 0), (m0, 0)], [(s3, 1), (m1, 0)]],
    )
    part_a = feature_dots(
        after(flags, *part_in),
        grads,
        [
            ([(s12, 0)], STEPS, 0, 2 * STEPS, False),
            ([(s3, 0)], 2 * STEPS, 2 * STEPS, STEPS, True),
        ],
    )
    totals, next_grads, last_grads = both_dots(after(flags, to_s7, s45, *part_a), grads, (s45, 0), ((m2, m5), (m3, m6)))
    parts = [jnp.concatenate(part, axis=1) for part in zip(part_own, part_a)]
    keep_a, give_a = after(parts, s6, m4, totals)
    core_a = swap(give_a, "rep")

    shards = [(basis_out, 0), (m4, 0), (m7, 0)]
    *part_b, part_c = partner_dots(
        after(flags, totals, core_a),
        [(s45, 0), (s45, STEPS), (s6, 0)],
        shards,
        next_grads,
        (s6, 0, depth),
        totals,
    )
    keep_in, give_in = after(part_in, part_c)
    core_in = swap(give_in, "rep")
    rot_in = gather_rows(chip_sum(*chip_parts(keep_in, core_in)).astype(jnp.bfloat16))
    rot_in = rot_in.reshape(tiles_here, TILE, 4 * cols)
    keep_b, give_b = part_b
    keep_b, give_b = chip_parts(
        jnp.concatenate([keep_a, keep_b], axis=1),
        jnp.concatenate([core_a, swap(give_b, "rep")], axis=1),
    )
    sums = chip_sum(keep_b, give_b)
    sum_own, sum_a, sum_b = [sums[:, i * tok_rows : (i + 1) * tok_rows] for i in range(3)]
    sums = sums[:, 3 * tok_rows :].astype(jnp.bfloat16)
    keep_last, give_last = partner_dots(
        after(flags, part_c),
        [(s7, 0)],
        shards,
        last_grads,
        (s7, 0, depth),
        part_c,
    )
    keep_last, give_last = after((keep_last, give_last), give_b)
    sum_last = chip_sum(*chip_parts(keep_last, swap(give_last, "rep")))
    sum_c, sum_last = sum_last[:, :tok_rows], sum_last[:, tok_rows:].astype(jnp.bfloat16)

    rowmask, ignored = tile_layout(pair_tiles, last_rows, plane * tiles_here, tiles_here, TILE)
    keep = rowmask.reshape(1, tok_rows).astype(jnp.bfloat16)

    def tile_prods(rot_out):
        return jnp.einsum(
            "etr,tra->tea",
            (rot_out.astype(jnp.bfloat16) * keep).reshape(slim, tiles_here, TILE),
            rot_in,
            preferred_element_type=jnp.float32,
        ).astype(jnp.bfloat16)

    def pair_scores(*received):
        prods = jnp.concatenate([x for x, source in received])
        scores = jnp.einsum("tea,jea->tj", prods, precond, preferred_element_type=jnp.float32)
        onehot = jnp.concatenate([
            tile_layout(pair_tiles, last_rows, source * tiles_here, tiles_here, TILE)[1]
            for x, source in received
        ])
        return jnp.sum(jnp.where(onehot[:, :, None], scores[:, None, :], 0.0), axis=0)

    prods_own = tile_prods(sum_own)
    prods_middle = tile_prods(sum_b)
    from_middle = middle(prods_middle)
    last = lax.ppermute(after(sum_last, prods_own, prods_middle), "cand", SIDE)
    back = lax.ppermute(sums, "cand", SIDE)
    back = jnp.where(end, back, jnp.zeros_like(back)).reshape(slim, 3, tok_rows - TILE)
    last = jnp.where(end, last, jnp.zeros_like(last)).reshape(slim, 3, TILE)

    def with_partner(whole, at):
        return whole + jnp.concatenate([back[:, at], last[:, at]], axis=1).astype(jnp.float32)

    prods_a = tile_prods(with_partner(sum_a, 0))
    prods_b = tile_prods(with_partner(sum_b, 1))
    prods_c = tile_prods(with_partner(sum_c, 2))
    from_far = lax.ppermute(prods_c, ALL, far)
    from_two = lax.ppermute(pick(prods_b, prods_c), "cand", TWO)
    from_side = lax.ppermute(prods_a, "cand", SIDE)
    total = pair_scores(
        (prods_own, plane),
        (from_side, plane ^ 1),
        (from_two, plane ^ 2),
        (pick(from_far, from_middle), plane ^ 3),
    )
    return final_sum(total)


def final_sum(total):
    npairs, ntest = total.shape
    blocks = total.reshape(4, npairs // 4, 4, ntest // 4).transpose(0, 2, 1, 3)
    blocks = blocks.reshape(16, npairs // 4, ntest // 4)
    return jnp.sum(lax.all_to_all(blocks, ALL, 0, 0, tiled=True), axis=0)


def gather_plan(acts, grads, basis_in, basis_out, eigval, test_grads, pair_tiles, last_rows):
    ncand = lax.axis_size("cand")
    nfeat = lax.axis_size(FEAT)
    tok_rows = acts.shape[0]
    width_in = basis_in.shape[1] * ncand
    width_out = basis_out.shape[1] * ncand
    slim = width_out // (ncand * nfeat)
    part_in = jnp.dot(
        acts,
        lax.all_gather(basis_in, "cand", axis=1, tiled=True),
        preferred_element_type=jnp.float32,
    )
    part_out = jnp.dot(
        grads,
        lax.all_gather(basis_out, "cand", axis=1, tiled=True),
        preferred_element_type=jnp.float32,
    )
    part_out = part_out.reshape(tok_rows, ncand, nfeat, slim).transpose(0, 2, 1, 3)
    part_out = part_out.reshape(tok_rows, nfeat * ncand * slim)
    summed_in, summed_out = lax.psum((part_in, part_out), FEAT)
    own = lax.dynamic_slice_in_dim(
        summed_out, lax.axis_index(FEAT) * (ncand * slim), ncand * slim, 1
    )
    rot_in = summed_in.astype(jnp.bfloat16)
    rot_out = own.astype(jnp.bfloat16)
    tiles_here = tok_rows // TILE
    rowmask, ignored = tile_layout(
        pair_tiles, last_rows, lax.axis_index("cand") * tiles_here, tiles_here, TILE
    )
    masked = rot_out.reshape(tiles_here, TILE, ncand * slim) * rowmask[:, :, None].astype(
        jnp.bfloat16
    )
    prods = jnp.einsum(
        "tre,tra->tea",
        masked,
        rot_in.reshape(tiles_here, TILE, width_in),
        preferred_element_type=jnp.float32,
    ).astype(jnp.bfloat16)
    prods = prods.reshape(tiles_here, ncand, slim, width_in)
    received = lax.all_to_all(prods, "cand", split_axis=1, concat_axis=0, tiled=True)
    all_tiles = received.shape[0]
    received = received.reshape(all_tiles, slim, width_in)
    precond = (test_grads.astype(jnp.float32) / (eigval + damping)).astype(jnp.bfloat16)
    tile_part = jnp.einsum("tea,jea->tj", received, precond, preferred_element_type=jnp.float32)
    ignored_mask, onehot = tile_layout(pair_tiles, last_rows, 0, all_tiles, TILE)
    pair_part = jnp.dot(onehot.astype(jnp.float32).T, tile_part, precision=lax.Precision.HIGHEST)
    npairs = pair_part.shape[0]
    ntest = pair_part.shape[1]
    total = lax.psum(pair_part, ("cand", "eig", "rep"))
    rows = lax.dynamic_slice_in_dim(
        total, lax.axis_index("cand") * (npairs // ncand), npairs // ncand, 0
    )
    return lax.dynamic_slice_in_dim(
        rows, lax.axis_index(FEAT) * (ntest // nfeat), ntest // nfeat, 1
    )


def solution(mesh):
    in_specs = (
        P(("groups", "cand"), ("eig", "rep")),
        P(("groups", "cand"), ("eig", "rep")),
        P(("groups", "eig", "rep"), "cand"),
        P(("groups", "eig", "rep"), "cand"),
        P(("groups", "cand", "eig", "rep"), None),
        P("groups", ("cand", "eig", "rep"), None),
        P("groups"),
        P("groups"),
    )
    out_specs = P(("groups", "cand"), ("eig", "rep"))
    sizes = (mesh.shape["cand"], mesh.shape["eig"], mesh.shape["rep"])
    per_device = line_plan if sizes == (4, 2, 2) else gather_plan
    return jax.shard_map(
        per_device, mesh=mesh, in_specs=in_specs, out_specs=out_specs, check_vma=False
    )
```

```python
import jax
import jax.numpy as jnp
from jax import lax
from jax.experimental import pallas as pl
from jax.experimental.pallas import tpu as pltpu
from jax.sharding import PartitionSpec as P

TILE = 128
FEAT = ("eig", "rep")
ALL = ("cand", "eig", "rep")
STEPS = 3
PARAMS = pltpu.CompilerParams(vmem_limit_bytes=20 << 20)
SHORT = pl.CostEstimate(flops=1, bytes_accessed=1, transcendentals=0)
SIDE = ((0, 1), (1, 0), (2, 3), (3, 2))
TWO = ((0, 2), (2, 0), (1, 3), (3, 1))

damping = 0.01


def tile_layout(pair_tiles, last_rows, first_tile, count, tile_rows):
    tiles = first_tile + jnp.arange(count, dtype=jnp.int32)
    ends = jnp.cumsum(pair_tiles)
    owner = jnp.sum((ends[None, :] <= tiles[:, None]).astype(jnp.int32), axis=1)
    onehot = owner[:, None] == jnp.arange(pair_tiles.shape[0], dtype=jnp.int32)[None, :]
    last_of = jnp.sum(jnp.where(onehot, last_rows[None, :], 0), axis=1)
    end_of = jnp.sum(jnp.where(onehot, ends[None, :], 0), axis=1)
    limit = jnp.where(tiles == end_of - 1, last_of, tile_rows)
    rowmask = jnp.arange(tile_rows, dtype=jnp.int32)[None, :] < limit[:, None]
    return (rowmask, onehot)


def after(x, *earlier):
    return lax.optimization_barrier((x, *earlier))[0]


def swap(x, axis_name):
    return lax.ppermute(x, axis_name, [(0, 1), (1, 0)])


def halves(x, axis_name):
    first = lax.axis_index(axis_name) == 0
    low, high = jnp.split(x, 2)
    return jnp.where(first, low, high), jnp.where(first, high, low)


def chip_parts(keep, received):
    keep, their_keep = halves(keep, "eig")
    received, their_received = halves(received, "eig")
    return keep + received, (their_keep + their_received).astype(jnp.bfloat16)


def chip_sum(keep, give):
    return keep + swap(give, "eig").astype(jnp.float32)


def gather_rows(x):
    other = swap(x, "eig")
    first = lax.axis_index("eig") == 0
    both = jnp.stack([jnp.where(first, x, other), jnp.where(first, other, x)])
    other = swap(both, "rep")
    first = lax.axis_index("rep") == 0
    whole = jnp.stack([jnp.where(first, both, other), jnp.where(first, other, both)], axis=1)
    return whole.reshape((-1,) + x.shape[1:])


def split_rows(full_ref, keep_ref, give_ref, rep, columns=None):
    rows = full_ref.shape[0] // 4
    columns = slice(None) if columns is None else columns
    for e in range(2):
        here = pl.ds(e * rows, rows)
        mine = pl.ds(pl.multiple_of((2 * e + rep) * rows, rows), rows)
        theirs = pl.ds(pl.multiple_of((2 * e + 1 - rep) * rows, rows), rows)
        keep_ref[here, columns] = full_ref[mine, :]
        give_ref[here, columns] = full_ref[theirs, :]


def add_dot(total_ref, rows_ref, shard):
    half = total_ref.shape[0] // 2
    for here in (pl.ds(0, half), pl.ds(half, half)):
        total_ref[here, :] += jnp.dot(
            rows_ref[here, :], shard, preferred_element_type=jnp.float32
        )


def feature_dots(flags, grads, segments, start=None, split=True):
    tok = grads.shape[0]
    cols = segments[0][0][0][0].shape[1]
    depth = grads.shape[1] // (3 * STEPS)
    firsts = [sum(s[3] for s in segments[:at]) for at in range(len(segments))]
    total = sum(s[3] for s in segments)

    def grads_at(i, flags_ref):
        at = 0
        for first, (choices, at_end, at_middle, steps, only) in zip(firsts, segments):
            base = at_end + flags_ref[0] * 0 if at_end == at_middle else (
                flags_ref[0] * at_end + (1 - flags_ref[0]) * at_middle
            )
            at = jnp.where(i >= first, base + i - first, at)
        return (0, at)

    def rows_at(first, steps, row, wanted):
        def index(i, flags_ref):
            step = jnp.clip(i - first, 0, steps - 1)
            if wanted is not None:
                step = step * (flags_ref[0] if wanted else 1 - flags_ref[0])
            return (row + step, 0)

        return index

    operands, specs = [grads], [pl.BlockSpec((tok, depth), grads_at)]
    for first, (choices, at_end, at_middle, steps, only) in zip(firsts, segments):
        for which, (array, row) in enumerate(choices):
            wanted = None if len(choices) == 1 else which == 0
            operands.append(array)
            specs.append(pl.BlockSpec((depth, cols), rows_at(first, steps, row, wanted)))
    if start is not None:
        operands.append(start)
        specs.append(pl.BlockSpec((tok, cols), lambda i, flags_ref: (0, 0)))

    def kernel(flags_ref, grads_ref, *refs):
        i = pl.program_id(0)
        end = flags_ref[0] == 1
        inputs, rest = list(refs[: len(operands) - 1]), refs[len(operands) - 1 :]
        if split:
            keep_ref, give_ref, total_ref, turned_ref = rest
        else:
            (total_ref,) = rest

        @pl.when(i == 0)
        def begin():
            total_ref[...] = jnp.zeros_like(total_ref) if start is None else inputs[-1][...]

        at = 0
        for first, (choices, at_end, at_middle, steps, only) in zip(firsts, segments):
            here = inputs[at : at + len(choices)]
            at += len(choices)
            active = (i >= first) & (i < first + steps)
            if only:
                active = active & (flags_ref[0] == 0)

            @pl.when(active)
            def add(here=here):
                shard = here[0][...]
                if len(here) == 2:
                    shard = jnp.where(end, shard, here[1][...])
                add_dot(total_ref, grads_ref, shard)

        if split:

            @pl.when(i == total - 1)
            def finish():
                turned_ref[...] = total_ref[...].T
                split_rows(turned_ref, keep_ref, give_ref, flags_ref[1])

    whole = lambda i, flags_ref: (0, 0)
    if split:
        out_shape = [jax.ShapeDtypeStruct((cols // 2, tok), jnp.float32)] * 2
        out_specs = [pl.BlockSpec((cols // 2, tok), whole)] * 2
        scratch = [pltpu.VMEM((tok, cols), jnp.float32), pltpu.VMEM((cols, tok), jnp.float32)]
    else:
        out_shape = jax.ShapeDtypeStruct((tok, cols), jnp.float32)
        out_specs = pl.BlockSpec((tok, cols), whole)
        scratch = []
    return pl.pallas_call(
        kernel,
        out_shape=out_shape,
        grid_spec=pltpu.PrefetchScalarGridSpec(
            num_scalar_prefetch=1,
            grid=(total,),
            in_specs=specs,
            out_specs=out_specs,
            scratch_shapes=scratch,
        ),
        compiler_params=PARAMS,
        cost_estimate=SHORT,
    )(flags, *operands)


def both_dots(flags, grads, at_end, at_middle):
    tok = grads.shape[0]
    cols = at_end[0].shape[1]
    step = grads.shape[1] // (3 * STEPS)

    def third_at(first):
        def index(i, flags_ref):
            return (jnp.clip(i - first, 0, STEPS - 1) * (1 - flags_ref[0]), 0)

        return index

    operands = [grads, at_end[0]] + [array for pair in at_middle for array in pair] + [grads]
    specs = [
        pl.BlockSpec((tok, step), lambda i, flags_ref: (0, STEPS + i)),
        pl.BlockSpec((step, cols), lambda i, flags_ref: (at_end[1] + i * flags_ref[0], 0)),
    ]
    for first in (0, STEPS):
        specs += [pl.BlockSpec((step, cols), third_at(first))] * 2
    specs.append(
        pl.BlockSpec(
            (tok, step),
            lambda i, flags_ref: (0, flags_ref[0] * STEPS + jnp.minimum(i, STEPS - 1)),
        )
    )

    def kernel(flags_ref, grads_ref, end_ref, b1_ref, c1_ref, b2_ref, c2_ref, next_ref, *out_refs):
        total_ref, handed_ref, last_ref = out_refs
        i = pl.program_id(0)

        @pl.when(i == 0)
        def begin():
            total_ref[...] = jnp.zeros_like(total_ref)

        @pl.when(i < STEPS)
        def hand_on_next():
            handed_ref[...] = next_ref[...]

        @pl.when(i >= STEPS)
        def hand_on_last():
            last_ref[...] = grads_ref[...]

        @pl.when(flags_ref[0] == 1)
        def one():
            total_ref[:, :cols] += jnp.dot(
                grads_ref[...], end_ref[...], preferred_element_type=jnp.float32
            )

        for first, b_ref, c_ref in ((0, b1_ref, c1_ref), (STEPS, b2_ref, c2_ref)):

            @pl.when((flags_ref[0] == 0) & (i >= first) & (i < first + STEPS))
            def two(b_ref=b_ref, c_ref=c_ref):
                shards = jnp.concatenate([b_ref[...], c_ref[...]], axis=1)
                total_ref[...] += jnp.dot(
                    grads_ref[...], shards, preferred_element_type=jnp.float32
                )

    third = jax.ShapeDtypeStruct((tok, STEPS * step), grads.dtype)
    return pl.pallas_call(
        kernel,
        out_shape=[jax.ShapeDtypeStruct((tok, 2 * cols), jnp.float32), third, third],
        grid_spec=pltpu.PrefetchScalarGridSpec(
            num_scalar_prefetch=1,
            grid=(2 * STEPS,),
            in_specs=specs,
            out_specs=[
                pl.BlockSpec((tok, 2 * cols), lambda i, flags_ref: (0, 0)),
                pl.BlockSpec((tok, step), lambda i, flags_ref: (0, jnp.minimum(i, STEPS - 1))),
                pl.BlockSpec((tok, step), lambda i, flags_ref: (0, jnp.maximum(i - STEPS, 0))),
            ],
        ),
        compiler_params=PARAMS,
        cost_estimate=SHORT,
    )(flags, *operands)


def partner_dots(flags, pieces, shards, grads, shard, start):
    tok = grads.shape[0]
    cols = shards[0][0].shape[1]
    step = shard[2] // STEPS
    count = len(pieces)
    two = start.shape[1] == 2 * cols
    width = tok + len(shards) * count * TILE

    def at(row):
        return lambda i, flags_ref: (row + i, 0)

    whole = lambda i, flags_ref: (0, 0)
    operands, specs = [], []
    for array, row in list(pieces) + list(shards) + [shard[:2]]:
        operands.append(array)
        specs.append(pl.BlockSpec((step, cols), at(row)))
    operands += [grads, start]
    specs.append(pl.BlockSpec((tok, step), lambda i, flags_ref: (0, i)))
    specs.append(pl.BlockSpec(start.shape, whole))

    def kernel(flags_ref, *refs):
        i = pl.program_id(0)
        piece_refs, shard_refs = refs[:count], refs[count : count + len(shards)]
        end_ref, grads_ref, start_ref = refs[count + len(shards) : count + len(shards) + 3]
        keep_ref, give_ref, *rest = refs[len(operands) :]
        if two:
            second_ref, total_ref, sums_ref, turned_ref, wide_ref = rest
        else:
            total_ref, sums_ref, turned_ref, wide_ref = rest

        @pl.when(i == 0)
        def begin():
            total_ref[...] = start_ref[...]
            sums_ref[...] = jnp.zeros_like(sums_ref)

        @pl.when(flags_ref[0] == 1)
        def at_an_end_plane():
            total_ref[:, total_ref.shape[1] - cols :] += jnp.dot(
                grads_ref[...], end_ref[...], preferred_element_type=jnp.float32
            )

        @pl.when(flags_ref[0] == 0)
        def at_a_middle_plane():
            side_by_side = jnp.concatenate([ref[...] for ref in shard_refs], axis=1)
            tokens = jnp.concatenate(
                [
                    jnp.concatenate(
                        [ref[q * TILE : (q + 1) * TILE, :] for q in range(step // TILE)], axis=1
                    )
                    for ref in piece_refs
                ]
            )
            sums_ref[...] += jnp.dot(tokens, side_by_side, preferred_element_type=jnp.float32)
            if two:
                total_ref[...] += jnp.dot(
                    grads_ref[...], side_by_side[:, cols:], preferred_element_type=jnp.float32
                )

        @pl.when(i == STEPS - 1)
        def finish():
            wide_ref[...] = total_ref[:, :cols].T
            split_rows(wide_ref, keep_ref, give_ref, flags_ref[1], pl.ds(0, tok))
            for j in range(len(shards)):
                turned_ref[...] = sums_ref[:, j * cols : (j + 1) * cols].T
                columns = pl.ds(tok + j * count * TILE, count * TILE)
                split_rows(turned_ref, keep_ref, give_ref, flags_ref[1], columns)
            if two:
                second_ref[...] = total_ref[:, cols:]

    out_shape = [jax.ShapeDtypeStruct((cols // 2, width), jnp.float32)] * 2
    out_specs = [pl.BlockSpec((cols // 2, width), whole)] * 2
    if two:
        out_shape.append(jax.ShapeDtypeStruct((tok, cols), jnp.float32))
        out_specs.append(pl.BlockSpec((tok, cols), whole))
    return pl.pallas_call(
        kernel,
        out_shape=out_shape,
        grid_spec=pltpu.PrefetchScalarGridSpec(
            num_scalar_prefetch=1,
            grid=(STEPS,),
            in_specs=specs,
            out_specs=out_specs,
            scratch_shapes=[
                pltpu.VMEM(start.shape, jnp.float32),
                pltpu.VMEM((count * TILE, len(shards) * cols), jnp.float32),
                pltpu.VMEM((cols, count * TILE), jnp.float32),
                pltpu.VMEM((cols, tok), jnp.float32),
            ],
        ),
        compiler_params=PARAMS,
        cost_estimate=SHORT,
    )(flags, *operands)


def stack_blocks(flags, grads, depth):
    tiles = grads.shape[0] // TILE
    firsts = [0] + list(range(tiles // 2, tiles))
    counts = [tiles // 2] + [1] * (tiles // 2)

    def kernel(flags_ref, grads_ref, *out_refs):
        t = pl.program_id(0)
        for first, count, out_ref in zip(firsts, counts, out_refs):

            @pl.when((t >= first) & (t < first + count))
            def copy(out_ref=out_ref):
                for q in range(depth // TILE):
                    here = slice(q * TILE, (q + 1) * TILE)
                    out_ref[here, :] = grads_ref[:, here]

    def place(first, count):
        return lambda t, flags_ref: (jnp.clip(t - first, 0, count - 1), 0)

    return pl.pallas_call(
        kernel,
        out_shape=[jax.ShapeDtypeStruct((count * depth, TILE), grads.dtype) for count in counts],
        grid_spec=pltpu.PrefetchScalarGridSpec(
            num_scalar_prefetch=1,
            grid=(tiles,),
            in_specs=[pl.BlockSpec((TILE, depth), lambda t, flags_ref: (t, 0))],
            out_specs=[
                pl.BlockSpec((depth, TILE), place(first, count))
                for first, count in zip(firsts, counts)
            ],
        ),
        compiler_params=PARAMS,
        cost_estimate=SHORT,
    )(flags, grads)


def input_dots(flags, acts, shards):
    tok, depth = acts.shape
    cols = shards[0][0][0].shape[1]
    operands, specs = [acts], [pl.BlockSpec((tok, depth), lambda i, flags_ref: (0, 0))]
    for choices in shards:
        for array, row in choices:
            operands.append(array)
            specs.append(pl.BlockSpec((depth, cols), lambda i, flags_ref, row=row: (row, 0)))

    def kernel(flags_ref, acts_ref, *refs):
        i = pl.program_id(0)
        inputs = list(refs[: len(operands) - 1])
        keep_ref, give_ref, part_ref = refs[len(operands) - 1 :]
        at = 0
        for slot, choices in enumerate(shards):
            here = inputs[at : at + len(choices)]
            at += len(choices)

            @pl.when(i == slot)
            def add(here=here):
                shard = here[0][...]
                if len(here) == 2:
                    shard = jnp.where(flags_ref[0] == 1, shard, here[1][...])
                part_ref[...] = jnp.dot(acts_ref[...], shard, preferred_element_type=jnp.float32)

        split_rows(part_ref, keep_ref, give_ref, flags_ref[1])

    place = pl.BlockSpec((tok // 2, cols), lambda i, flags_ref: (0, flags_ref[2 + i]))
    return pl.pallas_call(
        kernel,
        out_shape=[jax.ShapeDtypeStruct((tok // 2, cols * len(shards)), jnp.float32)] * 2,
        grid_spec=pltpu.PrefetchScalarGridSpec(
            num_scalar_prefetch=1,
            grid=(len(shards),),
            in_specs=specs,
            out_specs=[place, place],
            scratch_shapes=[pltpu.VMEM((tok, cols), jnp.float32)],
        ),
        compiler_params=PARAMS,
        cost_estimate=SHORT,
    )(flags, *operands)


def line_plan(acts, grads, basis_in, basis_out, eigval, test_grads, pair_tiles, last_rows):
    plane = lax.axis_index("cand")
    end = (plane == 0) | (plane == 3)
    tok_rows = acts.shape[0]
    cols = basis_in.shape[1]
    tiles_here = tok_rows // TILE
    slim = cols // 4
    depth = basis_out.shape[0] // 3
    rows_in = basis_in.shape[0]

    def pick(at_end, at_middle):
        return jnp.where(end, at_end, at_middle)

    def side(at_end, at_middle):
        return lax.ppermute(pick(at_end, at_middle), "cand", SIDE)

    among, far = [], []
    for at in range(16):
        between = 4 <= at < 12
        across = 12 - 4 * (at // 4) + at % 4
        among.append((at, across if between else at ^ 1))
        far.append((at, at ^ 1 if between else across))

    def middle(x):
        return lax.ppermute(x, ALL, among)

    at_b = jnp.where(end, plane ^ 2, plane ^ 3)
    at_c = jnp.where(end, plane ^ 3, plane ^ 2)
    rep = lax.axis_index("rep")
    flags = jnp.stack([end.astype(jnp.int32), rep, plane, plane ^ 1, at_b, at_c])

    rows = lax.dynamic_slice_in_dim(basis_out, jnp.where(end, 0, depth), 2 * depth, 0)
    s0 = lax.ppermute(basis_in, "cand", SIDE)
    m0 = middle(basis_in)
    s12 = lax.ppermute(rows, "cand", SIDE)
    second = basis_out[depth : 2 * depth]
    m2 = middle(second)
    started = after(flags, rows, second)
    stacked, *more_stacked = stack_blocks(started, grads, depth)
    part_own = feature_dots(
        after(started, s0, m0), grads, [([(basis_out, 0)], 0, 0, 3 * STEPS, False)]
    )
    precond = (test_grads.astype(jnp.float32) / (eigval + damping)).astype(jnp.bfloat16)
    m1 = middle(after(s0, m0))
    third = jnp.concatenate([basis_out[2 * depth :], basis_out[: 2 * rows_in - depth]])
    s3 = side(third, jnp.concatenate([m0, m1]))
    m3 = middle(after(basis_out[2 * depth :], precond, stacked, *more_stacked, *part_own))
    m5 = middle(s12[depth:])
    to_s45 = pick(stacked, jnp.concatenate([m2, m3]))
    s45 = lax.ppermute(after(to_s45, s3), "cand", SIDE)
    m6 = middle(s3[:depth])
    m4 = middle(after(basis_out[:depth], m5))
    s6 = side(more_stacked[0], m5)
    to_s7 = pick(after(more_stacked[1], s45), m6)
    s7 = lax.ppermute(to_s7, "cand", SIDE)
    m7 = middle(after(s12[:depth], m6))

    part_in = input_dots(
        after(flags, s3, m5),
        acts,
        [[(basis_in, 0)], [(s0, 0)], [(s3, 0), (m0, 0)], [(s3, 1), (m1, 0)]],
    )
    part_a = feature_dots(
        after(flags, *part_in),
        grads,
        [
            ([(s12, 0)], STEPS, 0, 2 * STEPS, False),
            ([(s3, 0)], 2 * STEPS, 2 * STEPS, STEPS, True),
        ],
    )
    totals, next_grads, last_grads = both_dots(after(flags, to_s7, s45, *part_a), grads, (s45, 0), ((m2, m5), (m3, m6)))
    parts = [jnp.concatenate(part, axis=1) for part in zip(part_own, part_a)]
    keep_a, give_a = after(parts, s6, m4, totals)
    core_a = swap(give_a, "rep")

    shards = [(basis_out, 0), (m4, 0), (m7, 0)]
    *part_b, part_c = partner_dots(
        after(flags, totals, core_a),
        [(s45, 0), (s45, STEPS), (s6, 0)],
        shards,
        next_grads,
        (s6, 0, depth),
        totals,
    )
    keep_in, give_in = after(part_in, part_c)
    core_in = swap(give_in, "rep")
    keep_in, give_in = chip_parts(keep_in, core_in)
    rot_in = gather_rows(chip_sum(keep_in, give_in).astype(jnp.bfloat16))
    rot_in = rot_in.reshape(tiles_here, TILE, 4 * cols)
    keep_b, give_b = part_b
    keep_b, give_b = chip_parts(
        jnp.concatenate([keep_a, keep_b], axis=1),
        jnp.concatenate([core_a, swap(give_b, "rep")], axis=1),
    )
    sums = chip_sum(keep_b, give_b)
    sum_own, sum_a, sum_b = [sums[:, i * tok_rows : (i + 1) * tok_rows] for i in range(3)]
    sums = sums[:, 3 * tok_rows :].astype(jnp.bfloat16)
    keep_last, give_last = partner_dots(
        after(flags, part_c, give_b, give_in),
        [(s7, 0)],
        shards,
        last_grads,
        (s7, 0, depth),
        part_c,
    )
    sum_last = chip_sum(*chip_parts(keep_last, swap(give_last, "rep")))
    sum_c, sum_last = sum_last[:, :tok_rows], sum_last[:, tok_rows:].astype(jnp.bfloat16)

    rowmask, ignored = tile_layout(pair_tiles, last_rows, plane * tiles_here, tiles_here, TILE)
    keep = rowmask.reshape(1, tok_rows).astype(jnp.bfloat16)

    def tile_prods(rot_out):
        return jnp.einsum(
            "etr,tra->tea",
            (rot_out.astype(jnp.bfloat16) * keep).reshape(slim, tiles_here, TILE),
            rot_in,
            preferred_element_type=jnp.float32,
        ).astype(jnp.bfloat16)

    def pair_scores(*received):
        prods = jnp.concatenate([x for x, source in received])
        scores = jnp.einsum("tea,jea->tj", prods, precond, preferred_element_type=jnp.float32)
        onehot = jnp.concatenate([
            tile_layout(pair_tiles, last_rows, source * tiles_here, tiles_here, TILE)[1]
            for x, source in received
        ])
        return jnp.sum(jnp.where(onehot[:, :, None], scores[:, None, :], 0.0), axis=0)

    prods_own = tile_prods(sum_own)
    prods_middle = tile_prods(sum_b)
    from_middle = middle(prods_middle)
    last = lax.ppermute(after(sum_last, prods_own, prods_middle), "cand", SIDE)
    back = lax.ppermute(sums, "cand", SIDE)
    back = jnp.where(end, back, jnp.zeros_like(back)).reshape(slim, 3, tok_rows - TILE)
    last = jnp.where(end, last, jnp.zeros_like(last)).reshape(slim, 3, TILE)

    def with_partner(whole, at):
        return whole + jnp.concatenate([back[:, at], last[:, at]], axis=1).astype(jnp.float32)

    prods_a = tile_prods(with_partner(sum_a, 0))
    prods_b = tile_prods(with_partner(sum_b, 1))
    prods_c = tile_prods(with_partner(sum_c, 2))
    from_far = lax.ppermute(prods_c, ALL, far)
    from_two = lax.ppermute(pick(prods_b, prods_c), "cand", TWO)
    from_side = lax.ppermute(prods_a, "cand", SIDE)
    total = pair_scores(
        (prods_own, plane),
        (from_side, plane ^ 1),
        (from_two, plane ^ 2),
        (pick(from_far, from_middle), plane ^ 3),
    )
    return final_sum(total)


def final_sum(total):
    npairs, ntest = total.shape
    keep, give = halves(total.reshape(npairs, 2, 2, ntest // 4).transpose(2, 0, 1, 3), "rep")
    blocks = (keep + swap(give, "rep")).reshape(4, npairs // 4, 2, ntest // 4).transpose(0, 2, 1, 3)
    blocks = blocks.reshape(8, npairs // 4, ntest // 4)
    return jnp.sum(lax.all_to_all(blocks, ("cand", "eig"), 0, 0, tiled=True), axis=0)


def gather_plan(acts, grads, basis_in, basis_out, eigval, test_grads, pair_tiles, last_rows):
    ncand = lax.axis_size("cand")
    nfeat = lax.axis_size(FEAT)
    tok_rows = acts.shape[0]
    width_in = basis_in.shape[1] * ncand
    width_out = basis_out.shape[1] * ncand
    slim = width_out // (ncand * nfeat)
    part_in = jnp.dot(
        acts,
        lax.all_gather(basis_in, "cand", axis=1, tiled=True),
        preferred_element_type=jnp.float32,
    )
    part_out = jnp.dot(
        grads,
        lax.all_gather(basis_out, "cand", axis=1, tiled=True),
        preferred_element_type=jnp.float32,
    )
    part_out = part_out.reshape(tok_rows, ncand, nfeat, slim).transpose(0, 2, 1, 3)
    part_out = part_out.reshape(tok_rows, nfeat * ncand * slim)
    summed_in, summed_out = lax.psum((part_in, part_out), FEAT)
    own = lax.dynamic_slice_in_dim(
        summed_out, lax.axis_index(FEAT) * (ncand * slim), ncand * slim, 1
    )
    rot_in = summed_in.astype(jnp.bfloat16)
    rot_out = own.astype(jnp.bfloat16)
    tiles_here = tok_rows // TILE
    rowmask, ignored = tile_layout(
        pair_tiles, last_rows, lax.axis_index("cand") * tiles_here, tiles_here, TILE
    )
    masked = rot_out.reshape(tiles_here, TILE, ncand * slim) * rowmask[:, :, None].astype(
        jnp.bfloat16
    )
    prods = jnp.einsum(
        "tre,tra->tea",
        masked,
        rot_in.reshape(tiles_here, TILE, width_in),
        preferred_element_type=jnp.float32,
    ).astype(jnp.bfloat16)
    prods = prods.reshape(tiles_here, ncand, slim, width_in)
    received = lax.all_to_all(prods, "cand", split_axis=1, concat_axis=0, tiled=True)
    all_tiles = received.shape[0]
    received = received.reshape(all_tiles, slim, width_in)
    precond = (test_grads.astype(jnp.float32) / (eigval + damping)).astype(jnp.bfloat16)
    tile_part = jnp.einsum("tea,jea->tj", received, precond, preferred_element_type=jnp.float32)
    ignored_mask, onehot = tile_layout(pair_tiles, last_rows, 0, all_tiles, TILE)
    pair_part = jnp.dot(onehot.astype(jnp.float32).T, tile_part, precision=lax.Precision.HIGHEST)
    npairs = pair_part.shape[0]
    ntest = pair_part.shape[1]
    total = lax.psum(pair_part, ("cand", "eig", "rep"))
    rows = lax.dynamic_slice_in_dim(
        total, lax.axis_index("cand") * (npairs // ncand), npairs // ncand, 0
    )
    return lax.dynamic_slice_in_dim(
        rows, lax.axis_index(FEAT) * (ntest // nfeat), ntest // nfeat, 1
    )


def solution(mesh):
    in_specs = (
        P(("groups", "cand"), ("eig", "rep")),
        P(("groups", "cand"), ("eig", "rep")),
        P(("groups", "eig", "rep"), "cand"),
        P(("groups", "eig", "rep"), "cand"),
        P(("groups", "cand", "eig", "rep"), None),
        P("groups", ("cand", "eig", "rep"), None),
        P("groups"),
        P("groups"),
    )
    out_specs = P(("groups", "cand"), ("eig", "rep"))
    sizes = (mesh.shape["cand"], mesh.shape["eig"], mesh.shape["rep"])
    per_device = line_plan if sizes == (4, 2, 2) else gather_plan
    return jax.shard_map(
        per_device, mesh=mesh, in_specs=in_specs, out_specs=out_specs, check_vma=False
    )
```

```python
import jax
import jax.numpy as jnp
from jax import lax
from jax.experimental import pallas as pl
from jax.experimental.pallas import tpu as pltpu
from jax.sharding import PartitionSpec as P

TILE = 128
FEAT = ("eig", "rep")
ALL = ("cand", "eig", "rep")
STEPS = 3
PARAMS = pltpu.CompilerParams(vmem_limit_bytes=20 << 20)
SHORT = pl.CostEstimate(flops=1, bytes_accessed=1, transcendentals=0)
SIDE = ((0, 1), (1, 0), (2, 3), (3, 2))
TWO = ((0, 2), (2, 0), (1, 3), (3, 1))

damping = 0.01


def tile_layout(pair_tiles, last_rows, first_tile, count, tile_rows):
    tiles = first_tile + jnp.arange(count, dtype=jnp.int32)
    ends = jnp.cumsum(pair_tiles)
    owner = jnp.sum((ends[None, :] <= tiles[:, None]).astype(jnp.int32), axis=1)
    onehot = owner[:, None] == jnp.arange(pair_tiles.shape[0], dtype=jnp.int32)[None, :]
    last_of = jnp.sum(jnp.where(onehot, last_rows[None, :], 0), axis=1)
    end_of = jnp.sum(jnp.where(onehot, ends[None, :], 0), axis=1)
    limit = jnp.where(tiles == end_of - 1, last_of, tile_rows)
    rowmask = jnp.arange(tile_rows, dtype=jnp.int32)[None, :] < limit[:, None]
    return (rowmask, onehot)


def after(x, *earlier):
    return lax.optimization_barrier((x, *earlier))[0]


def swap(x, axis_name):
    return lax.ppermute(x, axis_name, [(0, 1), (1, 0)])


def halves(x, axis_name):
    first = lax.axis_index(axis_name) == 0
    low, high = jnp.split(x, 2)
    return jnp.where(first, low, high), jnp.where(first, high, low)


def chip_parts(keep, received):
    keep, their_keep = halves(keep, "eig")
    received, their_received = halves(received, "eig")
    return keep + received, (their_keep + their_received).astype(jnp.bfloat16)


def chip_sum(keep, give):
    return keep + swap(give, "eig").astype(jnp.float32)


def all_rows(core_sum, give):
    mine = (core_sum + swap(give, "eig").astype(jnp.float32)).astype(jnp.bfloat16)
    other = swap(mine, "rep")
    first = lax.axis_index("rep") == 0
    mine, other = mine.reshape(2, -1, mine.shape[1]), other.reshape(2, -1, mine.shape[1])
    whole = jnp.stack([jnp.where(first, mine, other), jnp.where(first, other, mine)], axis=1)
    return whole.reshape(-1, whole.shape[-1])


def split_rows(full_ref, keep_ref, give_ref, rep, columns=None):
    rows = full_ref.shape[0] // 4
    columns = slice(None) if columns is None else columns
    for e in range(2):
        here = pl.ds(e * rows, rows)
        mine = pl.ds(pl.multiple_of((2 * e + rep) * rows, rows), rows)
        theirs = pl.ds(pl.multiple_of((2 * e + 1 - rep) * rows, rows), rows)
        keep_ref[here, columns] = full_ref[mine, :]
        give_ref[here, columns] = full_ref[theirs, :]


def add_dot(total_ref, rows_ref, shard):
    half = total_ref.shape[0] // 2
    for here in (pl.ds(0, half), pl.ds(half, half)):
        total_ref[here, :] += jnp.dot(
            rows_ref[here, :], shard, preferred_element_type=jnp.float32
        )


def feature_dots(flags, grads, segments, start=None, split=True):
    tok = grads.shape[0]
    cols = segments[0][0][0][0].shape[1]
    depth = grads.shape[1] // (3 * STEPS)
    firsts = [sum(s[3] for s in segments[:at]) for at in range(len(segments))]
    total = sum(s[3] for s in segments)

    def grads_at(i, flags_ref):
        at = 0
        for first, (choices, at_end, at_middle, steps, only) in zip(firsts, segments):
            base = at_end + flags_ref[0] * 0 if at_end == at_middle else (
                flags_ref[0] * at_end + (1 - flags_ref[0]) * at_middle
            )
            at = jnp.where(i >= first, base + i - first, at)
        return (0, at)

    def rows_at(first, steps, row, wanted):
        def index(i, flags_ref):
            step = jnp.clip(i - first, 0, steps - 1)
            if wanted is not None:
                step = step * (flags_ref[0] if wanted else 1 - flags_ref[0])
            return (row + step, 0)

        return index

    operands, specs = [grads], [pl.BlockSpec((tok, depth), grads_at)]
    for first, (choices, at_end, at_middle, steps, only) in zip(firsts, segments):
        for which, (array, row) in enumerate(choices):
            wanted = None if len(choices) == 1 else which == 0
            operands.append(array)
            specs.append(pl.BlockSpec((depth, cols), rows_at(first, steps, row, wanted)))
    if start is not None:
        operands.append(start)
        specs.append(pl.BlockSpec((tok, cols), lambda i, flags_ref: (0, 0)))

    def kernel(flags_ref, grads_ref, *refs):
        i = pl.program_id(0)
        end = flags_ref[0] == 1
        inputs, rest = list(refs[: len(operands) - 1]), refs[len(operands) - 1 :]
        if split:
            keep_ref, give_ref, total_ref, turned_ref = rest
        else:
            (total_ref,) = rest

        @pl.when(i == 0)
        def begin():
            total_ref[...] = jnp.zeros_like(total_ref) if start is None else inputs[-1][...]

        at = 0
        for first, (choices, at_end, at_middle, steps, only) in zip(firsts, segments):
            here = inputs[at : at + len(choices)]
            at += len(choices)
            active = (i >= first) & (i < first + steps)
            if only:
                active = active & (flags_ref[0] == 0)

            @pl.when(active)
            def add(here=here):
                shard = here[0][...]
                if len(here) == 2:
                    shard = jnp.where(end, shard, here[1][...])
                add_dot(total_ref, grads_ref, shard)

        if split:

            @pl.when(i == total - 1)
            def finish():
                turned_ref[...] = total_ref[...].T
                split_rows(turned_ref, keep_ref, give_ref, flags_ref[1])

    whole = lambda i, flags_ref: (0, 0)
    if split:
        out_shape = [jax.ShapeDtypeStruct((cols // 2, tok), jnp.float32)] * 2
        out_specs = [pl.BlockSpec((cols // 2, tok), whole)] * 2
        scratch = [pltpu.VMEM((tok, cols), jnp.float32), pltpu.VMEM((cols, tok), jnp.float32)]
    else:
        out_shape = jax.ShapeDtypeStruct((tok, cols), jnp.float32)
        out_specs = pl.BlockSpec((tok, cols), whole)
        scratch = []
    return pl.pallas_call(
        kernel,
        out_shape=out_shape,
        grid_spec=pltpu.PrefetchScalarGridSpec(
            num_scalar_prefetch=1,
            grid=(total,),
            in_specs=specs,
            out_specs=out_specs,
            scratch_shapes=scratch,
        ),
        compiler_params=PARAMS,
        cost_estimate=SHORT,
    )(flags, *operands)


def both_dots(flags, grads, at_end, at_middle):
    tok = grads.shape[0]
    cols = at_end[0].shape[1]
    step = grads.shape[1] // (3 * STEPS)

    def third_at(first):
        def index(i, flags_ref):
            return (jnp.clip(i - first, 0, STEPS - 1) * (1 - flags_ref[0]), 0)

        return index

    operands = [grads, at_end[0]] + [array for pair in at_middle for array in pair] + [grads]
    specs = [
        pl.BlockSpec((tok, step), lambda i, flags_ref: (0, STEPS + i)),
        pl.BlockSpec((step, cols), lambda i, flags_ref: (at_end[1] + i * flags_ref[0], 0)),
    ]
    for first in (0, STEPS):
        specs += [pl.BlockSpec((step, cols), third_at(first))] * 2
    specs.append(
        pl.BlockSpec(
            (tok, step),
            lambda i, flags_ref: (0, flags_ref[0] * STEPS + jnp.minimum(i, STEPS - 1)),
        )
    )

    def kernel(flags_ref, grads_ref, end_ref, b1_ref, c1_ref, b2_ref, c2_ref, next_ref, *out_refs):
        total_ref, handed_ref, last_ref = out_refs
        i = pl.program_id(0)

        @pl.when(i == 0)
        def begin():
            total_ref[...] = jnp.zeros_like(total_ref)

        @pl.when(i < STEPS)
        def hand_on_next():
            handed_ref[...] = next_ref[...]

        @pl.when(i >= STEPS)
        def hand_on_last():
            last_ref[...] = grads_ref[...]

        @pl.when(flags_ref[0] == 1)
        def one():
            total_ref[:, :cols] += jnp.dot(
                grads_ref[...], end_ref[...], preferred_element_type=jnp.float32
            )

        for first, b_ref, c_ref in ((0, b1_ref, c1_ref), (STEPS, b2_ref, c2_ref)):

            @pl.when((flags_ref[0] == 0) & (i >= first) & (i < first + STEPS))
            def two(b_ref=b_ref, c_ref=c_ref):
                shards = jnp.concatenate([b_ref[...], c_ref[...]], axis=1)
                total_ref[...] += jnp.dot(
                    grads_ref[...], shards, preferred_element_type=jnp.float32
                )

    third = jax.ShapeDtypeStruct((tok, STEPS * step), grads.dtype)
    return pl.pallas_call(
        kernel,
        out_shape=[jax.ShapeDtypeStruct((tok, 2 * cols), jnp.float32), third, third],
        grid_spec=pltpu.PrefetchScalarGridSpec(
            num_scalar_prefetch=1,
            grid=(2 * STEPS,),
            in_specs=specs,
            out_specs=[
                pl.BlockSpec((tok, 2 * cols), lambda i, flags_ref: (0, 0)),
                pl.BlockSpec((tok, step), lambda i, flags_ref: (0, jnp.minimum(i, STEPS - 1))),
                pl.BlockSpec((tok, step), lambda i, flags_ref: (0, jnp.maximum(i - STEPS, 0))),
            ],
        ),
        compiler_params=PARAMS,
        cost_estimate=SHORT,
    )(flags, *operands)


def partner_dots(flags, pieces, shards, grads, shard, start):
    tok = grads.shape[0]
    cols = shards[0][0].shape[1]
    step = shard[2] // STEPS
    count = len(pieces)
    two = start.shape[1] == 2 * cols
    width = tok + len(shards) * count * TILE

    def at(row):
        return lambda i, flags_ref: (row + i, 0)

    whole = lambda i, flags_ref: (0, 0)
    operands, specs = [], []
    for array, row in list(pieces) + list(shards) + [shard[:2]]:
        operands.append(array)
        specs.append(pl.BlockSpec((step, cols), at(row)))
    operands += [grads, start]
    specs.append(pl.BlockSpec((tok, step), lambda i, flags_ref: (0, i)))
    specs.append(pl.BlockSpec(start.shape, whole))

    def kernel(flags_ref, *refs):
        i = pl.program_id(0)
        piece_refs, shard_refs = refs[:count], refs[count : count + len(shards)]
        end_ref, grads_ref, start_ref = refs[count + len(shards) : count + len(shards) + 3]
        keep_ref, give_ref, *rest = refs[len(operands) :]
        if two:
            second_ref, total_ref, sums_ref, turned_ref, wide_ref = rest
        else:
            total_ref, sums_ref, turned_ref, wide_ref = rest

        @pl.when(i == 0)
        def begin():
            total_ref[...] = start_ref[...]
            sums_ref[...] = jnp.zeros_like(sums_ref)

        @pl.when(flags_ref[0] == 1)
        def at_an_end_plane():
            total_ref[:, total_ref.shape[1] - cols :] += jnp.dot(
                grads_ref[...], end_ref[...], preferred_element_type=jnp.float32
            )

        @pl.when(flags_ref[0] == 0)
        def at_a_middle_plane():
            side_by_side = jnp.concatenate([ref[...] for ref in shard_refs], axis=1)
            tokens = jnp.concatenate(
                [
                    jnp.concatenate(
                        [ref[q * TILE : (q + 1) * TILE, :] for q in range(step // TILE)], axis=1
                    )
                    for ref in piece_refs
                ]
            )
            sums_ref[...] += jnp.dot(tokens, side_by_side, preferred_element_type=jnp.float32)
            if two:
                total_ref[...] += jnp.dot(
                    grads_ref[...], side_by_side[:, cols:], preferred_element_type=jnp.float32
                )

        @pl.when(i == STEPS - 1)
        def finish():
            wide_ref[...] = total_ref[:, :cols].T
            split_rows(wide_ref, keep_ref, give_ref, flags_ref[1], pl.ds(0, tok))
            for j in range(len(shards)):
                turned_ref[...] = sums_ref[:, j * cols : (j + 1) * cols].T
                columns = pl.ds(tok + j * count * TILE, count * TILE)
                split_rows(turned_ref, keep_ref, give_ref, flags_ref[1], columns)
            if two:
                second_ref[...] = total_ref[:, cols:]

    out_shape = [jax.ShapeDtypeStruct((cols // 2, width), jnp.float32)] * 2
    out_specs = [pl.BlockSpec((cols // 2, width), whole)] * 2
    if two:
        out_shape.append(jax.ShapeDtypeStruct((tok, cols), jnp.float32))
        out_specs.append(pl.BlockSpec((tok, cols), whole))
    return pl.pallas_call(
        kernel,
        out_shape=out_shape,
        grid_spec=pltpu.PrefetchScalarGridSpec(
            num_scalar_prefetch=1,
            grid=(STEPS,),
            in_specs=specs,
            out_specs=out_specs,
            scratch_shapes=[
                pltpu.VMEM(start.shape, jnp.float32),
                pltpu.VMEM((count * TILE, len(shards) * cols), jnp.float32),
                pltpu.VMEM((cols, count * TILE), jnp.float32),
                pltpu.VMEM((cols, tok), jnp.float32),
            ],
        ),
        compiler_params=PARAMS,
        cost_estimate=SHORT,
    )(flags, *operands)


def stack_blocks(flags, grads, depth):
    tiles = grads.shape[0] // TILE
    firsts = [0] + list(range(tiles // 2, tiles))
    counts = [tiles // 2] + [1] * (tiles // 2)

    def kernel(flags_ref, grads_ref, *out_refs):
        t = pl.program_id(0)
        for first, count, out_ref in zip(firsts, counts, out_refs):

            @pl.when((t >= first) & (t < first + count))
            def copy(out_ref=out_ref):
                for q in range(depth // TILE):
                    here = slice(q * TILE, (q + 1) * TILE)
                    out_ref[here, :] = grads_ref[:, here]

    def place(first, count):
        return lambda t, flags_ref: (jnp.clip(t - first, 0, count - 1), 0)

    return pl.pallas_call(
        kernel,
        out_shape=[jax.ShapeDtypeStruct((count * depth, TILE), grads.dtype) for count in counts],
        grid_spec=pltpu.PrefetchScalarGridSpec(
            num_scalar_prefetch=1,
            grid=(tiles,),
            in_specs=[pl.BlockSpec((TILE, depth), lambda t, flags_ref: (t, 0))],
            out_specs=[
                pl.BlockSpec((depth, TILE), place(first, count))
                for first, count in zip(firsts, counts)
            ],
        ),
        compiler_params=PARAMS,
        cost_estimate=SHORT,
    )(flags, grads)


def input_dots(flags, acts, shards):
    tok, depth = acts.shape
    cols = shards[0][0][0].shape[1]
    operands, specs = [acts], [pl.BlockSpec((tok, depth), lambda i, flags_ref: (0, 0))]
    for choices in shards:
        for array, row in choices:
            operands.append(array)
            specs.append(pl.BlockSpec((depth, cols), lambda i, flags_ref, row=row: (row, 0)))

    def kernel(flags_ref, acts_ref, *refs):
        i = pl.program_id(0)
        inputs = list(refs[: len(operands) - 1])
        keep_ref, give_ref, part_ref = refs[len(operands) - 1 :]
        at = 0
        for slot, choices in enumerate(shards):
            here = inputs[at : at + len(choices)]
            at += len(choices)

            @pl.when(i == slot)
            def add(here=here):
                shard = here[0][...]
                if len(here) == 2:
                    shard = jnp.where(flags_ref[0] == 1, shard, here[1][...])
                part_ref[...] = jnp.dot(acts_ref[...], shard, preferred_element_type=jnp.float32)

        split_rows(part_ref, keep_ref, give_ref, flags_ref[1])

    place = pl.BlockSpec((tok // 2, cols), lambda i, flags_ref: (0, flags_ref[2 + i]))
    return pl.pallas_call(
        kernel,
        out_shape=[jax.ShapeDtypeStruct((tok // 2, cols * len(shards)), jnp.float32)] * 2,
        grid_spec=pltpu.PrefetchScalarGridSpec(
            num_scalar_prefetch=1,
            grid=(len(shards),),
            in_specs=specs,
            out_specs=[place, place],
            scratch_shapes=[pltpu.VMEM((tok, cols), jnp.float32)],
        ),
        compiler_params=PARAMS,
        cost_estimate=SHORT,
    )(flags, *operands)


def line_plan(acts, grads, basis_in, basis_out, eigval, test_grads, pair_tiles, last_rows):
    plane = lax.axis_index("cand")
    end = (plane == 0) | (plane == 3)
    tok_rows = acts.shape[0]
    cols = basis_in.shape[1]
    tiles_here = tok_rows // TILE
    slim = cols // 4
    depth = basis_out.shape[0] // 3
    rows_in = basis_in.shape[0]

    def pick(at_end, at_middle):
        return jnp.where(end, at_end, at_middle)

    def side(at_end, at_middle):
        return lax.ppermute(pick(at_end, at_middle), "cand", SIDE)

    among, far = [], []
    for at in range(16):
        between = 4 <= at < 12
        across = 12 - 4 * (at // 4) + at % 4
        among.append((at, across if between else at ^ 1))
        far.append((at, at ^ 1 if between else across))

    def middle(x):
        return lax.ppermute(x, ALL, among)

    at_b = jnp.where(end, plane ^ 2, plane ^ 3)
    at_c = jnp.where(end, plane ^ 3, plane ^ 2)
    rep = lax.axis_index("rep")
    flags = jnp.stack([end.astype(jnp.int32), rep, plane, plane ^ 1, at_b, at_c])

    rows = lax.dynamic_slice_in_dim(basis_out, jnp.where(end, 0, depth), 2 * depth, 0)
    s0 = lax.ppermute(basis_in, "cand", SIDE)
    m0 = middle(basis_in)
    s12 = lax.ppermute(rows, "cand", SIDE)
    second = basis_out[depth : 2 * depth]
    m2 = middle(second)
    started = after(flags, rows, second)
    stacked, *more_stacked = stack_blocks(started, grads, depth)
    part_own = feature_dots(
        after(started, s0, m0), grads, [([(basis_out, 0)], 0, 0, 3 * STEPS, False)]
    )
    precond = (test_grads.astype(jnp.float32) / (eigval + damping)).astype(jnp.bfloat16)
    m1 = middle(after(s0, m0))
    third = jnp.concatenate([basis_out[2 * depth :], basis_out[: 2 * rows_in - depth]])
    s3 = side(third, jnp.concatenate([m0, m1]))
    m3 = middle(after(basis_out[2 * depth :], precond, stacked, *more_stacked, *part_own))
    m5 = middle(s12[depth:])
    to_s45 = pick(stacked, jnp.concatenate([m2, m3]))
    s45 = lax.ppermute(after(to_s45, s3), "cand", SIDE)
    m6 = middle(s3[:depth])
    m4 = middle(after(basis_out[:depth], m5))
    s6 = side(more_stacked[0], m5)
    to_s7 = pick(after(more_stacked[1], s45), m6)
    s7 = lax.ppermute(to_s7, "cand", SIDE)
    m7 = middle(after(s12[:depth], m6))

    part_in = input_dots(
        after(flags, s3, m5),
        acts,
        [[(basis_in, 0)], [(s0, 0)], [(s3, 0), (m0, 0)], [(s3, 1), (m1, 0)]],
    )
    part_a = feature_dots(
        after(flags, *part_in),
        grads,
        [
            ([(s12, 0)], STEPS, 0, 2 * STEPS, False),
            ([(s3, 0)], 2 * STEPS, 2 * STEPS, STEPS, True),
        ],
    )
    totals, next_grads, last_grads = both_dots(after(flags, to_s7, s45, *part_a), grads, (s45, 0), ((m2, m5), (m3, m6)))
    parts = [jnp.concatenate(part, axis=1) for part in zip(part_own, part_a)]
    keep_a, give_a = after(parts, s6, m4, totals)
    core_a = swap(give_a, "rep")

    shards = [(basis_out, 0), (m4, 0), (m7, 0)]
    *part_b, part_c = partner_dots(
        after(flags, totals, core_a),
        [(s45, 0), (s45, STEPS), (s6, 0)],
        shards,
        next_grads,
        (s6, 0, depth),
        totals,
    )
    keep_in, give_in = after(part_in, part_c)
    core_in = keep_in + swap(give_in, "rep")
    give_in = core_in.astype(jnp.bfloat16)
    rot_in = all_rows(core_in, give_in)
    rot_in = rot_in.reshape(tiles_here, TILE, 4 * cols)
    keep_b, give_b = part_b
    keep_b, give_b = chip_parts(
        jnp.concatenate([keep_a, keep_b], axis=1),
        jnp.concatenate([core_a, swap(give_b, "rep")], axis=1),
    )
    sums = chip_sum(keep_b, give_b)
    sum_own, sum_a, sum_b = [sums[:, i * tok_rows : (i + 1) * tok_rows] for i in range(3)]
    sums = sums[:, 3 * tok_rows :].astype(jnp.bfloat16)
    keep_last, give_last = partner_dots(
        after(flags, part_c, give_b, give_in),
        [(s7, 0)],
        shards,
        last_grads,
        (s7, 0, depth),
        part_c,
    )
    sum_last = chip_sum(*chip_parts(keep_last, swap(give_last, "rep")))
    sum_c, sum_last = sum_last[:, :tok_rows], sum_last[:, tok_rows:].astype(jnp.bfloat16)

    rowmask, ignored = tile_layout(pair_tiles, last_rows, plane * tiles_here, tiles_here, TILE)
    keep = rowmask.reshape(1, tok_rows).astype(jnp.bfloat16)

    def tile_prods(rot_out):
        return jnp.einsum(
            "etr,tra->tea",
            (rot_out.astype(jnp.bfloat16) * keep).reshape(slim, tiles_here, TILE),
            rot_in,
            preferred_element_type=jnp.float32,
        ).astype(jnp.bfloat16)

    def pair_scores(*received):
        prods = jnp.concatenate([x for x, source in received])
        scores = jnp.einsum("tea,jea->tj", prods, precond, preferred_element_type=jnp.float32)
        onehot = jnp.concatenate([
            tile_layout(pair_tiles, last_rows, source * tiles_here, tiles_here, TILE)[1]
            for x, source in received
        ])
        return jnp.sum(jnp.where(onehot[:, :, None], scores[:, None, :], 0.0), axis=0)

    prods_own = tile_prods(sum_own)
    prods_middle = tile_prods(sum_b)
    from_middle = middle(prods_middle)
    last = lax.ppermute(sum_last, "cand", SIDE)
    back = lax.ppermute(sums, "cand", SIDE)
    back = jnp.where(end, back, jnp.zeros_like(back)).reshape(slim, 3, tok_rows - TILE)
    last = jnp.where(end, last, jnp.zeros_like(last)).reshape(slim, 3, TILE)

    def with_partner(whole, at):
        return whole + jnp.concatenate([back[:, at], last[:, at]], axis=1).astype(jnp.float32)

    prods_a = tile_prods(with_partner(sum_a, 0))
    prods_b = tile_prods(with_partner(sum_b, 1))
    prods_c = tile_prods(with_partner(sum_c, 2))
    to_two = pick(prods_b, prods_c)
    from_two = lax.ppermute(to_two, "cand", TWO)
    from_far = lax.ppermute(after(prods_c, to_two), ALL, far)
    from_side = lax.ppermute(after(prods_a, to_two), "cand", SIDE)
    total = pair_scores(
        (prods_own, plane),
        (from_side, plane ^ 1),
        (from_two, plane ^ 2),
        (pick(from_far, from_middle), plane ^ 3),
    )
    return final_sum(total)


def final_sum(total):
    npairs, ntest = total.shape
    blocks = total.reshape(4, npairs // 4, 4, ntest // 4).transpose(0, 2, 1, 3)
    blocks = blocks.reshape(16, npairs // 4, ntest // 4)
    return jnp.sum(lax.all_to_all(blocks, ALL, 0, 0, tiled=True), axis=0)


def gather_plan(acts, grads, basis_in, basis_out, eigval, test_grads, pair_tiles, last_rows):
    ncand = lax.axis_size("cand")
    nfeat = lax.axis_size(FEAT)
    tok_rows = acts.shape[0]
    width_in = basis_in.shape[1] * ncand
    width_out = basis_out.shape[1] * ncand
    slim = width_out // (ncand * nfeat)
    part_in = jnp.dot(
        acts,
        lax.all_gather(basis_in, "cand", axis=1, tiled=True),
        preferred_element_type=jnp.float32,
    )
    part_out = jnp.dot(
        grads,
        lax.all_gather(basis_out, "cand", axis=1, tiled=True),
        preferred_element_type=jnp.float32,
    )
    part_out = part_out.reshape(tok_rows, ncand, nfeat, slim).transpose(0, 2, 1, 3)
    part_out = part_out.reshape(tok_rows, nfeat * ncand * slim)
    summed_in, summed_out = lax.psum((part_in, part_out), FEAT)
    own = lax.dynamic_slice_in_dim(
        summed_out, lax.axis_index(FEAT) * (ncand * slim), ncand * slim, 1
    )
    rot_in = summed_in.astype(jnp.bfloat16)
    rot_out = own.astype(jnp.bfloat16)
    tiles_here = tok_rows // TILE
    rowmask, ignored = tile_layout(
        pair_tiles, last_rows, lax.axis_index("cand") * tiles_here, tiles_here, TILE
    )
    masked = rot_out.reshape(tiles_here, TILE, ncand * slim) * rowmask[:, :, None].astype(
        jnp.bfloat16
    )
    prods = jnp.einsum(
        "tre,tra->tea",
        masked,
        rot_in.reshape(tiles_here, TILE, width_in),
        preferred_element_type=jnp.float32,
    ).astype(jnp.bfloat16)
    prods = prods.reshape(tiles_here, ncand, slim, width_in)
    received = lax.all_to_all(prods, "cand", split_axis=1, concat_axis=0, tiled=True)
    all_tiles = received.shape[0]
    received = received.reshape(all_tiles, slim, width_in)
    precond = (test_grads.astype(jnp.float32) / (eigval + damping)).astype(jnp.bfloat16)
    tile_part = jnp.einsum("tea,jea->tj", received, precond, preferred_element_type=jnp.float32)
    ignored_mask, onehot = tile_layout(pair_tiles, last_rows, 0, all_tiles, TILE)
    pair_part = jnp.dot(onehot.astype(jnp.float32).T, tile_part, precision=lax.Precision.HIGHEST)
    npairs = pair_part.shape[0]
    ntest = pair_part.shape[1]
    total = lax.psum(pair_part, ("cand", "eig", "rep"))
    rows = lax.dynamic_slice_in_dim(
        total, lax.axis_index("cand") * (npairs // ncand), npairs // ncand, 0
    )
    return lax.dynamic_slice_in_dim(
        rows, lax.axis_index(FEAT) * (ntest // nfeat), ntest // nfeat, 1
    )


def solution(mesh):
    in_specs = (
        P(("groups", "cand"), ("eig", "rep")),
        P(("groups", "cand"), ("eig", "rep")),
        P(("groups", "eig", "rep"), "cand"),
        P(("groups", "eig", "rep"), "cand"),
        P(("groups", "cand", "eig", "rep"), None),
        P("groups", ("cand", "eig", "rep"), None),
        P("groups"),
        P("groups"),
    )
    out_specs = P(("groups", "cand"), ("eig", "rep"))
    sizes = (mesh.shape["cand"], mesh.shape["eig"], mesh.shape["rep"])
    per_device = line_plan if sizes == (4, 2, 2) else gather_plan
    return jax.shard_map(
        per_device, mesh=mesh, in_specs=in_specs, out_specs=out_specs, check_vma=False
    )
```

```python
import jax
import jax.numpy as jnp
from jax import lax
from jax.experimental import pallas as pl
from jax.experimental.pallas import tpu as pltpu
from jax.sharding import PartitionSpec as P

TILE = 128
FEAT = ("eig", "rep")
ALL = ("cand", "eig", "rep")
STEPS = 3
PARAMS = pltpu.CompilerParams(vmem_limit_bytes=20 << 20)
SHORT = pl.CostEstimate(flops=1, bytes_accessed=1, transcendentals=0)
SIDE = ((0, 1), (1, 0), (2, 3), (3, 2))
TWO = ((0, 2), (2, 0), (1, 3), (3, 1))

damping = 0.01


def tile_layout(pair_tiles, last_rows, first_tile, count, tile_rows):
    tiles = first_tile + jnp.arange(count, dtype=jnp.int32)
    ends = jnp.cumsum(pair_tiles)
    owner = jnp.sum((ends[None, :] <= tiles[:, None]).astype(jnp.int32), axis=1)
    onehot = owner[:, None] == jnp.arange(pair_tiles.shape[0], dtype=jnp.int32)[None, :]
    last_of = jnp.sum(jnp.where(onehot, last_rows[None, :], 0), axis=1)
    end_of = jnp.sum(jnp.where(onehot, ends[None, :], 0), axis=1)
    limit = jnp.where(tiles == end_of - 1, last_of, tile_rows)
    rowmask = jnp.arange(tile_rows, dtype=jnp.int32)[None, :] < limit[:, None]
    return (rowmask, onehot)


def after(x, *earlier):
    return lax.optimization_barrier((x, *earlier))[0]


def swap(x, axis_name):
    return lax.ppermute(x, axis_name, [(0, 1), (1, 0)])


def halves(x, axis_name):
    first = lax.axis_index(axis_name) == 0
    low, high = jnp.split(x, 2)
    return jnp.where(first, low, high), jnp.where(first, high, low)


def chip_parts(keep, received):
    keep, their_keep = halves(keep, "eig")
    received, their_received = halves(received, "eig")
    return keep + received, (their_keep + their_received).astype(jnp.bfloat16)


def chip_sum(keep, give):
    return keep + swap(give, "eig").astype(jnp.float32)


def all_rows(core_sum, give):
    mine = (core_sum + swap(give, "eig").astype(jnp.float32)).astype(jnp.bfloat16)
    other = swap(mine, "rep")
    first = lax.axis_index("rep") == 0
    mine, other = mine.reshape(2, -1, mine.shape[1]), other.reshape(2, -1, mine.shape[1])
    whole = jnp.stack([jnp.where(first, mine, other), jnp.where(first, other, mine)], axis=1)
    return whole.reshape(-1, whole.shape[-1])


def split_rows(full_ref, keep_ref, give_ref, rep, columns=None):
    rows = full_ref.shape[0] // 4
    columns = slice(None) if columns is None else columns
    for e in range(2):
        here = pl.ds(e * rows, rows)
        mine = pl.ds(pl.multiple_of((2 * e + rep) * rows, rows), rows)
        theirs = pl.ds(pl.multiple_of((2 * e + 1 - rep) * rows, rows), rows)
        keep_ref[here, columns] = full_ref[mine, :]
        give_ref[here, columns] = full_ref[theirs, :]


def add_dot(total_ref, rows_ref, shard):
    half = total_ref.shape[0] // 2
    for here in (pl.ds(0, half), pl.ds(half, half)):
        total_ref[here, :] += jnp.dot(
            rows_ref[here, :], shard, preferred_element_type=jnp.float32
        )


def feature_dots(flags, grads, segments, start=None, split=True):
    tok = grads.shape[0]
    cols = segments[0][0][0][0].shape[1]
    depth = grads.shape[1] // (3 * STEPS)
    firsts = [sum(s[3] for s in segments[:at]) for at in range(len(segments))]
    total = sum(s[3] for s in segments)

    def grads_at(i, flags_ref):
        at = 0
        for first, (choices, at_end, at_middle, steps, only) in zip(firsts, segments):
            base = at_end + flags_ref[0] * 0 if at_end == at_middle else (
                flags_ref[0] * at_end + (1 - flags_ref[0]) * at_middle
            )
            at = jnp.where(i >= first, base + i - first, at)
        return (0, at)

    def rows_at(first, steps, row, wanted):
        def index(i, flags_ref):
            step = jnp.clip(i - first, 0, steps - 1)
            if wanted is not None:
                step = step * (flags_ref[0] if wanted else 1 - flags_ref[0])
            return (row + step, 0)

        return index

    operands, specs = [grads], [pl.BlockSpec((tok, depth), grads_at)]
    for first, (choices, at_end, at_middle, steps, only) in zip(firsts, segments):
        for which, (array, row) in enumerate(choices):
            wanted = None if len(choices) == 1 else which == 0
            operands.append(array)
            specs.append(pl.BlockSpec((depth, cols), rows_at(first, steps, row, wanted)))
    if start is not None:
        operands.append(start)
        specs.append(pl.BlockSpec((tok, cols), lambda i, flags_ref: (0, 0)))

    def kernel(flags_ref, grads_ref, *refs):
        i = pl.program_id(0)
        end = flags_ref[0] == 1
        inputs, rest = list(refs[: len(operands) - 1]), refs[len(operands) - 1 :]
        if split:
            keep_ref, give_ref, total_ref, turned_ref = rest
        else:
            (total_ref,) = rest

        @pl.when(i == 0)
        def begin():
            total_ref[...] = jnp.zeros_like(total_ref) if start is None else inputs[-1][...]

        at = 0
        for first, (choices, at_end, at_middle, steps, only) in zip(firsts, segments):
            here = inputs[at : at + len(choices)]
            at += len(choices)
            active = (i >= first) & (i < first + steps)
            if only:
                active = active & (flags_ref[0] == 0)

            @pl.when(active)
            def add(here=here):
                shard = here[0][...]
                if len(here) == 2:
                    shard = jnp.where(end, shard, here[1][...])
                add_dot(total_ref, grads_ref, shard)

        if split:

            @pl.when(i == total - 1)
            def finish():
                turned_ref[...] = total_ref[...].T
                split_rows(turned_ref, keep_ref, give_ref, flags_ref[1])

    whole = lambda i, flags_ref: (0, 0)
    if split:
        out_shape = [jax.ShapeDtypeStruct((cols // 2, tok), jnp.float32)] * 2
        out_specs = [pl.BlockSpec((cols // 2, tok), whole)] * 2
        scratch = [pltpu.VMEM((tok, cols), jnp.float32), pltpu.VMEM((cols, tok), jnp.float32)]
    else:
        out_shape = jax.ShapeDtypeStruct((tok, cols), jnp.float32)
        out_specs = pl.BlockSpec((tok, cols), whole)
        scratch = []
    return pl.pallas_call(
        kernel,
        out_shape=out_shape,
        grid_spec=pltpu.PrefetchScalarGridSpec(
            num_scalar_prefetch=1,
            grid=(total,),
            in_specs=specs,
            out_specs=out_specs,
            scratch_shapes=scratch,
        ),
        compiler_params=PARAMS,
        cost_estimate=SHORT,
    )(flags, *operands)


def both_dots(flags, grads, at_end, at_middle):
    tok = grads.shape[0]
    cols = at_end[0].shape[1]
    step = grads.shape[1] // (3 * STEPS)

    def third_at(first):
        def index(i, flags_ref):
            return (jnp.clip(i - first, 0, STEPS - 1) * (1 - flags_ref[0]), 0)

        return index

    operands = [grads, at_end[0]] + [array for pair in at_middle for array in pair] + [grads]
    specs = [
        pl.BlockSpec((tok, step), lambda i, flags_ref: (0, STEPS + i)),
        pl.BlockSpec((step, cols), lambda i, flags_ref: (at_end[1] + i * flags_ref[0], 0)),
    ]
    for first in (0, STEPS):
        specs += [pl.BlockSpec((step, cols), third_at(first))] * 2
    specs.append(
        pl.BlockSpec(
            (tok, step),
            lambda i, flags_ref: (0, flags_ref[0] * STEPS + jnp.minimum(i, STEPS - 1)),
        )
    )

    def kernel(flags_ref, grads_ref, end_ref, b1_ref, c1_ref, b2_ref, c2_ref, next_ref, *out_refs):
        total_ref, handed_ref, last_ref = out_refs
        i = pl.program_id(0)

        @pl.when(i == 0)
        def begin():
            total_ref[...] = jnp.zeros_like(total_ref)

        @pl.when(i < STEPS)
        def hand_on_next():
            handed_ref[...] = next_ref[...]

        @pl.when(i >= STEPS)
        def hand_on_last():
            last_ref[...] = grads_ref[...]

        @pl.when(flags_ref[0] == 1)
        def one():
            total_ref[:, :cols] += jnp.dot(
                grads_ref[...], end_ref[...], preferred_element_type=jnp.float32
            )

        for first, b_ref, c_ref in ((0, b1_ref, c1_ref), (STEPS, b2_ref, c2_ref)):

            @pl.when((flags_ref[0] == 0) & (i >= first) & (i < first + STEPS))
            def two(b_ref=b_ref, c_ref=c_ref):
                shards = jnp.concatenate([b_ref[...], c_ref[...]], axis=1)
                total_ref[...] += jnp.dot(
                    grads_ref[...], shards, preferred_element_type=jnp.float32
                )

    third = jax.ShapeDtypeStruct((tok, STEPS * step), grads.dtype)
    return pl.pallas_call(
        kernel,
        out_shape=[jax.ShapeDtypeStruct((tok, 2 * cols), jnp.float32), third, third],
        grid_spec=pltpu.PrefetchScalarGridSpec(
            num_scalar_prefetch=1,
            grid=(2 * STEPS,),
            in_specs=specs,
            out_specs=[
                pl.BlockSpec((tok, 2 * cols), lambda i, flags_ref: (0, 0)),
                pl.BlockSpec((tok, step), lambda i, flags_ref: (0, jnp.minimum(i, STEPS - 1))),
                pl.BlockSpec((tok, step), lambda i, flags_ref: (0, jnp.maximum(i - STEPS, 0))),
            ],
        ),
        compiler_params=PARAMS,
        cost_estimate=SHORT,
    )(flags, *operands)


def partner_dots(flags, pieces, shards, grads, shard, start):
    tok = grads.shape[0]
    cols = shards[0][0].shape[1]
    step = shard[2] // STEPS
    count = len(pieces)
    two = start.shape[1] == 2 * cols
    width = tok + len(shards) * count * TILE

    def at(row):
        return lambda i, flags_ref: (row + i, 0)

    whole = lambda i, flags_ref: (0, 0)
    operands, specs = [], []
    for array, row in list(pieces) + list(shards) + [shard[:2]]:
        operands.append(array)
        specs.append(pl.BlockSpec((step, cols), at(row)))
    operands += [grads, start]
    specs.append(pl.BlockSpec((tok, step), lambda i, flags_ref: (0, i)))
    specs.append(pl.BlockSpec(start.shape, whole))

    def kernel(flags_ref, *refs):
        i = pl.program_id(0)
        piece_refs, shard_refs = refs[:count], refs[count : count + len(shards)]
        end_ref, grads_ref, start_ref = refs[count + len(shards) : count + len(shards) + 3]
        keep_ref, give_ref, *rest = refs[len(operands) :]
        if two:
            second_ref, total_ref, sums_ref, turned_ref, wide_ref = rest
        else:
            total_ref, sums_ref, turned_ref, wide_ref = rest

        @pl.when(i == 0)
        def begin():
            total_ref[...] = start_ref[...]
            sums_ref[...] = jnp.zeros_like(sums_ref)

        @pl.when(flags_ref[0] == 1)
        def at_an_end_plane():
            total_ref[:, total_ref.shape[1] - cols :] += jnp.dot(
                grads_ref[...], end_ref[...], preferred_element_type=jnp.float32
            )

        @pl.when(flags_ref[0] == 0)
        def at_a_middle_plane():
            side_by_side = jnp.concatenate([ref[...] for ref in shard_refs], axis=1)
            tokens = jnp.concatenate(
                [
                    jnp.concatenate(
                        [ref[q * TILE : (q + 1) * TILE, :] for q in range(step // TILE)], axis=1
                    )
                    for ref in piece_refs
                ]
            )
            sums_ref[...] += jnp.dot(tokens, side_by_side, preferred_element_type=jnp.float32)
            if two:
                total_ref[...] += jnp.dot(
                    grads_ref[...], side_by_side[:, cols:], preferred_element_type=jnp.float32
                )

        @pl.when(i == STEPS - 1)
        def finish():
            wide_ref[...] = total_ref[:, :cols].T
            split_rows(wide_ref, keep_ref, give_ref, flags_ref[1], pl.ds(0, tok))
            for j in range(len(shards)):
                turned_ref[...] = sums_ref[:, j * cols : (j + 1) * cols].T
                columns = pl.ds(tok + j * count * TILE, count * TILE)
                split_rows(turned_ref, keep_ref, give_ref, flags_ref[1], columns)
            if two:
                second_ref[...] = total_ref[:, cols:]

    out_shape = [jax.ShapeDtypeStruct((cols // 2, width), jnp.float32)] * 2
    out_specs = [pl.BlockSpec((cols // 2, width), whole)] * 2
    if two:
        out_shape.append(jax.ShapeDtypeStruct((tok, cols), jnp.float32))
        out_specs.append(pl.BlockSpec((tok, cols), whole))
    return pl.pallas_call(
        kernel,
        out_shape=out_shape,
        grid_spec=pltpu.PrefetchScalarGridSpec(
            num_scalar_prefetch=1,
            grid=(STEPS,),
            in_specs=specs,
            out_specs=out_specs,
            scratch_shapes=[
                pltpu.VMEM(start.shape, jnp.float32),
                pltpu.VMEM((count * TILE, len(shards) * cols), jnp.float32),
                pltpu.VMEM((cols, count * TILE), jnp.float32),
                pltpu.VMEM((cols, tok), jnp.float32),
            ],
        ),
        compiler_params=PARAMS,
        cost_estimate=SHORT,
    )(flags, *operands)


def stack_blocks(flags, grads, depth):
    tiles = grads.shape[0] // TILE
    firsts = [0] + list(range(tiles // 2, tiles))
    counts = [tiles // 2] + [1] * (tiles // 2)

    def kernel(flags_ref, grads_ref, *out_refs):
        t = pl.program_id(0)
        for first, count, out_ref in zip(firsts, counts, out_refs):

            @pl.when((t >= first) & (t < first + count))
            def copy(out_ref=out_ref):
                for q in range(depth // TILE):
                    here = slice(q * TILE, (q + 1) * TILE)
                    out_ref[here, :] = grads_ref[:, here]

    def place(first, count):
        return lambda t, flags_ref: (jnp.clip(t - first, 0, count - 1), 0)

    return pl.pallas_call(
        kernel,
        out_shape=[jax.ShapeDtypeStruct((count * depth, TILE), grads.dtype) for count in counts],
        grid_spec=pltpu.PrefetchScalarGridSpec(
            num_scalar_prefetch=1,
            grid=(tiles,),
            in_specs=[pl.BlockSpec((TILE, depth), lambda t, flags_ref: (t, 0))],
            out_specs=[
                pl.BlockSpec((depth, TILE), place(first, count))
                for first, count in zip(firsts, counts)
            ],
        ),
        compiler_params=PARAMS,
        cost_estimate=SHORT,
    )(flags, grads)


def input_dots(flags, acts, shards):
    tok, depth = acts.shape
    cols = shards[0][0][0].shape[1]
    operands, specs = [acts], [pl.BlockSpec((tok, depth), lambda i, flags_ref: (0, 0))]
    for choices in shards:
        for array, row in choices:
            operands.append(array)
            specs.append(pl.BlockSpec((depth, cols), lambda i, flags_ref, row=row: (row, 0)))

    def kernel(flags_ref, acts_ref, *refs):
        i = pl.program_id(0)
        inputs = list(refs[: len(operands) - 1])
        keep_ref, give_ref, part_ref = refs[len(operands) - 1 :]
        at = 0
        for slot, choices in enumerate(shards):
            here = inputs[at : at + len(choices)]
            at += len(choices)

            @pl.when(i == slot)
            def add(here=here):
                shard = here[0][...]
                if len(here) == 2:
                    shard = jnp.where(flags_ref[0] == 1, shard, here[1][...])
                part_ref[...] = jnp.dot(acts_ref[...], shard, preferred_element_type=jnp.float32)

        split_rows(part_ref, keep_ref, give_ref, flags_ref[1])

    place = pl.BlockSpec((tok // 2, cols), lambda i, flags_ref: (0, flags_ref[2 + i]))
    return pl.pallas_call(
        kernel,
        out_shape=[jax.ShapeDtypeStruct((tok // 2, cols * len(shards)), jnp.float32)] * 2,
        grid_spec=pltpu.PrefetchScalarGridSpec(
            num_scalar_prefetch=1,
            grid=(len(shards),),
            in_specs=specs,
            out_specs=[place, place],
            scratch_shapes=[pltpu.VMEM((tok, cols), jnp.float32)],
        ),
        compiler_params=PARAMS,
        cost_estimate=SHORT,
    )(flags, *operands)


def line_plan(acts, grads, basis_in, basis_out, eigval, test_grads, pair_tiles, last_rows):
    plane = lax.axis_index("cand")
    end = (plane == 0) | (plane == 3)
    tok_rows = acts.shape[0]
    cols = basis_in.shape[1]
    tiles_here = tok_rows // TILE
    slim = cols // 4
    depth = basis_out.shape[0] // 3
    rows_in = basis_in.shape[0]

    def pick(at_end, at_middle):
        return jnp.where(end, at_end, at_middle)

    def side(at_end, at_middle):
        return lax.ppermute(pick(at_end, at_middle), "cand", SIDE)

    among, far = [], []
    for at in range(16):
        between = 4 <= at < 12
        across = 12 - 4 * (at // 4) + at % 4
        among.append((at, across if between else at ^ 1))
        far.append((at, at ^ 1 if between else across))

    def middle(x):
        return lax.ppermute(x, ALL, among)

    at_b = jnp.where(end, plane ^ 2, plane ^ 3)
    at_c = jnp.where(end, plane ^ 3, plane ^ 2)
    rep = lax.axis_index("rep")
    flags = jnp.stack([end.astype(jnp.int32), rep, plane, plane ^ 1, at_b, at_c])

    rows = lax.dynamic_slice_in_dim(basis_out, jnp.where(end, 0, depth), 2 * depth, 0)
    s0 = lax.ppermute(basis_in, "cand", SIDE)
    m0 = middle(basis_in)
    s12 = lax.ppermute(rows, "cand", SIDE)
    second = basis_out[depth : 2 * depth]
    m2 = middle(second)
    started = after(flags, rows, second)
    stacked, *more_stacked = stack_blocks(started, grads, depth)
    part_own = feature_dots(
        after(started, s0, m0), grads, [([(basis_out, 0)], 0, 0, 3 * STEPS, False)]
    )
    precond = (test_grads.astype(jnp.float32) / (eigval + damping)).astype(jnp.bfloat16)
    m1 = middle(after(s0, m0))
    third = jnp.concatenate([basis_out[2 * depth :], basis_out[: 2 * rows_in - depth]])
    s3 = side(third, jnp.concatenate([m0, m1]))
    m3 = middle(after(basis_out[2 * depth :], precond, stacked, *more_stacked, *part_own))
    m5 = middle(s12[depth:])
    to_s45 = pick(stacked, jnp.concatenate([m2, m3]))
    s45 = lax.ppermute(after(to_s45, s3), "cand", SIDE)
    m6 = middle(s3[:depth])
    m4 = middle(after(basis_out[:depth], m5))
    s6 = side(more_stacked[0], m5)
    to_s7 = pick(after(more_stacked[1], s45), m6)
    s7 = lax.ppermute(to_s7, "cand", SIDE)
    m7 = middle(after(s12[:depth], m6))

    part_in = input_dots(
        after(flags, s3, m5),
        acts,
        [[(basis_in, 0)], [(s0, 0)], [(s3, 0), (m0, 0)], [(s3, 1), (m1, 0)]],
    )
    part_a = feature_dots(
        after(flags, *part_in),
        grads,
        [
            ([(s12, 0)], STEPS, 0, 2 * STEPS, False),
            ([(s3, 0)], 2 * STEPS, 2 * STEPS, STEPS, True),
        ],
    )
    totals, next_grads, last_grads = both_dots(after(flags, to_s7, s45, *part_a), grads, (s45, 0), ((m2, m5), (m3, m6)))
    parts = [jnp.concatenate(part, axis=1) for part in zip(part_own, part_a)]
    keep_a, give_a = after(parts, s6, m4, totals)
    core_a = swap(give_a, "rep")

    shards = [(basis_out, 0), (m4, 0), (m7, 0)]
    *part_b, part_c = partner_dots(
        after(flags, totals, core_a),
        [(s45, 0), (s45, STEPS), (s6, 0)],
        shards,
        next_grads,
        (s6, 0, depth),
        totals,
    )
    keep_in, give_in = after(part_in, part_c)
    core_in = keep_in + swap(give_in, "rep")
    give_in = core_in.astype(jnp.bfloat16)
    rot_in = all_rows(core_in, give_in)
    rot_in = rot_in.reshape(tiles_here, TILE, 4 * cols)
    keep_b, give_b = part_b
    keep_b, give_b = chip_parts(
        jnp.concatenate([keep_a, keep_b], axis=1),
        jnp.concatenate([core_a, swap(give_b, "rep")], axis=1),
    )
    sums = chip_sum(keep_b, give_b)
    sum_own, sum_a, sum_b = [sums[:, i * tok_rows : (i + 1) * tok_rows] for i in range(3)]
    sums = sums[:, 3 * tok_rows :].astype(jnp.bfloat16)
    keep_last, give_last = partner_dots(
        after(flags, part_c, give_b, give_in),
        [(s7, 0)],
        shards,
        last_grads,
        (s7, 0, depth),
        part_c,
    )
    sum_last = chip_sum(*chip_parts(keep_last, swap(give_last, "rep")))
    sum_c, sum_last = sum_last[:, :tok_rows], sum_last[:, tok_rows:].astype(jnp.bfloat16)

    rowmask, ignored = tile_layout(pair_tiles, last_rows, plane * tiles_here, tiles_here, TILE)
    keep = rowmask.reshape(1, tok_rows).astype(jnp.bfloat16)

    def tile_prods(rot_out):
        return jnp.einsum(
            "etr,tra->tea",
            (rot_out.astype(jnp.bfloat16) * keep).reshape(slim, tiles_here, TILE),
            rot_in,
            preferred_element_type=jnp.float32,
        ).astype(jnp.bfloat16)

    def pair_scores(*received):
        prods = jnp.concatenate([x for x, source in received])
        scores = jnp.einsum("tea,jea->tj", prods, precond, preferred_element_type=jnp.float32)
        onehot = jnp.concatenate([
            tile_layout(pair_tiles, last_rows, source * tiles_here, tiles_here, TILE)[1]
            for x, source in received
        ])
        return jnp.sum(jnp.where(onehot[:, :, None], scores[:, None, :], 0.0), axis=0)

    prods_own = tile_prods(sum_own)
    prods_middle = tile_prods(sum_b)
    from_middle = middle(prods_middle)
    last = lax.ppermute(after(sum_last, rot_in), "cand", SIDE)
    back = lax.ppermute(sums, "cand", SIDE)
    back = jnp.where(end, back, jnp.zeros_like(back)).reshape(slim, 3, tok_rows - TILE)
    last = jnp.where(end, last, jnp.zeros_like(last)).reshape(slim, 3, TILE)

    def with_partner(whole, at):
        return whole + jnp.concatenate([back[:, at], last[:, at]], axis=1).astype(jnp.float32)

    prods_a = tile_prods(with_partner(sum_a, 0))
    prods_b = tile_prods(with_partner(sum_b, 1))
    prods_c = tile_prods(with_partner(sum_c, 2))
    to_two = pick(prods_b, prods_c)
    from_two = lax.ppermute(to_two, "cand", TWO)
    from_far = lax.ppermute(after(prods_c, to_two), ALL, far)
    from_side = lax.ppermute(after(prods_a, to_two), "cand", SIDE)
    total = pair_scores(
        (prods_own, plane),
        (from_side, plane ^ 1),
        (from_two, plane ^ 2),
        (pick(from_far, from_middle), plane ^ 3),
    )
    return final_sum(total)


def final_sum(total):
    npairs, ntest = total.shape
    blocks = total.reshape(4, npairs // 4, 4, ntest // 4).transpose(0, 2, 1, 3)
    blocks = blocks.reshape(16, npairs // 4, ntest // 4)
    return jnp.sum(lax.all_to_all(blocks, ALL, 0, 0, tiled=True), axis=0)


def gather_plan(acts, grads, basis_in, basis_out, eigval, test_grads, pair_tiles, last_rows):
    ncand = lax.axis_size("cand")
    nfeat = lax.axis_size(FEAT)
    tok_rows = acts.shape[0]
    width_in = basis_in.shape[1] * ncand
    width_out = basis_out.shape[1] * ncand
    slim = width_out // (ncand * nfeat)
    part_in = jnp.dot(
        acts,
        lax.all_gather(basis_in, "cand", axis=1, tiled=True),
        preferred_element_type=jnp.float32,
    )
    part_out = jnp.dot(
        grads,
        lax.all_gather(basis_out, "cand", axis=1, tiled=True),
        preferred_element_type=jnp.float32,
    )
    part_out = part_out.reshape(tok_rows, ncand, nfeat, slim).transpose(0, 2, 1, 3)
    part_out = part_out.reshape(tok_rows, nfeat * ncand * slim)
    summed_in, summed_out = lax.psum((part_in, part_out), FEAT)
    own = lax.dynamic_slice_in_dim(
        summed_out, lax.axis_index(FEAT) * (ncand * slim), ncand * slim, 1
    )
    rot_in = summed_in.astype(jnp.bfloat16)
    rot_out = own.astype(jnp.bfloat16)
    tiles_here = tok_rows // TILE
    rowmask, ignored = tile_layout(
        pair_tiles, last_rows, lax.axis_index("cand") * tiles_here, tiles_here, TILE
    )
    masked = rot_out.reshape(tiles_here, TILE, ncand * slim) * rowmask[:, :, None].astype(
        jnp.bfloat16
    )
    prods = jnp.einsum(
        "tre,tra->tea",
        masked,
        rot_in.reshape(tiles_here, TILE, width_in),
        preferred_element_type=jnp.float32,
    ).astype(jnp.bfloat16)
    prods = prods.reshape(tiles_here, ncand, slim, width_in)
    received = lax.all_to_all(prods, "cand", split_axis=1, concat_axis=0, tiled=True)
    all_tiles = received.shape[0]
    received = received.reshape(all_tiles, slim, width_in)
    precond = (test_grads.astype(jnp.float32) / (eigval + damping)).astype(jnp.bfloat16)
    tile_part = jnp.einsum("tea,jea->tj", received, precond, preferred_element_type=jnp.float32)
    ignored_mask, onehot = tile_layout(pair_tiles, last_rows, 0, all_tiles, TILE)
    pair_part = jnp.dot(onehot.astype(jnp.float32).T, tile_part, precision=lax.Precision.HIGHEST)
    npairs = pair_part.shape[0]
    ntest = pair_part.shape[1]
    total = lax.psum(pair_part, ("cand", "eig", "rep"))
    rows = lax.dynamic_slice_in_dim(
        total, lax.axis_index("cand") * (npairs // ncand), npairs // ncand, 0
    )
    return lax.dynamic_slice_in_dim(
        rows, lax.axis_index(FEAT) * (ntest // nfeat), ntest // nfeat, 1
    )


def solution(mesh):
    in_specs = (
        P(("groups", "cand"), ("eig", "rep")),
        P(("groups", "cand"), ("eig", "rep")),
        P(("groups", "eig", "rep"), "cand"),
        P(("groups", "eig", "rep"), "cand"),
        P(("groups", "cand", "eig", "rep"), None),
        P("groups", ("cand", "eig", "rep"), None),
        P("groups"),
        P("groups"),
    )
    out_specs = P(("groups", "cand"), ("eig", "rep"))
    sizes = (mesh.shape["cand"], mesh.shape["eig"], mesh.shape["rep"])
    per_device = line_plan if sizes == (4, 2, 2) else gather_plan
    return jax.shard_map(
        per_device, mesh=mesh, in_specs=in_specs, out_specs=out_specs, check_vma=False
    )
```

```python
import jax
import jax.numpy as jnp
from jax import lax
from jax.experimental import pallas as pl
from jax.experimental.pallas import tpu as pltpu
from jax.sharding import PartitionSpec as P

TILE = 128
FEAT = ("eig", "rep")
ALL = ("cand", "eig", "rep")
STEPS = 3
PARAMS = pltpu.CompilerParams(vmem_limit_bytes=20 << 20)
SHORT = pl.CostEstimate(flops=1, bytes_accessed=1, transcendentals=0)
SIDE = ((0, 1), (1, 0), (2, 3), (3, 2))
TWO = ((0, 2), (2, 0), (1, 3), (3, 1))

damping = 0.01


def tile_layout(pair_tiles, last_rows, first_tile, count, tile_rows):
    tiles = first_tile + jnp.arange(count, dtype=jnp.int32)
    ends = jnp.cumsum(pair_tiles)
    owner = jnp.sum((ends[None, :] <= tiles[:, None]).astype(jnp.int32), axis=1)
    onehot = owner[:, None] == jnp.arange(pair_tiles.shape[0], dtype=jnp.int32)[None, :]
    last_of = jnp.sum(jnp.where(onehot, last_rows[None, :], 0), axis=1)
    end_of = jnp.sum(jnp.where(onehot, ends[None, :], 0), axis=1)
    limit = jnp.where(tiles == end_of - 1, last_of, tile_rows)
    rowmask = jnp.arange(tile_rows, dtype=jnp.int32)[None, :] < limit[:, None]
    return (rowmask, onehot)


def after(x, *earlier):
    return lax.optimization_barrier((x, *earlier))[0]


def swap(x, axis_name):
    return lax.ppermute(x, axis_name, [(0, 1), (1, 0)])


def halves(x, axis_name):
    first = lax.axis_index(axis_name) == 0
    low, high = jnp.split(x, 2)
    return jnp.where(first, low, high), jnp.where(first, high, low)


def chip_parts(keep, received):
    keep, their_keep = halves(keep, "eig")
    received, their_received = halves(received, "eig")
    return keep + received, (their_keep + their_received).astype(jnp.bfloat16)


def chip_sum(keep, give):
    return keep + swap(give, "eig").astype(jnp.float32)


def all_rows(core_sum, give):
    mine = (core_sum + swap(give, "eig").astype(jnp.float32)).astype(jnp.bfloat16)
    other = swap(mine, "rep")
    first = lax.axis_index("rep") == 0
    mine, other = mine.reshape(2, -1, mine.shape[1]), other.reshape(2, -1, mine.shape[1])
    whole = jnp.stack([jnp.where(first, mine, other), jnp.where(first, other, mine)], axis=1)
    return whole.reshape(-1, whole.shape[-1])


def split_rows(full_ref, keep_ref, give_ref, rep, columns=None):
    rows = full_ref.shape[0] // 4
    columns = slice(None) if columns is None else columns
    for e in range(2):
        here = pl.ds(e * rows, rows)
        mine = pl.ds(pl.multiple_of((2 * e + rep) * rows, rows), rows)
        theirs = pl.ds(pl.multiple_of((2 * e + 1 - rep) * rows, rows), rows)
        keep_ref[here, columns] = full_ref[mine, :]
        give_ref[here, columns] = full_ref[theirs, :]


def add_dot(total_ref, rows_ref, shard):
    half = total_ref.shape[0] // 2
    for here in (pl.ds(0, half), pl.ds(half, half)):
        total_ref[here, :] += jnp.dot(
            rows_ref[here, :], shard, preferred_element_type=jnp.float32
        )


def feature_dots(flags, grads, segments, start=None, split=True):
    tok = grads.shape[0]
    cols = segments[0][0][0][0].shape[1]
    depth = grads.shape[1] // (3 * STEPS)
    firsts = [sum(s[3] for s in segments[:at]) for at in range(len(segments))]
    total = sum(s[3] for s in segments)

    def grads_at(i, flags_ref):
        at = 0
        for first, (choices, at_end, at_middle, steps, only) in zip(firsts, segments):
            base = at_end + flags_ref[0] * 0 if at_end == at_middle else (
                flags_ref[0] * at_end + (1 - flags_ref[0]) * at_middle
            )
            at = jnp.where(i >= first, base + i - first, at)
        return (0, at)

    def rows_at(first, steps, row, wanted):
        def index(i, flags_ref):
            step = jnp.clip(i - first, 0, steps - 1)
            if wanted is not None:
                step = step * (flags_ref[0] if wanted else 1 - flags_ref[0])
            return (row + step, 0)

        return index

    operands, specs = [grads], [pl.BlockSpec((tok, depth), grads_at)]
    for first, (choices, at_end, at_middle, steps, only) in zip(firsts, segments):
        for which, (array, row) in enumerate(choices):
            wanted = None if len(choices) == 1 else which == 0
            operands.append(array)
            specs.append(pl.BlockSpec((depth, cols), rows_at(first, steps, row, wanted)))
    if start is not None:
        operands.append(start)
        specs.append(pl.BlockSpec((tok, cols), lambda i, flags_ref: (0, 0)))

    def kernel(flags_ref, grads_ref, *refs):
        i = pl.program_id(0)
        end = flags_ref[0] == 1
        inputs, rest = list(refs[: len(operands) - 1]), refs[len(operands) - 1 :]
        if split:
            keep_ref, give_ref, total_ref, turned_ref = rest
        else:
            (total_ref,) = rest

        @pl.when(i == 0)
        def begin():
            total_ref[...] = jnp.zeros_like(total_ref) if start is None else inputs[-1][...]

        at = 0
        for first, (choices, at_end, at_middle, steps, only) in zip(firsts, segments):
            here = inputs[at : at + len(choices)]
            at += len(choices)
            active = (i >= first) & (i < first + steps)
            if only:
                active = active & (flags_ref[0] == 0)

            @pl.when(active)
            def add(here=here):
                shard = here[0][...]
                if len(here) == 2:
                    shard = jnp.where(end, shard, here[1][...])
                add_dot(total_ref, grads_ref, shard)

        if split:

            @pl.when(i == total - 1)
            def finish():
                turned_ref[...] = total_ref[...].T
                split_rows(turned_ref, keep_ref, give_ref, flags_ref[1])

    whole = lambda i, flags_ref: (0, 0)
    if split:
        out_shape = [jax.ShapeDtypeStruct((cols // 2, tok), jnp.float32)] * 2
        out_specs = [pl.BlockSpec((cols // 2, tok), whole)] * 2
        scratch = [pltpu.VMEM((tok, cols), jnp.float32), pltpu.VMEM((cols, tok), jnp.float32)]
    else:
        out_shape = jax.ShapeDtypeStruct((tok, cols), jnp.float32)
        out_specs = pl.BlockSpec((tok, cols), whole)
        scratch = []
    return pl.pallas_call(
        kernel,
        out_shape=out_shape,
        grid_spec=pltpu.PrefetchScalarGridSpec(
            num_scalar_prefetch=1,
            grid=(total,),
            in_specs=specs,
            out_specs=out_specs,
            scratch_shapes=scratch,
        ),
        compiler_params=PARAMS,
        cost_estimate=SHORT,
    )(flags, *operands)


def both_dots(flags, grads, at_end, at_middle):
    tok = grads.shape[0]
    cols = at_end[0].shape[1]
    step = grads.shape[1] // (3 * STEPS)

    def third_at(first):
        def index(i, flags_ref):
            return (jnp.clip(i - first, 0, STEPS - 1) * (1 - flags_ref[0]), 0)

        return index

    operands = [grads, at_end[0]] + [array for pair in at_middle for array in pair] + [grads]
    specs = [
        pl.BlockSpec((tok, step), lambda i, flags_ref: (0, STEPS + i)),
        pl.BlockSpec((step, cols), lambda i, flags_ref: (at_end[1] + i * flags_ref[0], 0)),
    ]
    for first in (0, STEPS):
        specs += [pl.BlockSpec((step, cols), third_at(first))] * 2
    specs.append(
        pl.BlockSpec(
            (tok, step),
            lambda i, flags_ref: (0, flags_ref[0] * STEPS + jnp.minimum(i, STEPS - 1)),
        )
    )

    def kernel(flags_ref, grads_ref, end_ref, b1_ref, c1_ref, b2_ref, c2_ref, next_ref, *out_refs):
        total_ref, handed_ref, last_ref = out_refs
        i = pl.program_id(0)

        @pl.when(i == 0)
        def begin():
            total_ref[...] = jnp.zeros_like(total_ref)

        @pl.when(i < STEPS)
        def hand_on_next():
            handed_ref[...] = next_ref[...]

        @pl.when(i >= STEPS)
        def hand_on_last():
            last_ref[...] = grads_ref[...]

        @pl.when(flags_ref[0] == 1)
        def one():
            total_ref[:, :cols] += jnp.dot(
                grads_ref[...], end_ref[...], preferred_element_type=jnp.float32
            )

        for first, b_ref, c_ref in ((0, b1_ref, c1_ref), (STEPS, b2_ref, c2_ref)):

            @pl.when((flags_ref[0] == 0) & (i >= first) & (i < first + STEPS))
            def two(b_ref=b_ref, c_ref=c_ref):
                shards = jnp.concatenate([b_ref[...], c_ref[...]], axis=1)
                total_ref[...] += jnp.dot(
                    grads_ref[...], shards, preferred_element_type=jnp.float32
                )

    third = jax.ShapeDtypeStruct((tok, STEPS * step), grads.dtype)
    return pl.pallas_call(
        kernel,
        out_shape=[jax.ShapeDtypeStruct((tok, 2 * cols), jnp.float32), third, third],
        grid_spec=pltpu.PrefetchScalarGridSpec(
            num_scalar_prefetch=1,
            grid=(2 * STEPS,),
            in_specs=specs,
            out_specs=[
                pl.BlockSpec((tok, 2 * cols), lambda i, flags_ref: (0, 0)),
                pl.BlockSpec((tok, step), lambda i, flags_ref: (0, jnp.minimum(i, STEPS - 1))),
                pl.BlockSpec((tok, step), lambda i, flags_ref: (0, jnp.maximum(i - STEPS, 0))),
            ],
        ),
        compiler_params=PARAMS,
        cost_estimate=SHORT,
    )(flags, *operands)


def partner_dots(flags, pieces, shards, grads, shard, start):
    tok = grads.shape[0]
    cols = shards[0][0].shape[1]
    step = shard[2] // STEPS
    count = len(pieces)
    two = start.shape[1] == 2 * cols
    width = tok + len(shards) * count * TILE

    def at(row):
        return lambda i, flags_ref: (row + i, 0)

    whole = lambda i, flags_ref: (0, 0)
    operands, specs = [], []
    for array, row in list(pieces) + list(shards) + [shard[:2]]:
        operands.append(array)
        specs.append(pl.BlockSpec((step, cols), at(row)))
    operands += [grads, start]
    specs.append(pl.BlockSpec((tok, step), lambda i, flags_ref: (0, i)))
    specs.append(pl.BlockSpec(start.shape, whole))

    def kernel(flags_ref, *refs):
        i = pl.program_id(0)
        piece_refs, shard_refs = refs[:count], refs[count : count + len(shards)]
        end_ref, grads_ref, start_ref = refs[count + len(shards) : count + len(shards) + 3]
        keep_ref, give_ref, *rest = refs[len(operands) :]
        if two:
            second_ref, total_ref, sums_ref, turned_ref, wide_ref = rest
        else:
            total_ref, sums_ref, turned_ref, wide_ref = rest

        @pl.when(i == 0)
        def begin():
            total_ref[...] = start_ref[...]
            sums_ref[...] = jnp.zeros_like(sums_ref)

        @pl.when(flags_ref[0] == 1)
        def at_an_end_plane():
            total_ref[:, total_ref.shape[1] - cols :] += jnp.dot(
                grads_ref[...], end_ref[...], preferred_element_type=jnp.float32
            )

        @pl.when(flags_ref[0] == 0)
        def at_a_middle_plane():
            side_by_side = jnp.concatenate([ref[...] for ref in shard_refs], axis=1)
            tokens = jnp.concatenate(
                [
                    jnp.concatenate(
                        [ref[q * TILE : (q + 1) * TILE, :] for q in range(step // TILE)], axis=1
                    )
                    for ref in piece_refs
                ]
            )
            sums_ref[...] += jnp.dot(tokens, side_by_side, preferred_element_type=jnp.float32)
            if two:
                total_ref[...] += jnp.dot(
                    grads_ref[...], side_by_side[:, cols:], preferred_element_type=jnp.float32
                )

        @pl.when(i == STEPS - 1)
        def finish():
            wide_ref[...] = total_ref[:, :cols].T
            split_rows(wide_ref, keep_ref, give_ref, flags_ref[1], pl.ds(0, tok))
            for j in range(len(shards)):
                turned_ref[...] = sums_ref[:, j * cols : (j + 1) * cols].T
                columns = pl.ds(tok + j * count * TILE, count * TILE)
                split_rows(turned_ref, keep_ref, give_ref, flags_ref[1], columns)
            if two:
                second_ref[...] = total_ref[:, cols:]

    out_shape = [jax.ShapeDtypeStruct((cols // 2, width), jnp.float32)] * 2
    out_specs = [pl.BlockSpec((cols // 2, width), whole)] * 2
    if two:
        out_shape.append(jax.ShapeDtypeStruct((tok, cols), jnp.float32))
        out_specs.append(pl.BlockSpec((tok, cols), whole))
    return pl.pallas_call(
        kernel,
        out_shape=out_shape,
        grid_spec=pltpu.PrefetchScalarGridSpec(
            num_scalar_prefetch=1,
            grid=(STEPS,),
            in_specs=specs,
            out_specs=out_specs,
            scratch_shapes=[
                pltpu.VMEM(start.shape, jnp.float32),
                pltpu.VMEM((count * TILE, len(shards) * cols), jnp.float32),
                pltpu.VMEM((cols, count * TILE), jnp.float32),
                pltpu.VMEM((cols, tok), jnp.float32),
            ],
        ),
        compiler_params=PARAMS,
        cost_estimate=SHORT,
    )(flags, *operands)


def stack_blocks(flags, grads, depth):
    tiles = grads.shape[0] // TILE
    firsts = [0] + list(range(tiles // 2, tiles))
    counts = [tiles // 2] + [1] * (tiles // 2)

    def kernel(flags_ref, grads_ref, *out_refs):
        t = pl.program_id(0)
        for first, count, out_ref in zip(firsts, counts, out_refs):

            @pl.when((t >= first) & (t < first + count))
            def copy(out_ref=out_ref):
                for q in range(depth // TILE):
                    here = slice(q * TILE, (q + 1) * TILE)
                    out_ref[here, :] = grads_ref[:, here]

    def place(first, count):
        return lambda t, flags_ref: (jnp.clip(t - first, 0, count - 1), 0)

    return pl.pallas_call(
        kernel,
        out_shape=[jax.ShapeDtypeStruct((count * depth, TILE), grads.dtype) for count in counts],
        grid_spec=pltpu.PrefetchScalarGridSpec(
            num_scalar_prefetch=1,
            grid=(tiles,),
            in_specs=[pl.BlockSpec((TILE, depth), lambda t, flags_ref: (t, 0))],
            out_specs=[
                pl.BlockSpec((depth, TILE), place(first, count))
                for first, count in zip(firsts, counts)
            ],
        ),
        compiler_params=PARAMS,
        cost_estimate=SHORT,
    )(flags, grads)


def input_dots(flags, acts, shards):
    tok, depth = acts.shape
    cols = shards[0][0][0].shape[1]
    operands, specs = [acts], [pl.BlockSpec((tok, depth), lambda i, flags_ref: (0, 0))]
    for choices in shards:
        for array, row in choices:
            operands.append(array)
            specs.append(pl.BlockSpec((depth, cols), lambda i, flags_ref, row=row: (row, 0)))

    def kernel(flags_ref, acts_ref, *refs):
        i = pl.program_id(0)
        inputs = list(refs[: len(operands) - 1])
        keep_ref, give_ref, part_ref = refs[len(operands) - 1 :]
        at = 0
        for slot, choices in enumerate(shards):
            here = inputs[at : at + len(choices)]
            at += len(choices)

            @pl.when(i == slot)
            def add(here=here):
                shard = here[0][...]
                if len(here) == 2:
                    shard = jnp.where(flags_ref[0] == 1, shard, here[1][...])
                part_ref[...] = jnp.dot(acts_ref[...], shard, preferred_element_type=jnp.float32)

        split_rows(part_ref, keep_ref, give_ref, flags_ref[1])

    place = pl.BlockSpec((tok // 2, cols), lambda i, flags_ref: (0, flags_ref[2 + i]))
    return pl.pallas_call(
        kernel,
        out_shape=[jax.ShapeDtypeStruct((tok // 2, cols * len(shards)), jnp.float32)] * 2,
        grid_spec=pltpu.PrefetchScalarGridSpec(
            num_scalar_prefetch=1,
            grid=(len(shards),),
            in_specs=specs,
            out_specs=[place, place],
            scratch_shapes=[pltpu.VMEM((tok, cols), jnp.float32)],
        ),
        compiler_params=PARAMS,
        cost_estimate=SHORT,
    )(flags, *operands)


def line_plan(acts, grads, basis_in, basis_out, eigval, test_grads, pair_tiles, last_rows):
    plane = lax.axis_index("cand")
    end = (plane == 0) | (plane == 3)
    tok_rows = acts.shape[0]
    cols = basis_in.shape[1]
    tiles_here = tok_rows // TILE
    slim = cols // 4
    depth = basis_out.shape[0] // 3
    rows_in = basis_in.shape[0]

    def pick(at_end, at_middle):
        return jnp.where(end, at_end, at_middle)

    def side(at_end, at_middle):
        return lax.ppermute(pick(at_end, at_middle), "cand", SIDE)

    among, far = [], []
    for at in range(16):
        between = 4 <= at < 12
        across = 12 - 4 * (at // 4) + at % 4
        among.append((at, across if between else at ^ 1))
        far.append((at, at ^ 1 if between else across))

    def middle(x):
        return lax.ppermute(x, ALL, among)

    at_b = jnp.where(end, plane ^ 2, plane ^ 3)
    at_c = jnp.where(end, plane ^ 3, plane ^ 2)
    rep = lax.axis_index("rep")
    flags = jnp.stack([end.astype(jnp.int32), rep, plane, plane ^ 1, at_b, at_c])

    rows = lax.dynamic_slice_in_dim(basis_out, jnp.where(end, 0, depth), 2 * depth, 0)
    s0 = lax.ppermute(basis_in, "cand", SIDE)
    m0 = middle(basis_in)
    s12 = lax.ppermute(rows, "cand", SIDE)
    second = basis_out[depth : 2 * depth]
    m2 = middle(second)
    started = after(flags, rows, second)
    stacked, *more_stacked = stack_blocks(started, grads, depth)
    part_own = feature_dots(
        after(started, s0, m0), grads, [([(basis_out, 0)], 0, 0, 3 * STEPS, False)]
    )
    precond = (test_grads.astype(jnp.float32) / (eigval + damping)).astype(jnp.bfloat16)
    m1 = middle(after(s0, m0))
    third = jnp.concatenate([basis_out[2 * depth :], basis_out[: 2 * rows_in - depth]])
    s3 = side(third, jnp.concatenate([m0, m1]))
    m3 = middle(after(basis_out[2 * depth :], precond, stacked, *more_stacked, *part_own))
    m5 = middle(s12[depth:])
    to_s45 = pick(stacked, jnp.concatenate([m2, m3]))
    s45 = lax.ppermute(to_s45, "cand", SIDE)
    m6 = middle(s3[:depth])
    m4 = middle(after(basis_out[:depth], m5))
    s6 = side(more_stacked[0], m5)
    to_s7 = pick(after(more_stacked[1], s45), m6)
    s7 = lax.ppermute(to_s7, "cand", SIDE)
    m7 = middle(after(s12[:depth], m6))

    part_in = input_dots(
        after(flags, s3, m5),
        acts,
        [[(basis_in, 0)], [(s0, 0)], [(s3, 0), (m0, 0)], [(s3, 1), (m1, 0)]],
    )
    part_a = feature_dots(
        after(flags, *part_in),
        grads,
        [
            ([(s12, 0)], STEPS, 0, 2 * STEPS, False),
            ([(s3, 0)], 2 * STEPS, 2 * STEPS, STEPS, True),
        ],
    )
    totals, next_grads, last_grads = both_dots(after(flags, to_s7, s45, *part_a), grads, (s45, 0), ((m2, m5), (m3, m6)))
    parts = [jnp.concatenate(part, axis=1) for part in zip(part_own, part_a)]
    keep_a, give_a = after(parts, m4, totals)
    core_a = swap(give_a, "rep")

    shards = [(basis_out, 0), (m4, 0), (m7, 0)]
    *part_b, part_c = partner_dots(
        after(flags, totals, core_a),
        [(s45, 0), (s45, STEPS), (s6, 0)],
        shards,
        next_grads,
        (s6, 0, depth),
        totals,
    )
    keep_in, give_in = after(part_in, part_c)
    core_in = keep_in + swap(give_in, "rep")
    give_in = core_in.astype(jnp.bfloat16)
    rot_in = all_rows(core_in, give_in)
    rot_in = rot_in.reshape(tiles_here, TILE, 4 * cols)
    keep_b, give_b = part_b
    keep_b, give_b = chip_parts(
        jnp.concatenate([keep_a, keep_b], axis=1),
        jnp.concatenate([core_a, swap(give_b, "rep")], axis=1),
    )
    sums = chip_sum(keep_b, give_b)
    sum_own, sum_a, sum_b = [sums[:, i * tok_rows : (i + 1) * tok_rows] for i in range(3)]
    sums = sums[:, 3 * tok_rows :].astype(jnp.bfloat16)
    keep_last, give_last = partner_dots(
        after(flags, part_c, give_b, give_in),
        [(s7, 0)],
        shards,
        last_grads,
        (s7, 0, depth),
        part_c,
    )
    sum_last = chip_sum(*chip_parts(keep_last, swap(give_last, "rep")))
    sum_c, sum_last = sum_last[:, :tok_rows], sum_last[:, tok_rows:].astype(jnp.bfloat16)

    rowmask, ignored = tile_layout(pair_tiles, last_rows, plane * tiles_here, tiles_here, TILE)
    keep = rowmask.reshape(1, tok_rows).astype(jnp.bfloat16)

    def tile_prods(rot_out):
        return jnp.einsum(
            "etr,tra->tea",
            (rot_out.astype(jnp.bfloat16) * keep).reshape(slim, tiles_here, TILE),
            rot_in,
            preferred_element_type=jnp.float32,
        ).astype(jnp.bfloat16)

    def pair_scores(*received):
        prods = jnp.concatenate([x for x, source in received])
        scores = jnp.einsum("tea,jea->tj", prods, precond, preferred_element_type=jnp.float32)
        onehot = jnp.concatenate([
            tile_layout(pair_tiles, last_rows, source * tiles_here, tiles_here, TILE)[1]
            for x, source in received
        ])
        return jnp.sum(jnp.where(onehot[:, :, None], scores[:, None, :], 0.0), axis=0)

    prods_own = tile_prods(sum_own)
    prods_middle = tile_prods(sum_b)
    from_middle = middle(prods_middle)
    last = lax.ppermute(after(sum_last, rot_in, prods_middle), "cand", SIDE)
    back = lax.ppermute(sums, "cand", SIDE)
    back = jnp.where(end, back, jnp.zeros_like(back)).reshape(slim, 3, tok_rows - TILE)
    last = jnp.where(end, last, jnp.zeros_like(last)).reshape(slim, 3, TILE)

    def with_partner(whole, at):
        return whole + jnp.concatenate([back[:, at], last[:, at]], axis=1).astype(jnp.float32)

    prods_a = tile_prods(with_partner(sum_a, 0))
    prods_b = tile_prods(with_partner(sum_b, 1))
    prods_c = tile_prods(with_partner(sum_c, 2))
    to_two = pick(prods_b, prods_c)
    from_two = lax.ppermute(to_two, "cand", TWO)
    from_far = lax.ppermute(after(prods_c, to_two, from_middle), ALL, far)
    from_side = lax.ppermute(after(prods_a, to_two), "cand", SIDE)
    total = pair_scores(
        (prods_own, plane),
        (from_side, plane ^ 1),
        (from_two, plane ^ 2),
        (pick(from_far, from_middle), plane ^ 3),
    )
    return final_sum(total)


def final_sum(total):
    npairs, ntest = total.shape
    blocks = total.reshape(4, npairs // 4, 4, ntest // 4).transpose(0, 2, 1, 3)
    blocks = blocks.reshape(16, npairs // 4, ntest // 4)
    return jnp.sum(lax.all_to_all(blocks, ALL, 0, 0, tiled=True), axis=0)


def gather_plan(acts, grads, basis_in, basis_out, eigval, test_grads, pair_tiles, last_rows):
    ncand = lax.axis_size("cand")
    nfeat = lax.axis_size(FEAT)
    tok_rows = acts.shape[0]
    width_in = basis_in.shape[1] * ncand
    width_out = basis_out.shape[1] * ncand
    slim = width_out // (ncand * nfeat)
    part_in = jnp.dot(
        acts,
        lax.all_gather(basis_in, "cand", axis=1, tiled=True),
        preferred_element_type=jnp.float32,
    )
    part_out = jnp.dot(
        grads,
        lax.all_gather(basis_out, "cand", axis=1, tiled=True),
        preferred_element_type=jnp.float32,
    )
    part_out = part_out.reshape(tok_rows, ncand, nfeat, slim).transpose(0, 2, 1, 3)
    part_out = part_out.reshape(tok_rows, nfeat * ncand * slim)
    summed_in, summed_out = lax.psum((part_in, part_out), FEAT)
    own = lax.dynamic_slice_in_dim(
        summed_out, lax.axis_index(FEAT) * (ncand * slim), ncand * slim, 1
    )
    rot_in = summed_in.astype(jnp.bfloat16)
    rot_out = own.astype(jnp.bfloat16)
    tiles_here = tok_rows // TILE
    rowmask, ignored = tile_layout(
        pair_tiles, last_rows, lax.axis_index("cand") * tiles_here, tiles_here, TILE
    )
    masked = rot_out.reshape(tiles_here, TILE, ncand * slim) * rowmask[:, :, None].astype(
        jnp.bfloat16
    )
    prods = jnp.einsum(
        "tre,tra->tea",
        masked,
        rot_in.reshape(tiles_here, TILE, width_in),
        preferred_element_type=jnp.float32,
    ).astype(jnp.bfloat16)
    prods = prods.reshape(tiles_here, ncand, slim, width_in)
    received = lax.all_to_all(prods, "cand", split_axis=1, concat_axis=0, tiled=True)
    all_tiles = received.shape[0]
    received = received.reshape(all_tiles, slim, width_in)
    precond = (test_grads.astype(jnp.float32) / (eigval + damping)).astype(jnp.bfloat16)
    tile_part = jnp.einsum("tea,jea->tj", received, precond, preferred_element_type=jnp.float32)
    ignored_mask, onehot = tile_layout(pair_tiles, last_rows, 0, all_tiles, TILE)
    pair_part = jnp.dot(onehot.astype(jnp.float32).T, tile_part, precision=lax.Precision.HIGHEST)
    npairs = pair_part.shape[0]
    ntest = pair_part.shape[1]
    total = lax.psum(pair_part, ("cand", "eig", "rep"))
    rows = lax.dynamic_slice_in_dim(
        total, lax.axis_index("cand") * (npairs // ncand), npairs // ncand, 0
    )
    return lax.dynamic_slice_in_dim(
        rows, lax.axis_index(FEAT) * (ntest // nfeat), ntest // nfeat, 1
    )


def solution(mesh):
    in_specs = (
        P(("groups", "cand"), ("eig", "rep")),
        P(("groups", "cand"), ("eig", "rep")),
        P(("groups", "eig", "rep"), "cand"),
        P(("groups", "eig", "rep"), "cand"),
        P(("groups", "cand", "eig", "rep"), None),
        P("groups", ("cand", "eig", "rep"), None),
        P("groups"),
        P("groups"),
    )
    out_specs = P(("groups", "cand"), ("eig", "rep"))
    sizes = (mesh.shape["cand"], mesh.shape["eig"], mesh.shape["rep"])
    per_device = line_plan if sizes == (4, 2, 2) else gather_plan
    return jax.shard_map(
        per_device, mesh=mesh, in_specs=in_specs, out_specs=out_specs, check_vma=False
    )
```

```python
import jax
import jax.numpy as jnp
from jax import lax
from jax.experimental import pallas as pl
from jax.experimental.pallas import tpu as pltpu
from jax.sharding import PartitionSpec as P

TILE = 128
FEAT = ("eig", "rep")
ALL = ("cand", "eig", "rep")
STEPS = 3
PARAMS = pltpu.CompilerParams(vmem_limit_bytes=20 << 20)
SHORT = pl.CostEstimate(flops=1, bytes_accessed=1, transcendentals=0)
SIDE = ((0, 1), (1, 0), (2, 3), (3, 2))
TWO = ((0, 2), (2, 0), (1, 3), (3, 1))

damping = 0.01


def tile_layout(pair_tiles, last_rows, first_tile, count, tile_rows):
    tiles = first_tile + jnp.arange(count, dtype=jnp.int32)
    ends = jnp.cumsum(pair_tiles)
    owner = jnp.sum((ends[None, :] <= tiles[:, None]).astype(jnp.int32), axis=1)
    onehot = owner[:, None] == jnp.arange(pair_tiles.shape[0], dtype=jnp.int32)[None, :]
    last_of = jnp.sum(jnp.where(onehot, last_rows[None, :], 0), axis=1)
    end_of = jnp.sum(jnp.where(onehot, ends[None, :], 0), axis=1)
    limit = jnp.where(tiles == end_of - 1, last_of, tile_rows)
    rowmask = jnp.arange(tile_rows, dtype=jnp.int32)[None, :] < limit[:, None]
    return (rowmask, onehot)


def after(x, *earlier):
    return lax.optimization_barrier((x, *earlier))[0]


def swap(x, axis_name):
    return lax.ppermute(x, axis_name, [(0, 1), (1, 0)])


def halves(x, axis_name):
    first = lax.axis_index(axis_name) == 0
    low, high = jnp.split(x, 2)
    return jnp.where(first, low, high), jnp.where(first, high, low)


def chip_parts(keep, received):
    keep, their_keep = halves(keep, "eig")
    received, their_received = halves(received, "eig")
    return keep + received, (their_keep + their_received).astype(jnp.bfloat16)


def chip_sum(keep, give):
    return keep + swap(give, "eig").astype(jnp.float32)


def all_rows(mine, other):
    first = lax.axis_index("rep") == 0
    mine, other = mine.reshape(2, -1, mine.shape[1]), other.reshape(2, -1, mine.shape[1])
    whole = jnp.stack([jnp.where(first, mine, other), jnp.where(first, other, mine)], axis=1)
    return whole.reshape(-1, whole.shape[-1])


def split_rows(full_ref, keep_ref, give_ref, rep, columns=None):
    rows = full_ref.shape[0] // 4
    columns = slice(None) if columns is None else columns
    for e in range(2):
        here = pl.ds(e * rows, rows)
        mine = pl.ds(pl.multiple_of((2 * e + rep) * rows, rows), rows)
        theirs = pl.ds(pl.multiple_of((2 * e + 1 - rep) * rows, rows), rows)
        keep_ref[here, columns] = full_ref[mine, :]
        give_ref[here, columns] = full_ref[theirs, :]


def add_dot(total_ref, rows_ref, shard):
    half = total_ref.shape[0] // 2
    for here in (pl.ds(0, half), pl.ds(half, half)):
        total_ref[here, :] += jnp.dot(
            rows_ref[here, :], shard, preferred_element_type=jnp.float32
        )


def feature_dots(flags, grads, segments, start=None, split=True):
    tok = grads.shape[0]
    cols = segments[0][0][0][0].shape[1]
    depth = grads.shape[1] // (3 * STEPS)
    firsts = [sum(s[3] for s in segments[:at]) for at in range(len(segments))]
    total = sum(s[3] for s in segments)

    def grads_at(i, flags_ref):
        at = 0
        for first, (choices, at_end, at_middle, steps, only) in zip(firsts, segments):
            base = at_end + flags_ref[0] * 0 if at_end == at_middle else (
                flags_ref[0] * at_end + (1 - flags_ref[0]) * at_middle
            )
            at = jnp.where(i >= first, base + i - first, at)
        return (0, at)

    def rows_at(first, steps, row, wanted):
        def index(i, flags_ref):
            step = jnp.clip(i - first, 0, steps - 1)
            if wanted is not None:
                step = step * (flags_ref[0] if wanted else 1 - flags_ref[0])
            return (row + step, 0)

        return index

    operands, specs = [grads], [pl.BlockSpec((tok, depth), grads_at)]
    for first, (choices, at_end, at_middle, steps, only) in zip(firsts, segments):
        for which, (array, row) in enumerate(choices):
            wanted = None if len(choices) == 1 else which == 0
            operands.append(array)
            specs.append(pl.BlockSpec((depth, cols), rows_at(first, steps, row, wanted)))
    if start is not None:
        operands.append(start)
        specs.append(pl.BlockSpec((tok, cols), lambda i, flags_ref: (0, 0)))

    def kernel(flags_ref, grads_ref, *refs):
        i = pl.program_id(0)
        end = flags_ref[0] == 1
        inputs, rest = list(refs[: len(operands) - 1]), refs[len(operands) - 1 :]
        if split:
            keep_ref, give_ref, total_ref, turned_ref = rest
        else:
            (total_ref,) = rest

        @pl.when(i == 0)
        def begin():
            total_ref[...] = jnp.zeros_like(total_ref) if start is None else inputs[-1][...]

        at = 0
        for first, (choices, at_end, at_middle, steps, only) in zip(firsts, segments):
            here = inputs[at : at + len(choices)]
            at += len(choices)
            active = (i >= first) & (i < first + steps)
            if only:
                active = active & (flags_ref[0] == 0)

            @pl.when(active)
            def add(here=here):
                shard = here[0][...]
                if len(here) == 2:
                    shard = jnp.where(end, shard, here[1][...])
                add_dot(total_ref, grads_ref, shard)

        if split:

            @pl.when(i == total - 1)
            def finish():
                turned_ref[...] = total_ref[...].T
                split_rows(turned_ref, keep_ref, give_ref, flags_ref[1])

    whole = lambda i, flags_ref: (0, 0)
    if split:
        out_shape = [jax.ShapeDtypeStruct((cols // 2, tok), jnp.float32)] * 2
        out_specs = [pl.BlockSpec((cols // 2, tok), whole)] * 2
        scratch = [pltpu.VMEM((tok, cols), jnp.float32), pltpu.VMEM((cols, tok), jnp.float32)]
    else:
        out_shape = jax.ShapeDtypeStruct((tok, cols), jnp.float32)
        out_specs = pl.BlockSpec((tok, cols), whole)
        scratch = []
    return pl.pallas_call(
        kernel,
        out_shape=out_shape,
        grid_spec=pltpu.PrefetchScalarGridSpec(
            num_scalar_prefetch=1,
            grid=(total,),
            in_specs=specs,
            out_specs=out_specs,
            scratch_shapes=scratch,
        ),
        compiler_params=PARAMS,
        cost_estimate=SHORT,
    )(flags, *operands)


def both_dots(flags, grads, at_end, at_middle):
    tok = grads.shape[0]
    cols = at_end[0].shape[1]
    step = grads.shape[1] // (3 * STEPS)

    def third_at(first):
        def index(i, flags_ref):
            return (jnp.clip(i - first, 0, STEPS - 1) * (1 - flags_ref[0]), 0)

        return index

    operands = [grads, at_end[0]] + [array for pair in at_middle for array in pair] + [grads]
    specs = [
        pl.BlockSpec((tok, step), lambda i, flags_ref: (0, STEPS + i)),
        pl.BlockSpec((step, cols), lambda i, flags_ref: (at_end[1] + i * flags_ref[0], 0)),
    ]
    for first in (0, STEPS):
        specs += [pl.BlockSpec((step, cols), third_at(first))] * 2
    specs.append(
        pl.BlockSpec(
            (tok, step),
            lambda i, flags_ref: (0, flags_ref[0] * STEPS + jnp.minimum(i, STEPS - 1)),
        )
    )

    def kernel(flags_ref, grads_ref, end_ref, b1_ref, c1_ref, b2_ref, c2_ref, next_ref, *out_refs):
        total_ref, handed_ref, last_ref = out_refs
        i = pl.program_id(0)

        @pl.when(i == 0)
        def begin():
            total_ref[...] = jnp.zeros_like(total_ref)

        @pl.when(i < STEPS)
        def hand_on_next():
            handed_ref[...] = next_ref[...]

        @pl.when(i >= STEPS)
        def hand_on_last():
            last_ref[...] = grads_ref[...]

        @pl.when(flags_ref[0] == 1)
        def one():
            total_ref[:, :cols] += jnp.dot(
                grads_ref[...], end_ref[...], preferred_element_type=jnp.float32
            )

        for first, b_ref, c_ref in ((0, b1_ref, c1_ref), (STEPS, b2_ref, c2_ref)):

            @pl.when((flags_ref[0] == 0) & (i >= first) & (i < first + STEPS))
            def two(b_ref=b_ref, c_ref=c_ref):
                shards = jnp.concatenate([b_ref[...], c_ref[...]], axis=1)
                total_ref[...] += jnp.dot(
                    grads_ref[...], shards, preferred_element_type=jnp.float32
                )

    third = jax.ShapeDtypeStruct((tok, STEPS * step), grads.dtype)
    return pl.pallas_call(
        kernel,
        out_shape=[jax.ShapeDtypeStruct((tok, 2 * cols), jnp.float32), third, third],
        grid_spec=pltpu.PrefetchScalarGridSpec(
            num_scalar_prefetch=1,
            grid=(2 * STEPS,),
            in_specs=specs,
            out_specs=[
                pl.BlockSpec((tok, 2 * cols), lambda i, flags_ref: (0, 0)),
                pl.BlockSpec((tok, step), lambda i, flags_ref: (0, jnp.minimum(i, STEPS - 1))),
                pl.BlockSpec((tok, step), lambda i, flags_ref: (0, jnp.maximum(i - STEPS, 0))),
            ],
        ),
        compiler_params=PARAMS,
        cost_estimate=SHORT,
    )(flags, *operands)


def partner_dots(flags, pieces, shards, grads, shard, start):
    tok = grads.shape[0]
    cols = shards[0][0].shape[1]
    step = shard[2] // STEPS
    count = len(pieces)
    two = start.shape[1] == 2 * cols
    width = tok + len(shards) * count * TILE

    def at(row):
        return lambda i, flags_ref: (row + i, 0)

    whole = lambda i, flags_ref: (0, 0)
    operands, specs = [], []
    for array, row in list(pieces) + list(shards) + [shard[:2]]:
        operands.append(array)
        specs.append(pl.BlockSpec((step, cols), at(row)))
    operands += [grads, start]
    specs.append(pl.BlockSpec((tok, step), lambda i, flags_ref: (0, i)))
    specs.append(pl.BlockSpec(start.shape, whole))

    def kernel(flags_ref, *refs):
        i = pl.program_id(0)
        piece_refs, shard_refs = refs[:count], refs[count : count + len(shards)]
        end_ref, grads_ref, start_ref = refs[count + len(shards) : count + len(shards) + 3]
        keep_ref, give_ref, *rest = refs[len(operands) :]
        if two:
            second_ref, total_ref, sums_ref, turned_ref, wide_ref = rest
        else:
            total_ref, sums_ref, turned_ref, wide_ref = rest

        @pl.when(i == 0)
        def begin():
            total_ref[...] = start_ref[...]
            sums_ref[...] = jnp.zeros_like(sums_ref)

        @pl.when(flags_ref[0] == 1)
        def at_an_end_plane():
            total_ref[:, total_ref.shape[1] - cols :] += jnp.dot(
                grads_ref[...], end_ref[...], preferred_element_type=jnp.float32
            )

        @pl.when(flags_ref[0] == 0)
        def at_a_middle_plane():
            side_by_side = jnp.concatenate([ref[...] for ref in shard_refs], axis=1)
            tokens = jnp.concatenate(
                [
                    jnp.concatenate(
                        [ref[q * TILE : (q + 1) * TILE, :] for q in range(step // TILE)], axis=1
                    )
                    for ref in piece_refs
                ]
            )
            sums_ref[...] += jnp.dot(tokens, side_by_side, preferred_element_type=jnp.float32)
            if two:
                total_ref[...] += jnp.dot(
                    grads_ref[...], side_by_side[:, cols:], preferred_element_type=jnp.float32
                )

        @pl.when(i == STEPS - 1)
        def finish():
            wide_ref[...] = total_ref[:, :cols].T
            split_rows(wide_ref, keep_ref, give_ref, flags_ref[1], pl.ds(0, tok))
            for j in range(len(shards)):
                turned_ref[...] = sums_ref[:, j * cols : (j + 1) * cols].T
                columns = pl.ds(tok + j * count * TILE, count * TILE)
                split_rows(turned_ref, keep_ref, give_ref, flags_ref[1], columns)
            if two:
                second_ref[...] = total_ref[:, cols:]

    out_shape = [jax.ShapeDtypeStruct((cols // 2, width), jnp.float32)] * 2
    out_specs = [pl.BlockSpec((cols // 2, width), whole)] * 2
    if two:
        out_shape.append(jax.ShapeDtypeStruct((tok, cols), jnp.float32))
        out_specs.append(pl.BlockSpec((tok, cols), whole))
    return pl.pallas_call(
        kernel,
        out_shape=out_shape,
        grid_spec=pltpu.PrefetchScalarGridSpec(
            num_scalar_prefetch=1,
            grid=(STEPS,),
            in_specs=specs,
            out_specs=out_specs,
            scratch_shapes=[
                pltpu.VMEM(start.shape, jnp.float32),
                pltpu.VMEM((count * TILE, len(shards) * cols), jnp.float32),
                pltpu.VMEM((cols, count * TILE), jnp.float32),
                pltpu.VMEM((cols, tok), jnp.float32),
            ],
        ),
        compiler_params=PARAMS,
        cost_estimate=SHORT,
    )(flags, *operands)


def stack_blocks(flags, grads, depth):
    tiles = grads.shape[0] // TILE
    firsts = [0] + list(range(tiles // 2, tiles))
    counts = [tiles // 2] + [1] * (tiles // 2)

    def kernel(flags_ref, grads_ref, *out_refs):
        t = pl.program_id(0)
        for first, count, out_ref in zip(firsts, counts, out_refs):

            @pl.when((t >= first) & (t < first + count))
            def copy(out_ref=out_ref):
                for q in range(depth // TILE):
                    here = slice(q * TILE, (q + 1) * TILE)
                    out_ref[here, :] = grads_ref[:, here]

    def place(first, count):
        return lambda t, flags_ref: (jnp.clip(t - first, 0, count - 1), 0)

    return pl.pallas_call(
        kernel,
        out_shape=[jax.ShapeDtypeStruct((count * depth, TILE), grads.dtype) for count in counts],
        grid_spec=pltpu.PrefetchScalarGridSpec(
            num_scalar_prefetch=1,
            grid=(tiles,),
            in_specs=[pl.BlockSpec((TILE, depth), lambda t, flags_ref: (t, 0))],
            out_specs=[
                pl.BlockSpec((depth, TILE), place(first, count))
                for first, count in zip(firsts, counts)
            ],
        ),
        compiler_params=PARAMS,
        cost_estimate=SHORT,
    )(flags, grads)


def input_dots(flags, acts, shards):
    tok, depth = acts.shape
    cols = shards[0][0][0].shape[1]
    operands, specs = [acts], [pl.BlockSpec((tok, depth), lambda i, flags_ref: (0, 0))]
    for choices in shards:
        for array, row in choices:
            operands.append(array)
            specs.append(pl.BlockSpec((depth, cols), lambda i, flags_ref, row=row: (row, 0)))

    def kernel(flags_ref, acts_ref, *refs):
        i = pl.program_id(0)
        inputs = list(refs[: len(operands) - 1])
        keep_ref, give_ref, part_ref = refs[len(operands) - 1 :]
        at = 0
        for slot, choices in enumerate(shards):
            here = inputs[at : at + len(choices)]
            at += len(choices)

            @pl.when(i == slot)
            def add(here=here):
                shard = here[0][...]
                if len(here) == 2:
                    shard = jnp.where(flags_ref[0] == 1, shard, here[1][...])
                part_ref[...] = jnp.dot(acts_ref[...], shard, preferred_element_type=jnp.float32)

        split_rows(part_ref, keep_ref, give_ref, flags_ref[1])

    place = pl.BlockSpec((tok // 2, cols), lambda i, flags_ref: (0, flags_ref[2 + i]))
    return pl.pallas_call(
        kernel,
        out_shape=[jax.ShapeDtypeStruct((tok // 2, cols * len(shards)), jnp.float32)] * 2,
        grid_spec=pltpu.PrefetchScalarGridSpec(
            num_scalar_prefetch=1,
            grid=(len(shards),),
            in_specs=specs,
            out_specs=[place, place],
            scratch_shapes=[pltpu.VMEM((tok, cols), jnp.float32)],
        ),
        compiler_params=PARAMS,
        cost_estimate=SHORT,
    )(flags, *operands)


def line_plan(acts, grads, basis_in, basis_out, eigval, test_grads, pair_tiles, last_rows):
    plane = lax.axis_index("cand")
    end = (plane == 0) | (plane == 3)
    tok_rows = acts.shape[0]
    cols = basis_in.shape[1]
    tiles_here = tok_rows // TILE
    slim = cols // 4
    depth = basis_out.shape[0] // 3
    rows_in = basis_in.shape[0]

    def pick(at_end, at_middle):
        return jnp.where(end, at_end, at_middle)

    def side(at_end, at_middle):
        return lax.ppermute(pick(at_end, at_middle), "cand", SIDE)

    among, far = [], []
    for at in range(16):
        between = 4 <= at < 12
        across = 12 - 4 * (at // 4) + at % 4
        among.append((at, across if between else at ^ 1))
        far.append((at, at ^ 1 if between else across))

    def middle(x):
        return lax.ppermute(x, ALL, among)

    at_b = jnp.where(end, plane ^ 2, plane ^ 3)
    at_c = jnp.where(end, plane ^ 3, plane ^ 2)
    rep = lax.axis_index("rep")
    flags = jnp.stack([end.astype(jnp.int32), rep, plane, plane ^ 1, at_b, at_c])

    rows = lax.dynamic_slice_in_dim(basis_out, jnp.where(end, 0, depth), 2 * depth, 0)
    s0 = lax.ppermute(basis_in, "cand", SIDE)
    m0 = middle(basis_in)
    s12 = lax.ppermute(rows, "cand", SIDE)
    second = basis_out[depth : 2 * depth]
    m2 = middle(second)
    started = after(flags, rows, second)
    stacked, *more_stacked = stack_blocks(started, grads, depth)
    part_own = feature_dots(
        after(started, s0, m0), grads, [([(basis_out, 0)], 0, 0, 3 * STEPS, False)]
    )
    precond = (test_grads.astype(jnp.float32) / (eigval + damping)).astype(jnp.bfloat16)
    m1 = middle(after(s0, m0))
    third = jnp.concatenate([basis_out[2 * depth :], basis_out[: 2 * rows_in - depth]])
    s3 = side(third, jnp.concatenate([m0, m1]))
    m3 = middle(after(basis_out[2 * depth :], precond, stacked, *more_stacked, *part_own))
    m5 = middle(s12[depth:])
    to_s45 = pick(stacked, jnp.concatenate([m2, m3]))
    s45 = lax.ppermute(to_s45, "cand", SIDE)
    m6 = middle(s3[:depth])
    m4 = middle(after(basis_out[:depth], m5))
    s6 = side(more_stacked[0], m5)
    to_s7 = pick(after(more_stacked[1], s45), m6)
    s7 = lax.ppermute(to_s7, "cand", SIDE)
    m7 = middle(after(s12[:depth], m6))

    part_in = input_dots(
        after(flags, s3, m5),
        acts,
        [[(basis_in, 0)], [(s0, 0)], [(s3, 0), (m0, 0)], [(s3, 1), (m1, 0)]],
    )
    part_a = feature_dots(
        after(flags, *part_in),
        grads,
        [
            ([(s12, 0)], STEPS, 0, 2 * STEPS, False),
            ([(s3, 0)], 2 * STEPS, 2 * STEPS, STEPS, True),
        ],
    )
    totals, next_grads, last_grads = both_dots(after(flags, to_s7, s45, *part_a), grads, (s45, 0), ((m2, m5), (m3, m6)))
    parts = [jnp.concatenate(part, axis=1) for part in zip(part_own, part_a)]
    keep_a, give_a = after(parts, m4, totals)
    core_a = swap(give_a, "rep")

    shards = [(basis_out, 0), (m4, 0), (m7, 0)]
    *part_b, part_c = partner_dots(
        after(flags, totals, core_a),
        [(s45, 0), (s45, STEPS), (s6, 0)],
        shards,
        next_grads,
        (s6, 0, depth),
        totals,
    )
    keep_in, give_in = after(part_in, part_c)
    core_in = keep_in + swap(give_in, "rep")
    give_in = core_in.astype(jnp.bfloat16)
    rows_here = chip_sum(core_in, give_in).astype(jnp.bfloat16)
    rows_there = swap(rows_here, "rep")
    rot_in = all_rows(rows_here, rows_there)
    rot_in = rot_in.reshape(tiles_here, TILE, 4 * cols)
    keep_b, give_b = part_b
    keep_b, give_b = chip_parts(
        jnp.concatenate([keep_a, keep_b], axis=1),
        jnp.concatenate([core_a, swap(give_b, "rep")], axis=1),
    )
    sums = chip_sum(keep_b, give_b)
    sum_own, sum_a, sum_b = [sums[:, i * tok_rows : (i + 1) * tok_rows] for i in range(3)]
    sums = sums[:, 3 * tok_rows :].astype(jnp.bfloat16)
    keep_last, give_last = partner_dots(
        after(flags, part_c, give_b, give_in),
        [(s7, 0)],
        shards,
        last_grads,
        (s7, 0, depth),
        part_c,
    )
    keep_last, give_last = chip_parts(keep_last, swap(give_last, "rep"))
    sum_last = chip_sum(keep_last, give_last)
    sum_c, sum_last = sum_last[:, :tok_rows], sum_last[:, tok_rows:].astype(jnp.bfloat16)

    rowmask, ignored = tile_layout(pair_tiles, last_rows, plane * tiles_here, tiles_here, TILE)
    keep = rowmask.reshape(1, tok_rows).astype(jnp.bfloat16)

    def tile_prods(rot_out):
        return jnp.einsum(
            "etr,tra->tea",
            (rot_out.astype(jnp.bfloat16) * keep).reshape(slim, tiles_here, TILE),
            rot_in,
            preferred_element_type=jnp.float32,
        ).astype(jnp.bfloat16)

    def pair_scores(*received):
        prods = jnp.concatenate([x for x, source in received])
        scores = jnp.einsum("tea,jea->tj", prods, precond, preferred_element_type=jnp.float32)
        onehot = jnp.concatenate([
            tile_layout(pair_tiles, last_rows, source * tiles_here, tiles_here, TILE)[1]
            for x, source in received
        ])
        return jnp.sum(jnp.where(onehot[:, :, None], scores[:, None, :], 0.0), axis=0)

    prods_own = tile_prods(sum_own)
    prods_middle = tile_prods(sum_b)
    from_middle = middle(prods_middle)
    last = lax.ppermute(after(sum_last, rows_there), "cand", SIDE)
    back = after(lax.ppermute(sums, "cand", SIDE), give_last)
    few = tok_rows - TILE

    def with_partner(whole, at):
        parts = [back[:, at * few : (at + 1) * few], last[:, at * TILE : (at + 1) * TILE]]
        parts = jnp.concatenate(parts, axis=1).astype(jnp.float32)
        return whole + jnp.where(end, parts, 0.0)

    prods_a = tile_prods(with_partner(sum_a, 0))
    prods_b = tile_prods(with_partner(sum_b, 1))
    prods_c = tile_prods(with_partner(sum_c, 2))
    to_two = pick(prods_b, prods_c)
    from_two = lax.ppermute(to_two, "cand", TWO)
    from_far = lax.ppermute(after(prods_c, to_two, from_middle), ALL, far)
    from_side = lax.ppermute(after(prods_a, to_two), "cand", SIDE)
    total = pair_scores(
        (prods_own, plane),
        (from_side, plane ^ 1),
        (from_two, plane ^ 2),
        (pick(from_far, from_middle), plane ^ 3),
    )
    return final_sum(total)


def final_sum(total):
    npairs, ntest = total.shape
    blocks = total.reshape(4, npairs // 4, 4, ntest // 4).transpose(0, 2, 1, 3)
    blocks = blocks.reshape(16, npairs // 4, ntest // 4)
    return jnp.sum(lax.all_to_all(blocks, ALL, 0, 0, tiled=True), axis=0)


def gather_plan(acts, grads, basis_in, basis_out, eigval, test_grads, pair_tiles, last_rows):
    ncand = lax.axis_size("cand")
    nfeat = lax.axis_size(FEAT)
    tok_rows = acts.shape[0]
    width_in = basis_in.shape[1] * ncand
    width_out = basis_out.shape[1] * ncand
    slim = width_out // (ncand * nfeat)
    part_in = jnp.dot(
        acts,
        lax.all_gather(basis_in, "cand", axis=1, tiled=True),
        preferred_element_type=jnp.float32,
    )
    part_out = jnp.dot(
        grads,
        lax.all_gather(basis_out, "cand", axis=1, tiled=True),
        preferred_element_type=jnp.float32,
    )
    part_out = part_out.reshape(tok_rows, ncand, nfeat, slim).transpose(0, 2, 1, 3)
    part_out = part_out.reshape(tok_rows, nfeat * ncand * slim)
    summed_in, summed_out = lax.psum((part_in, part_out), FEAT)
    own = lax.dynamic_slice_in_dim(
        summed_out, lax.axis_index(FEAT) * (ncand * slim), ncand * slim, 1
    )
    rot_in = summed_in.astype(jnp.bfloat16)
    rot_out = own.astype(jnp.bfloat16)
    tiles_here = tok_rows // TILE
    rowmask, ignored = tile_layout(
        pair_tiles, last_rows, lax.axis_index("cand") * tiles_here, tiles_here, TILE
    )
    masked = rot_out.reshape(tiles_here, TILE, ncand * slim) * rowmask[:, :, None].astype(
        jnp.bfloat16
    )
    prods = jnp.einsum(
        "tre,tra->tea",
        masked,
        rot_in.reshape(tiles_here, TILE, width_in),
        preferred_element_type=jnp.float32,
    ).astype(jnp.bfloat16)
    prods = prods.reshape(tiles_here, ncand, slim, width_in)
    received = lax.all_to_all(prods, "cand", split_axis=1, concat_axis=0, tiled=True)
    all_tiles = received.shape[0]
    received = received.reshape(all_tiles, slim, width_in)
    precond = (test_grads.astype(jnp.float32) / (eigval + damping)).astype(jnp.bfloat16)
    tile_part = jnp.einsum("tea,jea->tj", received, precond, preferred_element_type=jnp.float32)
    ignored_mask, onehot = tile_layout(pair_tiles, last_rows, 0, all_tiles, TILE)
    pair_part = jnp.dot(onehot.astype(jnp.float32).T, tile_part, precision=lax.Precision.HIGHEST)
    npairs = pair_part.shape[0]
    ntest = pair_part.shape[1]
    total = lax.psum(pair_part, ("cand", "eig", "rep"))
    rows = lax.dynamic_slice_in_dim(
        total, lax.axis_index("cand") * (npairs // ncand), npairs // ncand, 0
    )
    return lax.dynamic_slice_in_dim(
        rows, lax.axis_index(FEAT) * (ntest // nfeat), ntest // nfeat, 1
    )


def solution(mesh):
    in_specs = (
        P(("groups", "cand"), ("eig", "rep")),
        P(("groups", "cand"), ("eig", "rep")),
        P(("groups", "eig", "rep"), "cand"),
        P(("groups", "eig", "rep"), "cand"),
        P(("groups", "cand", "eig", "rep"), None),
        P("groups", ("cand", "eig", "rep"), None),
        P("groups"),
        P("groups"),
    )
    out_specs = P(("groups", "cand"), ("eig", "rep"))
    sizes = (mesh.shape["cand"], mesh.shape["eig"], mesh.shape["rep"])
    per_device = line_plan if sizes == (4, 2, 2) else gather_plan
    return jax.shard_map(
        per_device, mesh=mesh, in_specs=in_specs, out_specs=out_specs, check_vma=False
    )
```

```python
import jax
import jax.numpy as jnp
from jax import lax
from jax.experimental import pallas as pl
from jax.experimental.pallas import tpu as pltpu
from jax.sharding import PartitionSpec as P

TILE = 128
FEAT = ("eig", "rep")
ALL = ("cand", "eig", "rep")
STEPS = 3
PARAMS = pltpu.CompilerParams(vmem_limit_bytes=20 << 20)
SHORT = pl.CostEstimate(flops=1, bytes_accessed=1, transcendentals=0)
SIDE = ((0, 1), (1, 0), (2, 3), (3, 2))
TWO = ((0, 2), (2, 0), (1, 3), (3, 1))

damping = 0.01


def tile_layout(pair_tiles, last_rows, first_tile, count, tile_rows):
    tiles = first_tile + jnp.arange(count, dtype=jnp.int32)
    ends = jnp.cumsum(pair_tiles)
    owner = jnp.sum((ends[None, :] <= tiles[:, None]).astype(jnp.int32), axis=1)
    onehot = owner[:, None] == jnp.arange(pair_tiles.shape[0], dtype=jnp.int32)[None, :]
    last_of = jnp.sum(jnp.where(onehot, last_rows[None, :], 0), axis=1)
    end_of = jnp.sum(jnp.where(onehot, ends[None, :], 0), axis=1)
    limit = jnp.where(tiles == end_of - 1, last_of, tile_rows)
    rowmask = jnp.arange(tile_rows, dtype=jnp.int32)[None, :] < limit[:, None]
    return (rowmask, onehot)


def after(x, *earlier):
    return lax.optimization_barrier((x, *earlier))[0]


def swap(x, axis_name):
    return lax.ppermute(x, axis_name, [(0, 1), (1, 0)])


def halves(x, axis_name):
    first = lax.axis_index(axis_name) == 0
    low, high = jnp.split(x, 2)
    return jnp.where(first, low, high), jnp.where(first, high, low)


def chip_parts(keep, received):
    keep, their_keep = halves(keep, "eig")
    received, their_received = halves(received, "eig")
    return keep + received, (their_keep + their_received).astype(jnp.bfloat16)


def chip_sum(keep, give):
    return keep + swap(give, "eig").astype(jnp.float32)


def all_rows(mine, other):
    first = lax.axis_index("rep") == 0
    mine, other = mine.reshape(2, -1, mine.shape[1]), other.reshape(2, -1, mine.shape[1])
    whole = jnp.stack([jnp.where(first, mine, other), jnp.where(first, other, mine)], axis=1)
    return whole.reshape(-1, whole.shape[-1])


def split_rows(full_ref, keep_ref, give_ref, rep, columns=None):
    rows = full_ref.shape[0] // 4
    columns = slice(None) if columns is None else columns
    for e in range(2):
        here = pl.ds(e * rows, rows)
        mine = pl.ds(pl.multiple_of((2 * e + rep) * rows, rows), rows)
        theirs = pl.ds(pl.multiple_of((2 * e + 1 - rep) * rows, rows), rows)
        keep_ref[here, columns] = full_ref[mine, :]
        give_ref[here, columns] = full_ref[theirs, :]


def add_dot(total_ref, rows_ref, shard):
    half = total_ref.shape[0] // 2
    for here in (pl.ds(0, half), pl.ds(half, half)):
        total_ref[here, :] += jnp.dot(
            rows_ref[here, :], shard, preferred_element_type=jnp.float32
        )


def feature_dots(flags, grads, segments, start=None, split=True):
    tok = grads.shape[0]
    cols = segments[0][0][0][0].shape[1]
    depth = grads.shape[1] // (3 * STEPS)
    firsts = [sum(s[3] for s in segments[:at]) for at in range(len(segments))]
    total = sum(s[3] for s in segments)

    def grads_at(i, flags_ref):
        at = 0
        for first, (choices, at_end, at_middle, steps, only) in zip(firsts, segments):
            base = at_end + flags_ref[0] * 0 if at_end == at_middle else (
                flags_ref[0] * at_end + (1 - flags_ref[0]) * at_middle
            )
            at = jnp.where(i >= first, base + i - first, at)
        return (0, at)

    def rows_at(first, steps, row, wanted):
        def index(i, flags_ref):
            step = jnp.clip(i - first, 0, steps - 1)
            if wanted is not None:
                step = step * (flags_ref[0] if wanted else 1 - flags_ref[0])
            return (row + step, 0)

        return index

    operands, specs = [grads], [pl.BlockSpec((tok, depth), grads_at)]
    for first, (choices, at_end, at_middle, steps, only) in zip(firsts, segments):
        for which, (array, row) in enumerate(choices):
            wanted = None if len(choices) == 1 else which == 0
            operands.append(array)
            specs.append(pl.BlockSpec((depth, cols), rows_at(first, steps, row, wanted)))
    if start is not None:
        operands.append(start)
        specs.append(pl.BlockSpec((tok, cols), lambda i, flags_ref: (0, 0)))

    def kernel(flags_ref, grads_ref, *refs):
        i = pl.program_id(0)
        end = flags_ref[0] == 1
        inputs, rest = list(refs[: len(operands) - 1]), refs[len(operands) - 1 :]
        if split:
            keep_ref, give_ref, total_ref, turned_ref = rest
        else:
            (total_ref,) = rest

        @pl.when(i == 0)
        def begin():
            total_ref[...] = jnp.zeros_like(total_ref) if start is None else inputs[-1][...]

        at = 0
        for first, (choices, at_end, at_middle, steps, only) in zip(firsts, segments):
            here = inputs[at : at + len(choices)]
            at += len(choices)
            active = (i >= first) & (i < first + steps)
            if only:
                active = active & (flags_ref[0] == 0)

            @pl.when(active)
            def add(here=here):
                shard = here[0][...]
                if len(here) == 2:
                    shard = jnp.where(end, shard, here[1][...])
                add_dot(total_ref, grads_ref, shard)

        if split:

            @pl.when(i == total - 1)
            def finish():
                turned_ref[...] = total_ref[...].T
                split_rows(turned_ref, keep_ref, give_ref, flags_ref[1])

    whole = lambda i, flags_ref: (0, 0)
    if split:
        out_shape = [jax.ShapeDtypeStruct((cols // 2, tok), jnp.float32)] * 2
        out_specs = [pl.BlockSpec((cols // 2, tok), whole)] * 2
        scratch = [pltpu.VMEM((tok, cols), jnp.float32), pltpu.VMEM((cols, tok), jnp.float32)]
    else:
        out_shape = jax.ShapeDtypeStruct((tok, cols), jnp.float32)
        out_specs = pl.BlockSpec((tok, cols), whole)
        scratch = []
    return pl.pallas_call(
        kernel,
        out_shape=out_shape,
        grid_spec=pltpu.PrefetchScalarGridSpec(
            num_scalar_prefetch=1,
            grid=(total,),
            in_specs=specs,
            out_specs=out_specs,
            scratch_shapes=scratch,
        ),
        compiler_params=PARAMS,
        cost_estimate=SHORT,
    )(flags, *operands)


def both_dots(flags, grads, at_end, at_middle):
    tok = grads.shape[0]
    cols = at_end[0].shape[1]
    step = grads.shape[1] // (3 * STEPS)

    def third_at(first):
        def index(i, flags_ref):
            return (jnp.clip(i - first, 0, STEPS - 1) * (1 - flags_ref[0]), 0)

        return index

    operands = [grads, at_end[0]] + [array for pair in at_middle for array in pair] + [grads]
    specs = [
        pl.BlockSpec((tok, step), lambda i, flags_ref: (0, STEPS + i)),
        pl.BlockSpec((step, cols), lambda i, flags_ref: (at_end[1] + i * flags_ref[0], 0)),
    ]
    for first in (0, STEPS):
        specs += [pl.BlockSpec((step, cols), third_at(first))] * 2
    specs.append(
        pl.BlockSpec(
            (tok, step),
            lambda i, flags_ref: (0, flags_ref[0] * STEPS + jnp.minimum(i, STEPS - 1)),
        )
    )

    def kernel(flags_ref, grads_ref, end_ref, b1_ref, c1_ref, b2_ref, c2_ref, next_ref, *out_refs):
        total_ref, handed_ref, last_ref = out_refs
        i = pl.program_id(0)

        @pl.when(i == 0)
        def begin():
            total_ref[...] = jnp.zeros_like(total_ref)

        @pl.when(i < STEPS)
        def hand_on_next():
            handed_ref[...] = next_ref[...]

        @pl.when(i >= STEPS)
        def hand_on_last():
            last_ref[...] = grads_ref[...]

        @pl.when(flags_ref[0] == 1)
        def one():
            total_ref[:, :cols] += jnp.dot(
                grads_ref[...], end_ref[...], preferred_element_type=jnp.float32
            )

        for first, b_ref, c_ref in ((0, b1_ref, c1_ref), (STEPS, b2_ref, c2_ref)):

            @pl.when((flags_ref[0] == 0) & (i >= first) & (i < first + STEPS))
            def two(b_ref=b_ref, c_ref=c_ref):
                shards = jnp.concatenate([b_ref[...], c_ref[...]], axis=1)
                total_ref[...] += jnp.dot(
                    grads_ref[...], shards, preferred_element_type=jnp.float32
                )

    third = jax.ShapeDtypeStruct((tok, STEPS * step), grads.dtype)
    return pl.pallas_call(
        kernel,
        out_shape=[jax.ShapeDtypeStruct((tok, 2 * cols), jnp.float32), third, third],
        grid_spec=pltpu.PrefetchScalarGridSpec(
            num_scalar_prefetch=1,
            grid=(2 * STEPS,),
            in_specs=specs,
            out_specs=[
                pl.BlockSpec((tok, 2 * cols), lambda i, flags_ref: (0, 0)),
                pl.BlockSpec((tok, step), lambda i, flags_ref: (0, jnp.minimum(i, STEPS - 1))),
                pl.BlockSpec((tok, step), lambda i, flags_ref: (0, jnp.maximum(i - STEPS, 0))),
            ],
        ),
        compiler_params=PARAMS,
        cost_estimate=SHORT,
    )(flags, *operands)


def partner_dots(flags, pieces, shards, grads, shard, start):
    tok = grads.shape[0]
    cols = shards[0][0].shape[1]
    step = shard[2] // STEPS
    count = len(pieces)
    two = start.shape[1] == 2 * cols
    width = tok + len(shards) * count * TILE

    def at(row):
        return lambda i, flags_ref: (row + i, 0)

    whole = lambda i, flags_ref: (0, 0)
    operands, specs = [], []
    for array, row in list(pieces) + list(shards) + [shard[:2]]:
        operands.append(array)
        specs.append(pl.BlockSpec((step, cols), at(row)))
    operands += [grads, start]
    specs.append(pl.BlockSpec((tok, step), lambda i, flags_ref: (0, i)))
    specs.append(pl.BlockSpec(start.shape, whole))

    def kernel(flags_ref, *refs):
        i = pl.program_id(0)
        piece_refs, shard_refs = refs[:count], refs[count : count + len(shards)]
        end_ref, grads_ref, start_ref = refs[count + len(shards) : count + len(shards) + 3]
        keep_ref, give_ref, *rest = refs[len(operands) :]
        if two:
            second_ref, total_ref, sums_ref, turned_ref, wide_ref = rest
        else:
            total_ref, sums_ref, turned_ref, wide_ref = rest

        @pl.when(i == 0)
        def begin():
            total_ref[...] = start_ref[...]
            sums_ref[...] = jnp.zeros_like(sums_ref)

        @pl.when(flags_ref[0] == 1)
        def at_an_end_plane():
            total_ref[:, total_ref.shape[1] - cols :] += jnp.dot(
                grads_ref[...], end_ref[...], preferred_element_type=jnp.float32
            )

        @pl.when(flags_ref[0] == 0)
        def at_a_middle_plane():
            side_by_side = jnp.concatenate([ref[...] for ref in shard_refs], axis=1)
            tokens = jnp.concatenate(
                [
                    jnp.concatenate(
                        [ref[q * TILE : (q + 1) * TILE, :] for q in range(step // TILE)], axis=1
                    )
                    for ref in piece_refs
                ]
            )
            sums_ref[...] += jnp.dot(tokens, side_by_side, preferred_element_type=jnp.float32)
            if two:
                total_ref[...] += jnp.dot(
                    grads_ref[...], side_by_side[:, cols:], preferred_element_type=jnp.float32
                )

        @pl.when(i == STEPS - 1)
        def finish():
            wide_ref[...] = total_ref[:, :cols].T
            split_rows(wide_ref, keep_ref, give_ref, flags_ref[1], pl.ds(0, tok))
            for j in range(len(shards)):
                turned_ref[...] = sums_ref[:, j * cols : (j + 1) * cols].T
                columns = pl.ds(tok + j * count * TILE, count * TILE)
                split_rows(turned_ref, keep_ref, give_ref, flags_ref[1], columns)
            if two:
                second_ref[...] = total_ref[:, cols:]

    out_shape = [jax.ShapeDtypeStruct((cols // 2, width), jnp.float32)] * 2
    out_specs = [pl.BlockSpec((cols // 2, width), whole)] * 2
    if two:
        out_shape.append(jax.ShapeDtypeStruct((tok, cols), jnp.float32))
        out_specs.append(pl.BlockSpec((tok, cols), whole))
    return pl.pallas_call(
        kernel,
        out_shape=out_shape,
        grid_spec=pltpu.PrefetchScalarGridSpec(
            num_scalar_prefetch=1,
            grid=(STEPS,),
            in_specs=specs,
            out_specs=out_specs,
            scratch_shapes=[
                pltpu.VMEM(start.shape, jnp.float32),
                pltpu.VMEM((count * TILE, len(shards) * cols), jnp.float32),
                pltpu.VMEM((cols, count * TILE), jnp.float32),
                pltpu.VMEM((cols, tok), jnp.float32),
            ],
        ),
        compiler_params=PARAMS,
        cost_estimate=SHORT,
    )(flags, *operands)


def stack_blocks(flags, grads, depth):
    tiles = grads.shape[0] // TILE
    firsts = [0] + list(range(tiles // 2, tiles))
    counts = [tiles // 2] + [1] * (tiles // 2)

    def kernel(flags_ref, grads_ref, *out_refs):
        t = pl.program_id(0)
        for first, count, out_ref in zip(firsts, counts, out_refs):

            @pl.when((t >= first) & (t < first + count))
            def copy(out_ref=out_ref):
                for q in range(depth // TILE):
                    here = slice(q * TILE, (q + 1) * TILE)
                    out_ref[here, :] = grads_ref[:, here]

    def place(first, count):
        return lambda t, flags_ref: (jnp.clip(t - first, 0, count - 1), 0)

    return pl.pallas_call(
        kernel,
        out_shape=[jax.ShapeDtypeStruct((count * depth, TILE), grads.dtype) for count in counts],
        grid_spec=pltpu.PrefetchScalarGridSpec(
            num_scalar_prefetch=1,
            grid=(tiles,),
            in_specs=[pl.BlockSpec((TILE, depth), lambda t, flags_ref: (t, 0))],
            out_specs=[
                pl.BlockSpec((depth, TILE), place(first, count))
                for first, count in zip(firsts, counts)
            ],
        ),
        compiler_params=PARAMS,
        cost_estimate=SHORT,
    )(flags, grads)


def input_dots(flags, acts, shards):
    tok, depth = acts.shape
    cols = shards[0][0][0].shape[1]
    operands, specs = [acts], [pl.BlockSpec((tok, depth), lambda i, flags_ref: (0, 0))]
    for choices in shards:
        for array, row in choices:
            operands.append(array)
            specs.append(pl.BlockSpec((depth, cols), lambda i, flags_ref, row=row: (row, 0)))

    def kernel(flags_ref, acts_ref, *refs):
        i = pl.program_id(0)
        inputs = list(refs[: len(operands) - 1])
        keep_ref, give_ref, part_ref = refs[len(operands) - 1 :]
        at = 0
        for slot, choices in enumerate(shards):
            here = inputs[at : at + len(choices)]
            at += len(choices)

            @pl.when(i == slot)
            def add(here=here):
                shard = here[0][...]
                if len(here) == 2:
                    shard = jnp.where(flags_ref[0] == 1, shard, here[1][...])
                part_ref[...] = jnp.dot(acts_ref[...], shard, preferred_element_type=jnp.float32)

        split_rows(part_ref, keep_ref, give_ref, flags_ref[1])

    place = pl.BlockSpec((tok // 2, cols), lambda i, flags_ref: (0, flags_ref[2 + i]))
    return pl.pallas_call(
        kernel,
        out_shape=[jax.ShapeDtypeStruct((tok // 2, cols * len(shards)), jnp.float32)] * 2,
        grid_spec=pltpu.PrefetchScalarGridSpec(
            num_scalar_prefetch=1,
            grid=(len(shards),),
            in_specs=specs,
            out_specs=[place, place],
            scratch_shapes=[pltpu.VMEM((tok, cols), jnp.float32)],
        ),
        compiler_params=PARAMS,
        cost_estimate=SHORT,
    )(flags, *operands)


def line_plan(acts, grads, basis_in, basis_out, eigval, test_grads, pair_tiles, last_rows):
    plane = lax.axis_index("cand")
    end = (plane == 0) | (plane == 3)
    tok_rows = acts.shape[0]
    cols = basis_in.shape[1]
    tiles_here = tok_rows // TILE
    slim = cols // 4
    depth = basis_out.shape[0] // 3
    rows_in = basis_in.shape[0]

    def pick(at_end, at_middle):
        return jnp.where(end, at_end, at_middle)

    def side(at_end, at_middle):
        return lax.ppermute(pick(at_end, at_middle), "cand", SIDE)

    among, far = [], []
    for at in range(16):
        between = 4 <= at < 12
        across = 12 - 4 * (at // 4) + at % 4
        among.append((at, across if between else at ^ 1))
        far.append((at, at ^ 1 if between else across))

    def middle(x):
        return lax.ppermute(x, ALL, among)

    at_b = jnp.where(end, plane ^ 2, plane ^ 3)
    at_c = jnp.where(end, plane ^ 3, plane ^ 2)
    rep = lax.axis_index("rep")
    flags = jnp.stack([end.astype(jnp.int32), rep, plane, plane ^ 1, at_b, at_c])

    rows = lax.dynamic_slice_in_dim(basis_out, jnp.where(end, 0, depth), 2 * depth, 0)
    s0 = lax.ppermute(basis_in, "cand", SIDE)
    m0 = middle(basis_in)
    s12 = lax.ppermute(rows, "cand", SIDE)
    second = basis_out[depth : 2 * depth]
    m2 = middle(second)
    started = after(flags, rows, second)
    stacked, *more_stacked = stack_blocks(started, grads, depth)
    part_own = feature_dots(
        after(started, s0, m0), grads, [([(basis_out, 0)], 0, 0, 3 * STEPS, False)]
    )
    precond = (test_grads.astype(jnp.float32) / (eigval + damping)).astype(jnp.bfloat16)
    m1 = middle(after(s0, m0))
    third = jnp.concatenate([basis_out[2 * depth :], basis_out[: 2 * rows_in - depth]])
    s3 = side(third, jnp.concatenate([m0, m1]))
    m3 = middle(after(basis_out[2 * depth :], precond, stacked, *more_stacked, *part_own))
    m5 = middle(s12[depth:])
    to_s45 = pick(stacked, jnp.concatenate([m2, m3]))
    s45 = lax.ppermute(to_s45, "cand", SIDE)
    m6 = middle(s3[:depth])
    m4 = middle(after(basis_out[:depth], m5))
    s6 = side(more_stacked[0], m5)
    to_s7 = pick(after(more_stacked[1], s45), m6)
    s7 = lax.ppermute(to_s7, "cand", SIDE)
    m7 = middle(after(s12[:depth], m6))

    part_in = input_dots(
        after(flags, s3, m5),
        acts,
        [[(basis_in, 0)], [(s0, 0)], [(s3, 0), (m0, 0)], [(s3, 1), (m1, 0)]],
    )
    part_a = feature_dots(
        after(flags, *part_in),
        grads,
        [
            ([(s12, 0)], STEPS, 0, 2 * STEPS, False),
            ([(s3, 0)], 2 * STEPS, 2 * STEPS, STEPS, True),
        ],
    )
    totals, next_grads, last_grads = both_dots(after(flags, to_s7, s45, *part_a), grads, (s45, 0), ((m2, m5), (m3, m6)))
    parts = [jnp.concatenate(part, axis=1) for part in zip(part_own, part_a)]
    keep_a, give_a = after(parts, m4, totals)
    core_a = swap(give_a, "rep")

    shards = [(basis_out, 0), (m4, 0), (m7, 0)]
    *part_b, part_c = partner_dots(
        after(flags, totals, core_a),
        [(s45, 0), (s45, STEPS), (s6, 0)],
        shards,
        next_grads,
        (s6, 0, depth),
        totals,
    )
    keep_in, give_in = after(part_in, part_c)
    core_in = keep_in + swap(give_in, "rep")
    give_in = core_in.astype(jnp.bfloat16)
    rows_here = chip_sum(core_in, give_in).astype(jnp.bfloat16)
    rows_there = swap(rows_here, "rep")
    rot_in = all_rows(rows_here, rows_there)
    rot_in = rot_in.reshape(tiles_here, TILE, 4 * cols)
    keep_b, give_b = part_b
    keep_b, give_b = chip_parts(
        jnp.concatenate([keep_a, keep_b], axis=1),
        jnp.concatenate([core_a, swap(give_b, "rep")], axis=1),
    )
    sums = chip_sum(keep_b, give_b)
    sum_own, sum_a, sum_b = [sums[:, i * tok_rows : (i + 1) * tok_rows] for i in range(3)]
    sums = sums[:, 3 * tok_rows :].astype(jnp.bfloat16)
    keep_last, give_last = partner_dots(
        after(flags, part_c, give_b, give_in),
        [(s7, 0)],
        shards,
        last_grads,
        (s7, 0, depth),
        part_c,
    )
    keep_last, give_last = chip_parts(keep_last, swap(give_last, "rep"))
    sum_last = chip_sum(keep_last, give_last)
    sum_c, sum_last = sum_last[:, :tok_rows], sum_last[:, tok_rows:].astype(jnp.bfloat16)

    rowmask, ignored = tile_layout(pair_tiles, last_rows, plane * tiles_here, tiles_here, TILE)
    keep = rowmask.reshape(1, tok_rows).astype(jnp.bfloat16)

    def tile_prods(rot_out):
        return jnp.einsum(
            "etr,tra->tea",
            (rot_out.astype(jnp.bfloat16) * keep).reshape(slim, tiles_here, TILE),
            rot_in,
            preferred_element_type=jnp.float32,
        ).astype(jnp.bfloat16)

    def pair_scores(*received):
        prods = jnp.concatenate([x for x, source in received])
        scores = jnp.einsum("tea,jea->tj", prods, precond, preferred_element_type=jnp.float32)
        onehot = jnp.concatenate([
            tile_layout(pair_tiles, last_rows, source * tiles_here, tiles_here, TILE)[1]
            for x, source in received
        ])
        return jnp.sum(jnp.where(onehot[:, :, None], scores[:, None, :], 0.0), axis=0)

    prods_own = tile_prods(sum_own)
    prods_middle = tile_prods(sum_b)
    from_middle = middle(prods_middle)
    last = after(lax.ppermute(after(sum_last, rows_there), "cand", SIDE), prods_middle)
    back = after(lax.ppermute(sums, "cand", SIDE), rows_there)
    few = tok_rows - TILE

    def with_partner(whole, at):
        parts = [back[:, at * few : (at + 1) * few], last[:, at * TILE : (at + 1) * TILE]]
        parts = jnp.concatenate(parts, axis=1).astype(jnp.float32)
        return whole + jnp.where(end, parts, 0.0)

    prods_a = tile_prods(with_partner(sum_a, 0))
    prods_b = tile_prods(with_partner(sum_b, 1))
    prods_c = tile_prods(with_partner(sum_c, 2))
    to_two = pick(prods_b, prods_c)
    from_two = lax.ppermute(to_two, "cand", TWO)
    from_far = lax.ppermute(after(prods_c, to_two), ALL, far)
    from_side = lax.ppermute(after(prods_a, to_two), "cand", SIDE)
    total = pair_scores(
        (prods_own, plane),
        (from_side, plane ^ 1),
        (from_two, plane ^ 2),
        (pick(from_far, from_middle), plane ^ 3),
    )
    return final_sum(total)


def final_sum(total):
    npairs, ntest = total.shape
    blocks = total.reshape(4, npairs // 4, 4, ntest // 4).transpose(0, 2, 1, 3)
    blocks = blocks.reshape(16, npairs // 4, ntest // 4)
    return jnp.sum(lax.all_to_all(blocks, ALL, 0, 0, tiled=True), axis=0)


def gather_plan(acts, grads, basis_in, basis_out, eigval, test_grads, pair_tiles, last_rows):
    ncand = lax.axis_size("cand")
    nfeat = lax.axis_size(FEAT)
    tok_rows = acts.shape[0]
    width_in = basis_in.shape[1] * ncand
    width_out = basis_out.shape[1] * ncand
    slim = width_out // (ncand * nfeat)
    part_in = jnp.dot(
        acts,
        lax.all_gather(basis_in, "cand", axis=1, tiled=True),
        preferred_element_type=jnp.float32,
    )
    part_out = jnp.dot(
        grads,
        lax.all_gather(basis_out, "cand", axis=1, tiled=True),
        preferred_element_type=jnp.float32,
    )
    part_out = part_out.reshape(tok_rows, ncand, nfeat, slim).transpose(0, 2, 1, 3)
    part_out = part_out.reshape(tok_rows, nfeat * ncand * slim)
    summed_in, summed_out = lax.psum((part_in, part_out), FEAT)
    own = lax.dynamic_slice_in_dim(
        summed_out, lax.axis_index(FEAT) * (ncand * slim), ncand * slim, 1
    )
    rot_in = summed_in.astype(jnp.bfloat16)
    rot_out = own.astype(jnp.bfloat16)
    tiles_here = tok_rows // TILE
    rowmask, ignored = tile_layout(
        pair_tiles, last_rows, lax.axis_index("cand") * tiles_here, tiles_here, TILE
    )
    masked = rot_out.reshape(tiles_here, TILE, ncand * slim) * rowmask[:, :, None].astype(
        jnp.bfloat16
    )
    prods = jnp.einsum(
        "tre,tra->tea",
        masked,
        rot_in.reshape(tiles_here, TILE, width_in),
        preferred_element_type=jnp.float32,
    ).astype(jnp.bfloat16)
    prods = prods.reshape(tiles_here, ncand, slim, width_in)
    received = lax.all_to_all(prods, "cand", split_axis=1, concat_axis=0, tiled=True)
    all_tiles = received.shape[0]
    received = received.reshape(all_tiles, slim, width_in)
    precond = (test_grads.astype(jnp.float32) / (eigval + damping)).astype(jnp.bfloat16)
    tile_part = jnp.einsum("tea,jea->tj", received, precond, preferred_element_type=jnp.float32)
    ignored_mask, onehot = tile_layout(pair_tiles, last_rows, 0, all_tiles, TILE)
    pair_part = jnp.dot(onehot.astype(jnp.float32).T, tile_part, precision=lax.Precision.HIGHEST)
    npairs = pair_part.shape[0]
    ntest = pair_part.shape[1]
    total = lax.psum(pair_part, ("cand", "eig", "rep"))
    rows = lax.dynamic_slice_in_dim(
        total, lax.axis_index("cand") * (npairs // ncand), npairs // ncand, 0
    )
    return lax.dynamic_slice_in_dim(
        rows, lax.axis_index(FEAT) * (ntest // nfeat), ntest // nfeat, 1
    )


def solution(mesh):
    in_specs = (
        P(("groups", "cand"), ("eig", "rep")),
        P(("groups", "cand"), ("eig", "rep")),
        P(("groups", "eig", "rep"), "cand"),
        P(("groups", "eig", "rep"), "cand"),
        P(("groups", "cand", "eig", "rep"), None),
        P("groups", ("cand", "eig", "rep"), None),
        P("groups"),
        P("groups"),
    )
    out_specs = P(("groups", "cand"), ("eig", "rep"))
    sizes = (mesh.shape["cand"], mesh.shape["eig"], mesh.shape["rep"])
    per_device = line_plan if sizes == (4, 2, 2) else gather_plan
    return jax.shard_map(
        per_device, mesh=mesh, in_specs=in_specs, out_specs=out_specs, check_vma=False
    )
```

```python
import jax
import jax.numpy as jnp
from jax import lax
from jax.experimental import pallas as pl
from jax.experimental.pallas import tpu as pltpu
from jax.sharding import PartitionSpec as P

TILE = 128
FEAT = ("eig", "rep")
ALL = ("cand", "eig", "rep")
STEPS = 3
PARAMS = pltpu.CompilerParams(vmem_limit_bytes=20 << 20)
SHORT = pl.CostEstimate(flops=1, bytes_accessed=1, transcendentals=0)
SIDE = ((0, 1), (1, 0), (2, 3), (3, 2))
TWO = ((0, 2), (2, 0), (1, 3), (3, 1))

damping = 0.01


def tile_layout(pair_tiles, last_rows, first_tile, count, tile_rows):
    tiles = first_tile + jnp.arange(count, dtype=jnp.int32)
    ends = jnp.cumsum(pair_tiles)
    owner = jnp.sum((ends[None, :] <= tiles[:, None]).astype(jnp.int32), axis=1)
    onehot = owner[:, None] == jnp.arange(pair_tiles.shape[0], dtype=jnp.int32)[None, :]
    last_of = jnp.sum(jnp.where(onehot, last_rows[None, :], 0), axis=1)
    end_of = jnp.sum(jnp.where(onehot, ends[None, :], 0), axis=1)
    limit = jnp.where(tiles == end_of - 1, last_of, tile_rows)
    rowmask = jnp.arange(tile_rows, dtype=jnp.int32)[None, :] < limit[:, None]
    return (rowmask, onehot)


def after(x, *earlier):
    return lax.optimization_barrier((x, *earlier))[0]


def swap(x, axis_name):
    return lax.ppermute(x, axis_name, [(0, 1), (1, 0)])


def halves(x, axis_name):
    first = lax.axis_index(axis_name) == 0
    low, high = jnp.split(x, 2)
    return jnp.where(first, low, high), jnp.where(first, high, low)


def chip_parts(keep, received):
    keep, their_keep = halves(keep, "eig")
    received, their_received = halves(received, "eig")
    return keep + received, (their_keep + their_received).astype(jnp.bfloat16)


def chip_sum(keep, give):
    return keep + swap(give, "eig").astype(jnp.float32)


def all_rows(mine, other):
    first = lax.axis_index("rep") == 0
    mine, other = mine.reshape(2, -1, mine.shape[1]), other.reshape(2, -1, mine.shape[1])
    whole = jnp.stack([jnp.where(first, mine, other), jnp.where(first, other, mine)], axis=1)
    return whole.reshape(-1, whole.shape[-1])


def split_rows(full_ref, keep_ref, give_ref, rep, columns=None):
    rows = full_ref.shape[0] // 4
    columns = slice(None) if columns is None else columns
    for e in range(2):
        here = pl.ds(e * rows, rows)
        mine = pl.ds(pl.multiple_of((2 * e + rep) * rows, rows), rows)
        theirs = pl.ds(pl.multiple_of((2 * e + 1 - rep) * rows, rows), rows)
        keep_ref[here, columns] = full_ref[mine, :]
        give_ref[here, columns] = full_ref[theirs, :]


def add_dot(total_ref, rows_ref, shard):
    half = total_ref.shape[0] // 2
    for here in (pl.ds(0, half), pl.ds(half, half)):
        total_ref[here, :] += jnp.dot(
            rows_ref[here, :], shard, preferred_element_type=jnp.float32
        )


def feature_dots(flags, grads, segments, start=None, split=True):
    tok = grads.shape[0]
    cols = segments[0][0][0][0].shape[1]
    depth = grads.shape[1] // (3 * STEPS)
    firsts = [sum(s[3] for s in segments[:at]) for at in range(len(segments))]
    total = sum(s[3] for s in segments)

    def grads_at(i, flags_ref):
        at = 0
        for first, (choices, at_end, at_middle, steps, only) in zip(firsts, segments):
            base = at_end + flags_ref[0] * 0 if at_end == at_middle else (
                flags_ref[0] * at_end + (1 - flags_ref[0]) * at_middle
            )
            at = jnp.where(i >= first, base + i - first, at)
        return (0, at)

    def rows_at(first, steps, row, wanted):
        def index(i, flags_ref):
            step = jnp.clip(i - first, 0, steps - 1)
            if wanted is not None:
                step = step * (flags_ref[0] if wanted else 1 - flags_ref[0])
            return (row + step, 0)

        return index

    operands, specs = [grads], [pl.BlockSpec((tok, depth), grads_at)]
    for first, (choices, at_end, at_middle, steps, only) in zip(firsts, segments):
        for which, (array, row) in enumerate(choices):
            wanted = None if len(choices) == 1 else which == 0
            operands.append(array)
            specs.append(pl.BlockSpec((depth, cols), rows_at(first, steps, row, wanted)))
    if start is not None:
        operands.append(start)
        specs.append(pl.BlockSpec((tok, cols), lambda i, flags_ref: (0, 0)))

    def kernel(flags_ref, grads_ref, *refs):
        i = pl.program_id(0)
        end = flags_ref[0] == 1
        inputs, rest = list(refs[: len(operands) - 1]), refs[len(operands) - 1 :]
        if split:
            keep_ref, give_ref, total_ref, turned_ref = rest
        else:
            (total_ref,) = rest

        @pl.when(i == 0)
        def begin():
            total_ref[...] = jnp.zeros_like(total_ref) if start is None else inputs[-1][...]

        at = 0
        for first, (choices, at_end, at_middle, steps, only) in zip(firsts, segments):
            here = inputs[at : at + len(choices)]
            at += len(choices)
            active = (i >= first) & (i < first + steps)
            if only:
                active = active & (flags_ref[0] == 0)

            @pl.when(active)
            def add(here=here):
                shard = here[0][...]
                if len(here) == 2:
                    shard = jnp.where(end, shard, here[1][...])
                add_dot(total_ref, grads_ref, shard)

        if split:

            @pl.when(i == total - 1)
            def finish():
                turned_ref[...] = total_ref[...].T
                split_rows(turned_ref, keep_ref, give_ref, flags_ref[1])

    whole = lambda i, flags_ref: (0, 0)
    if split:
        out_shape = [jax.ShapeDtypeStruct((cols // 2, tok), jnp.float32)] * 2
        out_specs = [pl.BlockSpec((cols // 2, tok), whole)] * 2
        scratch = [pltpu.VMEM((tok, cols), jnp.float32), pltpu.VMEM((cols, tok), jnp.float32)]
    else:
        out_shape = jax.ShapeDtypeStruct((tok, cols), jnp.float32)
        out_specs = pl.BlockSpec((tok, cols), whole)
        scratch = []
    return pl.pallas_call(
        kernel,
        out_shape=out_shape,
        grid_spec=pltpu.PrefetchScalarGridSpec(
            num_scalar_prefetch=1,
            grid=(total,),
            in_specs=specs,
            out_specs=out_specs,
            scratch_shapes=scratch,
        ),
        compiler_params=PARAMS,
        cost_estimate=SHORT,
    )(flags, *operands)


def both_dots(flags, grads, at_end, at_middle):
    tok = grads.shape[0]
    cols = at_end[0].shape[1]
    step = grads.shape[1] // (3 * STEPS)

    def third_at(first):
        def index(i, flags_ref):
            return (jnp.clip(i - first, 0, STEPS - 1) * (1 - flags_ref[0]), 0)

        return index

    operands = [grads, at_end[0]] + [array for pair in at_middle for array in pair] + [grads]
    specs = [
        pl.BlockSpec((tok, step), lambda i, flags_ref: (0, STEPS + i)),
        pl.BlockSpec((step, cols), lambda i, flags_ref: (at_end[1] + i * flags_ref[0], 0)),
    ]
    for first in (0, STEPS):
        specs += [pl.BlockSpec((step, cols), third_at(first))] * 2
    specs.append(
        pl.BlockSpec(
            (tok, step),
            lambda i, flags_ref: (0, flags_ref[0] * STEPS + jnp.minimum(i, STEPS - 1)),
        )
    )

    def kernel(flags_ref, grads_ref, end_ref, b1_ref, c1_ref, b2_ref, c2_ref, next_ref, *out_refs):
        total_ref, handed_ref, last_ref = out_refs
        i = pl.program_id(0)

        @pl.when(i == 0)
        def begin():
            total_ref[...] = jnp.zeros_like(total_ref)

        @pl.when(i < STEPS)
        def hand_on_next():
            handed_ref[...] = next_ref[...]

        @pl.when(i >= STEPS)
        def hand_on_last():
            last_ref[...] = grads_ref[...]

        @pl.when(flags_ref[0] == 1)
        def one():
            total_ref[:, :cols] += jnp.dot(
                grads_ref[...], end_ref[...], preferred_element_type=jnp.float32
            )

        for first, b_ref, c_ref in ((0, b1_ref, c1_ref), (STEPS, b2_ref, c2_ref)):

            @pl.when((flags_ref[0] == 0) & (i >= first) & (i < first + STEPS))
            def two(b_ref=b_ref, c_ref=c_ref):
                shards = jnp.concatenate([b_ref[...], c_ref[...]], axis=1)
                total_ref[...] += jnp.dot(
                    grads_ref[...], shards, preferred_element_type=jnp.float32
                )

    third = jax.ShapeDtypeStruct((tok, STEPS * step), grads.dtype)
    return pl.pallas_call(
        kernel,
        out_shape=[jax.ShapeDtypeStruct((tok, 2 * cols), jnp.float32), third, third],
        grid_spec=pltpu.PrefetchScalarGridSpec(
            num_scalar_prefetch=1,
            grid=(2 * STEPS,),
            in_specs=specs,
            out_specs=[
                pl.BlockSpec((tok, 2 * cols), lambda i, flags_ref: (0, 0)),
                pl.BlockSpec((tok, step), lambda i, flags_ref: (0, jnp.minimum(i, STEPS - 1))),
                pl.BlockSpec((tok, step), lambda i, flags_ref: (0, jnp.maximum(i - STEPS, 0))),
            ],
        ),
        compiler_params=PARAMS,
        cost_estimate=SHORT,
    )(flags, *operands)


def partner_dots(flags, pieces, shards, grads, shard, start):
    tok = grads.shape[0]
    cols = shards[0][0].shape[1]
    step = shard[2] // STEPS
    count = len(pieces)
    two = start.shape[1] == 2 * cols
    width = tok + len(shards) * count * TILE

    def at(row):
        return lambda i, flags_ref: (row + i, 0)

    whole = lambda i, flags_ref: (0, 0)
    operands, specs = [], []
    for array, row in list(pieces) + list(shards) + [shard[:2]]:
        operands.append(array)
        specs.append(pl.BlockSpec((step, cols), at(row)))
    operands += [grads, start]
    specs.append(pl.BlockSpec((tok, step), lambda i, flags_ref: (0, i)))
    specs.append(pl.BlockSpec(start.shape, whole))

    def kernel(flags_ref, *refs):
        i = pl.program_id(0)
        piece_refs, shard_refs = refs[:count], refs[count : count + len(shards)]
        end_ref, grads_ref, start_ref = refs[count + len(shards) : count + len(shards) + 3]
        keep_ref, give_ref, *rest = refs[len(operands) :]
        if two:
            second_ref, total_ref, sums_ref, turned_ref, wide_ref = rest
        else:
            total_ref, sums_ref, turned_ref, wide_ref = rest

        @pl.when(i == 0)
        def begin():
            total_ref[...] = start_ref[...]
            sums_ref[...] = jnp.zeros_like(sums_ref)

        @pl.when(flags_ref[0] == 1)
        def at_an_end_plane():
            total_ref[:, total_ref.shape[1] - cols :] += jnp.dot(
                grads_ref[...], end_ref[...], preferred_element_type=jnp.float32
            )

        @pl.when(flags_ref[0] == 0)
        def at_a_middle_plane():
            side_by_side = jnp.concatenate([ref[...] for ref in shard_refs], axis=1)
            tokens = jnp.concatenate(
                [
                    jnp.concatenate(
                        [ref[q * TILE : (q + 1) * TILE, :] for q in range(step // TILE)], axis=1
                    )
                    for ref in piece_refs
                ]
            )
            sums_ref[...] += jnp.dot(tokens, side_by_side, preferred_element_type=jnp.float32)
            if two:
                total_ref[...] += jnp.dot(
                    grads_ref[...], side_by_side[:, cols:], preferred_element_type=jnp.float32
                )

        @pl.when(i == STEPS - 1)
        def finish():
            wide_ref[...] = total_ref[:, :cols].T
            split_rows(wide_ref, keep_ref, give_ref, flags_ref[1], pl.ds(0, tok))
            for j in range(len(shards)):
                turned_ref[...] = sums_ref[:, j * cols : (j + 1) * cols].T
                columns = pl.ds(tok + j * count * TILE, count * TILE)
                split_rows(turned_ref, keep_ref, give_ref, flags_ref[1], columns)
            if two:
                second_ref[...] = total_ref[:, cols:]

    out_shape = [jax.ShapeDtypeStruct((cols // 2, width), jnp.float32)] * 2
    out_specs = [pl.BlockSpec((cols // 2, width), whole)] * 2
    if two:
        out_shape.append(jax.ShapeDtypeStruct((tok, cols), jnp.float32))
        out_specs.append(pl.BlockSpec((tok, cols), whole))
    return pl.pallas_call(
        kernel,
        out_shape=out_shape,
        grid_spec=pltpu.PrefetchScalarGridSpec(
            num_scalar_prefetch=1,
            grid=(STEPS,),
            in_specs=specs,
            out_specs=out_specs,
            scratch_shapes=[
                pltpu.VMEM(start.shape, jnp.float32),
                pltpu.VMEM((count * TILE, len(shards) * cols), jnp.float32),
                pltpu.VMEM((cols, count * TILE), jnp.float32),
                pltpu.VMEM((cols, tok), jnp.float32),
            ],
        ),
        compiler_params=PARAMS,
        cost_estimate=SHORT,
    )(flags, *operands)


def stack_blocks(flags, grads, depth):
    tiles = grads.shape[0] // TILE
    firsts = [0] + list(range(tiles // 2, tiles))
    counts = [tiles // 2] + [1] * (tiles // 2)

    def kernel(flags_ref, grads_ref, *out_refs):
        t = pl.program_id(0)
        for first, count, out_ref in zip(firsts, counts, out_refs):

            @pl.when((t >= first) & (t < first + count))
            def copy(out_ref=out_ref):
                for q in range(depth // TILE):
                    here = slice(q * TILE, (q + 1) * TILE)
                    out_ref[here, :] = grads_ref[:, here]

    def place(first, count):
        return lambda t, flags_ref: (jnp.clip(t - first, 0, count - 1), 0)

    return pl.pallas_call(
        kernel,
        out_shape=[jax.ShapeDtypeStruct((count * depth, TILE), grads.dtype) for count in counts],
        grid_spec=pltpu.PrefetchScalarGridSpec(
            num_scalar_prefetch=1,
            grid=(tiles,),
            in_specs=[pl.BlockSpec((TILE, depth), lambda t, flags_ref: (t, 0))],
            out_specs=[
                pl.BlockSpec((depth, TILE), place(first, count))
                for first, count in zip(firsts, counts)
            ],
        ),
        compiler_params=PARAMS,
        cost_estimate=SHORT,
    )(flags, grads)


def input_dots(flags, acts, shards):
    tok, depth = acts.shape
    cols = shards[0][0][0].shape[1]
    operands, specs = [acts], [pl.BlockSpec((tok, depth), lambda i, flags_ref: (0, 0))]
    for choices in shards:
        for array, row in choices:
            operands.append(array)
            specs.append(pl.BlockSpec((depth, cols), lambda i, flags_ref, row=row: (row, 0)))

    def kernel(flags_ref, acts_ref, *refs):
        i = pl.program_id(0)
        inputs = list(refs[: len(operands) - 1])
        keep_ref, give_ref, part_ref = refs[len(operands) - 1 :]
        at = 0
        for slot, choices in enumerate(shards):
            here = inputs[at : at + len(choices)]
            at += len(choices)

            @pl.when(i == slot)
            def add(here=here):
                shard = here[0][...]
                if len(here) == 2:
                    shard = jnp.where(flags_ref[0] == 1, shard, here[1][...])
                part_ref[...] = jnp.dot(acts_ref[...], shard, preferred_element_type=jnp.float32)

        split_rows(part_ref, keep_ref, give_ref, flags_ref[1])

    place = pl.BlockSpec((tok // 2, cols), lambda i, flags_ref: (0, flags_ref[2 + i]))
    return pl.pallas_call(
        kernel,
        out_shape=[jax.ShapeDtypeStruct((tok // 2, cols * len(shards)), jnp.float32)] * 2,
        grid_spec=pltpu.PrefetchScalarGridSpec(
            num_scalar_prefetch=1,
            grid=(len(shards),),
            in_specs=specs,
            out_specs=[place, place],
            scratch_shapes=[pltpu.VMEM((tok, cols), jnp.float32)],
        ),
        compiler_params=PARAMS,
        cost_estimate=SHORT,
    )(flags, *operands)


def line_plan(acts, grads, basis_in, basis_out, eigval, test_grads, pair_tiles, last_rows):
    plane = lax.axis_index("cand")
    end = (plane == 0) | (plane == 3)
    tok_rows = acts.shape[0]
    cols = basis_in.shape[1]
    tiles_here = tok_rows // TILE
    slim = cols // 4
    depth = basis_out.shape[0] // 3
    rows_in = basis_in.shape[0]

    def pick(at_end, at_middle):
        return jnp.where(end, at_end, at_middle)

    def side(at_end, at_middle):
        return lax.ppermute(pick(at_end, at_middle), "cand", SIDE)

    among, far = [], []
    for at in range(16):
        between = 4 <= at < 12
        across = 12 - 4 * (at // 4) + at % 4
        among.append((at, across if between else at ^ 1))
        far.append((at, at ^ 1 if between else across))

    def middle(x):
        return lax.ppermute(x, ALL, among)

    at_b = jnp.where(end, plane ^ 2, plane ^ 3)
    at_c = jnp.where(end, plane ^ 3, plane ^ 2)
    rep = lax.axis_index("rep")
    flags = jnp.stack([end.astype(jnp.int32), rep, plane, plane ^ 1, at_b, at_c])

    rows = lax.dynamic_slice_in_dim(basis_out, jnp.where(end, 0, depth), 2 * depth, 0)
    s0 = lax.ppermute(basis_in, "cand", SIDE)
    m0 = middle(basis_in)
    s12 = lax.ppermute(rows, "cand", SIDE)
    second = basis_out[depth : 2 * depth]
    m2 = middle(second)
    started = after(flags, rows, second)
    stacked, *more_stacked = stack_blocks(started, grads, depth)
    part_own = feature_dots(
        after(started, s0, m0), grads, [([(basis_out, 0)], 0, 0, 3 * STEPS, False)]
    )
    precond = (test_grads.astype(jnp.float32) / (eigval + damping)).astype(jnp.bfloat16)
    m1 = middle(after(s0, m0))
    third = jnp.concatenate([basis_out[2 * depth :], basis_out[: 2 * rows_in - depth]])
    s3 = side(third, jnp.concatenate([m0, m1]))
    m3 = middle(after(basis_out[2 * depth :], precond, stacked, *more_stacked, *part_own))
    m5 = middle(s12[depth:])
    to_s45 = pick(stacked, jnp.concatenate([m2, m3]))
    s45 = lax.ppermute(to_s45, "cand", SIDE)
    m6 = middle(s3[:depth])
    m4 = middle(after(basis_out[:depth], m5))
    s6 = side(more_stacked[0], m5)
    to_s7 = pick(after(more_stacked[1], s45), m6)
    s7 = lax.ppermute(to_s7, "cand", SIDE)
    m7 = middle(after(s12[:depth], m6))

    part_in = input_dots(
        after(flags, s3, m5),
        acts,
        [[(basis_in, 0)], [(s0, 0)], [(s3, 0), (m0, 0)], [(s3, 1), (m1, 0)]],
    )
    part_a = feature_dots(
        after(flags, *part_in),
        grads,
        [
            ([(s12, 0)], STEPS, 0, 2 * STEPS, False),
            ([(s3, 0)], 2 * STEPS, 2 * STEPS, STEPS, True),
        ],
    )
    totals, next_grads, last_grads = both_dots(after(flags, to_s7, s45, *part_a), grads, (s45, 0), ((m2, m5), (m3, m6)))
    keep_in, give_in = after(part_in, s6, m7, totals)
    core_in = keep_in + swap(give_in, "rep")
    give_in = core_in.astype(jnp.bfloat16)
    rows_here = chip_sum(core_in, give_in).astype(jnp.bfloat16)
    rows_there = swap(rows_here, "rep")
    rot_in = all_rows(rows_here, rows_there)
    rot_in = rot_in.reshape(tiles_here, TILE, 4 * cols)
    parts = [jnp.concatenate(part, axis=1) for part in zip(part_own, part_a)]
    keep_a, give_a = after(parts, m4, totals)
    core_a = swap(give_a, "rep")

    shards = [(basis_out, 0), (m4, 0), (m7, 0)]
    *part_b, part_c = partner_dots(
        after(flags, totals, core_a, core_in),
        [(s45, 0), (s45, STEPS), (s6, 0)],
        shards,
        next_grads,
        (s6, 0, depth),
        totals,
    )
    keep_b, give_b = part_b
    keep_b, give_b = chip_parts(
        jnp.concatenate([keep_a, keep_b], axis=1),
        jnp.concatenate([core_a, swap(give_b, "rep")], axis=1),
    )
    sums = chip_sum(keep_b, give_b)
    sum_own, sum_a, sum_b = [sums[:, i * tok_rows : (i + 1) * tok_rows] for i in range(3)]
    sums = sums[:, 3 * tok_rows :].astype(jnp.bfloat16)
    keep_last, give_last = partner_dots(
        after(flags, part_c, give_b),
        [(s7, 0)],
        shards,
        last_grads,
        (s7, 0, depth),
        part_c,
    )
    keep_last, give_last = chip_parts(keep_last, swap(give_last, "rep"))
    sum_last = chip_sum(keep_last, give_last)
    sum_c, sum_last = sum_last[:, :tok_rows], sum_last[:, tok_rows:].astype(jnp.bfloat16)

    rowmask, ignored = tile_layout(pair_tiles, last_rows, plane * tiles_here, tiles_here, TILE)
    keep = rowmask.reshape(1, tok_rows).astype(jnp.bfloat16)

    def tile_prods(rot_out):
        return jnp.einsum(
            "etr,tra->tea",
            (rot_out.astype(jnp.bfloat16) * keep).reshape(slim, tiles_here, TILE),
            rot_in,
            preferred_element_type=jnp.float32,
        ).astype(jnp.bfloat16)

    def pair_scores(*received):
        prods = jnp.concatenate([x for x, source in received])
        scores = jnp.einsum("tea,jea->tj", prods, precond, preferred_element_type=jnp.float32)
        onehot = jnp.concatenate([
            tile_layout(pair_tiles, last_rows, source * tiles_here, tiles_here, TILE)[1]
            for x, source in received
        ])
        return jnp.sum(jnp.where(onehot[:, :, None], scores[:, None, :], 0.0), axis=0)

    prods_own = tile_prods(sum_own)
    prods_middle = tile_prods(sum_b)
    from_middle = middle(prods_middle)
    last = after(lax.ppermute(after(sum_last, rows_there), "cand", SIDE), prods_middle)
    back = after(lax.ppermute(sums, "cand", SIDE), sum_last)
    few = tok_rows - TILE

    def with_partner(whole, at):
        parts = [back[:, at * few : (at + 1) * few], last[:, at * TILE : (at + 1) * TILE]]
        parts = jnp.concatenate(parts, axis=1).astype(jnp.float32)
        return whole + jnp.where(end, parts, 0.0)

    prods_a = tile_prods(with_partner(sum_a, 0))
    prods_b = tile_prods(with_partner(sum_b, 1))
    prods_c = tile_prods(with_partner(sum_c, 2))
    to_two = pick(prods_b, prods_c)
    from_two = lax.ppermute(to_two, "cand", TWO)
    from_far = lax.ppermute(after(prods_c, to_two), ALL, far)
    from_side = lax.ppermute(after(prods_a, to_two), "cand", SIDE)
    total = pair_scores(
        (prods_own, plane),
        (from_side, plane ^ 1),
        (from_two, plane ^ 2),
        (pick(from_far, from_middle), plane ^ 3),
    )
    return final_sum(total)


def final_sum(total):
    npairs, ntest = total.shape
    blocks = total.reshape(4, npairs // 4, 4, ntest // 4).transpose(0, 2, 1, 3)
    blocks = blocks.reshape(16, npairs // 4, ntest // 4)
    return jnp.sum(lax.all_to_all(blocks, ALL, 0, 0, tiled=True), axis=0)


def gather_plan(acts, grads, basis_in, basis_out, eigval, test_grads, pair_tiles, last_rows):
    ncand = lax.axis_size("cand")
    nfeat = lax.axis_size(FEAT)
    tok_rows = acts.shape[0]
    width_in = basis_in.shape[1] * ncand
    width_out = basis_out.shape[1] * ncand
    slim = width_out // (ncand * nfeat)
    part_in = jnp.dot(
        acts,
        lax.all_gather(basis_in, "cand", axis=1, tiled=True),
        preferred_element_type=jnp.float32,
    )
    part_out = jnp.dot(
        grads,
        lax.all_gather(basis_out, "cand", axis=1, tiled=True),
        preferred_element_type=jnp.float32,
    )
    part_out = part_out.reshape(tok_rows, ncand, nfeat, slim).transpose(0, 2, 1, 3)
    part_out = part_out.reshape(tok_rows, nfeat * ncand * slim)
    summed_in, summed_out = lax.psum((part_in, part_out), FEAT)
    own = lax.dynamic_slice_in_dim(
        summed_out, lax.axis_index(FEAT) * (ncand * slim), ncand * slim, 1
    )
    rot_in = summed_in.astype(jnp.bfloat16)
    rot_out = own.astype(jnp.bfloat16)
    tiles_here = tok_rows // TILE
    rowmask, ignored = tile_layout(
        pair_tiles, last_rows, lax.axis_index("cand") * tiles_here, tiles_here, TILE
    )
    masked = rot_out.reshape(tiles_here, TILE, ncand * slim) * rowmask[:, :, None].astype(
        jnp.bfloat16
    )
    prods = jnp.einsum(
        "tre,tra->tea",
        masked,
        rot_in.reshape(tiles_here, TILE, width_in),
        preferred_element_type=jnp.float32,
    ).astype(jnp.bfloat16)
    prods = prods.reshape(tiles_here, ncand, slim, width_in)
    received = lax.all_to_all(prods, "cand", split_axis=1, concat_axis=0, tiled=True)
    all_tiles = received.shape[0]
    received = received.reshape(all_tiles, slim, width_in)
    precond = (test_grads.astype(jnp.float32) / (eigval + damping)).astype(jnp.bfloat16)
    tile_part = jnp.einsum("tea,jea->tj", received, precond, preferred_element_type=jnp.float32)
    ignored_mask, onehot = tile_layout(pair_tiles, last_rows, 0, all_tiles, TILE)
    pair_part = jnp.dot(onehot.astype(jnp.float32).T, tile_part, precision=lax.Precision.HIGHEST)
    npairs = pair_part.shape[0]
    ntest = pair_part.shape[1]
    total = lax.psum(pair_part, ("cand", "eig", "rep"))
    rows = lax.dynamic_slice_in_dim(
        total, lax.axis_index("cand") * (npairs // ncand), npairs // ncand, 0
    )
    return lax.dynamic_slice_in_dim(
        rows, lax.axis_index(FEAT) * (ntest // nfeat), ntest // nfeat, 1
    )


def solution(mesh):
    in_specs = (
        P(("groups", "cand"), ("eig", "rep")),
        P(("groups", "cand"), ("eig", "rep")),
        P(("groups", "eig", "rep"), "cand"),
        P(("groups", "eig", "rep"), "cand"),
        P(("groups", "cand", "eig", "rep"), None),
        P("groups", ("cand", "eig", "rep"), None),
        P("groups"),
        P("groups"),
    )
    out_specs = P(("groups", "cand"), ("eig", "rep"))
    sizes = (mesh.shape["cand"], mesh.shape["eig"], mesh.shape["rep"])
    per_device = line_plan if sizes == (4, 2, 2) else gather_plan
    return jax.shard_map(
        per_device, mesh=mesh, in_specs=in_specs, out_specs=out_specs, check_vma=False
    )
```

```python
import jax
import jax.numpy as jnp
from jax import lax
from jax.experimental import pallas as pl
from jax.experimental.pallas import tpu as pltpu
from jax.sharding import PartitionSpec as P

TILE = 128
FEAT = ("eig", "rep")
ALL = ("cand", "eig", "rep")
STEPS = 3
PARAMS = pltpu.CompilerParams(vmem_limit_bytes=20 << 20)
SHORT = pl.CostEstimate(flops=1, bytes_accessed=1, transcendentals=0)
SIDE = ((0, 1), (1, 0), (2, 3), (3, 2))
TWO = ((0, 2), (2, 0), (1, 3), (3, 1))

damping = 0.01


def tile_layout(pair_tiles, last_rows, first_tile, count, tile_rows):
    tiles = first_tile + jnp.arange(count, dtype=jnp.int32)
    ends = jnp.cumsum(pair_tiles)
    owner = jnp.sum((ends[None, :] <= tiles[:, None]).astype(jnp.int32), axis=1)
    onehot = owner[:, None] == jnp.arange(pair_tiles.shape[0], dtype=jnp.int32)[None, :]
    last_of = jnp.sum(jnp.where(onehot, last_rows[None, :], 0), axis=1)
    end_of = jnp.sum(jnp.where(onehot, ends[None, :], 0), axis=1)
    limit = jnp.where(tiles == end_of - 1, last_of, tile_rows)
    rowmask = jnp.arange(tile_rows, dtype=jnp.int32)[None, :] < limit[:, None]
    return (rowmask, onehot)


def after(x, *earlier):
    return lax.optimization_barrier((x, *earlier))[0]


def swap(x, axis_name):
    return lax.ppermute(x, axis_name, [(0, 1), (1, 0)])


def halves(x, axis_name):
    first = lax.axis_index(axis_name) == 0
    low, high = jnp.split(x, 2)
    return jnp.where(first, low, high), jnp.where(first, high, low)


def chip_parts(keep, received):
    keep, their_keep = halves(keep, "eig")
    received, their_received = halves(received, "eig")
    return keep + received, (their_keep + their_received).astype(jnp.bfloat16)


def chip_sum(keep, give):
    return keep + swap(give, "eig").astype(jnp.float32)


def all_rows(mine, other):
    first = lax.axis_index("rep") == 0
    mine, other = mine.reshape(2, -1, mine.shape[1]), other.reshape(2, -1, mine.shape[1])
    whole = jnp.stack([jnp.where(first, mine, other), jnp.where(first, other, mine)], axis=1)
    return whole.reshape(-1, whole.shape[-1])


def split_rows(full_ref, keep_ref, give_ref, rep, columns=None):
    rows = full_ref.shape[0] // 4
    columns = slice(None) if columns is None else columns
    for e in range(2):
        here = pl.ds(e * rows, rows)
        mine = pl.ds(pl.multiple_of((2 * e + rep) * rows, rows), rows)
        theirs = pl.ds(pl.multiple_of((2 * e + 1 - rep) * rows, rows), rows)
        keep_ref[here, columns] = full_ref[mine, :]
        give_ref[here, columns] = full_ref[theirs, :]


def add_dot(total_ref, rows_ref, shard):
    half = total_ref.shape[0] // 2
    for here in (pl.ds(0, half), pl.ds(half, half)):
        total_ref[here, :] += jnp.dot(
            rows_ref[here, :], shard, preferred_element_type=jnp.float32
        )


def feature_dots(flags, grads, segments, start=None, split=True):
    tok = grads.shape[0]
    cols = segments[0][0][0][0].shape[1]
    depth = grads.shape[1] // (3 * STEPS)
    firsts = [sum(s[3] for s in segments[:at]) for at in range(len(segments))]
    total = sum(s[3] for s in segments)

    def grads_at(i, flags_ref):
        at = 0
        for first, (choices, at_end, at_middle, steps, only) in zip(firsts, segments):
            base = at_end + flags_ref[0] * 0 if at_end == at_middle else (
                flags_ref[0] * at_end + (1 - flags_ref[0]) * at_middle
            )
            at = jnp.where(i >= first, base + i - first, at)
        return (0, at)

    def rows_at(first, steps, row, wanted):
        def index(i, flags_ref):
            step = jnp.clip(i - first, 0, steps - 1)
            if wanted is not None:
                step = step * (flags_ref[0] if wanted else 1 - flags_ref[0])
            return (row + step, 0)

        return index

    operands, specs = [grads], [pl.BlockSpec((tok, depth), grads_at)]
    for first, (choices, at_end, at_middle, steps, only) in zip(firsts, segments):
        for which, (array, row) in enumerate(choices):
            wanted = None if len(choices) == 1 else which == 0
            operands.append(array)
            specs.append(pl.BlockSpec((depth, cols), rows_at(first, steps, row, wanted)))
    if start is not None:
        operands.append(start)
        specs.append(pl.BlockSpec((tok, cols), lambda i, flags_ref: (0, 0)))

    def kernel(flags_ref, grads_ref, *refs):
        i = pl.program_id(0)
        end = flags_ref[0] == 1
        inputs, rest = list(refs[: len(operands) - 1]), refs[len(operands) - 1 :]
        if split:
            keep_ref, give_ref, total_ref, turned_ref = rest
        else:
            (total_ref,) = rest

        @pl.when(i == 0)
        def begin():
            total_ref[...] = jnp.zeros_like(total_ref) if start is None else inputs[-1][...]

        at = 0
        for first, (choices, at_end, at_middle, steps, only) in zip(firsts, segments):
            here = inputs[at : at + len(choices)]
            at += len(choices)
            active = (i >= first) & (i < first + steps)
            if only:
                active = active & (flags_ref[0] == 0)

            @pl.when(active)
            def add(here=here):
                shard = here[0][...]
                if len(here) == 2:
                    shard = jnp.where(end, shard, here[1][...])
                add_dot(total_ref, grads_ref, shard)

        if split:

            @pl.when(i == total - 1)
            def finish():
                turned_ref[...] = total_ref[...].T
                split_rows(turned_ref, keep_ref, give_ref, flags_ref[1])

    whole = lambda i, flags_ref: (0, 0)
    if split:
        out_shape = [jax.ShapeDtypeStruct((cols // 2, tok), jnp.float32)] * 2
        out_specs = [pl.BlockSpec((cols // 2, tok), whole)] * 2
        scratch = [pltpu.VMEM((tok, cols), jnp.float32), pltpu.VMEM((cols, tok), jnp.float32)]
    else:
        out_shape = jax.ShapeDtypeStruct((tok, cols), jnp.float32)
        out_specs = pl.BlockSpec((tok, cols), whole)
        scratch = []
    return pl.pallas_call(
        kernel,
        out_shape=out_shape,
        grid_spec=pltpu.PrefetchScalarGridSpec(
            num_scalar_prefetch=1,
            grid=(total,),
            in_specs=specs,
            out_specs=out_specs,
            scratch_shapes=scratch,
        ),
        compiler_params=PARAMS,
        cost_estimate=SHORT,
    )(flags, *operands)


def both_dots(flags, grads, at_end, at_middle):
    tok = grads.shape[0]
    cols = at_end[0].shape[1]
    step = grads.shape[1] // (3 * STEPS)

    def third_at(first):
        def index(i, flags_ref):
            return (jnp.clip(i - first, 0, STEPS - 1) * (1 - flags_ref[0]), 0)

        return index

    operands = [grads, at_end[0]] + [array for pair in at_middle for array in pair] + [grads]
    specs = [
        pl.BlockSpec((tok, step), lambda i, flags_ref: (0, STEPS + i)),
        pl.BlockSpec((step, cols), lambda i, flags_ref: (at_end[1] + i * flags_ref[0], 0)),
    ]
    for first in (0, STEPS):
        specs += [pl.BlockSpec((step, cols), third_at(first))] * 2
    specs.append(
        pl.BlockSpec(
            (tok, step),
            lambda i, flags_ref: (0, flags_ref[0] * STEPS + jnp.minimum(i, STEPS - 1)),
        )
    )

    def kernel(flags_ref, grads_ref, end_ref, b1_ref, c1_ref, b2_ref, c2_ref, next_ref, *out_refs):
        total_ref, handed_ref, last_ref = out_refs
        i = pl.program_id(0)

        @pl.when(i == 0)
        def begin():
            total_ref[...] = jnp.zeros_like(total_ref)

        @pl.when(i < STEPS)
        def hand_on_next():
            handed_ref[...] = next_ref[...]

        @pl.when(i >= STEPS)
        def hand_on_last():
            last_ref[...] = grads_ref[...]

        @pl.when(flags_ref[0] == 1)
        def one():
            total_ref[:, :cols] += jnp.dot(
                grads_ref[...], end_ref[...], preferred_element_type=jnp.float32
            )

        for first, b_ref, c_ref in ((0, b1_ref, c1_ref), (STEPS, b2_ref, c2_ref)):

            @pl.when((flags_ref[0] == 0) & (i >= first) & (i < first + STEPS))
            def two(b_ref=b_ref, c_ref=c_ref):
                shards = jnp.concatenate([b_ref[...], c_ref[...]], axis=1)
                total_ref[...] += jnp.dot(
                    grads_ref[...], shards, preferred_element_type=jnp.float32
                )

    third = jax.ShapeDtypeStruct((tok, STEPS * step), grads.dtype)
    return pl.pallas_call(
        kernel,
        out_shape=[jax.ShapeDtypeStruct((tok, 2 * cols), jnp.float32), third, third],
        grid_spec=pltpu.PrefetchScalarGridSpec(
            num_scalar_prefetch=1,
            grid=(2 * STEPS,),
            in_specs=specs,
            out_specs=[
                pl.BlockSpec((tok, 2 * cols), lambda i, flags_ref: (0, 0)),
                pl.BlockSpec((tok, step), lambda i, flags_ref: (0, jnp.minimum(i, STEPS - 1))),
                pl.BlockSpec((tok, step), lambda i, flags_ref: (0, jnp.maximum(i - STEPS, 0))),
            ],
        ),
        compiler_params=PARAMS,
        cost_estimate=SHORT,
    )(flags, *operands)


def partner_dots(flags, pieces, shards, grads, shard, start):
    tok = grads.shape[0]
    cols = shards[0][0].shape[1]
    step = shard[2] // STEPS
    count = len(pieces)
    two = start.shape[1] == 2 * cols
    width = tok + len(shards) * count * TILE

    def at(row):
        return lambda i, flags_ref: (row + i, 0)

    whole = lambda i, flags_ref: (0, 0)
    operands, specs = [], []
    for array, row in list(pieces) + list(shards) + [shard[:2]]:
        operands.append(array)
        specs.append(pl.BlockSpec((step, cols), at(row)))
    operands += [grads, start]
    specs.append(pl.BlockSpec((tok, step), lambda i, flags_ref: (0, i)))
    specs.append(pl.BlockSpec(start.shape, whole))

    def kernel(flags_ref, *refs):
        i = pl.program_id(0)
        piece_refs, shard_refs = refs[:count], refs[count : count + len(shards)]
        end_ref, grads_ref, start_ref = refs[count + len(shards) : count + len(shards) + 3]
        keep_ref, give_ref, *rest = refs[len(operands) :]
        if two:
            second_ref, total_ref, sums_ref, turned_ref, wide_ref = rest
        else:
            total_ref, sums_ref, turned_ref, wide_ref = rest

        @pl.when(i == 0)
        def begin():
            total_ref[...] = start_ref[...]
            sums_ref[...] = jnp.zeros_like(sums_ref)

        @pl.when(flags_ref[0] == 1)
        def at_an_end_plane():
            total_ref[:, total_ref.shape[1] - cols :] += jnp.dot(
                grads_ref[...], end_ref[...], preferred_element_type=jnp.float32
            )

        @pl.when(flags_ref[0] == 0)
        def at_a_middle_plane():
            side_by_side = jnp.concatenate([ref[...] for ref in shard_refs], axis=1)
            tokens = jnp.concatenate(
                [
                    jnp.concatenate(
                        [ref[q * TILE : (q + 1) * TILE, :] for q in range(step // TILE)], axis=1
                    )
                    for ref in piece_refs
                ]
            )
            sums_ref[...] += jnp.dot(tokens, side_by_side, preferred_element_type=jnp.float32)
            if two:
                total_ref[...] += jnp.dot(
                    grads_ref[...], side_by_side[:, cols:], preferred_element_type=jnp.float32
                )

        @pl.when(i == STEPS - 1)
        def finish():
            wide_ref[...] = total_ref[:, :cols].T
            split_rows(wide_ref, keep_ref, give_ref, flags_ref[1], pl.ds(0, tok))
            for j in range(len(shards)):
                turned_ref[...] = sums_ref[:, j * cols : (j + 1) * cols].T
                columns = pl.ds(tok + j * count * TILE, count * TILE)
                split_rows(turned_ref, keep_ref, give_ref, flags_ref[1], columns)
            if two:
                second_ref[...] = total_ref[:, cols:]

    out_shape = [jax.ShapeDtypeStruct((cols // 2, width), jnp.float32)] * 2
    out_specs = [pl.BlockSpec((cols // 2, width), whole)] * 2
    if two:
        out_shape.append(jax.ShapeDtypeStruct((tok, cols), jnp.float32))
        out_specs.append(pl.BlockSpec((tok, cols), whole))
    return pl.pallas_call(
        kernel,
        out_shape=out_shape,
        grid_spec=pltpu.PrefetchScalarGridSpec(
            num_scalar_prefetch=1,
            grid=(STEPS,),
            in_specs=specs,
            out_specs=out_specs,
            scratch_shapes=[
                pltpu.VMEM(start.shape, jnp.float32),
                pltpu.VMEM((count * TILE, len(shards) * cols), jnp.float32),
                pltpu.VMEM((cols, count * TILE), jnp.float32),
                pltpu.VMEM((cols, tok), jnp.float32),
            ],
        ),
        compiler_params=PARAMS,
        cost_estimate=SHORT,
    )(flags, *operands)


def stack_blocks(flags, grads, depth):
    tiles = grads.shape[0] // TILE
    firsts = [0] + list(range(tiles // 2, tiles))
    counts = [tiles // 2] + [1] * (tiles // 2)

    def kernel(flags_ref, grads_ref, *out_refs):
        t = pl.program_id(0)
        for first, count, out_ref in zip(firsts, counts, out_refs):

            @pl.when((t >= first) & (t < first + count))
            def copy(out_ref=out_ref):
                for q in range(depth // TILE):
                    here = slice(q * TILE, (q + 1) * TILE)
                    out_ref[here, :] = grads_ref[:, here]

    def place(first, count):
        return lambda t, flags_ref: (jnp.clip(t - first, 0, count - 1), 0)

    return pl.pallas_call(
        kernel,
        out_shape=[jax.ShapeDtypeStruct((count * depth, TILE), grads.dtype) for count in counts],
        grid_spec=pltpu.PrefetchScalarGridSpec(
            num_scalar_prefetch=1,
            grid=(tiles,),
            in_specs=[pl.BlockSpec((TILE, depth), lambda t, flags_ref: (t, 0))],
            out_specs=[
                pl.BlockSpec((depth, TILE), place(first, count))
                for first, count in zip(firsts, counts)
            ],
        ),
        compiler_params=PARAMS,
        cost_estimate=SHORT,
    )(flags, grads)


def input_dots(flags, acts, shards):
    tok, depth = acts.shape
    cols = shards[0][0][0].shape[1]
    operands, specs = [acts], [pl.BlockSpec((tok, depth), lambda i, flags_ref: (0, 0))]
    for choices in shards:
        for array, row in choices:
            operands.append(array)
            specs.append(pl.BlockSpec((depth, cols), lambda i, flags_ref, row=row: (row, 0)))

    def kernel(flags_ref, acts_ref, *refs):
        i = pl.program_id(0)
        inputs = list(refs[: len(operands) - 1])
        keep_ref, give_ref, part_ref = refs[len(operands) - 1 :]
        at = 0
        for slot, choices in enumerate(shards):
            here = inputs[at : at + len(choices)]
            at += len(choices)

            @pl.when(i == slot)
            def add(here=here):
                shard = here[0][...]
                if len(here) == 2:
                    shard = jnp.where(flags_ref[0] == 1, shard, here[1][...])
                part_ref[...] = jnp.dot(acts_ref[...], shard, preferred_element_type=jnp.float32)

        split_rows(part_ref, keep_ref, give_ref, flags_ref[1])

    place = pl.BlockSpec((tok // 2, cols), lambda i, flags_ref: (0, flags_ref[2 + i]))
    return pl.pallas_call(
        kernel,
        out_shape=[jax.ShapeDtypeStruct((tok // 2, cols * len(shards)), jnp.float32)] * 2,
        grid_spec=pltpu.PrefetchScalarGridSpec(
            num_scalar_prefetch=1,
            grid=(len(shards),),
            in_specs=specs,
            out_specs=[place, place],
            scratch_shapes=[pltpu.VMEM((tok, cols), jnp.float32)],
        ),
        compiler_params=PARAMS,
        cost_estimate=SHORT,
    )(flags, *operands)


def line_plan(acts, grads, basis_in, basis_out, eigval, test_grads, pair_tiles, last_rows):
    plane = lax.axis_index("cand")
    end = (plane == 0) | (plane == 3)
    tok_rows = acts.shape[0]
    cols = basis_in.shape[1]
    tiles_here = tok_rows // TILE
    slim = cols // 4
    depth = basis_out.shape[0] // 3
    rows_in = basis_in.shape[0]

    def pick(at_end, at_middle):
        return jnp.where(end, at_end, at_middle)

    def side(at_end, at_middle):
        return lax.ppermute(pick(at_end, at_middle), "cand", SIDE)

    among, far = [], []
    for at in range(16):
        between = 4 <= at < 12
        across = 12 - 4 * (at // 4) + at % 4
        among.append((at, across if between else at ^ 1))
        far.append((at, at ^ 1 if between else across))

    def middle(x):
        return lax.ppermute(x, ALL, among)

    at_b = jnp.where(end, plane ^ 2, plane ^ 3)
    at_c = jnp.where(end, plane ^ 3, plane ^ 2)
    rep = lax.axis_index("rep")
    flags = jnp.stack([end.astype(jnp.int32), rep, plane, plane ^ 1, at_b, at_c])

    rows = lax.dynamic_slice_in_dim(basis_out, jnp.where(end, 0, depth), 2 * depth, 0)
    s0 = lax.ppermute(basis_in, "cand", SIDE)
    m0 = middle(basis_in)
    s12 = lax.ppermute(rows, "cand", SIDE)
    second = basis_out[depth : 2 * depth]
    m2 = middle(second)
    started = after(flags, rows, second)
    stacked, *more_stacked = stack_blocks(started, grads, depth)
    part_own = feature_dots(
        after(started, s0, m0), grads, [([(basis_out, 0)], 0, 0, 3 * STEPS, False)]
    )
    precond = (test_grads.astype(jnp.float32) / (eigval + damping)).astype(jnp.bfloat16)
    m1 = middle(after(s0, m0))
    third = jnp.concatenate([basis_out[2 * depth :], basis_out[: 2 * rows_in - depth]])
    s3 = side(third, jnp.concatenate([m0, m1]))
    m3 = middle(after(basis_out[2 * depth :], precond, stacked, *more_stacked, *part_own))
    m5 = middle(s12[depth:])
    to_s45 = pick(stacked, jnp.concatenate([m2, m3]))
    s45 = lax.ppermute(to_s45, "cand", SIDE)
    m6 = middle(s3[:depth])
    m4 = middle(after(basis_out[:depth], m5))
    s6 = side(more_stacked[0], m5)
    to_s7 = pick(after(more_stacked[1], s45), m6)
    s7 = lax.ppermute(to_s7, "cand", SIDE)
    m7 = middle(after(s12[:depth], m6))

    part_in = input_dots(
        after(flags, s3, m5),
        acts,
        [[(basis_in, 0)], [(s0, 0)], [(s3, 0), (m0, 0)], [(s3, 1), (m1, 0)]],
    )
    part_a = feature_dots(
        after(flags, *part_in),
        grads,
        [
            ([(s12, 0)], STEPS, 0, 2 * STEPS, False),
            ([(s3, 0)], 2 * STEPS, 2 * STEPS, STEPS, True),
        ],
    )
    totals, next_grads, last_grads = both_dots(after(flags, to_s7, s45, *part_a), grads, (s45, 0), ((m2, m5), (m3, m6)))
    parts = [jnp.concatenate(part, axis=1) for part in zip(part_own, part_a)]
    keep_a, give_a = after(parts, m4, totals)
    core_a = swap(give_a, "rep")

    shards = [(basis_out, 0), (m4, 0), (m7, 0)]
    *part_b, part_c = partner_dots(
        after(flags, totals, core_a),
        [(s45, 0), (s45, STEPS), (s6, 0)],
        shards,
        next_grads,
        (s6, 0, depth),
        totals,
    )
    keep_in, give_in = after(part_in, m7, totals, core_a)
    core_in = keep_in + swap(give_in, "rep")
    give_in = core_in.astype(jnp.bfloat16)
    rows_here = chip_sum(core_in, give_in).astype(jnp.bfloat16)
    rows_there = swap(rows_here, "rep")
    rot_in = all_rows(rows_here, rows_there)
    rot_in = rot_in.reshape(tiles_here, TILE, 4 * cols)
    keep_b, give_b = part_b
    keep_b, give_b = chip_parts(
        jnp.concatenate([keep_a, keep_b], axis=1),
        jnp.concatenate([core_a, swap(give_b, "rep")], axis=1),
    )
    sums = chip_sum(keep_b, give_b)
    sum_own, sum_a, sum_b = [sums[:, i * tok_rows : (i + 1) * tok_rows] for i in range(3)]
    sums = sums[:, 3 * tok_rows :].astype(jnp.bfloat16)
    keep_last, give_last = partner_dots(
        after(flags, part_c, give_b, give_in),
        [(s7, 0)],
        shards,
        last_grads,
        (s7, 0, depth),
        part_c,
    )
    keep_last, give_last = chip_parts(keep_last, swap(give_last, "rep"))
    sum_last = chip_sum(keep_last, give_last)
    sum_c, sum_last = sum_last[:, :tok_rows], sum_last[:, tok_rows:].astype(jnp.bfloat16)

    rowmask, ignored = tile_layout(pair_tiles, last_rows, plane * tiles_here, tiles_here, TILE)
    keep = rowmask.reshape(1, tok_rows).astype(jnp.bfloat16)

    def tile_prods(rot_out):
        return jnp.einsum(
            "etr,tra->tea",
            (rot_out.astype(jnp.bfloat16) * keep).reshape(slim, tiles_here, TILE),
            rot_in,
            preferred_element_type=jnp.float32,
        ).astype(jnp.bfloat16)

    def pair_scores(*received):
        prods = jnp.concatenate([x for x, source in received])
        scores = jnp.einsum("tea,jea->tj", prods, precond, preferred_element_type=jnp.float32)
        onehot = jnp.concatenate([
            tile_layout(pair_tiles, last_rows, source * tiles_here, tiles_here, TILE)[1]
            for x, source in received
        ])
        return jnp.sum(jnp.where(onehot[:, :, None], scores[:, None, :], 0.0), axis=0)

    prods_own = tile_prods(sum_own)
    prods_middle = tile_prods(sum_b)
    from_middle = middle(prods_middle)
    last = after(lax.ppermute(after(sum_last, rows_here), "cand", SIDE), prods_middle)
    back = after(lax.ppermute(sums, "cand", SIDE), rows_there)
    few = tok_rows - TILE

    def with_partner(whole, at):
        parts = [back[:, at * few : (at + 1) * few], last[:, at * TILE : (at + 1) * TILE]]
        parts = jnp.concatenate(parts, axis=1).astype(jnp.float32)
        return whole + jnp.where(end, parts, 0.0)

    prods_a = tile_prods(with_partner(sum_a, 0))
    prods_b = tile_prods(with_partner(sum_b, 1))
    prods_c = tile_prods(with_partner(sum_c, 2))
    to_two = pick(prods_b, prods_c)
    from_two = lax.ppermute(to_two, "cand", TWO)
    from_far = lax.ppermute(after(prods_c, to_two), ALL, far)
    from_side = lax.ppermute(after(prods_a, to_two), "cand", SIDE)
    total = pair_scores(
        (prods_own, plane),
        (from_side, plane ^ 1),
        (from_two, plane ^ 2),
        (pick(from_far, from_middle), plane ^ 3),
    )
    return final_sum(total)


def final_sum(total):
    npairs, ntest = total.shape
    blocks = total.reshape(4, npairs // 4, 4, ntest // 4).transpose(0, 2, 1, 3)
    blocks = blocks.reshape(16, npairs // 4, ntest // 4)
    return jnp.sum(lax.all_to_all(blocks, ALL, 0, 0, tiled=True), axis=0)


def gather_plan(acts, grads, basis_in, basis_out, eigval, test_grads, pair_tiles, last_rows):
    ncand = lax.axis_size("cand")
    nfeat = lax.axis_size(FEAT)
    tok_rows = acts.shape[0]
    width_in = basis_in.shape[1] * ncand
    width_out = basis_out.shape[1] * ncand
    slim = width_out // (ncand * nfeat)
    part_in = jnp.dot(
        acts,
        lax.all_gather(basis_in, "cand", axis=1, tiled=True),
        preferred_element_type=jnp.float32,
    )
    part_out = jnp.dot(
        grads,
        lax.all_gather(basis_out, "cand", axis=1, tiled=True),
        preferred_element_type=jnp.float32,
    )
    part_out = part_out.reshape(tok_rows, ncand, nfeat, slim).transpose(0, 2, 1, 3)
    part_out = part_out.reshape(tok_rows, nfeat * ncand * slim)
    summed_in, summed_out = lax.psum((part_in, part_out), FEAT)
    own = lax.dynamic_slice_in_dim(
        summed_out, lax.axis_index(FEAT) * (ncand * slim), ncand * slim, 1
    )
    rot_in = summed_in.astype(jnp.bfloat16)
    rot_out = own.astype(jnp.bfloat16)
    tiles_here = tok_rows // TILE
    rowmask, ignored = tile_layout(
        pair_tiles, last_rows, lax.axis_index("cand") * tiles_here, tiles_here, TILE
    )
    masked = rot_out.reshape(tiles_here, TILE, ncand * slim) * rowmask[:, :, None].astype(
        jnp.bfloat16
    )
    prods = jnp.einsum(
        "tre,tra->tea",
        masked,
        rot_in.reshape(tiles_here, TILE, width_in),
        preferred_element_type=jnp.float32,
    ).astype(jnp.bfloat16)
    prods = prods.reshape(tiles_here, ncand, slim, width_in)
    received = lax.all_to_all(prods, "cand", split_axis=1, concat_axis=0, tiled=True)
    all_tiles = received.shape[0]
    received = received.reshape(all_tiles, slim, width_in)
    precond = (test_grads.astype(jnp.float32) / (eigval + damping)).astype(jnp.bfloat16)
    tile_part = jnp.einsum("tea,jea->tj", received, precond, preferred_element_type=jnp.float32)
    ignored_mask, onehot = tile_layout(pair_tiles, last_rows, 0, all_tiles, TILE)
    pair_part = jnp.dot(onehot.astype(jnp.float32).T, tile_part, precision=lax.Precision.HIGHEST)
    npairs = pair_part.shape[0]
    ntest = pair_part.shape[1]
    total = lax.psum(pair_part, ("cand", "eig", "rep"))
    rows = lax.dynamic_slice_in_dim(
        total, lax.axis_index("cand") * (npairs // ncand), npairs // ncand, 0
    )
    return lax.dynamic_slice_in_dim(
        rows, lax.axis_index(FEAT) * (ntest // nfeat), ntest // nfeat, 1
    )


def solution(mesh):
    in_specs = (
        P(("groups", "cand"), ("eig", "rep")),
        P(("groups", "cand"), ("eig", "rep")),
        P(("groups", "eig", "rep"), "cand"),
        P(("groups", "eig", "rep"), "cand"),
        P(("groups", "cand", "eig", "rep"), None),
        P("groups", ("cand", "eig", "rep"), None),
        P("groups"),
        P("groups"),
    )
    out_specs = P(("groups", "cand"), ("eig", "rep"))
    sizes = (mesh.shape["cand"], mesh.shape["eig"], mesh.shape["rep"])
    per_device = line_plan if sizes == (4, 2, 2) else gather_plan
    return jax.shard_map(
        per_device, mesh=mesh, in_specs=in_specs, out_specs=out_specs, check_vma=False
    )
```

```python
import jax
import jax.numpy as jnp
from jax import lax
from jax.experimental import pallas as pl
from jax.experimental.pallas import tpu as pltpu
from jax.sharding import PartitionSpec as P

TILE = 128
FEAT = ("eig", "rep")
ALL = ("cand", "eig", "rep")
STEPS = 3
PARAMS = pltpu.CompilerParams(vmem_limit_bytes=20 << 20)
SHORT = pl.CostEstimate(flops=1, bytes_accessed=1, transcendentals=0)
SIDE = ((0, 1), (1, 0), (2, 3), (3, 2))
TWO = ((0, 2), (2, 0), (1, 3), (3, 1))

damping = 0.01


def tile_layout(pair_tiles, last_rows, first_tile, count, tile_rows):
    tiles = first_tile + jnp.arange(count, dtype=jnp.int32)
    ends = jnp.cumsum(pair_tiles)
    owner = jnp.sum((ends[None, :] <= tiles[:, None]).astype(jnp.int32), axis=1)
    onehot = owner[:, None] == jnp.arange(pair_tiles.shape[0], dtype=jnp.int32)[None, :]
    last_of = jnp.sum(jnp.where(onehot, last_rows[None, :], 0), axis=1)
    end_of = jnp.sum(jnp.where(onehot, ends[None, :], 0), axis=1)
    limit = jnp.where(tiles == end_of - 1, last_of, tile_rows)
    rowmask = jnp.arange(tile_rows, dtype=jnp.int32)[None, :] < limit[:, None]
    return (rowmask, onehot)


def after(x, *earlier):
    return lax.optimization_barrier((x, *earlier))[0]


def swap(x, axis_name):
    return lax.ppermute(x, axis_name, [(0, 1), (1, 0)])


def halves(x, axis_name):
    first = lax.axis_index(axis_name) == 0
    low, high = jnp.split(x, 2)
    return jnp.where(first, low, high), jnp.where(first, high, low)


def chip_parts(keep, received):
    keep, their_keep = halves(keep, "eig")
    received, their_received = halves(received, "eig")
    return keep + received, (their_keep + their_received).astype(jnp.bfloat16)


def chip_sum(keep, give):
    return keep + swap(give, "eig").astype(jnp.float32)


def all_rows(mine, other):
    first = lax.axis_index("rep") == 0
    mine, other = mine.reshape(2, -1, mine.shape[1]), other.reshape(2, -1, mine.shape[1])
    whole = jnp.stack([jnp.where(first, mine, other), jnp.where(first, other, mine)], axis=1)
    return whole.reshape(-1, whole.shape[-1])


def split_rows(full_ref, keep_ref, give_ref, rep, columns=None):
    rows = full_ref.shape[0] // 4
    columns = slice(None) if columns is None else columns
    for e in range(2):
        here = pl.ds(e * rows, rows)
        mine = pl.ds(pl.multiple_of((2 * e + rep) * rows, rows), rows)
        theirs = pl.ds(pl.multiple_of((2 * e + 1 - rep) * rows, rows), rows)
        keep_ref[here, columns] = full_ref[mine, :]
        give_ref[here, columns] = full_ref[theirs, :]


def add_dot(total_ref, rows_ref, shard):
    half = total_ref.shape[0] // 2
    for here in (pl.ds(0, half), pl.ds(half, half)):
        total_ref[here, :] += jnp.dot(
            rows_ref[here, :], shard, preferred_element_type=jnp.float32
        )


def feature_dots(flags, grads, segments, start=None, split=True):
    tok = grads.shape[0]
    cols = segments[0][0][0][0].shape[1]
    depth = grads.shape[1] // (3 * STEPS)
    firsts = [sum(s[3] for s in segments[:at]) for at in range(len(segments))]
    total = sum(s[3] for s in segments)

    def grads_at(i, flags_ref):
        at = 0
        for first, (choices, at_end, at_middle, steps, only) in zip(firsts, segments):
            base = at_end + flags_ref[0] * 0 if at_end == at_middle else (
                flags_ref[0] * at_end + (1 - flags_ref[0]) * at_middle
            )
            at = jnp.where(i >= first, base + i - first, at)
        return (0, at)

    def rows_at(first, steps, row, wanted):
        def index(i, flags_ref):
            step = jnp.clip(i - first, 0, steps - 1)
            if wanted is not None:
                step = step * (flags_ref[0] if wanted else 1 - flags_ref[0])
            return (row + step, 0)

        return index

    operands, specs = [grads], [pl.BlockSpec((tok, depth), grads_at)]
    for first, (choices, at_end, at_middle, steps, only) in zip(firsts, segments):
        for which, (array, row) in enumerate(choices):
            wanted = None if len(choices) == 1 else which == 0
            operands.append(array)
            specs.append(pl.BlockSpec((depth, cols), rows_at(first, steps, row, wanted)))
    if start is not None:
        operands.append(start)
        specs.append(pl.BlockSpec((tok, cols), lambda i, flags_ref: (0, 0)))

    def kernel(flags_ref, grads_ref, *refs):
        i = pl.program_id(0)
        end = flags_ref[0] == 1
        inputs, rest = list(refs[: len(operands) - 1]), refs[len(operands) - 1 :]
        if split:
            keep_ref, give_ref, total_ref, turned_ref = rest
        else:
            (total_ref,) = rest

        @pl.when(i == 0)
        def begin():
            total_ref[...] = jnp.zeros_like(total_ref) if start is None else inputs[-1][...]

        at = 0
        for first, (choices, at_end, at_middle, steps, only) in zip(firsts, segments):
            here = inputs[at : at + len(choices)]
            at += len(choices)
            active = (i >= first) & (i < first + steps)
            if only:
                active = active & (flags_ref[0] == 0)

            @pl.when(active)
            def add(here=here):
                shard = here[0][...]
                if len(here) == 2:
                    shard = jnp.where(end, shard, here[1][...])
                add_dot(total_ref, grads_ref, shard)

        if split:

            @pl.when(i == total - 1)
            def finish():
                turned_ref[...] = total_ref[...].T
                split_rows(turned_ref, keep_ref, give_ref, flags_ref[1])

    whole = lambda i, flags_ref: (0, 0)
    if split:
        out_shape = [jax.ShapeDtypeStruct((cols // 2, tok), jnp.float32)] * 2
        out_specs = [pl.BlockSpec((cols // 2, tok), whole)] * 2
        scratch = [pltpu.VMEM((tok, cols), jnp.float32), pltpu.VMEM((cols, tok), jnp.float32)]
    else:
        out_shape = jax.ShapeDtypeStruct((tok, cols), jnp.float32)
        out_specs = pl.BlockSpec((tok, cols), whole)
        scratch = []
    return pl.pallas_call(
        kernel,
        out_shape=out_shape,
        grid_spec=pltpu.PrefetchScalarGridSpec(
            num_scalar_prefetch=1,
            grid=(total,),
            in_specs=specs,
            out_specs=out_specs,
            scratch_shapes=scratch,
        ),
        compiler_params=PARAMS,
        cost_estimate=SHORT,
    )(flags, *operands)


def both_dots(flags, grads, at_end, at_middle):
    tok = grads.shape[0]
    cols = at_end[0].shape[1]
    step = grads.shape[1] // (3 * STEPS)

    def third_at(first):
        def index(i, flags_ref):
            return (jnp.clip(i - first, 0, STEPS - 1) * (1 - flags_ref[0]), 0)

        return index

    operands = [grads, at_end[0]] + [array for pair in at_middle for array in pair] + [grads]
    specs = [
        pl.BlockSpec((tok, step), lambda i, flags_ref: (0, STEPS + i)),
        pl.BlockSpec((step, cols), lambda i, flags_ref: (at_end[1] + i * flags_ref[0], 0)),
    ]
    for first in (0, STEPS):
        specs += [pl.BlockSpec((step, cols), third_at(first))] * 2
    specs.append(
        pl.BlockSpec(
            (tok, step),
            lambda i, flags_ref: (0, flags_ref[0] * STEPS + jnp.minimum(i, STEPS - 1)),
        )
    )

    def kernel(flags_ref, grads_ref, end_ref, b1_ref, c1_ref, b2_ref, c2_ref, next_ref, *out_refs):
        total_ref, handed_ref, last_ref = out_refs
        i = pl.program_id(0)

        @pl.when(i == 0)
        def begin():
            total_ref[...] = jnp.zeros_like(total_ref)

        @pl.when(i < STEPS)
        def hand_on_next():
            handed_ref[...] = next_ref[...]

        @pl.when(i >= STEPS)
        def hand_on_last():
            last_ref[...] = grads_ref[...]

        @pl.when(flags_ref[0] == 1)
        def one():
            total_ref[:, :cols] += jnp.dot(
                grads_ref[...], end_ref[...], preferred_element_type=jnp.float32
            )

        for first, b_ref, c_ref in ((0, b1_ref, c1_ref), (STEPS, b2_ref, c2_ref)):

            @pl.when((flags_ref[0] == 0) & (i >= first) & (i < first + STEPS))
            def two(b_ref=b_ref, c_ref=c_ref):
                shards = jnp.concatenate([b_ref[...], c_ref[...]], axis=1)
                total_ref[...] += jnp.dot(
                    grads_ref[...], shards, preferred_element_type=jnp.float32
                )

    third = jax.ShapeDtypeStruct((tok, STEPS * step), grads.dtype)
    return pl.pallas_call(
        kernel,
        out_shape=[jax.ShapeDtypeStruct((tok, 2 * cols), jnp.float32), third, third],
        grid_spec=pltpu.PrefetchScalarGridSpec(
            num_scalar_prefetch=1,
            grid=(2 * STEPS,),
            in_specs=specs,
            out_specs=[
                pl.BlockSpec((tok, 2 * cols), lambda i, flags_ref: (0, 0)),
                pl.BlockSpec((tok, step), lambda i, flags_ref: (0, jnp.minimum(i, STEPS - 1))),
                pl.BlockSpec((tok, step), lambda i, flags_ref: (0, jnp.maximum(i - STEPS, 0))),
            ],
        ),
        compiler_params=PARAMS,
        cost_estimate=SHORT,
    )(flags, *operands)


def partner_dots(flags, pieces, shards, grads, shard, start):
    tok = grads.shape[0]
    cols = shards[0][0].shape[1]
    step = shard[2] // STEPS
    count = len(pieces)
    two = start.shape[1] == 2 * cols
    width = tok + len(shards) * count * TILE

    def at(row):
        return lambda i, flags_ref: (row + i, 0)

    whole = lambda i, flags_ref: (0, 0)
    fetched = [shards[1][0], shards[2][0], shard[0]] if two else []
    listed = list(pieces) + list(shards) + [shard[:2]]
    places = [[array is x for x in fetched].index(True) if any(array is x for x in fetched) else None
              for array, row in listed]
    operands, specs = list(fetched), [pl.BlockSpec(memory_space=pltpu.HBM)] * len(fetched)
    for (array, row), place in zip(listed, places):
        if place is None:
            operands.append(array)
            specs.append(pl.BlockSpec((step, cols), at(row)))
    blocked = len(operands) - len(fetched)
    operands += [grads, start]
    specs.append(pl.BlockSpec((tok, step), lambda i, flags_ref: (0, i)))
    specs.append(pl.BlockSpec(start.shape, whole))

    def kernel(flags_ref, *refs):
        i = pl.program_id(0)
        far_refs, block_refs = refs[: len(fetched)], list(refs[len(fetched) : len(fetched) + blocked])
        grads_ref, start_ref = refs[len(fetched) + blocked : len(operands)]
        keep_ref, give_ref, *rest = refs[len(operands) :]
        if fetched:
            *rest, held_ref, arrived = rest
            copies = [
                pltpu.make_async_copy(far_ref, held_ref.at[k], arrived.at[k])
                for k, far_ref in enumerate(far_refs)
            ]

            @pl.when(i == 0)
            def fetch():
                for copy in copies:
                    copy.start()
                for copy in copies:
                    copy.wait()

        here = pl.ds(pl.multiple_of(i * step, step), step)
        all_refs = [
            block_refs.pop(0) if place is None else held_ref.at[place, here] for place in places
        ]
        piece_refs, shard_refs, end_ref = all_refs[:count], all_refs[count:-1], all_refs[-1]
        if two:
            second_ref, total_ref, sums_ref, turned_ref, wide_ref = rest
        else:
            total_ref, sums_ref, turned_ref, wide_ref = rest

        @pl.when(i == 0)
        def begin():
            total_ref[...] = start_ref[...]
            sums_ref[...] = jnp.zeros_like(sums_ref)

        @pl.when(flags_ref[0] == 1)
        def at_an_end_plane():
            total_ref[:, total_ref.shape[1] - cols :] += jnp.dot(
                grads_ref[...], end_ref[...], preferred_element_type=jnp.float32
            )

        @pl.when(flags_ref[0] == 0)
        def at_a_middle_plane():
            side_by_side = jnp.concatenate([ref[...] for ref in shard_refs], axis=1)
            tokens = jnp.concatenate(
                [
                    jnp.concatenate(
                        [ref[q * TILE : (q + 1) * TILE, :] for q in range(step // TILE)], axis=1
                    )
                    for ref in piece_refs
                ]
            )
            sums_ref[...] += jnp.dot(tokens, side_by_side, preferred_element_type=jnp.float32)
            if two:
                total_ref[...] += jnp.dot(
                    grads_ref[...], side_by_side[:, cols:], preferred_element_type=jnp.float32
                )

        @pl.when(i == STEPS - 1)
        def finish():
            wide_ref[...] = total_ref[:, :cols].T
            split_rows(wide_ref, keep_ref, give_ref, flags_ref[1], pl.ds(0, tok))
            for j in range(len(shards)):
                turned_ref[...] = sums_ref[:, j * cols : (j + 1) * cols].T
                columns = pl.ds(tok + j * count * TILE, count * TILE)
                split_rows(turned_ref, keep_ref, give_ref, flags_ref[1], columns)
            if two:
                second_ref[...] = total_ref[:, cols:]

    out_shape = [jax.ShapeDtypeStruct((cols // 2, width), jnp.float32)] * 2
    out_specs = [pl.BlockSpec((cols // 2, width), whole)] * 2
    if two:
        out_shape.append(jax.ShapeDtypeStruct((tok, cols), jnp.float32))
        out_specs.append(pl.BlockSpec((tok, cols), whole))
    return pl.pallas_call(
        kernel,
        out_shape=out_shape,
        grid_spec=pltpu.PrefetchScalarGridSpec(
            num_scalar_prefetch=1,
            grid=(STEPS,),
            in_specs=specs,
            out_specs=out_specs,
            scratch_shapes=[
                pltpu.VMEM(start.shape, jnp.float32),
                pltpu.VMEM((count * TILE, len(shards) * cols), jnp.float32),
                pltpu.VMEM((cols, count * TILE), jnp.float32),
                pltpu.VMEM((cols, tok), jnp.float32),
            ]
            + [
                pltpu.VMEM((len(fetched), STEPS * step, cols), grads.dtype),
                pltpu.SemaphoreType.DMA((len(fetched),)),
            ]
            * bool(fetched),
        ),
        compiler_params=PARAMS,
        cost_estimate=SHORT,
    )(flags, *operands)


def stack_blocks(flags, grads, depth):
    tiles = grads.shape[0] // TILE
    firsts = [0] + list(range(tiles // 2, tiles))
    counts = [tiles // 2] + [1] * (tiles // 2)

    def kernel(flags_ref, grads_ref, *out_refs):
        t = pl.program_id(0)
        for first, count, out_ref in zip(firsts, counts, out_refs):

            @pl.when((t >= first) & (t < first + count))
            def copy(out_ref=out_ref):
                for q in range(depth // TILE):
                    here = slice(q * TILE, (q + 1) * TILE)
                    out_ref[here, :] = grads_ref[:, here]

    def place(first, count):
        return lambda t, flags_ref: (jnp.clip(t - first, 0, count - 1), 0)

    return pl.pallas_call(
        kernel,
        out_shape=[jax.ShapeDtypeStruct((count * depth, TILE), grads.dtype) for count in counts],
        grid_spec=pltpu.PrefetchScalarGridSpec(
            num_scalar_prefetch=1,
            grid=(tiles,),
            in_specs=[pl.BlockSpec((TILE, depth), lambda t, flags_ref: (t, 0))],
            out_specs=[
                pl.BlockSpec((depth, TILE), place(first, count))
                for first, count in zip(firsts, counts)
            ],
        ),
        compiler_params=PARAMS,
        cost_estimate=SHORT,
    )(flags, grads)


def input_dots(flags, acts, shards):
    tok, depth = acts.shape
    cols = shards[0][0][0].shape[1]
    operands, specs = [acts], [pl.BlockSpec((tok, depth), lambda i, flags_ref: (0, 0))]
    for choices in shards:
        for array, row in choices:
            operands.append(array)
            specs.append(pl.BlockSpec((depth, cols), lambda i, flags_ref, row=row: (row, 0)))

    def kernel(flags_ref, acts_ref, *refs):
        i = pl.program_id(0)
        inputs = list(refs[: len(operands) - 1])
        keep_ref, give_ref, part_ref = refs[len(operands) - 1 :]
        at = 0
        for slot, choices in enumerate(shards):
            here = inputs[at : at + len(choices)]
            at += len(choices)

            @pl.when(i == slot)
            def add(here=here):
                shard = here[0][...]
                if len(here) == 2:
                    shard = jnp.where(flags_ref[0] == 1, shard, here[1][...])
                part_ref[...] = jnp.dot(acts_ref[...], shard, preferred_element_type=jnp.float32)

        split_rows(part_ref, keep_ref, give_ref, flags_ref[1])

    place = pl.BlockSpec((tok // 2, cols), lambda i, flags_ref: (0, flags_ref[2 + i]))
    return pl.pallas_call(
        kernel,
        out_shape=[jax.ShapeDtypeStruct((tok // 2, cols * len(shards)), jnp.float32)] * 2,
        grid_spec=pltpu.PrefetchScalarGridSpec(
            num_scalar_prefetch=1,
            grid=(len(shards),),
            in_specs=specs,
            out_specs=[place, place],
            scratch_shapes=[pltpu.VMEM((tok, cols), jnp.float32)],
        ),
        compiler_params=PARAMS,
        cost_estimate=SHORT,
    )(flags, *operands)


def line_plan(acts, grads, basis_in, basis_out, eigval, test_grads, pair_tiles, last_rows):
    plane = lax.axis_index("cand")
    end = (plane == 0) | (plane == 3)
    tok_rows = acts.shape[0]
    cols = basis_in.shape[1]
    tiles_here = tok_rows // TILE
    slim = cols // 4
    depth = basis_out.shape[0] // 3
    rows_in = basis_in.shape[0]

    def pick(at_end, at_middle):
        return jnp.where(end, at_end, at_middle)

    def side(at_end, at_middle):
        return lax.ppermute(pick(at_end, at_middle), "cand", SIDE)

    among, far = [], []
    for at in range(16):
        between = 4 <= at < 12
        across = 12 - 4 * (at // 4) + at % 4
        among.append((at, across if between else at ^ 1))
        far.append((at, at ^ 1 if between else across))

    def middle(x):
        return lax.ppermute(x, ALL, among)

    at_b = jnp.where(end, plane ^ 2, plane ^ 3)
    at_c = jnp.where(end, plane ^ 3, plane ^ 2)
    rep = lax.axis_index("rep")
    flags = jnp.stack([end.astype(jnp.int32), rep, plane, plane ^ 1, at_b, at_c])

    rows = lax.dynamic_slice_in_dim(basis_out, jnp.where(end, 0, depth), 2 * depth, 0)
    s0 = lax.ppermute(basis_in, "cand", SIDE)
    m0 = middle(basis_in)
    s12 = lax.ppermute(rows, "cand", SIDE)
    second = basis_out[depth : 2 * depth]
    m2 = middle(second)
    started = after(flags, rows, second)
    stacked, *more_stacked = stack_blocks(started, grads, depth)
    part_own = feature_dots(
        after(started, s0, m0), grads, [([(basis_out, 0)], 0, 0, 3 * STEPS, False)]
    )
    precond = (test_grads.astype(jnp.float32) / (eigval + damping)).astype(jnp.bfloat16)
    m1 = middle(after(s0, m0))
    third = jnp.concatenate([basis_out[2 * depth :], basis_out[: 2 * rows_in - depth]])
    s3 = side(third, jnp.concatenate([m0, m1]))
    m3 = middle(after(basis_out[2 * depth :], precond, stacked, *more_stacked, *part_own))
    m5 = middle(s12[depth:])
    to_s45 = pick(stacked, jnp.concatenate([m2, m3]))
    s45 = lax.ppermute(to_s45, "cand", SIDE)
    m6 = middle(s3[:depth])
    m4 = middle(after(basis_out[:depth], m5))
    s6 = side(more_stacked[0], m5)
    to_s7 = pick(after(more_stacked[1], s45), m6)
    s7 = lax.ppermute(to_s7, "cand", SIDE)
    m7 = middle(after(s12[:depth], m6))

    part_in = input_dots(
        after(flags, s3, m5),
        acts,
        [[(basis_in, 0)], [(s0, 0)], [(s3, 0), (m0, 0)], [(s3, 1), (m1, 0)]],
    )
    part_a = feature_dots(
        after(flags, *part_in),
        grads,
        [
            ([(s12, 0)], STEPS, 0, 2 * STEPS, False),
            ([(s3, 0)], 2 * STEPS, 2 * STEPS, STEPS, True),
        ],
    )
    totals, next_grads, last_grads = both_dots(after(flags, to_s7, s45, *part_a), grads, (s45, 0), ((m2, m5), (m3, m6)))
    parts = [jnp.concatenate(part, axis=1) for part in zip(part_own, part_a)]
    keep_a, give_a = after(parts, m4, totals)
    core_a = swap(give_a, "rep")

    shards = [(basis_out, 0), (m4, 0), (m7, 0)]
    *part_b, part_c = partner_dots(
        after(flags, totals, core_a),
        [(s45, 0), (s45, STEPS), (s6, 0)],
        shards,
        next_grads,
        (s6, 0, depth),
        totals,
    )
    keep_in, give_in = after(part_in, m7, totals, core_a)
    core_in = keep_in + swap(give_in, "rep")
    give_in = core_in.astype(jnp.bfloat16)
    rows_here = chip_sum(core_in, give_in).astype(jnp.bfloat16)
    rows_there = swap(rows_here, "rep")
    rot_in = all_rows(rows_here, rows_there)
    rot_in = rot_in.reshape(tiles_here, TILE, 4 * cols)
    keep_b, give_b = part_b
    keep_b, give_b = chip_parts(
        jnp.concatenate([keep_a, keep_b], axis=1),
        jnp.concatenate([core_a, swap(give_b, "rep")], axis=1),
    )
    sums = chip_sum(keep_b, give_b)
    sum_own, sum_a, sum_b = [sums[:, i * tok_rows : (i + 1) * tok_rows] for i in range(3)]
    sums = sums[:, 3 * tok_rows :].astype(jnp.bfloat16)
    keep_last, give_last = partner_dots(
        after(flags, part_c, give_b, give_in),
        [(s7, 0)],
        shards,
        last_grads,
        (s7, 0, depth),
        part_c,
    )
    keep_last, give_last = chip_parts(keep_last, swap(give_last, "rep"))
    sum_last = chip_sum(keep_last, give_last)
    sum_c, sum_last = sum_last[:, :tok_rows], sum_last[:, tok_rows:].astype(jnp.bfloat16)

    rowmask, ignored = tile_layout(pair_tiles, last_rows, plane * tiles_here, tiles_here, TILE)
    keep = rowmask.reshape(1, tok_rows).astype(jnp.bfloat16)

    def tile_prods(rot_out):
        return jnp.einsum(
            "etr,tra->tea",
            (rot_out.astype(jnp.bfloat16) * keep).reshape(slim, tiles_here, TILE),
            rot_in,
            preferred_element_type=jnp.float32,
        ).astype(jnp.bfloat16)

    def pair_scores(*received):
        prods = jnp.concatenate([x for x, source in received])
        scores = jnp.einsum("tea,jea->tj", prods, precond, preferred_element_type=jnp.float32)
        onehot = jnp.concatenate([
            tile_layout(pair_tiles, last_rows, source * tiles_here, tiles_here, TILE)[1]
            for x, source in received
        ])
        return jnp.sum(jnp.where(onehot[:, :, None], scores[:, None, :], 0.0), axis=0)

    prods_own = tile_prods(sum_own)
    prods_middle = tile_prods(sum_b)
    from_middle = middle(prods_middle)
    last = after(lax.ppermute(after(sum_last, rows_here), "cand", SIDE), prods_middle)
    back = after(lax.ppermute(sums, "cand", SIDE), rows_there)
    few = tok_rows - TILE

    def with_partner(whole, at):
        parts = [back[:, at * few : (at + 1) * few], last[:, at * TILE : (at + 1) * TILE]]
        parts = jnp.concatenate(parts, axis=1).astype(jnp.float32)
        return whole + jnp.where(end, parts, 0.0)

    prods_a = tile_prods(with_partner(sum_a, 0))
    prods_b = tile_prods(with_partner(sum_b, 1))
    prods_c = tile_prods(with_partner(sum_c, 2))
    to_two = pick(prods_b, prods_c)
    from_two = lax.ppermute(to_two, "cand", TWO)
    from_far = lax.ppermute(after(prods_c, to_two), ALL, far)
    from_side = lax.ppermute(after(prods_a, to_two), "cand", SIDE)
    total = pair_scores(
        (prods_own, plane),
        (from_side, plane ^ 1),
        (from_two, plane ^ 2),
        (pick(from_far, from_middle), plane ^ 3),
    )
    return final_sum(total)


def final_sum(total):
    npairs, ntest = total.shape
    blocks = total.reshape(4, npairs // 4, 4, ntest // 4).transpose(0, 2, 1, 3)
    blocks = blocks.reshape(16, npairs // 4, ntest // 4)
    return jnp.sum(lax.all_to_all(blocks, ALL, 0, 0, tiled=True), axis=0)


def gather_plan(acts, grads, basis_in, basis_out, eigval, test_grads, pair_tiles, last_rows):
    ncand = lax.axis_size("cand")
    nfeat = lax.axis_size(FEAT)
    tok_rows = acts.shape[0]
    width_in = basis_in.shape[1] * ncand
    width_out = basis_out.shape[1] * ncand
    slim = width_out // (ncand * nfeat)
    part_in = jnp.dot(
        acts,
        lax.all_gather(basis_in, "cand", axis=1, tiled=True),
        preferred_element_type=jnp.float32,
    )
    part_out = jnp.dot(
        grads,
        lax.all_gather(basis_out, "cand", axis=1, tiled=True),
        preferred_element_type=jnp.float32,
    )
    part_out = part_out.reshape(tok_rows, ncand, nfeat, slim).transpose(0, 2, 1, 3)
    part_out = part_out.reshape(tok_rows, nfeat * ncand * slim)
    summed_in, summed_out = lax.psum((part_in, part_out), FEAT)
    own = lax.dynamic_slice_in_dim(
        summed_out, lax.axis_index(FEAT) * (ncand * slim), ncand * slim, 1
    )
    rot_in = summed_in.astype(jnp.bfloat16)
    rot_out = own.astype(jnp.bfloat16)
    tiles_here = tok_rows // TILE
    rowmask, ignored = tile_layout(
        pair_tiles, last_rows, lax.axis_index("cand") * tiles_here, tiles_here, TILE
    )
    masked = rot_out.reshape(tiles_here, TILE, ncand * slim) * rowmask[:, :, None].astype(
        jnp.bfloat16
    )
    prods = jnp.einsum(
        "tre,tra->tea",
        masked,
        rot_in.reshape(tiles_here, TILE, width_in),
        preferred_element_type=jnp.float32,
    ).astype(jnp.bfloat16)
    prods = prods.reshape(tiles_here, ncand, slim, width_in)
    received = lax.all_to_all(prods, "cand", split_axis=1, concat_axis=0, tiled=True)
    all_tiles = received.shape[0]
    received = received.reshape(all_tiles, slim, width_in)
    precond = (test_grads.astype(jnp.float32) / (eigval + damping)).astype(jnp.bfloat16)
    tile_part = jnp.einsum("tea,jea->tj", received, precond, preferred_element_type=jnp.float32)
    ignored_mask, onehot = tile_layout(pair_tiles, last_rows, 0, all_tiles, TILE)
    pair_part = jnp.dot(onehot.astype(jnp.float32).T, tile_part, precision=lax.Precision.HIGHEST)
    npairs = pair_part.shape[0]
    ntest = pair_part.shape[1]
    total = lax.psum(pair_part, ("cand", "eig", "rep"))
    rows = lax.dynamic_slice_in_dim(
        total, lax.axis_index("cand") * (npairs // ncand), npairs // ncand, 0
    )
    return lax.dynamic_slice_in_dim(
        rows, lax.axis_index(FEAT) * (ntest // nfeat), ntest // nfeat, 1
    )


def solution(mesh):
    in_specs = (
        P(("groups", "cand"), ("eig", "rep")),
        P(("groups", "cand"), ("eig", "rep")),
        P(("groups", "eig", "rep"), "cand"),
        P(("groups", "eig", "rep"), "cand"),
        P(("groups", "cand", "eig", "rep"), None),
        P("groups", ("cand", "eig", "rep"), None),
        P("groups"),
        P("groups"),
    )
    out_specs = P(("groups", "cand"), ("eig", "rep"))
    sizes = (mesh.shape["cand"], mesh.shape["eig"], mesh.shape["rep"])
    per_device = line_plan if sizes == (4, 2, 2) else gather_plan
    return jax.shard_map(
        per_device, mesh=mesh, in_specs=in_specs, out_specs=out_specs, check_vma=False
    )
```

```python
import jax
import jax.numpy as jnp
from jax import lax
from jax.experimental import pallas as pl
from jax.experimental.pallas import tpu as pltpu
from jax.sharding import PartitionSpec as P

TILE = 128
FEAT = ("eig", "rep")
ALL = ("cand", "eig", "rep")
STEPS = 3
PARAMS = pltpu.CompilerParams(vmem_limit_bytes=20 << 20)
SHORT = pl.CostEstimate(flops=1, bytes_accessed=1, transcendentals=0)
SIDE = ((0, 1), (1, 0), (2, 3), (3, 2))
TWO = ((0, 2), (2, 0), (1, 3), (3, 1))

damping = 0.01


def tile_layout(pair_tiles, last_rows, first_tile, count, tile_rows):
    tiles = first_tile + jnp.arange(count, dtype=jnp.int32)
    ends = jnp.cumsum(pair_tiles)
    owner = jnp.sum((ends[None, :] <= tiles[:, None]).astype(jnp.int32), axis=1)
    onehot = owner[:, None] == jnp.arange(pair_tiles.shape[0], dtype=jnp.int32)[None, :]
    last_of = jnp.sum(jnp.where(onehot, last_rows[None, :], 0), axis=1)
    end_of = jnp.sum(jnp.where(onehot, ends[None, :], 0), axis=1)
    limit = jnp.where(tiles == end_of - 1, last_of, tile_rows)
    rowmask = jnp.arange(tile_rows, dtype=jnp.int32)[None, :] < limit[:, None]
    return (rowmask, onehot)


def after(x, *earlier):
    return lax.optimization_barrier((x, *earlier))[0]


def swap(x, axis_name):
    return lax.ppermute(x, axis_name, [(0, 1), (1, 0)])


def halves(x, axis_name):
    first = lax.axis_index(axis_name) == 0
    low, high = jnp.split(x, 2)
    return jnp.where(first, low, high), jnp.where(first, high, low)


def chip_parts(keep, received):
    keep, their_keep = halves(keep, "eig")
    received, their_received = halves(received, "eig")
    return keep + received, (their_keep + their_received).astype(jnp.bfloat16)


def chip_sum(keep, give):
    return keep + swap(give, "eig").astype(jnp.float32)


def all_rows(mine, other):
    first = lax.axis_index("rep") == 0
    mine, other = mine.reshape(2, -1, mine.shape[1]), other.reshape(2, -1, mine.shape[1])
    whole = jnp.stack([jnp.where(first, mine, other), jnp.where(first, other, mine)], axis=1)
    return whole.reshape(-1, whole.shape[-1])


def split_rows(full_ref, keep_ref, give_ref, rep, columns=None):
    rows = full_ref.shape[0] // 4
    columns = slice(None) if columns is None else columns
    for e in range(2):
        here = pl.ds(e * rows, rows)
        mine = pl.ds(pl.multiple_of((2 * e + rep) * rows, rows), rows)
        theirs = pl.ds(pl.multiple_of((2 * e + 1 - rep) * rows, rows), rows)
        keep_ref[here, columns] = full_ref[mine, :]
        give_ref[here, columns] = full_ref[theirs, :]


def add_dot(total_ref, rows_ref, shard):
    half = total_ref.shape[0] // 2
    for here in (pl.ds(0, half), pl.ds(half, half)):
        total_ref[here, :] += jnp.dot(
            rows_ref[here, :], shard, preferred_element_type=jnp.float32
        )


def feature_dots(flags, grads, segments, start=None, split=True):
    tok = grads.shape[0]
    cols = segments[0][0][0][0].shape[1]
    depth = grads.shape[1] // (3 * STEPS)
    firsts = [sum(s[3] for s in segments[:at]) for at in range(len(segments))]
    total = sum(s[3] for s in segments)

    def grads_at(i, flags_ref):
        at = 0
        for first, (choices, at_end, at_middle, steps, only) in zip(firsts, segments):
            base = at_end + flags_ref[0] * 0 if at_end == at_middle else (
                flags_ref[0] * at_end + (1 - flags_ref[0]) * at_middle
            )
            at = jnp.where(i >= first, base + i - first, at)
        return (0, at)

    def rows_at(first, steps, row, wanted):
        def index(i, flags_ref):
            step = jnp.clip(i - first, 0, steps - 1)
            if wanted is not None:
                step = step * (flags_ref[0] if wanted else 1 - flags_ref[0])
            return (row + step, 0)

        return index

    operands, specs = [grads], [pl.BlockSpec((tok, depth), grads_at)]
    for first, (choices, at_end, at_middle, steps, only) in zip(firsts, segments):
        for which, (array, row) in enumerate(choices):
            wanted = None if len(choices) == 1 else which == 0
            operands.append(array)
            specs.append(pl.BlockSpec((depth, cols), rows_at(first, steps, row, wanted)))
    if start is not None:
        operands.append(start)
        specs.append(pl.BlockSpec((tok, cols), lambda i, flags_ref: (0, 0)))

    def kernel(flags_ref, grads_ref, *refs):
        i = pl.program_id(0)
        end = flags_ref[0] == 1
        inputs, rest = list(refs[: len(operands) - 1]), refs[len(operands) - 1 :]
        if split:
            keep_ref, give_ref, total_ref, turned_ref = rest
        else:
            (total_ref,) = rest

        @pl.when(i == 0)
        def begin():
            total_ref[...] = jnp.zeros_like(total_ref) if start is None else inputs[-1][...]

        at = 0
        for first, (choices, at_end, at_middle, steps, only) in zip(firsts, segments):
            here = inputs[at : at + len(choices)]
            at += len(choices)
            active = (i >= first) & (i < first + steps)
            if only:
                active = active & (flags_ref[0] == 0)

            @pl.when(active)
            def add(here=here):
                shard = here[0][...]
                if len(here) == 2:
                    shard = jnp.where(end, shard, here[1][...])
                add_dot(total_ref, grads_ref, shard)

        if split:

            @pl.when(i == total - 1)
            def finish():
                turned_ref[...] = total_ref[...].T
                split_rows(turned_ref, keep_ref, give_ref, flags_ref[1])

    whole = lambda i, flags_ref: (0, 0)
    if split:
        out_shape = [jax.ShapeDtypeStruct((cols // 2, tok), jnp.float32)] * 2
        out_specs = [pl.BlockSpec((cols // 2, tok), whole)] * 2
        scratch = [pltpu.VMEM((tok, cols), jnp.float32), pltpu.VMEM((cols, tok), jnp.float32)]
    else:
        out_shape = jax.ShapeDtypeStruct((tok, cols), jnp.float32)
        out_specs = pl.BlockSpec((tok, cols), whole)
        scratch = []
    return pl.pallas_call(
        kernel,
        out_shape=out_shape,
        grid_spec=pltpu.PrefetchScalarGridSpec(
            num_scalar_prefetch=1,
            grid=(total,),
            in_specs=specs,
            out_specs=out_specs,
            scratch_shapes=scratch,
        ),
        compiler_params=PARAMS,
        cost_estimate=SHORT,
    )(flags, *operands)


def both_dots(flags, grads, at_end, at_middle):
    tok = grads.shape[0]
    cols = at_end[0].shape[1]
    step = grads.shape[1] // (3 * STEPS)

    def third_at(first):
        def index(i, flags_ref):
            return (jnp.clip(i - first, 0, STEPS - 1) * (1 - flags_ref[0]), 0)

        return index

    operands = [grads, at_end[0]] + [array for pair in at_middle for array in pair] + [grads]
    specs = [
        pl.BlockSpec((tok, step), lambda i, flags_ref: (0, STEPS + i)),
        pl.BlockSpec((step, cols), lambda i, flags_ref: (at_end[1] + i * flags_ref[0], 0)),
    ]
    for first in (0, STEPS):
        specs += [pl.BlockSpec((step, cols), third_at(first))] * 2
    specs.append(
        pl.BlockSpec(
            (tok, step),
            lambda i, flags_ref: (0, flags_ref[0] * STEPS + jnp.minimum(i, STEPS - 1)),
        )
    )

    def kernel(flags_ref, grads_ref, end_ref, b1_ref, c1_ref, b2_ref, c2_ref, next_ref, *out_refs):
        total_ref, handed_ref, last_ref = out_refs
        i = pl.program_id(0)

        @pl.when(i == 0)
        def begin():
            total_ref[...] = jnp.zeros_like(total_ref)

        @pl.when(i < STEPS)
        def hand_on_next():
            handed_ref[...] = next_ref[...]

        @pl.when(i >= STEPS)
        def hand_on_last():
            last_ref[...] = grads_ref[...]

        @pl.when(flags_ref[0] == 1)
        def one():
            total_ref[:, :cols] += jnp.dot(
                grads_ref[...], end_ref[...], preferred_element_type=jnp.float32
            )

        for first, b_ref, c_ref in ((0, b1_ref, c1_ref), (STEPS, b2_ref, c2_ref)):

            @pl.when((flags_ref[0] == 0) & (i >= first) & (i < first + STEPS))
            def two(b_ref=b_ref, c_ref=c_ref):
                shards = jnp.concatenate([b_ref[...], c_ref[...]], axis=1)
                total_ref[...] += jnp.dot(
                    grads_ref[...], shards, preferred_element_type=jnp.float32
                )

    third = jax.ShapeDtypeStruct((tok, STEPS * step), grads.dtype)
    return pl.pallas_call(
        kernel,
        out_shape=[jax.ShapeDtypeStruct((tok, 2 * cols), jnp.float32), third, third],
        grid_spec=pltpu.PrefetchScalarGridSpec(
            num_scalar_prefetch=1,
            grid=(2 * STEPS,),
            in_specs=specs,
            out_specs=[
                pl.BlockSpec((tok, 2 * cols), lambda i, flags_ref: (0, 0)),
                pl.BlockSpec((tok, step), lambda i, flags_ref: (0, jnp.minimum(i, STEPS - 1))),
                pl.BlockSpec((tok, step), lambda i, flags_ref: (0, jnp.maximum(i - STEPS, 0))),
            ],
        ),
        compiler_params=PARAMS,
        cost_estimate=SHORT,
    )(flags, *operands)


def partner_dots(flags, pieces, shards, grads, shard, start):
    tok = grads.shape[0]
    cols = shards[0][0].shape[1]
    step = shard[2] // STEPS
    count = len(pieces)
    two = start.shape[1] == 2 * cols
    width = tok + len(shards) * count * TILE

    def at(row):
        return lambda i, flags_ref: (row + i, 0)

    whole = lambda i, flags_ref: (0, 0)
    fetched = [shards[1][0], shards[2][0], shard[0]] if two else []
    listed = list(pieces) + list(shards) + [shard[:2]]
    places = [[array is x for x in fetched].index(True) if any(array is x for x in fetched) else None
              for array, row in listed]
    operands, specs = list(fetched), [pl.BlockSpec(memory_space=pltpu.HBM)] * len(fetched)
    for (array, row), place in zip(listed, places):
        if place is None:
            operands.append(array)
            specs.append(pl.BlockSpec((step, cols), at(row)))
    blocked = len(operands) - len(fetched)
    operands += [grads, start]
    if two:
        specs += [pl.BlockSpec(memory_space=pltpu.HBM)] * 2
    else:
        specs.append(pl.BlockSpec((tok, step), lambda i, flags_ref: (0, i)))
        specs.append(pl.BlockSpec(start.shape, whole))

    def kernel(flags_ref, *refs):
        i = pl.program_id(0)
        far_refs, block_refs = refs[: len(fetched)], list(refs[len(fetched) : len(fetched) + blocked])
        grads_ref, start_ref = refs[len(fetched) + blocked : len(operands)]
        keep_ref, give_ref, *rest = refs[len(operands) :]
        if fetched:
            *rest, held_ref, held_grads_ref, arrived = rest
            pairs = [(far_ref, held_ref.at[k]) for k, far_ref in enumerate(far_refs)]
            pairs += [(grads_ref, held_grads_ref), (start_ref, rest[1])]
            copies = [
                pltpu.make_async_copy(source, target, arrived.at[k])
                for k, (source, target) in enumerate(pairs)
            ]
            columns_here = pl.ds(pl.multiple_of(i * step, step), step)
            grads_ref = held_grads_ref.at[:, columns_here]

            @pl.when(i == 0)
            def fetch():
                for copy in copies:
                    copy.start()
                for copy in copies:
                    copy.wait()

        here = pl.ds(pl.multiple_of(i * step, step), step)
        all_refs = [
            block_refs.pop(0) if place is None else held_ref.at[place, here] for place in places
        ]
        piece_refs, shard_refs, end_ref = all_refs[:count], all_refs[count:-1], all_refs[-1]
        if two:
            second_ref, total_ref, sums_ref, turned_ref, wide_ref = rest
        else:
            total_ref, sums_ref, turned_ref, wide_ref = rest

        @pl.when(i == 0)
        def begin():
            if not two:
                total_ref[...] = start_ref[...]
            sums_ref[...] = jnp.zeros_like(sums_ref)

        @pl.when(flags_ref[0] == 1)
        def at_an_end_plane():
            total_ref[:, total_ref.shape[1] - cols :] += jnp.dot(
                grads_ref[...], end_ref[...], preferred_element_type=jnp.float32
            )

        @pl.when(flags_ref[0] == 0)
        def at_a_middle_plane():
            side_by_side = jnp.concatenate([ref[...] for ref in shard_refs], axis=1)
            tokens = jnp.concatenate(
                [
                    jnp.concatenate(
                        [ref[q * TILE : (q + 1) * TILE, :] for q in range(step // TILE)], axis=1
                    )
                    for ref in piece_refs
                ]
            )
            sums_ref[...] += jnp.dot(tokens, side_by_side, preferred_element_type=jnp.float32)
            if two:
                total_ref[...] += jnp.dot(
                    grads_ref[...], side_by_side[:, cols:], preferred_element_type=jnp.float32
                )

        @pl.when(i == STEPS - 1)
        def finish():
            wide_ref[...] = total_ref[:, :cols].T
            split_rows(wide_ref, keep_ref, give_ref, flags_ref[1], pl.ds(0, tok))
            for j in range(len(shards)):
                turned_ref[...] = sums_ref[:, j * cols : (j + 1) * cols].T
                columns = pl.ds(tok + j * count * TILE, count * TILE)
                split_rows(turned_ref, keep_ref, give_ref, flags_ref[1], columns)
            if two:
                second_ref[...] = total_ref[:, cols:]

    out_shape = [jax.ShapeDtypeStruct((cols // 2, width), jnp.float32)] * 2
    out_specs = [pl.BlockSpec((cols // 2, width), whole)] * 2
    if two:
        out_shape.append(jax.ShapeDtypeStruct((tok, cols), jnp.float32))
        out_specs.append(pl.BlockSpec((tok, cols), whole))
    return pl.pallas_call(
        kernel,
        out_shape=out_shape,
        grid_spec=pltpu.PrefetchScalarGridSpec(
            num_scalar_prefetch=1,
            grid=(STEPS,),
            in_specs=specs,
            out_specs=out_specs,
            scratch_shapes=[
                pltpu.VMEM(start.shape, jnp.float32),
                pltpu.VMEM((count * TILE, len(shards) * cols), jnp.float32),
                pltpu.VMEM((cols, count * TILE), jnp.float32),
                pltpu.VMEM((cols, tok), jnp.float32),
            ]
            + [
                pltpu.VMEM((len(fetched), STEPS * step, cols), grads.dtype),
                pltpu.VMEM((tok, STEPS * step), grads.dtype),
                pltpu.SemaphoreType.DMA((len(fetched) + 2,)),
            ]
            * bool(fetched),
        ),
        compiler_params=PARAMS,
        cost_estimate=SHORT,
    )(flags, *operands)


def stack_blocks(flags, grads, depth):
    tiles = grads.shape[0] // TILE
    firsts = [0] + list(range(tiles // 2, tiles))
    counts = [tiles // 2] + [1] * (tiles // 2)

    def kernel(flags_ref, grads_ref, *out_refs):
        t = pl.program_id(0)
        for first, count, out_ref in zip(firsts, counts, out_refs):

            @pl.when((t >= first) & (t < first + count))
            def copy(out_ref=out_ref):
                for q in range(depth // TILE):
                    here = slice(q * TILE, (q + 1) * TILE)
                    out_ref[here, :] = grads_ref[:, here]

    def place(first, count):
        return lambda t, flags_ref: (jnp.clip(t - first, 0, count - 1), 0)

    return pl.pallas_call(
        kernel,
        out_shape=[jax.ShapeDtypeStruct((count * depth, TILE), grads.dtype) for count in counts],
        grid_spec=pltpu.PrefetchScalarGridSpec(
            num_scalar_prefetch=1,
            grid=(tiles,),
            in_specs=[pl.BlockSpec((TILE, depth), lambda t, flags_ref: (t, 0))],
            out_specs=[
                pl.BlockSpec((depth, TILE), place(first, count))
                for first, count in zip(firsts, counts)
            ],
        ),
        compiler_params=PARAMS,
        cost_estimate=SHORT,
    )(flags, grads)


def input_dots(flags, acts, shards):
    tok, depth = acts.shape
    cols = shards[0][0][0].shape[1]
    operands, specs = [acts], [pl.BlockSpec((tok, depth), lambda i, flags_ref: (0, 0))]
    for choices in shards:
        for array, row in choices:
            operands.append(array)
            specs.append(pl.BlockSpec((depth, cols), lambda i, flags_ref, row=row: (row, 0)))

    def kernel(flags_ref, acts_ref, *refs):
        i = pl.program_id(0)
        inputs = list(refs[: len(operands) - 1])
        keep_ref, give_ref, part_ref = refs[len(operands) - 1 :]
        at = 0
        for slot, choices in enumerate(shards):
            here = inputs[at : at + len(choices)]
            at += len(choices)

            @pl.when(i == slot)
            def add(here=here):
                shard = here[0][...]
                if len(here) == 2:
                    shard = jnp.where(flags_ref[0] == 1, shard, here[1][...])
                part_ref[...] = jnp.dot(acts_ref[...], shard, preferred_element_type=jnp.float32)

        split_rows(part_ref, keep_ref, give_ref, flags_ref[1])

    place = pl.BlockSpec((tok // 2, cols), lambda i, flags_ref: (0, flags_ref[2 + i]))
    return pl.pallas_call(
        kernel,
        out_shape=[jax.ShapeDtypeStruct((tok // 2, cols * len(shards)), jnp.float32)] * 2,
        grid_spec=pltpu.PrefetchScalarGridSpec(
            num_scalar_prefetch=1,
            grid=(len(shards),),
            in_specs=specs,
            out_specs=[place, place],
            scratch_shapes=[pltpu.VMEM((tok, cols), jnp.float32)],
        ),
        compiler_params=PARAMS,
        cost_estimate=SHORT,
    )(flags, *operands)


def line_plan(acts, grads, basis_in, basis_out, eigval, test_grads, pair_tiles, last_rows):
    plane = lax.axis_index("cand")
    end = (plane == 0) | (plane == 3)
    tok_rows = acts.shape[0]
    cols = basis_in.shape[1]
    tiles_here = tok_rows // TILE
    slim = cols // 4
    depth = basis_out.shape[0] // 3
    rows_in = basis_in.shape[0]

    def pick(at_end, at_middle):
        return jnp.where(end, at_end, at_middle)

    def side(at_end, at_middle):
        return lax.ppermute(pick(at_end, at_middle), "cand", SIDE)

    among, far = [], []
    for at in range(16):
        between = 4 <= at < 12
        across = 12 - 4 * (at // 4) + at % 4
        among.append((at, across if between else at ^ 1))
        far.append((at, at ^ 1 if between else across))

    def middle(x):
        return lax.ppermute(x, ALL, among)

    at_b = jnp.where(end, plane ^ 2, plane ^ 3)
    at_c = jnp.where(end, plane ^ 3, plane ^ 2)
    rep = lax.axis_index("rep")
    flags = jnp.stack([end.astype(jnp.int32), rep, plane, plane ^ 1, at_b, at_c])

    rows = lax.dynamic_slice_in_dim(basis_out, jnp.where(end, 0, depth), 2 * depth, 0)
    s0 = lax.ppermute(basis_in, "cand", SIDE)
    m0 = middle(basis_in)
    s12 = lax.ppermute(rows, "cand", SIDE)
    second = basis_out[depth : 2 * depth]
    m2 = middle(second)
    started = after(flags, rows, second)
    stacked, *more_stacked = stack_blocks(started, grads, depth)
    part_own = feature_dots(
        after(started, s0, m0), grads, [([(basis_out, 0)], 0, 0, 3 * STEPS, False)]
    )
    precond = (test_grads.astype(jnp.float32) / (eigval + damping)).astype(jnp.bfloat16)
    m1 = middle(after(s0, m0))
    third = jnp.concatenate([basis_out[2 * depth :], basis_out[: 2 * rows_in - depth]])
    s3 = side(third, jnp.concatenate([m0, m1]))
    m3 = middle(after(basis_out[2 * depth :], precond, stacked, *more_stacked, *part_own))
    m5 = middle(s12[depth:])
    to_s45 = pick(stacked, jnp.concatenate([m2, m3]))
    s45 = lax.ppermute(to_s45, "cand", SIDE)
    m6 = middle(s3[:depth])
    m4 = middle(after(basis_out[:depth], m5))
    s6 = side(more_stacked[0], m5)
    to_s7 = pick(after(more_stacked[1], s45), m6)
    s7 = lax.ppermute(to_s7, "cand", SIDE)
    m7 = middle(after(s12[:depth], m6))

    part_in = input_dots(
        after(flags, s3, m5),
        acts,
        [[(basis_in, 0)], [(s0, 0)], [(s3, 0), (m0, 0)], [(s3, 1), (m1, 0)]],
    )
    part_a = feature_dots(
        after(flags, *part_in),
        grads,
        [
            ([(s12, 0)], STEPS, 0, 2 * STEPS, False),
            ([(s3, 0)], 2 * STEPS, 2 * STEPS, STEPS, True),
        ],
    )
    totals, next_grads, last_grads = both_dots(after(flags, to_s7, s45, *part_a), grads, (s45, 0), ((m2, m5), (m3, m6)))
    parts = [jnp.concatenate(part, axis=1) for part in zip(part_own, part_a)]
    keep_a, give_a = after(parts, m4, totals)
    core_a = swap(give_a, "rep")

    shards = [(basis_out, 0), (m4, 0), (m7, 0)]
    *part_b, part_c = partner_dots(
        after(flags, totals, core_a),
        [(s45, 0), (s45, STEPS), (s6, 0)],
        shards,
        next_grads,
        (s6, 0, depth),
        totals,
    )
    keep_in, give_in = after(part_in, m7, totals, core_a)
    core_in = keep_in + swap(give_in, "rep")
    give_in = core_in.astype(jnp.bfloat16)
    rows_here = chip_sum(core_in, give_in).astype(jnp.bfloat16)
    rows_there = swap(rows_here, "rep")
    rot_in = all_rows(rows_here, rows_there)
    rot_in = rot_in.reshape(tiles_here, TILE, 4 * cols)
    keep_b, give_b = part_b
    keep_b, give_b = chip_parts(
        jnp.concatenate([keep_a, keep_b], axis=1),
        jnp.concatenate([core_a, swap(give_b, "rep")], axis=1),
    )
    sums = chip_sum(keep_b, give_b)
    sum_own, sum_a, sum_b = [sums[:, i * tok_rows : (i + 1) * tok_rows] for i in range(3)]
    sums = sums[:, 3 * tok_rows :].astype(jnp.bfloat16)
    keep_last, give_last = partner_dots(
        after(flags, part_c, give_b, give_in),
        [(s7, 0)],
        shards,
        last_grads,
        (s7, 0, depth),
        part_c,
    )
    keep_last, give_last = chip_parts(keep_last, swap(give_last, "rep"))
    sum_last = chip_sum(keep_last, give_last)
    sum_c, sum_last = sum_last[:, :tok_rows], sum_last[:, tok_rows:].astype(jnp.bfloat16)

    rowmask, ignored = tile_layout(pair_tiles, last_rows, plane * tiles_here, tiles_here, TILE)
    keep = rowmask.reshape(1, tok_rows).astype(jnp.bfloat16)

    def tile_prods(rot_out):
        return jnp.einsum(
            "etr,tra->tea",
            (rot_out.astype(jnp.bfloat16) * keep).reshape(slim, tiles_here, TILE),
            rot_in,
            preferred_element_type=jnp.float32,
        ).astype(jnp.bfloat16)

    def pair_scores(*received):
        prods = jnp.concatenate([x for x, source in received])
        scores = jnp.einsum("tea,jea->tj", prods, precond, preferred_element_type=jnp.float32)
        onehot = jnp.concatenate([
            tile_layout(pair_tiles, last_rows, source * tiles_here, tiles_here, TILE)[1]
            for x, source in received
        ])
        return jnp.sum(jnp.where(onehot[:, :, None], scores[:, None, :], 0.0), axis=0)

    prods_own = tile_prods(sum_own)
    prods_middle = tile_prods(sum_b)
    from_middle = middle(prods_middle)
    last = after(lax.ppermute(after(sum_last, rows_here), "cand", SIDE), prods_middle)
    back = after(lax.ppermute(sums, "cand", SIDE), rows_there)
    few = tok_rows - TILE

    def with_partner(whole, at):
        parts = [back[:, at * few : (at + 1) * few], last[:, at * TILE : (at + 1) * TILE]]
        parts = jnp.concatenate(parts, axis=1).astype(jnp.float32)
        return whole + jnp.where(end, parts, 0.0)

    prods_a = tile_prods(with_partner(sum_a, 0))
    prods_b = tile_prods(with_partner(sum_b, 1))
    prods_c = tile_prods(with_partner(sum_c, 2))
    to_two = pick(prods_b, prods_c)
    from_two = lax.ppermute(to_two, "cand", TWO)
    from_far = lax.ppermute(after(prods_c, to_two), ALL, far)
    from_side = lax.ppermute(after(prods_a, to_two), "cand", SIDE)
    total = pair_scores(
        (prods_own, plane),
        (from_side, plane ^ 1),
        (from_two, plane ^ 2),
        (pick(from_far, from_middle), plane ^ 3),
    )
    return final_sum(total)


def final_sum(total):
    npairs, ntest = total.shape
    blocks = total.reshape(4, npairs // 4, 4, ntest // 4).transpose(0, 2, 1, 3)
    blocks = blocks.reshape(16, npairs // 4, ntest // 4)
    return jnp.sum(lax.all_to_all(blocks, ALL, 0, 0, tiled=True), axis=0)


def gather_plan(acts, grads, basis_in, basis_out, eigval, test_grads, pair_tiles, last_rows):
    ncand = lax.axis_size("cand")
    nfeat = lax.axis_size(FEAT)
    tok_rows = acts.shape[0]
    width_in = basis_in.shape[1] * ncand
    width_out = basis_out.shape[1] * ncand
    slim = width_out // (ncand * nfeat)
    part_in = jnp.dot(
        acts,
        lax.all_gather(basis_in, "cand", axis=1, tiled=True),
        preferred_element_type=jnp.float32,
    )
    part_out = jnp.dot(
        grads,
        lax.all_gather(basis_out, "cand", axis=1, tiled=True),
        preferred_element_type=jnp.float32,
    )
    part_out = part_out.reshape(tok_rows, ncand, nfeat, slim).transpose(0, 2, 1, 3)
    part_out = part_out.reshape(tok_rows, nfeat * ncand * slim)
    summed_in, summed_out = lax.psum((part_in, part_out), FEAT)
    own = lax.dynamic_slice_in_dim(
        summed_out, lax.axis_index(FEAT) * (ncand * slim), ncand * slim, 1
    )
    rot_in = summed_in.astype(jnp.bfloat16)
    rot_out = own.astype(jnp.bfloat16)
    tiles_here = tok_rows // TILE
    rowmask, ignored = tile_layout(
        pair_tiles, last_rows, lax.axis_index("cand") * tiles_here, tiles_here, TILE
    )
    masked = rot_out.reshape(tiles_here, TILE, ncand * slim) * rowmask[:, :, None].astype(
        jnp.bfloat16
    )
    prods = jnp.einsum(
        "tre,tra->tea",
        masked,
        rot_in.reshape(tiles_here, TILE, width_in),
        preferred_element_type=jnp.float32,
    ).astype(jnp.bfloat16)
    prods = prods.reshape(tiles_here, ncand, slim, width_in)
    received = lax.all_to_all(prods, "cand", split_axis=1, concat_axis=0, tiled=True)
    all_tiles = received.shape[0]
    received = received.reshape(all_tiles, slim, width_in)
    precond = (test_grads.astype(jnp.float32) / (eigval + damping)).astype(jnp.bfloat16)
    tile_part = jnp.einsum("tea,jea->tj", received, precond, preferred_element_type=jnp.float32)
    ignored_mask, onehot = tile_layout(pair_tiles, last_rows, 0, all_tiles, TILE)
    pair_part = jnp.dot(onehot.astype(jnp.float32).T, tile_part, precision=lax.Precision.HIGHEST)
    npairs = pair_part.shape[0]
    ntest = pair_part.shape[1]
    total = lax.psum(pair_part, ("cand", "eig", "rep"))
    rows = lax.dynamic_slice_in_dim(
        total, lax.axis_index("cand") * (npairs // ncand), npairs // ncand, 0
    )
    return lax.dynamic_slice_in_dim(
        rows, lax.axis_index(FEAT) * (ntest // nfeat), ntest // nfeat, 1
    )


def solution(mesh):
    in_specs = (
        P(("groups", "cand"), ("eig", "rep")),
        P(("groups", "cand"), ("eig", "rep")),
        P(("groups", "eig", "rep"), "cand"),
        P(("groups", "eig", "rep"), "cand"),
        P(("groups", "cand", "eig", "rep"), None),
        P("groups", ("cand", "eig", "rep"), None),
        P("groups"),
        P("groups"),
    )
    out_specs = P(("groups", "cand"), ("eig", "rep"))
    sizes = (mesh.shape["cand"], mesh.shape["eig"], mesh.shape["rep"])
    per_device = line_plan if sizes == (4, 2, 2) else gather_plan
    return jax.shard_map(
        per_device, mesh=mesh, in_specs=in_specs, out_specs=out_specs, check_vma=False
    )
```

```python
import jax
import jax.numpy as jnp
from jax import lax
from jax.experimental import pallas as pl
from jax.experimental.pallas import tpu as pltpu
from jax.sharding import PartitionSpec as P

TILE = 128
FEAT = ("eig", "rep")
ALL = ("cand", "eig", "rep")
STEPS = 3
PARAMS = pltpu.CompilerParams(vmem_limit_bytes=20 << 20)
SHORT = pl.CostEstimate(flops=1, bytes_accessed=1, transcendentals=0)
SIDE = ((0, 1), (1, 0), (2, 3), (3, 2))
TWO = ((0, 2), (2, 0), (1, 3), (3, 1))
THREE = ((0, 3), (3, 0), (1, 2), (2, 1))

damping = 0.01


def tile_layout(pair_tiles, last_rows, first_tile, count, tile_rows):
    tiles = first_tile + jnp.arange(count, dtype=jnp.int32)
    ends = jnp.cumsum(pair_tiles)
    owner = jnp.sum((ends[None, :] <= tiles[:, None]).astype(jnp.int32), axis=1)
    onehot = owner[:, None] == jnp.arange(pair_tiles.shape[0], dtype=jnp.int32)[None, :]
    last_of = jnp.sum(jnp.where(onehot, last_rows[None, :], 0), axis=1)
    end_of = jnp.sum(jnp.where(onehot, ends[None, :], 0), axis=1)
    limit = jnp.where(tiles == end_of - 1, last_of, tile_rows)
    rowmask = jnp.arange(tile_rows, dtype=jnp.int32)[None, :] < limit[:, None]
    return (rowmask, onehot)


def after(x, *earlier):
    return lax.optimization_barrier((x, *earlier))[0]


def swap(x, axis_name):
    return lax.ppermute(x, axis_name, [(0, 1), (1, 0)])


def halves(x, axis_name):
    first = lax.axis_index(axis_name) == 0
    low, high = jnp.split(x, 2)
    return jnp.where(first, low, high), jnp.where(first, high, low)


def chip_parts(keep, received):
    keep, their_keep = halves(keep, "eig")
    received, their_received = halves(received, "eig")
    return keep + received, (their_keep + their_received).astype(jnp.bfloat16)


def chip_sum(keep, give):
    return keep + swap(give, "eig").astype(jnp.float32)


def all_rows(mine, other):
    first = lax.axis_index("rep") == 0
    mine, other = mine.reshape(2, -1, mine.shape[1]), other.reshape(2, -1, mine.shape[1])
    whole = jnp.stack([jnp.where(first, mine, other), jnp.where(first, other, mine)], axis=1)
    return whole.reshape(-1, whole.shape[-1])


def split_rows(full_ref, keep_ref, give_ref, rep, columns=None):
    rows = full_ref.shape[0] // 4
    columns = slice(None) if columns is None else columns
    for e in range(2):
        here = pl.ds(e * rows, rows)
        mine = pl.ds(pl.multiple_of((2 * e + rep) * rows, rows), rows)
        theirs = pl.ds(pl.multiple_of((2 * e + 1 - rep) * rows, rows), rows)
        keep_ref[here, columns] = full_ref[mine, :]
        give_ref[here, columns] = full_ref[theirs, :]


def add_dot(total_ref, rows_ref, shard):
    half = total_ref.shape[0] // 2
    for here in (pl.ds(0, half), pl.ds(half, half)):
        total_ref[here, :] += jnp.dot(
            rows_ref[here, :], shard, preferred_element_type=jnp.float32
        )


def feature_dots(flags, grads, segments, start=None, split=True):
    tok = grads.shape[0]
    cols = segments[0][0][0][0].shape[1]
    depth = grads.shape[1] // (3 * STEPS)
    firsts = [sum(s[3] for s in segments[:at]) for at in range(len(segments))]
    total = sum(s[3] for s in segments)

    def grads_at(i, flags_ref):
        at = 0
        for first, (choices, at_end, at_middle, steps, only) in zip(firsts, segments):
            base = at_end + flags_ref[0] * 0 if at_end == at_middle else (
                flags_ref[0] * at_end + (1 - flags_ref[0]) * at_middle
            )
            at = jnp.where(i >= first, base + i - first, at)
        return (0, at)

    def rows_at(first, steps, row, wanted):
        def index(i, flags_ref):
            step = jnp.clip(i - first, 0, steps - 1)
            if wanted is not None:
                step = step * (flags_ref[0] if wanted else 1 - flags_ref[0])
            return (row + step, 0)

        return index

    operands, specs = [grads], [pl.BlockSpec((tok, depth), grads_at)]
    for first, (choices, at_end, at_middle, steps, only) in zip(firsts, segments):
        for which, (array, row) in enumerate(choices):
            wanted = None if len(choices) == 1 else which == 0
            operands.append(array)
            specs.append(pl.BlockSpec((depth, cols), rows_at(first, steps, row, wanted)))
    if start is not None:
        operands.append(start)
        specs.append(pl.BlockSpec((tok, cols), lambda i, flags_ref: (0, 0)))

    def kernel(flags_ref, grads_ref, *refs):
        i = pl.program_id(0)
        end = flags_ref[0] == 1
        inputs, rest = list(refs[: len(operands) - 1]), refs[len(operands) - 1 :]
        if split:
            keep_ref, give_ref, total_ref, turned_ref = rest
        else:
            (total_ref,) = rest

        @pl.when(i == 0)
        def begin():
            total_ref[...] = jnp.zeros_like(total_ref) if start is None else inputs[-1][...]

        at = 0
        for first, (choices, at_end, at_middle, steps, only) in zip(firsts, segments):
            here = inputs[at : at + len(choices)]
            at += len(choices)
            active = (i >= first) & (i < first + steps)
            if only:
                active = active & (flags_ref[0] == 0)

            @pl.when(active)
            def add(here=here):
                shard = here[0][...]
                if len(here) == 2:
                    shard = jnp.where(end, shard, here[1][...])
                add_dot(total_ref, grads_ref, shard)

        if split:

            @pl.when(i == total - 1)
            def finish():
                turned_ref[...] = total_ref[...].T
                split_rows(turned_ref, keep_ref, give_ref, flags_ref[1])

    whole = lambda i, flags_ref: (0, 0)
    if split:
        out_shape = [jax.ShapeDtypeStruct((cols // 2, tok), jnp.float32)] * 2
        out_specs = [pl.BlockSpec((cols // 2, tok), whole)] * 2
        scratch = [pltpu.VMEM((tok, cols), jnp.float32), pltpu.VMEM((cols, tok), jnp.float32)]
    else:
        out_shape = jax.ShapeDtypeStruct((tok, cols), jnp.float32)
        out_specs = pl.BlockSpec((tok, cols), whole)
        scratch = []
    return pl.pallas_call(
        kernel,
        out_shape=out_shape,
        grid_spec=pltpu.PrefetchScalarGridSpec(
            num_scalar_prefetch=1,
            grid=(total,),
            in_specs=specs,
            out_specs=out_specs,
            scratch_shapes=scratch,
        ),
        compiler_params=PARAMS,
        cost_estimate=SHORT,
    )(flags, *operands)


def both_dots(flags, grads, at_end, at_middle):
    tok = grads.shape[0]
    cols = at_end[0].shape[1]
    step = grads.shape[1] // (3 * STEPS)

    def third_at(first):
        def index(i, flags_ref):
            return (jnp.clip(i - first, 0, STEPS - 1) * (1 - flags_ref[0]), 0)

        return index

    operands = [grads, at_end[0]] + [array for pair in at_middle for array in pair] + [grads]
    specs = [
        pl.BlockSpec((tok, step), lambda i, flags_ref: (0, STEPS + i)),
        pl.BlockSpec((step, cols), lambda i, flags_ref: (at_end[1] + i * flags_ref[0], 0)),
    ]
    for first in (0, STEPS):
        specs += [pl.BlockSpec((step, cols), third_at(first))] * 2
    specs.append(
        pl.BlockSpec(
            (tok, step),
            lambda i, flags_ref: (0, flags_ref[0] * STEPS + jnp.minimum(i, STEPS - 1)),
        )
    )

    def kernel(flags_ref, grads_ref, end_ref, b1_ref, c1_ref, b2_ref, c2_ref, next_ref, *out_refs):
        total_ref, handed_ref, last_ref = out_refs
        i = pl.program_id(0)

        @pl.when(i == 0)
        def begin():
            total_ref[...] = jnp.zeros_like(total_ref)

        @pl.when(i < STEPS)
        def hand_on_next():
            handed_ref[...] = next_ref[...]

        @pl.when(i >= STEPS)
        def hand_on_last():
            last_ref[...] = grads_ref[...]

        @pl.when(flags_ref[0] == 1)
        def one():
            total_ref[:, :cols] += jnp.dot(
                grads_ref[...], end_ref[...], preferred_element_type=jnp.float32
            )

        for first, b_ref, c_ref in ((0, b1_ref, c1_ref), (STEPS, b2_ref, c2_ref)):

            @pl.when((flags_ref[0] == 0) & (i >= first) & (i < first + STEPS))
            def two(b_ref=b_ref, c_ref=c_ref):
                shards = jnp.concatenate([b_ref[...], c_ref[...]], axis=1)
                total_ref[...] += jnp.dot(
                    grads_ref[...], shards, preferred_element_type=jnp.float32
                )

    third = jax.ShapeDtypeStruct((tok, STEPS * step), grads.dtype)
    return pl.pallas_call(
        kernel,
        out_shape=[jax.ShapeDtypeStruct((tok, 2 * cols), jnp.float32), third, third],
        grid_spec=pltpu.PrefetchScalarGridSpec(
            num_scalar_prefetch=1,
            grid=(2 * STEPS,),
            in_specs=specs,
            out_specs=[
                pl.BlockSpec((tok, 2 * cols), lambda i, flags_ref: (0, 0)),
                pl.BlockSpec((tok, step), lambda i, flags_ref: (0, jnp.minimum(i, STEPS - 1))),
                pl.BlockSpec((tok, step), lambda i, flags_ref: (0, jnp.maximum(i - STEPS, 0))),
            ],
        ),
        compiler_params=PARAMS,
        cost_estimate=SHORT,
    )(flags, *operands)


def partner_dots(flags, pieces, shards, grads, shard, start):
    tok = grads.shape[0]
    cols = shards[0][0].shape[1]
    step = shard[2] // STEPS
    count = len(pieces)
    two = start.shape[1] == 2 * cols
    width = tok + len(shards) * count * TILE

    def at(row):
        return lambda i, flags_ref: (row + i, 0)

    whole = lambda i, flags_ref: (0, 0)
    fetched = [shards[1][0], shards[2][0], shard[0]] if two else []
    listed = list(pieces) + list(shards) + [shard[:2]]
    places = [[array is x for x in fetched].index(True) if any(array is x for x in fetched) else None
              for array, row in listed]
    operands, specs = list(fetched), [pl.BlockSpec(memory_space=pltpu.HBM)] * len(fetched)
    for (array, row), place in zip(listed, places):
        if place is None:
            operands.append(array)
            specs.append(pl.BlockSpec((step, cols), at(row)))
    blocked = len(operands) - len(fetched)
    operands += [grads, start]
    if two:
        specs += [pl.BlockSpec(memory_space=pltpu.HBM)] * 2
    else:
        specs.append(pl.BlockSpec((tok, step), lambda i, flags_ref: (0, i)))
        specs.append(pl.BlockSpec(start.shape, whole))

    def kernel(flags_ref, *refs):
        i = pl.program_id(0)
        far_refs, block_refs = refs[: len(fetched)], list(refs[len(fetched) : len(fetched) + blocked])
        grads_ref, start_ref = refs[len(fetched) + blocked : len(operands)]
        keep_ref, give_ref, *rest = refs[len(operands) :]
        if fetched:
            *rest, held_ref, held_grads_ref, arrived = rest
            pairs = [(far_ref, held_ref.at[k]) for k, far_ref in enumerate(far_refs)]
            pairs += [(grads_ref, held_grads_ref), (start_ref, rest[1])]
            copies = [
                pltpu.make_async_copy(source, target, arrived.at[k])
                for k, (source, target) in enumerate(pairs)
            ]
            columns_here = pl.ds(pl.multiple_of(i * step, step), step)
            grads_ref = held_grads_ref.at[:, columns_here]

            @pl.when(i == 0)
            def fetch():
                for copy in copies:
                    copy.start()
                for copy in copies:
                    copy.wait()

        here = pl.ds(pl.multiple_of(i * step, step), step)
        all_refs = [
            block_refs.pop(0) if place is None else held_ref.at[place, here] for place in places
        ]
        piece_refs, shard_refs, end_ref = all_refs[:count], all_refs[count:-1], all_refs[-1]
        if two:
            second_ref, total_ref, sums_ref, turned_ref, wide_ref = rest
        else:
            total_ref, sums_ref, turned_ref, wide_ref = rest

        @pl.when(i == 0)
        def begin():
            if not two:
                total_ref[...] = start_ref[...]
            sums_ref[...] = jnp.zeros_like(sums_ref)

        @pl.when(flags_ref[0] == 1)
        def at_an_end_plane():
            total_ref[:, total_ref.shape[1] - cols :] += jnp.dot(
                grads_ref[...], end_ref[...], preferred_element_type=jnp.float32
            )

        @pl.when(flags_ref[0] == 0)
        def at_a_middle_plane():
            side_by_side = jnp.concatenate([ref[...] for ref in shard_refs], axis=1)
            tokens = jnp.concatenate(
                [
                    jnp.concatenate(
                        [ref[q * TILE : (q + 1) * TILE, :] for q in range(step // TILE)], axis=1
                    )
                    for ref in piece_refs
                ]
            )
            sums_ref[...] += jnp.dot(tokens, side_by_side, preferred_element_type=jnp.float32)
            if two:
                total_ref[...] += jnp.dot(
                    grads_ref[...], side_by_side[:, cols:], preferred_element_type=jnp.float32
                )

        @pl.when(i == STEPS - 1)
        def finish():
            wide_ref[...] = total_ref[:, :cols].T
            split_rows(wide_ref, keep_ref, give_ref, flags_ref[1], pl.ds(0, tok))
            for j in range(len(shards)):
                turned_ref[...] = sums_ref[:, j * cols : (j + 1) * cols].T
                columns = pl.ds(tok + j * count * TILE, count * TILE)
                split_rows(turned_ref, keep_ref, give_ref, flags_ref[1], columns)
            if two:
                second_ref[...] = total_ref[:, cols:]

    out_shape = [jax.ShapeDtypeStruct((cols // 2, width), jnp.float32)] * 2
    out_specs = [pl.BlockSpec((cols // 2, width), whole)] * 2
    if two:
        out_shape.append(jax.ShapeDtypeStruct((tok, cols), jnp.float32))
        out_specs.append(pl.BlockSpec((tok, cols), whole))
    return pl.pallas_call(
        kernel,
        out_shape=out_shape,
        grid_spec=pltpu.PrefetchScalarGridSpec(
            num_scalar_prefetch=1,
            grid=(STEPS,),
            in_specs=specs,
            out_specs=out_specs,
            scratch_shapes=[
                pltpu.VMEM(start.shape, jnp.float32),
                pltpu.VMEM((count * TILE, len(shards) * cols), jnp.float32),
                pltpu.VMEM((cols, count * TILE), jnp.float32),
                pltpu.VMEM((cols, tok), jnp.float32),
            ]
            + [
                pltpu.VMEM((len(fetched), STEPS * step, cols), grads.dtype),
                pltpu.VMEM((tok, STEPS * step), grads.dtype),
                pltpu.SemaphoreType.DMA((len(fetched) + 2,)),
            ]
            * bool(fetched),
        ),
        compiler_params=PARAMS,
        cost_estimate=SHORT,
    )(flags, *operands)


def stack_blocks(flags, grads, depth):
    tiles = grads.shape[0] // TILE
    firsts = [0] + list(range(tiles // 2, tiles))
    counts = [tiles // 2] + [1] * (tiles // 2)

    def kernel(flags_ref, grads_ref, *out_refs):
        t = pl.program_id(0)
        for first, count, out_ref in zip(firsts, counts, out_refs):

            @pl.when((t >= first) & (t < first + count))
            def copy(out_ref=out_ref):
                for q in range(depth // TILE):
                    here = slice(q * TILE, (q + 1) * TILE)
                    out_ref[here, :] = grads_ref[:, here]

    def place(first, count):
        return lambda t, flags_ref: (jnp.clip(t - first, 0, count - 1), 0)

    return pl.pallas_call(
        kernel,
        out_shape=[jax.ShapeDtypeStruct((count * depth, TILE), grads.dtype) for count in counts],
        grid_spec=pltpu.PrefetchScalarGridSpec(
            num_scalar_prefetch=1,
            grid=(tiles,),
            in_specs=[pl.BlockSpec((TILE, depth), lambda t, flags_ref: (t, 0))],
            out_specs=[
                pl.BlockSpec((depth, TILE), place(first, count))
                for first, count in zip(firsts, counts)
            ],
        ),
        compiler_params=PARAMS,
        cost_estimate=SHORT,
    )(flags, grads)


def input_dots(flags, acts, shards):
    tok, depth = acts.shape
    cols = shards[0][0][0].shape[1]
    operands, specs = [acts], [pl.BlockSpec((tok, depth), lambda i, flags_ref: (0, 0))]
    for choices in shards:
        for array, row in choices:
            operands.append(array)
            specs.append(pl.BlockSpec((depth, cols), lambda i, flags_ref, row=row: (row, 0)))

    def kernel(flags_ref, acts_ref, *refs):
        i = pl.program_id(0)
        inputs = list(refs[: len(operands) - 1])
        keep_ref, give_ref, part_ref = refs[len(operands) - 1 :]
        at = 0
        for slot, choices in enumerate(shards):
            here = inputs[at : at + len(choices)]
            at += len(choices)

            @pl.when(i == slot)
            def add(here=here):
                shard = here[0][...]
                if len(here) == 2:
                    shard = jnp.where(flags_ref[0] == 1, shard, here[1][...])
                part_ref[...] = jnp.dot(acts_ref[...], shard, preferred_element_type=jnp.float32)

        split_rows(part_ref, keep_ref, give_ref, flags_ref[1])

    place = pl.BlockSpec((tok // 2, cols), lambda i, flags_ref: (0, flags_ref[2 + i]))
    return pl.pallas_call(
        kernel,
        out_shape=[jax.ShapeDtypeStruct((tok // 2, cols * len(shards)), jnp.float32)] * 2,
        grid_spec=pltpu.PrefetchScalarGridSpec(
            num_scalar_prefetch=1,
            grid=(len(shards),),
            in_specs=specs,
            out_specs=[place, place],
            scratch_shapes=[pltpu.VMEM((tok, cols), jnp.float32)],
        ),
        compiler_params=PARAMS,
        cost_estimate=SHORT,
    )(flags, *operands)


def line_plan(acts, grads, basis_in, basis_out, eigval, test_grads, pair_tiles, last_rows):
    plane = lax.axis_index("cand")
    end = (plane == 0) | (plane == 3)
    tok_rows = acts.shape[0]
    cols = basis_in.shape[1]
    tiles_here = tok_rows // TILE
    slim = cols // 4
    depth = basis_out.shape[0] // 3
    rows_in = basis_in.shape[0]

    def pick(at_end, at_middle):
        return jnp.where(end, at_end, at_middle)

    def side(at_end, at_middle):
        return lax.ppermute(pick(at_end, at_middle), "cand", SIDE)

    among, far = [], []
    for at in range(16):
        between = 4 <= at < 12
        across = 12 - 4 * (at // 4) + at % 4
        among.append((at, across if between else at ^ 1))
        far.append((at, at ^ 1 if between else across))

    def middle(x):
        return lax.ppermute(x, ALL, among)

    at_b = jnp.where(end, plane ^ 2, plane ^ 3)
    at_c = jnp.where(end, plane ^ 3, plane ^ 2)
    rep = lax.axis_index("rep")
    flags = jnp.stack([end.astype(jnp.int32), rep, plane, plane ^ 1, at_b, at_c])

    rows = lax.dynamic_slice_in_dim(basis_out, jnp.where(end, 0, depth), 2 * depth, 0)
    s0 = lax.ppermute(basis_in, "cand", SIDE)
    m0 = middle(basis_in)
    s12 = lax.ppermute(rows, "cand", SIDE)
    second = basis_out[depth : 2 * depth]
    m2 = middle(second)
    started = after(flags, rows, second)
    stacked, *more_stacked = stack_blocks(started, grads, depth)
    part_own = feature_dots(
        after(started, s0, m0), grads, [([(basis_out, 0)], 0, 0, 3 * STEPS, False)]
    )
    precond = (test_grads.astype(jnp.float32) / (eigval + damping)).astype(jnp.bfloat16)
    m1 = middle(after(s0, m0))
    third = jnp.concatenate([basis_out[2 * depth :], basis_out[: 2 * rows_in - depth]])
    s3 = side(third, jnp.concatenate([m0, m1]))
    m3 = middle(after(basis_out[2 * depth :], precond, stacked, *more_stacked, *part_own))
    m5 = middle(s12[depth:])
    to_s45 = pick(stacked, jnp.concatenate([m2, m3]))
    s45 = lax.ppermute(to_s45, "cand", SIDE)
    m6 = middle(s3[:depth])
    m4 = middle(after(basis_out[:depth], m5))
    s6 = side(more_stacked[0], m5)
    to_s7 = pick(after(more_stacked[1], s45), m6)
    s7 = lax.ppermute(to_s7, "cand", SIDE)
    m7 = middle(after(s12[:depth], m6))

    part_in = input_dots(
        after(flags, s3, m5),
        acts,
        [[(basis_in, 0)], [(s0, 0)], [(s3, 0), (m0, 0)], [(s3, 1), (m1, 0)]],
    )
    part_a = feature_dots(
        after(flags, *part_in),
        grads,
        [
            ([(s12, 0)], STEPS, 0, 2 * STEPS, False),
            ([(s3, 0)], 2 * STEPS, 2 * STEPS, STEPS, True),
        ],
    )
    totals, next_grads, last_grads = both_dots(after(flags, to_s7, s45, *part_a), grads, (s45, 0), ((m2, m5), (m3, m6)))
    parts = [jnp.concatenate(part, axis=1) for part in zip(part_own, part_a)]
    keep_a, give_a = after(parts, m4, totals)
    core_a = swap(give_a, "rep")

    shards = [(basis_out, 0), (m4, 0), (m7, 0)]
    *part_b, part_c = partner_dots(
        after(flags, totals, core_a),
        [(s45, 0), (s45, STEPS), (s6, 0)],
        shards,
        next_grads,
        (s6, 0, depth),
        totals,
    )
    keep_in, give_in = after(part_in, m7, totals, core_a)
    core_in = keep_in + swap(give_in, "rep")
    give_in = core_in.astype(jnp.bfloat16)
    rows_here = chip_sum(core_in, give_in).astype(jnp.bfloat16)
    rows_there = swap(rows_here, "rep")
    rot_in = all_rows(rows_here, rows_there)
    rot_in = rot_in.reshape(tiles_here, TILE, 4 * cols)
    keep_b, give_b = part_b
    keep_b, give_b = chip_parts(
        jnp.concatenate([keep_a, keep_b], axis=1),
        jnp.concatenate([core_a, swap(give_b, "rep")], axis=1),
    )
    sums = chip_sum(keep_b, give_b)
    sum_own, sum_a, sum_b = [sums[:, i * tok_rows : (i + 1) * tok_rows] for i in range(3)]
    sums = sums[:, 3 * tok_rows :].astype(jnp.bfloat16)
    keep_last, give_last = partner_dots(
        after(flags, part_c, give_b, give_in),
        [(s7, 0)],
        shards,
        last_grads,
        (s7, 0, depth),
        part_c,
    )
    keep_last, give_last = chip_parts(keep_last, swap(give_last, "rep"))
    sum_last = chip_sum(keep_last, give_last)
    sum_c, sum_last = sum_last[:, :tok_rows], sum_last[:, tok_rows:].astype(jnp.bfloat16)

    rowmask, ignored = tile_layout(pair_tiles, last_rows, plane * tiles_here, tiles_here, TILE)
    keep = rowmask.reshape(1, tok_rows).astype(jnp.bfloat16)

    def tile_prods(rot_out):
        return jnp.einsum(
            "etr,tra->tea",
            (rot_out.astype(jnp.bfloat16) * keep).reshape(slim, tiles_here, TILE),
            rot_in,
            preferred_element_type=jnp.float32,
        ).astype(jnp.bfloat16)

    def pair_scores(*received):
        prods = jnp.concatenate([x for x, source in received])
        scores = jnp.einsum("tea,jea->tj", prods, precond, preferred_element_type=jnp.float32)
        onehot = jnp.concatenate([
            tile_layout(pair_tiles, last_rows, source * tiles_here, tiles_here, TILE)[1]
            for x, source in received
        ])
        return jnp.sum(jnp.where(onehot[:, :, None], scores[:, None, :], 0.0), axis=0)

    prods_own = tile_prods(sum_own)
    prods_middle = tile_prods(sum_b)
    last = after(lax.ppermute(after(sum_last, rows_here), "cand", SIDE), prods_middle)
    back = after(lax.ppermute(sums, "cand", SIDE), rows_there)
    few = tok_rows - TILE

    def with_partner(whole, at):
        parts = [back[:, at * few : (at + 1) * few], last[:, at * TILE : (at + 1) * TILE]]
        parts = jnp.concatenate(parts, axis=1).astype(jnp.float32)
        return whole + jnp.where(end, parts, 0.0)

    prods_a = tile_prods(with_partner(sum_a, 0))
    prods_b = tile_prods(with_partner(sum_b, 1))
    prods_c = tile_prods(with_partner(sum_c, 2))
    to_two = pick(prods_b, prods_c)
    from_two = lax.ppermute(to_two, "cand", TWO)
    to_three = after(pick(prods_c, prods_middle), to_two)
    from_three = lax.ppermute(to_three, "cand", THREE)
    from_side = lax.ppermute(after(prods_a, to_two), "cand", SIDE)
    total = pair_scores(
        (prods_own, plane),
        (from_side, plane ^ 1),
        (from_two, plane ^ 2),
        (from_three, plane ^ 3),
    )
    return final_sum(total)


def final_sum(total):
    npairs, ntest = total.shape
    blocks = total.reshape(4, npairs // 4, 4, ntest // 4).transpose(0, 2, 1, 3)
    blocks = blocks.reshape(16, npairs // 4, ntest // 4)
    return jnp.sum(lax.all_to_all(blocks, ALL, 0, 0, tiled=True), axis=0)


def gather_plan(acts, grads, basis_in, basis_out, eigval, test_grads, pair_tiles, last_rows):
    ncand = lax.axis_size("cand")
    nfeat = lax.axis_size(FEAT)
    tok_rows = acts.shape[0]
    width_in = basis_in.shape[1] * ncand
    width_out = basis_out.shape[1] * ncand
    slim = width_out // (ncand * nfeat)
    part_in = jnp.dot(
        acts,
        lax.all_gather(basis_in, "cand", axis=1, tiled=True),
        preferred_element_type=jnp.float32,
    )
    part_out = jnp.dot(
        grads,
        lax.all_gather(basis_out, "cand", axis=1, tiled=True),
        preferred_element_type=jnp.float32,
    )
    part_out = part_out.reshape(tok_rows, ncand, nfeat, slim).transpose(0, 2, 1, 3)
    part_out = part_out.reshape(tok_rows, nfeat * ncand * slim)
    summed_in, summed_out = lax.psum((part_in, part_out), FEAT)
    own = lax.dynamic_slice_in_dim(
        summed_out, lax.axis_index(FEAT) * (ncand * slim), ncand * slim, 1
    )
    rot_in = summed_in.astype(jnp.bfloat16)
    rot_out = own.astype(jnp.bfloat16)
    tiles_here = tok_rows // TILE
    rowmask, ignored = tile_layout(
        pair_tiles, last_rows, lax.axis_index("cand") * tiles_here, tiles_here, TILE
    )
    masked = rot_out.reshape(tiles_here, TILE, ncand * slim) * rowmask[:, :, None].astype(
        jnp.bfloat16
    )
    prods = jnp.einsum(
        "tre,tra->tea",
        masked,
        rot_in.reshape(tiles_here, TILE, width_in),
        preferred_element_type=jnp.float32,
    ).astype(jnp.bfloat16)
    prods = prods.reshape(tiles_here, ncand, slim, width_in)
    received = lax.all_to_all(prods, "cand", split_axis=1, concat_axis=0, tiled=True)
    all_tiles = received.shape[0]
    received = received.reshape(all_tiles, slim, width_in)
    precond = (test_grads.astype(jnp.float32) / (eigval + damping)).astype(jnp.bfloat16)
    tile_part = jnp.einsum("tea,jea->tj", received, precond, preferred_element_type=jnp.float32)
    ignored_mask, onehot = tile_layout(pair_tiles, last_rows, 0, all_tiles, TILE)
    pair_part = jnp.dot(onehot.astype(jnp.float32).T, tile_part, precision=lax.Precision.HIGHEST)
    npairs = pair_part.shape[0]
    ntest = pair_part.shape[1]
    total = lax.psum(pair_part, ("cand", "eig", "rep"))
    rows = lax.dynamic_slice_in_dim(
        total, lax.axis_index("cand") * (npairs // ncand), npairs // ncand, 0
    )
    return lax.dynamic_slice_in_dim(
        rows, lax.axis_index(FEAT) * (ntest // nfeat), ntest // nfeat, 1
    )


def solution(mesh):
    in_specs = (
        P(("groups", "cand"), ("eig", "rep")),
        P(("groups", "cand"), ("eig", "rep")),
        P(("groups", "eig", "rep"), "cand"),
        P(("groups", "eig", "rep"), "cand"),
        P(("groups", "cand", "eig", "rep"), None),
        P("groups", ("cand", "eig", "rep"), None),
        P("groups"),
        P("groups"),
    )
    out_specs = P(("groups", "cand"), ("eig", "rep"))
    sizes = (mesh.shape["cand"], mesh.shape["eig"], mesh.shape["rep"])
    per_device = line_plan if sizes == (4, 2, 2) else gather_plan
    return jax.shard_map(
        per_device, mesh=mesh, in_specs=in_specs, out_specs=out_specs, check_vma=False
    )
```
